32 devices in a mesh: dp: 16 (over z, x, core), rep: 2 (over y).
Axes of the slice: x: 2, y: 2, z: 4, core: 2. Of those that a mesh axis runs over, the one named last changes fastest.
Arguments:
- hidden_states: bfloat16 [512, 64, 768], P(('dp', 'rep')), may hold values from -6 to 6
- image_features: bfloat16 [512, 257, 1408], P(('dp', 'rep')), may hold values from -6 to 6
- caption_lengths: int32 [512, 2], P(('dp', 'rep')), may hold values from 4 to 16
- attn_weights: bfloat16 [6, 768, 768], replicated, may hold values from -0.21875 to 0.21875
- cross_kv: bfloat16 [2, 768, 1408], replicated, may hold values from -0.15625 to 0.15625
- ffn_in: bfloat16 [2, 768, 3072], replicated, may hold values from -0.21875 to 0.21875
- ffn_out: bfloat16 [2, 3072, 768], replicated, may hold values from -0.109375 to 0.109375
- projections: bfloat16 [2, 768, 256], replicated, may hold values from -0.21875 to 0.21875
- norm_gains: float32 [4, 768], replicated, may hold values from 0.25 to 1.75
- biases: float32 [12, 768], replicated, may hold values from -1.8 to 1.8
- ffn_bias: float32 [2, 3072], replicated, may hold values from -1.8 to 1.8
- proj_bias: float32 [2, 256], replicated, may hold values from -1.8 to 1.8
- out_grad: bfloat16 [512, 64, 768], P(('dp', 'rep')), may hold values from -6 to 6
Outputs:
- layer_out: bfloat16 [512, 64, 768], P(('dp', 'rep'))
- row_loss: float32 [512], P(('dp', 'rep'))
- input_grad: float32 [512, 64, 768], P(('dp', 'rep'))
- attn_grad: float32 [6, 768, 768], P('rep', 'dp')
- cross_grad: float32 [2, 768, 1408], P('rep', 'dp')
- ffn_in_grad: float32 [2, 768, 3072], P('rep', 'dp')
- ffn_out_grad: float32 [2, 3072, 768], P('rep', 'dp')
- proj_grad: float32 [2, 768, 256], P('rep', 'dp')
- gain_grad: float32 [4, 768], P('rep', 'dp')
- bias_grad: float32 [12, 768], P('rep', 'dp')
- ffn_bias_grad: float32 [2, 3072], P('rep', 'dp')
- proj_bias_grad: float32 [2, 256], P('rep', 'dp')
The draws below stay inside these ranges and needn't reach their ends.
Inputs may be any that keep to these rules, and one draw needn't show every extreme that they name: `caption_lengths`: caption 1 starts where caption 0 ends; the slots after both captions are padding.
All inputs are finite; a program needn't handle non-finite values.
Results may differ from the reference program's by a relative error of at most 0.018.
Values may be sent and summed in bfloat16 or wider, within the bound.
No kernel may reach another device: no remote copies, remote signals or barrier semaphores. Data moves between devices by JAX's collectives and lax.ppermute only.
A program may use at most 320 MiB of HBM per device.

```python
import jax
import jax.numpy as jnp
from jax import lax

D = 768
HEADS = 12
HEAD_DIM = 64
FF = 3072
VIS = 1408
PROJ = 256
QUERIES = 32
TEXT = 32
PATCHES = 257
SLOTS = 64
ROWS = 512


def plant(entries, rng, smallest, high):
    longest = entries.shape.index(max(entries.shape))
    spots = []
    for shift in (0, 1):
        where = [jax.random.randint(jax.random.fold_in(rng, axis), (), 0, length) for axis, length in enumerate(entries.shape)]
        where[longest] = (where[longest] + shift) % entries.shape[longest]
        spots.append(tuple(where))
    return entries.at[spots[0]].set(smallest).at[spots[1]].set(high)


def raised(array, key, source, target, shards_of, factor):
    def block_of(axis_at):
        return (jnp.arange(array.shape[axis_at]) // (array.shape[axis_at] // shards_of)).reshape((-1,) + (1,) * (array.ndim - 1 - axis_at))

    first = jax.random.permutation(key, shards_of)[block_of(target)]
    other_side = (block_of(target) + shards_of // 2) % shards_of
    return jnp.where((block_of(source) == first) | (block_of(source) == other_side), factor * array, array)


def block_levels(rng, shape, cuts, least, high):
    gain, own = 1.0, jax.random.fold_in(rng, 6)
    for axis_at, parts in cuts:
        draws = jnp.exp(jax.random.uniform(jax.random.fold_in(own, axis_at), (parts,), jnp.float32, least / len(cuts), high / len(cuts)))
        gain = gain * jnp.repeat(draws, shape[axis_at] // parts).reshape([-1 if axis == axis_at else 1 for axis in range(len(shape))])
    return gain


def normal_values(rng, extent, scale, limit, split=(), held_as=jnp.bfloat16):
    loudness = block_levels(rng, extent, split, -0.22, 0.18) if split else 1.0
    entries = jax.random.normal(rng, extent, jnp.float32) * scale * loudness
    return jnp.minimum(jnp.maximum(entries, -limit), limit).astype(held_as)


def noise_with(key, dims, scale, bound, cuts, heavy, dtype=jnp.bfloat16):
    array = scale * jax.random.normal(key, dims, jnp.float32)
    if cuts:
        array = array * block_levels(key, dims, cuts, -0.22, 0.18)
    return jnp.clip(raised(array, jax.random.fold_in(key, 3), *heavy), -bound, bound).astype(dtype)


def setup_inputs(seed: int = 0) -> dict:
    key_of = jax.random.split(jax.random.key(seed), 14)
    hidden_states = noise_with(key_of[0], (ROWS, SLOTS, D), 1.0, 6.0, ((0, 32),), (0, 2, 32, 2.75))
    image_features = normal_values(key_of[1], (ROWS, PATCHES, VIS), 1.0, 6.0, ((0, 32),))
    caption_lengths = plant(jax.random.randint(key_of[2], (ROWS, 2), 4, TEXT // 2 + 1), jax.random.fold_in(key_of[2], 1), 4, (TEXT // 2 + 1) - 1).astype(jnp.int32)
    attn_weights = normal_values(key_of[3], (6, D, D), D ** -0.5, 0.21875)
    cross_kv = normal_values(key_of[4], (2, D, VIS), VIS ** -0.5, 0.15625)
    ffn_in = normal_values(key_of[5], (2, D, FF), D ** -0.5, 0.21875)
    ffn_out = normal_values(key_of[6], (2, FF, D), FF ** -0.5, 0.109375)
    projections = normal_values(key_of[7], (2, D, PROJ), D ** -0.5, 0.21875)
    norm_gains = jnp.clip(1.0 + 0.15 * jax.random.normal(key_of[8], (4, D), jnp.float32), 0.25, 1.75)
    biases = normal_values(key_of[9], (12, D), 0.3, 1.8, (), jnp.float32)
    ffn_bias = normal_values(key_of[10], (2, FF), 0.3, 1.8, (), jnp.float32)
    proj_bias = normal_values(key_of[11], (2, PROJ), 0.3, 1.8, (), jnp.float32)
    out_grad = noise_with(key_of[12], (ROWS, SLOTS, D), 1.0, 6.0, ((0, 32),), (0, 2, 32, 2.75))
    return {"hidden_states": hidden_states, "image_features": image_features, "caption_lengths": caption_lengths, "attn_weights": attn_weights, "cross_kv": cross_kv, "ffn_in": ffn_in, "ffn_out": ffn_out, "projections": projections, "norm_gains": norm_gains, "biases": biases, "ffn_bias": ffn_bias, "proj_bias": proj_bias, "out_grad": out_grad}


@jax.custom_vjp
def low(v):
    return lax.optimization_barrier(v.astype(jnp.bfloat16)).astype(jnp.float32)

@jax.custom_vjp
def low_back(v):
    return v

def low_keep(v):
    return (low(v), None)

def low_pass(kept, grad):
    return (grad,)

def back_keep(v):
    return (v, None)

def back_low(kept, grad):
    return (low(grad),)
low.defvjp(low_keep, low_pass)
low_back.defvjp(back_keep, back_low)
blocked = -1000000000.0
epsilon = 1e-06
sharpness = 14.0
loss_weight = 16.0
row_group = 32
highest = lax.Precision.HIGHEST

def round_both(values):
    return low_back(low(values))

def product(left, right):
    return jnp.einsum('...k,kn->...n', left, right, precision=highest)

def layer_norm(values, gain_row, shift_row):
    center = values - lax.optimization_barrier(jnp.mean(values, -1, keepdims=True))
    spread = lax.optimization_barrier(jnp.mean(center * center, -1, keepdims=True))
    return center * lax.rsqrt(spread + epsilon) * gain_row + shift_row

def unit_rows(values):
    return values * lax.rsqrt(lax.optimization_barrier(jnp.sum(values * values, -1, keepdims=True)) + epsilon)

def caption_layout(length_rows):
    row_count = length_rows.shape[0]
    first_len = length_rows[:, 0:1]
    second_end = first_len + length_rows[:, 1:2]
    slot_index = lax.broadcasted_iota(jnp.int32, (row_count, TEXT), 1)
    text_group = (slot_index >= first_len).astype(jnp.int32) + (slot_index >= second_end).astype(jnp.int32)
    group_ids = jnp.concatenate([jnp.full((row_count, QUERIES), -1, jnp.int32), text_group], 1)
    allowed = group_ids[:, :, None] == group_ids[:, None, :]
    head_starts = jnp.concatenate([jnp.zeros_like(first_len), first_len], 1)
    pick_mask = slot_index[:, None, :] == head_starts[:, :, None]
    return (allowed, pick_mask)

def attend(queries, key_rows, value_rows, allowed):
    query_heads = queries.reshape(queries.shape[:-1] + (HEADS, HEAD_DIM))
    key_heads = key_rows.reshape(key_rows.shape[:-1] + (HEADS, HEAD_DIM))
    value_heads = value_rows.reshape(value_rows.shape[:-1] + (HEADS, HEAD_DIM))
    scores = jnp.einsum('rqhe,rkhe->rhqk', query_heads, key_heads, precision=highest) * HEAD_DIM ** (-0.5)
    if allowed is not None:
        scores = jnp.where(allowed[:, None], scores, blocked)
    scores = low_back(scores)
    weights = low(jax.nn.softmax(scores, axis=-1))
    mixture = jnp.einsum('rhqk,rkhe->rqhe', weights, value_heads, precision=highest)
    return round_both(mixture.reshape(mixture.shape[:2] + (-1,)))

def layer_rows(inputs, images, length_rows, weights):
    attn, cross, first_ffn, second_ffn, projs, gains, biases, ffn_bias, proj_bias = weights
    allowed, pick_mask = caption_layout(length_rows)
    self_q = round_both(product(inputs, attn[0]) + biases[0])
    self_k = round_both(product(inputs, attn[1]))
    self_v = round_both(product(inputs, attn[2]) + biases[1])
    branch_one = low_back(product(attend(self_q, self_k, self_v, allowed), attn[3]) + biases[2])
    first_norm = layer_norm(inputs + branch_one, gains[0], biases[8])
    first_low = low(first_norm)
    cross_q = round_both(product(first_low[:, :QUERIES], attn[4]) + biases[3])
    cross_k = round_both(jnp.einsum('rjc,dc->rjd', images, cross[0], precision=highest))
    cross_v = round_both(jnp.einsum('rjc,dc->rjd', images, cross[1], precision=highest) + biases[4])
    branch_two = low_back(product(attend(cross_q, cross_k, cross_v, None), attn[5]) + biases[5])
    second_norm = layer_norm(first_norm[:, :QUERIES] + branch_two, gains[1], biases[9])
    query_pre = low_back(product(low(second_norm), first_ffn[0]) + ffn_bias[0])
    query_act = low(jax.nn.gelu(query_pre, approximate=False))
    branch_three = low_back(product(query_act, second_ffn[0]) + biases[6])
    query_out = layer_norm(second_norm + branch_three, gains[2], biases[10])
    text_pre = low_back(product(first_low[:, QUERIES:], first_ffn[1]) + ffn_bias[1])
    text_act = low(jax.nn.gelu(text_pre, approximate=False))
    branch_four = low_back(product(text_act, second_ffn[1]) + biases[7])
    text_out = layer_norm(first_norm[:, QUERIES:] + branch_four, gains[3], biases[11])
    query_embed = low(unit_rows(low_back(product(low(query_out), projs[0]) + proj_bias[0])))
    caption_heads = jnp.einsum('rkt,rtd->rkd', pick_mask.astype(jnp.float32), low(text_out), precision=highest)
    caption_embed = low(unit_rows(low_back(product(caption_heads, projs[1]) + proj_bias[1])))
    return (jnp.concatenate([query_out, text_out], 1), query_embed, caption_embed)

def all_rows(inputs, weights, image_features, caption_lengths):
    blocks = ROWS // row_group

    def one_block(pieces):
        block_inputs, block_images, block_lengths = pieces
        return layer_rows(block_inputs, block_images.astype(jnp.float32), block_lengths, weights)
    outputs, query_embed, caption_embed = lax.map(jax.checkpoint(one_block), (inputs.reshape(blocks, row_group, SLOTS, D), image_features.reshape(blocks, row_group, PATCHES, VIS), caption_lengths.reshape(blocks, row_group, 2)))
    outputs = outputs.reshape(ROWS, SLOTS, D)
    captions = caption_embed.reshape(2 * ROWS, PROJ)

    def affinity_block(block_embed):
        sims = low_back(jnp.einsum('rqp,cp->rqc', block_embed, captions, precision=highest))
        return lax.optimization_barrier(jnp.mean(jnp.exp(sharpness * (sims - 1.0)), 1))
    affinity = lax.map(jax.checkpoint(affinity_block), query_embed).reshape(ROWS, 2 * ROWS)
    own_block = affinity.reshape(ROWS, ROWS, 2)
    diagonal = (lax.broadcasted_iota(jnp.int32, (ROWS, ROWS), 0) == lax.broadcasted_iota(jnp.int32, (ROWS, ROWS), 1)).astype(jnp.float32)
    positive = lax.optimization_barrier(jnp.sum(own_block * diagonal[:, :, None], 1))
    row_total = lax.optimization_barrier(jnp.sum(affinity, 1))
    col_total = lax.optimization_barrier(jnp.sum(affinity, 0)).reshape(ROWS, 2)
    row_loss = jnp.log(row_total) - jnp.log(positive[:, 0]) + lax.optimization_barrier(jnp.sum(jnp.log(col_total) - jnp.log(positive), 1))
    return (outputs, row_loss)

def reference(hidden_states, image_features, caption_lengths, attn_weights, cross_kv, ffn_in, ffn_out, projections, norm_gains, biases, ffn_bias, proj_bias, out_grad):
    weights = tuple((w.astype(jnp.float32) for w in (attn_weights, cross_kv, ffn_in, ffn_out, projections, norm_gains, biases, ffn_bias, proj_bias)))
    inputs = hidden_states.astype(jnp.float32)

    def forward(input_vals, weight_vals):
        return all_rows(input_vals, weight_vals, image_features, caption_lengths)
    (outputs, row_loss), pullback = jax.vjp(forward, inputs, weights)
    input_grad, weight_grads = pullback((out_grad.astype(jnp.float32), jnp.full_like(row_loss, loss_weight)))
    return (outputs.astype(jnp.bfloat16), row_loss, input_grad, weight_grads[0], weight_grads[1], weight_grads[2], weight_grads[3], weight_grads[4], weight_grads[5], weight_grads[6], weight_grads[7], weight_grads[8])
```

```python
import functools

import jax
import jax.numpy as jnp
from jax import lax
from jax.sharding import PartitionSpec as P

HEADS = 12
HEAD_DIM = 64
QUERIES = 32
TEXT = 32


blocked = -1000000000.0
epsilon = 1e-06
sharpness = 14.0
loss_weight = 16.0


def matmul(left, right):
    return jnp.einsum("...k,kn->...n", left, right, preferred_element_type=jnp.float32)


def matmul_back(grad_rows, right):
    return jnp.einsum("...n,kn->...k", grad_rows, right, preferred_element_type=jnp.float32)


def weight_grad(left, grad_rows):
    flat_left = left.reshape(-1, left.shape[-1])
    flat_grad = grad_rows.reshape(-1, grad_rows.shape[-1])
    return jnp.einsum("tk,tn->kn", flat_left, flat_grad, preferred_element_type=jnp.float32)


def bias_sum(grad_rows):
    return jnp.sum(grad_rows.reshape(-1, grad_rows.shape[-1]), 0, dtype=jnp.float32)


def layer_norm(values, gain_row, shift_row):
    center = values - jnp.mean(values, -1, keepdims=True)
    spread = jnp.mean(center * center, -1, keepdims=True)
    return center * lax.rsqrt(spread + epsilon) * gain_row + shift_row


def norm_back(values, gain_row, shift_row, grad_rows):
    unused, pullback = jax.vjp(layer_norm, values, gain_row, shift_row)
    return pullback(grad_rows)


def unit_rows(values):
    return values * lax.rsqrt(jnp.sum(values * values, -1, keepdims=True) + epsilon)


def unit_back(values, grad_rows):
    unused, pullback = jax.vjp(unit_rows, values)
    return pullback(grad_rows)[0]


def smooth_gate(values):
    return jax.nn.gelu(values, approximate=False)


def gate_back(values, grad_rows):
    unused, pullback = jax.vjp(smooth_gate, values)
    return pullback(grad_rows)[0]


def split_heads(values):
    return values.reshape(values.shape[:-1] + (HEADS, HEAD_DIM))


def join_heads(values):
    return values.reshape(values.shape[:-2] + (-1,))


def caption_layout(length_rows):
    row_count = length_rows.shape[0]
    first_len = length_rows[:, 0:1]
    second_end = first_len + length_rows[:, 1:2]
    slot_index = lax.broadcasted_iota(jnp.int32, (row_count, TEXT), 1)
    text_group = (slot_index >= first_len).astype(jnp.int32) + (slot_index >= second_end).astype(
        jnp.int32
    )
    group_ids = jnp.concatenate([jnp.full((row_count, QUERIES), -1, jnp.int32), text_group], 1)
    allowed = group_ids[:, :, None] == group_ids[:, None, :]
    head_starts = jnp.concatenate([jnp.zeros_like(first_len), first_len], 1)
    pick_mask = slot_index[:, None, :] == head_starts[:, :, None]
    return (allowed, pick_mask)


def attn_scores(queries, key_rows, allowed):
    scores = jnp.einsum(
        "rqhe,rkhe->rhqk",
        split_heads(queries),
        split_heads(key_rows),
        preferred_element_type=jnp.float32,
    ) * HEAD_DIM ** (-0.5)
    if allowed is None:
        return scores
    return jnp.where(allowed[:, None], scores, blocked)


def attn_forward(queries, key_rows, value_rows, allowed):
    scores = attn_scores(queries, key_rows, allowed)
    maximum = jnp.max(scores, -1, keepdims=True)
    log_total = maximum + jnp.log(jnp.sum(jnp.exp(scores - maximum), -1, keepdims=True))
    weights = jnp.exp(scores - log_total).astype(jnp.bfloat16)
    mixture = jnp.einsum(
        "rhqk,rkhe->rqhe", weights, split_heads(value_rows), preferred_element_type=jnp.float32
    )
    return (join_heads(mixture).astype(jnp.bfloat16), log_total)


def attn_backward(queries, key_rows, value_rows, allowed, log_total, grad_mix):
    scores = attn_scores(queries, key_rows, allowed)
    prob_rows = jnp.exp(scores - log_total)
    grad_heads = split_heads(grad_mix)
    grad_prob = jnp.einsum(
        "rqhe,rkhe->rhqk", grad_heads, split_heads(value_rows), preferred_element_type=jnp.float32
    )
    grad_values = jnp.einsum(
        "rhqk,rqhe->rkhe",
        prob_rows.astype(jnp.bfloat16),
        grad_heads,
        preferred_element_type=jnp.float32,
    )
    grad_scores = (
        prob_rows * (grad_prob - jnp.sum(grad_prob * prob_rows, -1, keepdims=True))
    ).astype(jnp.bfloat16)
    score_scale = HEAD_DIM ** (-0.5)
    grad_queries = (
        jnp.einsum(
            "rhqk,rkhe->rqhe",
            grad_scores,
            split_heads(key_rows),
            preferred_element_type=jnp.float32,
        )
        * score_scale
    )
    grad_keys = (
        jnp.einsum(
            "rhqk,rqhe->rkhe", grad_scores, split_heads(queries), preferred_element_type=jnp.float32
        )
        * score_scale
    )
    return (
        join_heads(grad_queries).astype(jnp.bfloat16),
        join_heads(grad_keys).astype(jnp.bfloat16),
        join_heads(grad_values).astype(jnp.bfloat16),
    )


def own_bit(stage):
    axis, bit = stage
    return (lax.axis_index(axis) >> bit) & 1


def swap(values, stage, sizes):
    axis, bit = stage
    return lax.ppermute(values, axis, [(i, i ^ (1 << bit)) for i in range(sizes[axis])])


def bit_stages(sizes):
    depth = sizes["dp"].bit_length() - 1
    return [("dp", bit) for bit in range(depth)]


def pick(term, places):
    array, fixed = term
    starts = [0] * array.ndim
    extent = list(array.shape)
    for dim, place in fixed.items():
        starts[dim] = place
        extent[dim] = 1
    for dim, place in places.items():
        starts[dim] = place
        extent[dim] = 1
    return lax.dynamic_slice(array, starts, extent)


def total(terms, places):
    return sum(pick(term, places).astype(jnp.float32) for term in terms)


def halve(terms, stage, dim, sizes):
    mine = own_bit(stage)
    send = total(terms, {dim: 1 - mine}).astype(jnp.bfloat16)
    arrived = swap(send, stage, sizes)
    kept = [(array, {**fixed, dim: mine}) for array, fixed in terms]
    return kept + [(arrived, {})]


def pair_scatter(first, second, order, sizes):
    depth = sizes["dp"].bit_length() - 1

    def spread(array):
        rows, cols = array.shape
        return array.reshape((2,) * depth + (rows // sizes["dp"], cols))

    streams = [[(spread(first), {})], [(spread(second), {})]]
    for stage in order:
        if stage[0] == "rep":
            mine = own_bit(stage)
            sums = [total(terms, {}) for terms in streams]
            send = jnp.where(mine == 0, sums[1], sums[0]).astype(jnp.bfloat16)
            keep = jnp.where(mine == 0, sums[0], sums[1])
            streams = [[(keep, {}), (swap(send, stage, sizes), {})]]
        else:
            dim = depth - 1 - stage[1]
            streams = [halve(terms, stage, dim, sizes) for terms in streams]
    result = total(streams[0], {})
    return result.reshape(result.shape[-2:])


def orders(sizes):
    stages = bit_stages(sizes)
    head, mid, tail = stages[:1], stages[1:3], stages[3:]
    ring = mid + [("rep", 0)]
    return [head + ring[k:] + ring[:k] + tail for k in range(3)]


def scatter_parts(first, second, sizes):
    cols = first.shape[1]
    lanes = cols // 128
    cuts = [0, 128 * ((lanes + 2) // 3), 128 * ((2 * lanes + 2) // 3), cols]
    done = [
        pair_scatter(first[:, a:b], second[:, a:b], order, sizes)
        for a, b, order in zip(cuts[:-1], cuts[1:], orders(sizes))
    ]
    return jnp.concatenate(done, 1)


def gather_rows(values, sizes):
    stages = [("rep", 0)] + bit_stages(sizes)
    for stage in stages:
        other = swap(values, stage, sizes)
        low = own_bit(stage) == 0
        values = jnp.concatenate([jnp.where(low, values, other), jnp.where(low, other, values)], 0)
    return values


def scatter_rows(values, sizes):
    stages = bit_stages(sizes)
    depth = len(stages)
    count = values.shape[0] // (2 * sizes["dp"])
    terms = [(values.reshape((2,) * (depth + 1) + (count, values.shape[1])), {})]
    for stage in stages:
        terms = halve(terms, stage, depth - 1 - stage[1], sizes)
    terms = halve(terms, ("rep", 0), depth, sizes)
    result = total(terms, {})
    return result.reshape(result.shape[-2:])


def shards(
    hidden_states,
    image_features,
    caption_lengths,
    attn_weights,
    cross_kv,
    ffn_in,
    ffn_out,
    projections,
    norm_gains,
    biases,
    ffn_bias,
    proj_bias,
    out_grad,
    sizes,
):
    row_count = hidden_states.shape[0]
    captions_here = 2 * row_count
    allowed, pick_mask = caption_layout(caption_lengths)
    pick_low = pick_mask.astype(jnp.bfloat16)
    pick_full = pick_mask.astype(jnp.float32)
    inputs_full = hidden_states.astype(jnp.float32)
    self_q = (matmul(hidden_states, attn_weights[0]) + biases[0]).astype(jnp.bfloat16)
    self_k = matmul(hidden_states, attn_weights[1]).astype(jnp.bfloat16)
    self_v = (matmul(hidden_states, attn_weights[2]) + biases[1]).astype(jnp.bfloat16)
    self_mix, self_total = attn_forward(self_q, self_k, self_v, allowed)
    first_sum = inputs_full + matmul(self_mix, attn_weights[3]) + biases[2]
    first_norm = layer_norm(first_sum, norm_gains[0], biases[8])
    first_low = first_norm.astype(jnp.bfloat16)
    query_low = first_low[:, :QUERIES]
    text_low = first_low[:, QUERIES:]
    text_pre = matmul(text_low, ffn_in[1]) + ffn_bias[1]
    text_act = smooth_gate(text_pre).astype(jnp.bfloat16)
    fourth_sum = first_norm[:, QUERIES:] + matmul(text_act, ffn_out[1]) + biases[7]
    text_out = layer_norm(fourth_sum, norm_gains[3], biases[11])
    text_out_low = text_out.astype(jnp.bfloat16)
    caption_heads = jnp.einsum(
        "rkt,rtd->rkd", pick_low, text_out_low, preferred_element_type=jnp.float32
    ).astype(jnp.bfloat16)
    caption_raw = matmul(caption_heads, projections[1]) + proj_bias[1]
    caption_embed = unit_rows(caption_raw).astype(jnp.bfloat16).reshape(captions_here, -1)
    every_caption = gather_rows(caption_embed, sizes)
    cross_q = (matmul(query_low, attn_weights[4]) + biases[3]).astype(jnp.bfloat16)
    cross_k = jnp.einsum(
        "rjc,dc->rjd", image_features, cross_kv[0], preferred_element_type=jnp.float32
    ).astype(jnp.bfloat16)
    cross_v = (
        jnp.einsum("rjc,dc->rjd", image_features, cross_kv[1], preferred_element_type=jnp.float32)
        + biases[4]
    ).astype(jnp.bfloat16)
    cross_mix, cross_total = attn_forward(cross_q, cross_k, cross_v, None)
    second_sum = first_norm[:, :QUERIES] + matmul(cross_mix, attn_weights[5]) + biases[5]
    second_norm = layer_norm(second_sum, norm_gains[1], biases[9])
    second_low = second_norm.astype(jnp.bfloat16)
    query_pre = matmul(second_low, ffn_in[0]) + ffn_bias[0]
    query_act = smooth_gate(query_pre).astype(jnp.bfloat16)
    third_sum = second_norm + matmul(query_act, ffn_out[0]) + biases[6]
    query_out = layer_norm(third_sum, norm_gains[2], biases[10])
    layer_out = jnp.concatenate([query_out, text_out], 1).astype(jnp.bfloat16)
    query_out_low = query_out.astype(jnp.bfloat16)
    query_raw = matmul(query_out_low, projections[0]) + proj_bias[0]
    query_embed = unit_rows(query_raw).astype(jnp.bfloat16)
    sims = jnp.einsum("rqp,cp->rqc", query_embed, every_caption, preferred_element_type=jnp.float32)
    expo = jnp.exp(sharpness * (sims - 1.0))
    affinity = jnp.mean(expo, 1)
    offset = lax.axis_index(("dp", "rep")) * captions_here
    own_block = lax.dynamic_slice_in_dim(affinity, offset, captions_here, 1).reshape(
        row_count, row_count, 2
    )
    diagonal = (
        lax.broadcasted_iota(jnp.int32, (row_count, row_count), 0)
        == lax.broadcasted_iota(jnp.int32, (row_count, row_count), 1)
    ).astype(jnp.float32)
    positive = jnp.sum(own_block * diagonal[:, :, None], 1)
    row_total = jnp.sum(affinity, 1)
    partial_cols = jnp.sum(affinity, 0)
    world = sizes["dp"] * sizes["rep"]
    all_cols = jnp.sum(
        lax.all_to_all(
            jnp.broadcast_to(partial_cols[None], (world,) + partial_cols.shape),
            ("dp", "rep"),
            0,
            0,
            tiled=True,
        ),
        0,
    )
    own_cols = lax.dynamic_slice_in_dim(all_cols, offset, captions_here, 0).reshape(row_count, 2)
    inverse_all = 1.0 / all_cols
    row_loss = (
        jnp.log(row_total)
        - jnp.log(positive[:, 0])
        + jnp.sum(jnp.log(own_cols) - jnp.log(positive), 1)
    )
    grad_affinity = loss_weight * (1.0 / row_total[:, None] + inverse_all[None, :])
    pair_weight = jnp.array([2.0, 1.0], jnp.float32)
    correction = (loss_weight * diagonal[:, :, None] * pair_weight / own_block).reshape(
        row_count, captions_here
    )
    own_grad = lax.dynamic_slice_in_dim(grad_affinity, offset, captions_here, 1) - correction
    grad_affinity = lax.dynamic_update_slice_in_dim(grad_affinity, own_grad, offset, 1)
    grad_sims = (grad_affinity[:, None, :] * expo * (sharpness / QUERIES)).astype(jnp.bfloat16)
    grad_query_embed = jnp.einsum(
        "rqc,cp->rqp", grad_sims, every_caption, preferred_element_type=jnp.float32
    )
    grad_caption_embed = scatter_rows(
        jnp.einsum("rqc,rqp->cp", grad_sims, query_embed, preferred_element_type=jnp.float32).astype(
            jnp.bfloat16
        ),
        sizes,
    )
    query_raw_grad = unit_back(query_raw, grad_query_embed).astype(jnp.bfloat16)
    caption_raw_grad = unit_back(caption_raw, grad_caption_embed.reshape(row_count, 2, -1)).astype(
        jnp.bfloat16
    )
    query_proj_grad = weight_grad(query_out_low, query_raw_grad)
    caption_proj_grad = weight_grad(caption_heads, caption_raw_grad)
    grad_heads = matmul_back(caption_raw_grad, projections[1])
    grad_full = out_grad.astype(jnp.float32)
    grad_query_out = grad_full[:, :QUERIES] + matmul_back(query_raw_grad, projections[0])
    grad_text_out = grad_full[:, QUERIES:] + jnp.sum(
        pick_full[:, :, :, None] * grad_heads[:, :, None, :], 1
    )
    grad_fourth, gain_four, shift_four = norm_back(
        fourth_sum, norm_gains[3], biases[11], grad_text_out
    )
    text_branch_grad = grad_fourth.astype(jnp.bfloat16)
    text_pre_grad = gate_back(text_pre, matmul_back(text_branch_grad, ffn_out[1])).astype(
        jnp.bfloat16
    )
    grad_third, gain_three, shift_three = norm_back(
        third_sum, norm_gains[2], biases[10], grad_query_out
    )
    query_branch_grad = grad_third.astype(jnp.bfloat16)
    query_pre_grad = gate_back(query_pre, matmul_back(query_branch_grad, ffn_out[0])).astype(
        jnp.bfloat16
    )
    low = jnp.bfloat16
    ffn_in_grad = scatter_parts(
        weight_grad(second_low, query_pre_grad).astype(low),
        weight_grad(text_low, text_pre_grad).astype(low),
        sizes,
    )
    ffn_out_grad = scatter_parts(
        weight_grad(query_act, query_branch_grad).astype(low),
        weight_grad(text_act, text_branch_grad).astype(low),
        sizes,
    )
    proj_grad = pair_scatter(
        query_proj_grad.astype(low), caption_proj_grad.astype(low), orders(sizes)[0], sizes
    )
    ffn_bias_grad = jnp.stack([bias_sum(query_pre_grad), bias_sum(text_pre_grad)])
    proj_bias_grad = jnp.stack([bias_sum(query_raw_grad), bias_sum(caption_raw_grad)])
    grad_second_norm = grad_third + matmul_back(query_pre_grad, ffn_in[0])
    grad_second, gain_two, shift_two = norm_back(
        second_sum, norm_gains[1], biases[9], grad_second_norm
    )
    cross_branch_grad = grad_second.astype(jnp.bfloat16)
    cross_mix_grad = matmul_back(cross_branch_grad, attn_weights[5]).astype(jnp.bfloat16)
    cross_q_grad, cross_k_grad, cross_v_grad = attn_backward(
        cross_q, cross_k, cross_v, None, cross_total, cross_mix_grad
    )
    grad_first_norm = jnp.concatenate(
        [
            grad_second + matmul_back(cross_q_grad, attn_weights[4]),
            grad_fourth + matmul_back(text_pre_grad, ffn_in[1]),
        ],
        1,
    )
    grad_first, gain_one, shift_one = norm_back(
        first_sum, norm_gains[0], biases[8], grad_first_norm
    )
    self_branch_grad = grad_first.astype(jnp.bfloat16)
    self_mix_grad = matmul_back(self_branch_grad, attn_weights[3]).astype(jnp.bfloat16)
    self_q_grad, self_k_grad, self_v_grad = attn_backward(
        self_q, self_k, self_v, allowed, self_total, self_mix_grad
    )
    input_grad = (
        grad_first
        + matmul_back(self_q_grad, attn_weights[0])
        + matmul_back(self_k_grad, attn_weights[1])
        + matmul_back(self_v_grad, attn_weights[2])
    )
    attn_pairs = (
        (weight_grad(hidden_states, self_q_grad), weight_grad(self_mix, self_branch_grad)),
        (weight_grad(hidden_states, self_k_grad), weight_grad(query_low, cross_q_grad)),
        (weight_grad(hidden_states, self_v_grad), weight_grad(cross_mix, cross_branch_grad)),
    )
    attn_grad = jnp.stack(
        [
            pair_scatter(one.astype(low), two.astype(low), order, sizes)
            for (one, two), order in zip(attn_pairs, orders(sizes))
        ]
    )
    cross_grad = scatter_parts(
        jnp.einsum(
            "rjd,rjc->dc", cross_k_grad, image_features, preferred_element_type=jnp.float32
        ).astype(low),
        jnp.einsum(
            "rjd,rjc->dc", cross_v_grad, image_features, preferred_element_type=jnp.float32
        ).astype(low),
        sizes,
    )
    gain_grad = jnp.stack([gain_one, gain_two, gain_three, gain_four])
    bias_grad = jnp.stack(
        [
            bias_sum(self_q_grad),
            bias_sum(self_v_grad),
            bias_sum(self_branch_grad),
            bias_sum(cross_q_grad),
            bias_sum(cross_v_grad),
            bias_sum(cross_branch_grad),
            bias_sum(query_branch_grad),
            bias_sum(text_branch_grad),
            shift_one,
            shift_two,
            shift_three,
            shift_four,
        ]
    )
    vectors = (gain_grad, bias_grad, ffn_bias_grad, proj_bias_grad)

    def deal(array):
        mats, cols = array.shape
        cut = array.reshape(sizes["rep"], mats // sizes["rep"], sizes["dp"], cols // sizes["dp"])
        return cut.transpose(2, 0, 1, 3).reshape(world, -1)

    dealt = jnp.concatenate([deal(array) for array in vectors], 1)
    arrived = jnp.sum(lax.all_to_all(dealt, ("dp", "rep"), 0, 0, tiled=True), 0)
    small = []
    start = 0
    for array in vectors:
        mats, cols = array.shape[0] // sizes["rep"], array.shape[1] // sizes["dp"]
        small.append(arrived[start : start + mats * cols].reshape(mats, cols))
        start += mats * cols
    return (
        layer_out,
        row_loss,
        input_grad,
        attn_grad,
        cross_grad[None],
        ffn_in_grad[None],
        ffn_out_grad[None],
        proj_grad[None],
        small[0],
        small[1],
        small[2],
        small[3],
    )


def solution(mesh):
    placed = (
        P(("dp", "rep"), None, None),
        P(("dp", "rep"), None, None),
        P(("dp", "rep"), None),
        P(),
        P(),
        P(),
        P(),
        P(),
        P(),
        P(),
        P(),
        P(),
        P(("dp", "rep"), None, None),
    )
    sizes = dict(mesh.shape)
    return jax.shard_map(
        functools.partial(shards, sizes=sizes),
        mesh=mesh,
        in_specs=placed,
        out_specs=(
            P(("dp", "rep"), None, None),
            P(("dp", "rep")),
            P(("dp", "rep"), None, None),
            P("rep", "dp", None),
            P("rep", "dp", None),
            P("rep", "dp", None),
            P("rep", "dp", None),
            P("rep", "dp", None),
            P("rep", "dp"),
            P("rep", "dp"),
            P("rep", "dp"),
            P("rep", "dp"),
        ),
        check_vma=False,
    )
```

```python
import functools

import jax
import jax.numpy as jnp
from jax import lax
from jax.experimental import pallas as pl
from jax.experimental.pallas import tpu as pltpu
from jax.sharding import PartitionSpec as P

HEADS = 12
QUERIES = 32
TEXT = 32
SLOTS = QUERIES + TEXT


blocked = -1000000000.0
epsilon = 1e-06
sharpness = 14.0
loss_weight = 16.0


def unit_rows(values):
    return values * lax.rsqrt(jnp.sum(values * values, -1, keepdims=True) + epsilon)


def unit_back(values, grad_rows):
    unused, pullback = jax.vjp(unit_rows, values)
    return pullback(grad_rows)[0]


def caption_layout(length_rows):
    row_count = length_rows.shape[0]
    first_len = length_rows[:, 0:1]
    second_end = first_len + length_rows[:, 1:2]
    slot_index = lax.broadcasted_iota(jnp.int32, (row_count, TEXT), 1)
    text_group = (slot_index >= first_len).astype(jnp.int32) + (slot_index >= second_end).astype(
        jnp.int32
    )
    group_ids = jnp.concatenate([jnp.full((row_count, QUERIES), -1, jnp.int32), text_group], 1)
    allowed = group_ids[:, :, None] == group_ids[:, None, :]
    head_starts = jnp.concatenate([jnp.zeros_like(first_len), first_len], 1)
    pick_mask = slot_index[:, None, :] == head_starts[:, :, None]
    return (allowed, pick_mask)


f32 = jnp.float32
bf16 = jnp.bfloat16
ROOT_HALF = 0.7071067811865476
ROOT_TAU = 0.3989422804014327
MIB = 1024 * 1024


def dot_nn(a, b):
    return lax.dot_general(a, b, (((1,), (0,)), ((), ())), preferred_element_type=f32)


def dot_nt(a, b):
    return lax.dot_general(a, b, (((1,), (1,)), ((), ())), preferred_element_type=f32)


def dot_tn(a, b):
    return lax.dot_general(a, b, (((0,), (0,)), ((), ())), preferred_element_type=f32)


def whole(shape):
    return pl.BlockSpec(shape, lambda *_: (0,) * len(shape))


def held(shape, index):
    return pl.BlockSpec(shape, index, pipeline_mode=pl.Buffered(1))


def params(mib):
    return pltpu.CompilerParams(vmem_limit_bytes=mib * MIB, dimension_semantics=("arbitrary",))


def norm_parts(values):
    center = values - jnp.mean(values, -1, keepdims=True)
    scale = lax.rsqrt(jnp.mean(center * center, -1, keepdims=True) + epsilon)
    return center * scale, scale


def norm_grads(values, gain_row, grad):
    unit, scale = norm_parts(values)
    inner = grad * gain_row
    first = jnp.mean(inner, -1, keepdims=True)
    second = jnp.mean(inner * unit, -1, keepdims=True)
    return (
        scale * (inner - first - unit * second),
        jnp.sum(grad * unit, 0, keepdims=True),
        jnp.sum(grad, 0, keepdims=True),
    )


def gate_parts(u):
    size = jnp.abs(u) * ROOT_HALF
    t = 1.0 / (1.0 + 0.3275911 * size)
    bell = jnp.exp(-size * size)
    poly = t * (
        0.127414796
        + t * (-0.142248368 + t * (0.7107068705 + t * (-0.7265760135 + t * 0.5307027145)))
    )
    tail = poly * bell
    cdf = jnp.where(u > 0, 1.0 - tail, tail)
    return u * cdf, cdf + (ROOT_TAU * u) * bell


def half_lanes(rows):
    low = (lax.broadcasted_iota(jnp.int32, (rows, 128), 1) < 64).astype(f32)
    return low.astype(bf16), (1.0 - low).astype(bf16)


def spread_heads(x, low, high):
    left, right = x[:, :128], x[:, 128:]
    none = jnp.zeros_like(left)
    return jnp.concatenate(
        [
            jnp.concatenate([left * low, none], 1),
            jnp.concatenate([left * high, none], 1),
            jnp.concatenate([none, right * low], 1),
            jnp.concatenate([none, right * high], 1),
        ],
        0,
    )


def collect_heads(o, n):
    low = lax.broadcasted_iota(jnp.int32, (n, 128), 1) < 64
    left = jnp.where(low, o[:n, :128], o[n : 2 * n, :128])
    right = jnp.where(low, o[2 * n : 3 * n, 128:], o[3 * n :, 128:])
    return jnp.concatenate([left, right], 1)


def columns_softmax(scores):
    raised = jnp.exp(scores - jnp.max(scores, 0, keepdims=True))
    return raised * (1.0 / jnp.sum(raised, 0, keepdims=True))


GROUPS = HEADS // 4


def self_forward_kernel(
    x_ref, w_ref, bias_ref, gain_ref, mask_ref, q_ref, k_ref, v_ref, mix_ref, sum_ref, norm_ref
):
    x = x_ref[...]
    q_ref[...] = (dot_nn(x, w_ref[0]) + bias_ref[0:1]).astype(bf16)
    k_ref[...] = dot_nn(x, w_ref[1]).astype(bf16)
    v_ref[...] = (dot_nn(x, w_ref[2]) + bias_ref[1:2]).astype(bf16)
    low, high = half_lanes(SLOTS)

    def one_row(r, carry):
        rows = pl.ds(pl.multiple_of(r * SLOTS, SLOTS), SLOTS)
        allowed = mask_ref[r] > 0.0
        for g in range(GROUPS):
            cols = slice(g * 256, (g + 1) * 256)
            queries = spread_heads(q_ref[rows, cols] * bf16(0.125), low, high)
            scores = jnp.where(allowed, dot_nt(k_ref[rows, cols], queries), blocked)
            prob = columns_softmax(scores).astype(bf16)
            mixed = dot_tn(prob, v_ref[rows, cols])
            mix_ref[rows, cols] = collect_heads(mixed, SLOTS).astype(bf16)
        return carry

    lax.fori_loop(0, x_ref.shape[0] // SLOTS, one_row, 0)
    total = x.astype(f32) + dot_nn(mix_ref[...], w_ref[3]) + bias_ref[2:3]
    sum_ref[...] = total
    unit, _ = norm_parts(total)
    norm_ref[...] = unit * gain_ref[0:1] + bias_ref[8:9]


def self_forward(x, weights, biases, gains, mask):
    tokens, width = x.shape
    step = 4 * SLOTS
    tile = pl.BlockSpec((step, width), lambda i: (i, 0))
    low, full = jax.ShapeDtypeStruct(x.shape, bf16), jax.ShapeDtypeStruct(x.shape, f32)
    return pl.pallas_call(
        self_forward_kernel,
        grid=(tokens // step,),
        in_specs=[
            tile,
            held((4, width, width), lambda i: (0, 0, 0)),
            whole(biases.shape),
            whole(gains.shape),
            pl.BlockSpec((4,) + mask.shape[1:], lambda i: (i, 0, 0)),
        ],
        out_specs=[tile] * 6,
        out_shape=[low, low, low, low, full, full],
        compiler_params=params(40),
        name="self_forward",
    )(x, weights, biases, gains, mask)


def self_backward_kernel(
    x_ref,
    w_ref,
    gain_ref,
    mask_ref,
    q_ref,
    k_ref,
    v_ref,
    mix_ref,
    sum_ref,
    top_ref,
    low_ref,
    dx_ref,
    dw_ref,
    side_ref,
    dq_all,
    dk_all,
    dv_all,
    branch_all,
    dmix_all,
):
    step = pl.program_id(0)
    count = sum_ref.shape[0]
    steps = x_ref.shape[0] // count
    low, high = half_lanes(SLOTS)

    @pl.when(step == 0)
    def _():
        side_ref[...] = jnp.zeros_like(side_ref)

    @pl.when(step < steps)
    def _():
        base = pl.multiple_of(step * count, count)
        here = pl.ds(base, count)
        grad = jnp.concatenate([top_ref[...], low_ref[...]], 1).reshape(count, -1)
        down, dgain, dshift = norm_grads(sum_ref[...], gain_ref[0:1], grad)
        branch = down.astype(bf16)
        branch_all[here] = branch
        dmix_all[...] = dot_nt(branch, w_ref[3]).astype(bf16)

        def one_row(r, carry):
            local = pl.ds(pl.multiple_of(r * SLOTS, SLOTS), SLOTS)
            rows = pl.ds(pl.multiple_of(base + r * SLOTS, SLOTS), SLOTS)
            allowed = mask_ref[r] > 0.0
            for g in range(GROUPS):
                cols = slice(g * 256, (g + 1) * 256)
                keys = k_ref[local, cols]
                queries = spread_heads(q_ref[local, cols] * bf16(0.125), low, high)
                outs = spread_heads(dmix_all[local, cols], low, high)
                prob = columns_softmax(jnp.where(allowed, dot_nt(keys, queries), blocked))
                dprob = dot_nt(v_ref[local, cols], outs)
                dscore = (prob * (dprob - jnp.sum(dprob * prob, 0, keepdims=True))).astype(bf16)
                dv_all[rows, cols] = dot_nn(prob.astype(bf16), outs).astype(bf16)
                dk_all[rows, cols] = dot_nn(dscore, queries).astype(bf16)
                dq_all[rows, cols] = (collect_heads(dot_tn(dscore, keys), SLOTS) * 0.125).astype(bf16)
            return carry

        lax.fori_loop(0, count // SLOTS, one_row, 0)
        dq, dk, dv = dq_all[here], dk_all[here], dv_all[here]
        dx_ref[...] = down + dot_nt(dq, w_ref[0]) + dot_nt(dk, w_ref[1]) + dot_nt(dv, w_ref[2])
        side_ref[0:1] += dgain
        side_ref[1:2] += dshift
        for place, rows in enumerate((dq, dv, branch)):
            side_ref[2 + place : 3 + place] += jnp.sum(rows.astype(f32), 0, keepdims=True)

    for place, right in enumerate((dq_all, dk_all, dv_all, branch_all)):

        @pl.when(step == steps + place)
        def _():
            left = mix_ref if place == 3 else x_ref
            dw_ref[0] = dot_tn(left[...], right[...]).astype(bf16)


def self_backward(x, weights, gains, mask, q, k, v, mix, total, top, text):
    tokens, width = x.shape
    count = 4 * SLOTS
    steps = tokens // count

    def near(i):
        return jnp.minimum(i, steps - 1)

    tile = pl.BlockSpec((count, width), lambda i: (near(i), 0))
    part = pl.BlockSpec((4, QUERIES, width), lambda i: (near(i), 0, 0))
    scratch = pltpu.VMEM((tokens, width), bf16)
    return pl.pallas_call(
        self_backward_kernel,
        grid=(steps + 4,),
        in_specs=[
            held(x.shape, lambda i: (0, 0)),
            held((4, width, width), lambda i: (0, 0, 0)),
            whole(gains.shape),
            pl.BlockSpec((4,) + mask.shape[1:], lambda i: (near(i), 0, 0)),
            tile,
            tile,
            tile,
            held(x.shape, lambda i: (0, 0)),
            tile,
            part,
            part,
        ],
        out_specs=[
            tile,
            pl.BlockSpec((1, width, width), lambda i: (jnp.maximum(i - steps, 0), 0, 0)),
            whole((8, width)),
        ],
        out_shape=[
            jax.ShapeDtypeStruct(x.shape, f32),
            jax.ShapeDtypeStruct((4, width, width), bf16),
            jax.ShapeDtypeStruct((8, width), f32),
        ],
        scratch_shapes=[scratch] * 4 + [pltpu.VMEM((count, width), bf16)],
        compiler_params=params(48),
        name="self_backward",
    )(x, weights, gains, mask, q, k, v, mix, total, top, text)


TAIL = 16


def cross_forward_kernel(
    image_ref,
    end_ref,
    kv_ref,
    w_ref,
    bias_ref,
    gain_ref,
    norm_ref,
    key_ref,
    value_ref,
    key_end_ref,
    value_end_ref,
    q_ref,
    mix_ref,
    sum_ref,
    out_ref,
):
    rows_here = image_ref.shape[0]
    main = image_ref.shape[1] - 1
    width = norm_ref.shape[-1]
    end = end_ref[...].reshape(rows_here * TAIL, -1)
    key_end_ref[...] = dot_nt(end, kv_ref[0]).astype(bf16)
    value_end_ref[...] = (dot_nt(end, kv_ref[1]) + bias_ref[4:5]).astype(bf16)
    residual = norm_ref[...].reshape(rows_here * QUERIES, width)
    q_ref[...] = (dot_nn(residual.astype(bf16), w_ref[0]) + bias_ref[3:4]).astype(bf16)
    low, high = half_lanes(QUERIES)
    shown = lax.broadcasted_iota(jnp.int32, (main + TAIL, 128), 0) <= main

    def one_row(r, carry):
        span = pl.ds(pl.multiple_of(r * main, main), main)
        last = pl.ds(pl.multiple_of(r * TAIL, TAIL), TAIL)
        mine = pl.ds(pl.multiple_of(r * QUERIES, QUERIES), QUERIES)
        tokens = image_ref[r, :main]
        key_ref[span] = dot_nt(tokens, kv_ref[0]).astype(bf16)
        value_ref[span] = (dot_nt(tokens, kv_ref[1]) + bias_ref[4:5]).astype(bf16)
        for g in range(GROUPS):
            cols = slice(g * 256, (g + 1) * 256)
            keys = jnp.concatenate([key_ref[span, cols], key_end_ref[last, cols]], 0)
            values = jnp.concatenate([value_ref[span, cols], value_end_ref[last, cols]], 0)
            queries = spread_heads(q_ref[mine, cols] * bf16(0.125), low, high)
            prob = columns_softmax(jnp.where(shown, dot_nt(keys, queries), blocked)).astype(bf16)
            mix_ref[mine, cols] = collect_heads(dot_tn(prob, values), QUERIES).astype(bf16)
        return carry

    lax.fori_loop(0, rows_here, one_row, 0)
    total = residual + dot_nn(mix_ref[...], w_ref[1]) + bias_ref[5:6]
    sum_ref[...] = total
    unit, _ = norm_parts(total)
    out_ref[...] = unit * gain_ref[1:2] + bias_ref[9:10]


def cross_forward(images, ends, kv, weights, biases, gains, norm):
    rows, patches, vis = images.shape
    main = patches - 1
    width = norm.shape[-1]
    take = 4
    keys = pl.BlockSpec((take * main, width), lambda i: (i, 0))
    tails = pl.BlockSpec((take * TAIL, width), lambda i: (i, 0))
    tile = pl.BlockSpec((take * QUERIES, width), lambda i: (i, 0))

    def shape(count, dtype):
        return jax.ShapeDtypeStruct((rows * count, width), dtype)

    return pl.pallas_call(
        cross_forward_kernel,
        grid=(rows // take,),
        in_specs=[
            pl.BlockSpec((take, patches, vis), lambda i: (i, 0, 0)),
            pl.BlockSpec((take, TAIL, vis), lambda i: (i, 0, 0)),
            held(kv.shape, lambda i: (0, 0, 0)),
            held((2, width, width), lambda i: (2, 0, 0)),
            whole(biases.shape),
            whole(gains.shape),
            pl.BlockSpec((take, QUERIES, width), lambda i: (i, 0, 0)),
        ],
        out_specs=[keys, keys, tails, tails, tile, tile, tile, tile],
        out_shape=[
            shape(main, bf16),
            shape(main, bf16),
            shape(TAIL, bf16),
            shape(TAIL, bf16),
            shape(QUERIES, bf16),
            shape(QUERIES, bf16),
            shape(QUERIES, f32),
            shape(QUERIES, f32),
        ],
        compiler_params=params(48),
        name="cross_forward",
    )(images, ends, kv, weights, biases, gains, norm)


def cross_backward_kernel(
    image_ref,
    end_ref,
    w_ref,
    norm_ref,
    key_ref,
    value_ref,
    key_end_ref,
    value_end_ref,
    q_ref,
    mix_ref,
    down_ref,
    dnorm_ref,
    dkey_w_ref,
    dvalue_w_ref,
    dw_ref,
    side_ref,
    key_sum,
    value_sum,
    w_sum,
    dkey,
    dvalue,
    dkey_end,
    dvalue_end,
    dq_all,
    dmix_all,
):
    step = pl.program_id(0)
    rows_here = image_ref.shape[0]
    main = image_ref.shape[1] - 1
    width = norm_ref.shape[-1]
    low, high = half_lanes(QUERIES)
    shown = lax.broadcasted_iota(jnp.int32, (main + TAIL, 128), 0) <= main

    @pl.when(step == 0)
    def _():
        side_ref[...] = jnp.zeros_like(side_ref)
        key_sum[...] = jnp.zeros_like(key_sum)
        value_sum[...] = jnp.zeros_like(value_sum)
        w_sum[...] = jnp.zeros_like(w_sum)

    down = down_ref[...]
    branch = down.astype(bf16)
    dmix_all[...] = dot_nt(branch, w_ref[1]).astype(bf16)

    def one_row(r, carry):
        span = pl.ds(pl.multiple_of(r * main, main), main)
        last = pl.ds(pl.multiple_of(r * TAIL, TAIL), TAIL)
        mine = pl.ds(pl.multiple_of(r * QUERIES, QUERIES), QUERIES)
        for g in range(GROUPS):
            cols = slice(g * 256, (g + 1) * 256)
            keys = jnp.concatenate([key_ref[span, cols], key_end_ref[last, cols]], 0)
            values = jnp.concatenate([value_ref[span, cols], value_end_ref[last, cols]], 0)
            queries = spread_heads(q_ref[mine, cols] * bf16(0.125), low, high)
            outs = spread_heads(dmix_all[mine, cols], low, high)
            prob = columns_softmax(jnp.where(shown, dot_nt(keys, queries), blocked))
            dprob = dot_nt(values, outs)
            dscore = (prob * (dprob - jnp.sum(dprob * prob, 0, keepdims=True))).astype(bf16)
            dv = dot_nn(prob.astype(bf16), outs).astype(bf16)
            dk = dot_nn(dscore, queries).astype(bf16)
            dvalue[span, cols] = dv[:main]
            dvalue_end[last, cols] = dv[main:]
            dkey[span, cols] = dk[:main]
            dkey_end[last, cols] = dk[main:]
            dq_all[mine, cols] = (collect_heads(dot_tn(dscore, keys), QUERIES) * 0.125).astype(bf16)
        return carry

    lax.fori_loop(0, rows_here, one_row, 0)
    end = end_ref[...].reshape(rows_here * TAIL, -1)
    for grads, grads_end, gathered in ((dkey, dkey_end, key_sum), (dvalue, dvalue_end, value_sum)):
        gathered[...] += dot_tn(grads_end[...], end)

        def add_row(r, carry):
            span = pl.ds(pl.multiple_of(r * main, main), main)
            gathered[...] += dot_tn(grads[span], image_ref[r, :main])
            return carry

        lax.fori_loop(0, rows_here, add_row, 0)
    dq = dq_all[...]
    dnorm_ref[...] = (down + dot_nt(dq, w_ref[0])).reshape(rows_here, QUERIES, width)
    low_norm = norm_ref[...].reshape(rows_here * QUERIES, width).astype(bf16)
    w_sum[0] += dot_tn(low_norm, dq)
    w_sum[1] += dot_tn(mix_ref[...], branch)
    side_ref[0:1] += jnp.sum(dq.astype(f32), 0, keepdims=True)
    side_ref[1:2] += jnp.sum(dvalue[...].astype(f32), 0, keepdims=True) + jnp.sum(
        dvalue_end[...].astype(f32), 0, keepdims=True
    )
    side_ref[2:3] += jnp.sum(branch.astype(f32), 0, keepdims=True)

    @pl.when(step == pl.num_programs(0) - 1)
    def _():
        dkey_w_ref[...] = key_sum[...].astype(bf16)
        dvalue_w_ref[...] = value_sum[...].astype(bf16)
        dw_ref[...] = w_sum[...].astype(bf16)


def cross_backward(images, ends, weights, norm, keys, values, key_ends, value_ends, q, mix, down):
    rows, patches, vis = images.shape
    main = patches - 1
    width = norm.shape[-1]
    take = 2
    span = pl.BlockSpec((take * main, width), lambda i: (i, 0))
    tails = pl.BlockSpec((take * TAIL, width), lambda i: (i, 0))
    tile = pl.BlockSpec((take * QUERIES, width), lambda i: (i, 0))
    part = pl.BlockSpec((take, QUERIES, width), lambda i: (i, 0, 0))
    return pl.pallas_call(
        cross_backward_kernel,
        grid=(rows // take,),
        in_specs=[
            pl.BlockSpec((take, patches, vis), lambda i: (i, 0, 0)),
            pl.BlockSpec((take, TAIL, vis), lambda i: (i, 0, 0)),
            held((2, width, width), lambda i: (2, 0, 0)),
            part,
            span,
            span,
            tails,
            tails,
            tile,
            tile,
            tile,
        ],
        out_specs=[
            part,
            held((width, vis), lambda i: (0, 0)),
            held((width, vis), lambda i: (0, 0)),
            held((2, width, width), lambda i: (0, 0, 0)),
            whole((8, width)),
        ],
        out_shape=[
            jax.ShapeDtypeStruct((rows, QUERIES, width), f32),
            jax.ShapeDtypeStruct((width, vis), bf16),
            jax.ShapeDtypeStruct((width, vis), bf16),
            jax.ShapeDtypeStruct((2, width, width), bf16),
            jax.ShapeDtypeStruct((8, width), f32),
        ],
        scratch_shapes=[
            pltpu.VMEM((width, vis), f32),
            pltpu.VMEM((width, vis), f32),
            pltpu.VMEM((2, width, width), f32),
            pltpu.VMEM((take * main, width), bf16),
            pltpu.VMEM((take * main, width), bf16),
            pltpu.VMEM((take * TAIL, width), bf16),
            pltpu.VMEM((take * TAIL, width), bf16),
            pltpu.VMEM((take * QUERIES, width), bf16),
            pltpu.VMEM((take * QUERIES, width), bf16),
        ],
        compiler_params=params(52),
        name="cross_backward",
    )(images, ends, weights, norm, keys, values, key_ends, value_ends, q, mix, down)


def ffn_forward_kernel(
    which,
    norm_ref,
    in_ref,
    in_bias_ref,
    out_ref,
    proj_ref,
    proj_bias_ref,
    bias_ref,
    gain_ref,
    *rest,
):
    act_ref, slope_ref, sum_ref, low_ref, raw_ref, embed_ref, rows_low = rest[-7:]
    step = pl.program_id(0)
    tokens, width = sum_ref.shape

    @pl.when(step == 0)
    def _():
        full = norm_ref[...].reshape(tokens, width)
        rows_low[...] = full.astype(bf16)
        sum_ref[...] = full + bias_ref[6 + which : 7 + which]

    u = dot_nn(rows_low[...], in_ref[0]) + in_bias_ref[which : which + 1]
    act, slope = gate_parts(u)
    act = act.astype(bf16)
    act_ref[...] = act
    slope_ref[...] = slope.astype(bf16)
    sum_ref[...] += dot_nn(act, out_ref[0])

    @pl.when(step == pl.num_programs(0) - 1)
    def _():
        unit, _ = norm_parts(sum_ref[...])
        low = (unit * gain_ref[2 + which : 3 + which] + bias_ref[10 + which : 11 + which]).astype(bf16)
        low_ref[...] = low.reshape(low_ref.shape)
        raw = dot_nn(low, proj_ref[0]) + proj_bias_ref[which : which + 1]
        raw_ref[...] = raw
        size = lax.rsqrt(jnp.sum(raw * raw, -1, keepdims=True) + epsilon)
        embed_ref[...] = (raw * size).astype(bf16)


def ffn_forward(which, part, norm, ffn_in, ffn_bias, ffn_out, projections, proj_bias, biases, gains, layer):
    rows, width = norm.shape[0], norm.shape[-1]
    tokens = rows * QUERIES
    hidden = ffn_in.shape[2]
    embed = projections.shape[2]
    chunk = 512
    cols = pl.BlockSpec((tokens, chunk), lambda j: (0, j))
    halves = [] if layer is None else [layer]
    return pl.pallas_call(
        functools.partial(ffn_forward_kernel, which),
        grid=(hidden // chunk,),
        in_specs=[
            held((rows, QUERIES, width), lambda j: (0, part, 0)),
            pl.BlockSpec((1, width, chunk), lambda j: (which, 0, j)),
            pl.BlockSpec((2, chunk), lambda j: (0, j)),
            pl.BlockSpec((1, chunk, width), lambda j: (which, j, 0)),
            held((1, width, embed), lambda j: (which, 0, 0)),
            whole(proj_bias.shape),
            whole(biases.shape),
            whole(gains.shape),
        ]
        + [pl.BlockSpec(memory_space=pl.ANY)] * len(halves),
        out_specs=[
            cols,
            cols,
            whole((tokens, width)),
            pl.BlockSpec((rows, QUERIES, width), lambda j: (0, which, 0)),
            whole((tokens, embed)),
            whole((tokens, embed)),
        ],
        out_shape=[
            jax.ShapeDtypeStruct((tokens, hidden), bf16),
            jax.ShapeDtypeStruct((tokens, hidden), bf16),
            jax.ShapeDtypeStruct((tokens, width), f32),
            jax.ShapeDtypeStruct((rows, SLOTS, width), bf16),
            jax.ShapeDtypeStruct((tokens, embed), f32),
            jax.ShapeDtypeStruct((tokens, embed), bf16),
        ],
        scratch_shapes=[pltpu.VMEM((tokens, width), bf16)],
        input_output_aliases={8: 3} if halves else {},
        compiler_params=params(48),
        name="ffn_forward",
    )(norm, ffn_in, ffn_bias, ffn_out, projections, proj_bias, biases, gains, *halves)


def ffn_backward_kernel(
    which,
    norm_ref,
    sum_ref,
    before_ref,
    layer_ref,
    grad_ref,
    raw_ref,
    proj_ref,
    gain_ref,
    in_ref,
    out_ref,
    act_ref,
    slope_ref,
    down_ref,
    din_ref,
    dout_ref,
    dproj_ref,
    side_ref,
    dbias_ref,
    dproj_bias_ref,
    branch_all,
    low_turned,
    rest,
):
    step = pl.program_id(0)
    tokens, width = sum_ref.shape

    @pl.when(step == 0)
    def _():
        raw = raw_ref[...]
        grad = grad_ref[...].reshape(tokens, width).astype(f32) + dot_nt(raw, proj_ref[0])
        down, dgain, dshift = norm_grads(sum_ref[...], gain_ref[2 + which : 3 + which], grad)
        branch = down.astype(bf16)
        branch_all[...] = branch
        rest[...] = down
        side_ref[...] = jnp.zeros_like(side_ref)
        side_ref[0:1] = dgain
        side_ref[1:2] = dshift
        side_ref[2:3] = jnp.sum(branch.astype(f32), 0, keepdims=True)
        dproj_ref[...] = dot_tn(layer_ref[...].reshape(tokens, width), raw).astype(bf16)
        dproj_bias_ref[...] = jnp.broadcast_to(
            jnp.sum(raw.astype(f32), 0, keepdims=True), dproj_bias_ref.shape
        )
        low_turned[...] = norm_ref[...].reshape(tokens, width).astype(bf16).T

    branch = branch_all[...]
    du = (dot_nt(branch, out_ref[0]) * slope_ref[...].astype(f32)).astype(bf16)
    rest[...] += dot_nt(du, in_ref[0])
    dout_ref[...] = dot_tn(act_ref[...], branch).astype(bf16)
    din_ref[...] = dot_nn(low_turned[...], du).astype(bf16)
    dbias_ref[...] = jnp.broadcast_to(jnp.sum(du.astype(f32), 0, keepdims=True), dbias_ref.shape)

    @pl.when(step == pl.num_programs(0) - 1)
    def _():
        if which == 0:
            down, dgain, dshift = norm_grads(before_ref[...], gain_ref[1:2], rest[...])
            side_ref[3:4] = dgain
            side_ref[4:5] = dshift
            down_ref[...] = down.reshape(down_ref.shape)
        else:
            down_ref[...] = rest[...].reshape(down_ref.shape)


def ffn_backward(
    which, part, norm, total, before, layer, grad, raw, projections, gains, ffn_in, ffn_out, act, slope
):
    rows = layer.shape[0]
    tokens, width = total.shape
    hidden = ffn_in.shape[2]
    embed = projections.shape[2]
    chunk = 512
    cols = pl.BlockSpec((tokens, chunk), lambda j: (0, j))
    before_spec = held(before.shape, lambda j: (0, 0))
    return pl.pallas_call(
        functools.partial(ffn_backward_kernel, which),
        grid=(hidden // chunk,),
        in_specs=[
            held((rows, QUERIES, width), lambda j: (0, part, 0)),
            held((tokens, width), lambda j: (0, 0)),
            before_spec,
            held((rows, QUERIES, width), lambda j: (0, which, 0)),
            held((rows, QUERIES, width), lambda j: (0, which, 0)),
            held((tokens, embed), lambda j: (0, 0)),
            held((1, width, embed), lambda j: (which, 0, 0)),
            whole(gains.shape),
            pl.BlockSpec((1, width, chunk), lambda j: (which, 0, j)),
            pl.BlockSpec((1, chunk, width), lambda j: (which, j, 0)),
            cols,
            cols,
        ],
        out_specs=[
            whole((rows, QUERIES, width)),
            pl.BlockSpec((width, chunk), lambda j: (0, j)),
            pl.BlockSpec((chunk, width), lambda j: (j, 0)),
            whole((width, embed)),
            whole((8, width)),
            pl.BlockSpec((8, chunk), lambda j: (0, j)),
            whole((8, embed)),
        ],
        out_shape=[
            jax.ShapeDtypeStruct((rows, QUERIES, width), f32),
            jax.ShapeDtypeStruct((width, hidden), bf16),
            jax.ShapeDtypeStruct((hidden, width), bf16),
            jax.ShapeDtypeStruct((width, embed), bf16),
            jax.ShapeDtypeStruct((8, width), f32),
            jax.ShapeDtypeStruct((8, hidden), f32),
            jax.ShapeDtypeStruct((8, embed), f32),
        ],
        scratch_shapes=[
            pltpu.VMEM((tokens, width), bf16),
            pltpu.VMEM((width, tokens), bf16),
            pltpu.VMEM((tokens, width), f32),
        ],
        compiler_params=params(52),
        name="ffn_backward",
    )(norm, total, before, layer, grad, raw, projections, gains, ffn_in, ffn_out, act, slope)


def own_bit(stage):
    axis, bit = stage
    return (lax.axis_index(axis) >> bit) & 1


def swap(values, stage, sizes):
    axis, bit = stage
    return lax.ppermute(values, axis, [(i, i ^ (1 << bit)) for i in range(sizes[axis])])


def bit_stages(sizes):
    depth = sizes["dp"].bit_length() - 1
    return [("dp", bit) for bit in range(depth)]


def pick(term, places):
    array, fixed = term
    starts = [0] * array.ndim
    extent = list(array.shape)
    for dim, place in fixed.items():
        starts[dim] = place
        extent[dim] = 1
    for dim, place in places.items():
        starts[dim] = place
        extent[dim] = 1
    return lax.dynamic_slice(array, starts, extent)


def total(terms, places):
    return sum(pick(term, places).astype(jnp.float32) for term in terms)


def halve(terms, stage, dim, sizes):
    mine = own_bit(stage)
    send = total(terms, {dim: 1 - mine}).astype(jnp.bfloat16)
    arrived = swap(send, stage, sizes)
    kept = [(array, {**fixed, dim: mine}) for array, fixed in terms]
    return kept + [(arrived, {})]


def pair_scatter(first, second, order, sizes):
    depth = sizes["dp"].bit_length() - 1

    def spread(array):
        rows, cols = array.shape
        return array.reshape((2,) * depth + (rows // sizes["dp"], cols))

    streams = [[(spread(first), {})], [(spread(second), {})]]
    for stage in order:
        if stage[0] == "rep":
            mine = own_bit(stage)
            sums = [total(terms, {}) for terms in streams]
            send = jnp.where(mine == 0, sums[1], sums[0]).astype(jnp.bfloat16)
            keep = jnp.where(mine == 0, sums[0], sums[1])
            streams = [[(keep, {}), (swap(send, stage, sizes), {})]]
        else:
            dim = depth - 1 - stage[1]
            streams = [halve(terms, stage, dim, sizes) for terms in streams]
    result = total(streams[0], {})
    return result.reshape(result.shape[-2:])


def orders(sizes):
    stages = bit_stages(sizes)
    head, mid, tail = stages[:1], stages[1:3], stages[3:]
    ring = mid + [("rep", 0)]
    return [head + ring[k:] + ring[:k] + tail for k in range(3)]


def scatter_parts(first, second, sizes):
    cols = first.shape[1]
    lanes = cols // 128
    cuts = [0, 128 * ((lanes + 2) // 3), 128 * ((2 * lanes + 2) // 3), cols]
    done = [
        pair_scatter(first[:, a:b], second[:, a:b], order, sizes)
        for a, b, order in zip(cuts[:-1], cuts[1:], orders(sizes))
    ]
    return jnp.concatenate(done, 1)


def gather_rows(values, sizes):
    stages = [("rep", 0)] + bit_stages(sizes)
    for stage in stages:
        other = swap(values, stage, sizes)
        low = own_bit(stage) == 0
        values = jnp.concatenate([jnp.where(low, values, other), jnp.where(low, other, values)], 0)
    return values


def scatter_rows(values, sizes):
    stages = bit_stages(sizes)
    depth = len(stages)
    count = values.shape[0] // (2 * sizes["dp"])
    terms = [(values.reshape((2,) * (depth + 1) + (count, values.shape[1])), {})]
    for stage in stages:
        terms = halve(terms, stage, depth - 1 - stage[1], sizes)
    terms = halve(terms, ("rep", 0), depth, sizes)
    result = total(terms, {})
    return result.reshape(result.shape[-2:])


def shards(
    hidden_states,
    image_features,
    caption_lengths,
    attn_weights,
    cross_kv,
    ffn_in,
    ffn_out,
    projections,
    norm_gains,
    biases,
    ffn_bias,
    proj_bias,
    out_grad,
    sizes,
):
    row_count, slots, width = hidden_states.shape
    captions_here = 2 * row_count
    world = sizes["dp"] * sizes["rep"]
    allowed, pick_mask = caption_layout(caption_lengths)
    pick_low = pick_mask.astype(bf16)
    pick_full = pick_mask.astype(f32)
    mask = jnp.tile(allowed.astype(f32), (1, 1, 4))
    inputs = hidden_states.reshape(row_count * slots, width)
    self_q, self_k, self_v, self_mix, first_sum, first_norm = self_forward(
        inputs, attn_weights, biases, norm_gains, mask
    )
    first_norm = first_norm.reshape(row_count, slots, width)
    text_act, text_slope, fourth_sum, layer_half, caption_raw, caption_all = ffn_forward(
        1, 1, first_norm, ffn_in, ffn_bias, ffn_out, projections, proj_bias, biases, norm_gains, None
    )
    caption_embed = (
        jnp.einsum(
            "rkt,rtd->rkd",
            pick_low,
            caption_all.reshape(row_count, TEXT, -1),
            preferred_element_type=f32,
        )
        .astype(bf16)
        .reshape(captions_here, -1)
    )
    every_caption = gather_rows(caption_embed, sizes)
    image_ends = jnp.pad(image_features[:, -1:], ((0, 0), (0, TAIL - 1), (0, 0)))
    keys, values, key_ends, value_ends, cross_q, cross_mix, second_sum, second_norm = cross_forward(
        image_features, image_ends, cross_kv, attn_weights, biases, norm_gains, first_norm
    )
    second_norm = second_norm.reshape(row_count, QUERIES, width)
    query_act, query_slope, third_sum, layer_out, query_raw, query_embed = ffn_forward(
        0,
        0,
        second_norm,
        ffn_in,
        ffn_bias,
        ffn_out,
        projections,
        proj_bias,
        biases,
        norm_gains,
        layer_half,
    )
    query_raw = query_raw.reshape(row_count, QUERIES, -1)
    query_embed = query_embed.reshape(row_count, QUERIES, -1)
    sims = jnp.einsum("rqp,cp->rqc", query_embed, every_caption, preferred_element_type=f32)
    expo = jnp.exp(sharpness * (sims - 1.0))
    affinity = jnp.mean(expo, 1)
    offset = lax.axis_index(("dp", "rep")) * captions_here
    own_block = lax.dynamic_slice_in_dim(affinity, offset, captions_here, 1).reshape(
        row_count, row_count, 2
    )
    diagonal = (
        lax.broadcasted_iota(jnp.int32, (row_count, row_count), 0)
        == lax.broadcasted_iota(jnp.int32, (row_count, row_count), 1)
    ).astype(f32)
    positive = jnp.sum(own_block * diagonal[:, :, None], 1)
    row_total = jnp.sum(affinity, 1)
    partial_cols = jnp.sum(affinity, 0)
    all_cols = jnp.sum(
        lax.all_to_all(
            jnp.broadcast_to(partial_cols[None], (world,) + partial_cols.shape),
            ("dp", "rep"),
            0,
            0,
            tiled=True,
        ),
        0,
    )
    own_cols = lax.dynamic_slice_in_dim(all_cols, offset, captions_here, 0).reshape(row_count, 2)
    inverse_all = 1.0 / all_cols
    row_loss = (
        jnp.log(row_total)
        - jnp.log(positive[:, 0])
        + jnp.sum(jnp.log(own_cols) - jnp.log(positive), 1)
    )
    grad_affinity = loss_weight * (1.0 / row_total[:, None] + inverse_all[None, :])
    pair_weight = jnp.array([2.0, 1.0], f32)
    correction = (loss_weight * diagonal[:, :, None] * pair_weight / own_block).reshape(
        row_count, captions_here
    )
    own_grad = lax.dynamic_slice_in_dim(grad_affinity, offset, captions_here, 1) - correction
    grad_affinity = lax.dynamic_update_slice_in_dim(grad_affinity, own_grad, offset, 1)
    grad_sims = (grad_affinity[:, None, :] * expo * (sharpness / QUERIES)).astype(bf16)
    grad_query_embed = jnp.einsum(
        "rqc,cp->rqp", grad_sims, every_caption, preferred_element_type=f32
    )
    grad_caption_embed = scatter_rows(
        jnp.einsum("rqc,rqp->cp", grad_sims, query_embed, preferred_element_type=f32).astype(bf16),
        sizes,
    )
    query_raw_grad = unit_back(query_raw, grad_query_embed).astype(bf16)
    head_raw = jnp.sum(
        pick_full[:, :, :, None] * caption_raw.reshape(row_count, 1, TEXT, -1), 2
    )
    head_raw_grad = unit_back(head_raw, grad_caption_embed.reshape(row_count, 2, -1)).astype(bf16)
    caption_raw_grad = jnp.einsum(
        "rkt,rkd->rtd", pick_low, head_raw_grad, preferred_element_type=f32
    ).astype(bf16)
    grad_second, query_din, query_dout, query_dproj, query_side, query_dbias, query_dproj_bias = (
        ffn_backward(
            0,
            0,
            second_norm,
            third_sum,
            second_sum,
            layer_out,
            out_grad,
            query_raw_grad.reshape(row_count * QUERIES, -1),
            projections,
            norm_gains,
            ffn_in,
            ffn_out,
            query_act,
            query_slope,
        )
    )
    text_first, text_din, text_dout, text_dproj, text_side, text_dbias, text_dproj_bias = (
        ffn_backward(
            1,
            1,
            first_norm,
            fourth_sum,
            fourth_sum,
            layer_out,
            out_grad,
            caption_raw_grad.reshape(row_count * TEXT, -1),
            projections,
            norm_gains,
            ffn_in,
            ffn_out,
            text_act,
            text_slope,
        )
    )
    ffn_in_grad = scatter_parts(query_din, text_din, sizes)
    ffn_out_grad = scatter_parts(query_dout, text_dout, sizes)
    proj_grad = pair_scatter(query_dproj, text_dproj, orders(sizes)[0], sizes)
    query_first, key_grad, value_grad, cross_dw, cross_side = cross_backward(
        image_features,
        image_ends,
        attn_weights,
        first_norm,
        keys,
        values,
        key_ends,
        value_ends,
        cross_q,
        cross_mix,
        grad_second.reshape(row_count * QUERIES, width),
    )
    cross_grad = scatter_parts(key_grad, value_grad, sizes)
    input_grad, self_dw, self_side = self_backward(
        inputs,
        attn_weights,
        norm_gains,
        mask,
        self_q,
        self_k,
        self_v,
        self_mix,
        first_sum,
        query_first,
        text_first,
    )
    attn_pairs = ((self_dw[0], self_dw[3]), (self_dw[1], cross_dw[0]), (self_dw[2], cross_dw[1]))
    attn_grad = jnp.stack(
        [
            pair_scatter(one, two, order, sizes)
            for (one, two), order in zip(attn_pairs, orders(sizes))
        ]
    )
    gain_grad = jnp.stack([self_side[0], query_side[3], query_side[0], text_side[0]])
    bias_grad = jnp.stack(
        [
            self_side[2],
            self_side[3],
            self_side[4],
            cross_side[0],
            cross_side[1],
            cross_side[2],
            query_side[2],
            text_side[2],
            self_side[1],
            query_side[4],
            query_side[1],
            text_side[1],
        ]
    )
    vectors = (
        gain_grad,
        bias_grad,
        jnp.stack([query_dbias[0], text_dbias[0]]),
        jnp.stack([query_dproj_bias[0], text_dproj_bias[0]]),
    )

    def deal(array):
        mats, cols = array.shape
        cut = array.reshape(sizes["rep"], mats // sizes["rep"], sizes["dp"], cols // sizes["dp"])
        return cut.transpose(2, 0, 1, 3).reshape(world, -1)

    dealt = jnp.concatenate([deal(array) for array in vectors], 1)
    arrived = jnp.sum(lax.all_to_all(dealt, ("dp", "rep"), 0, 0, tiled=True), 0)
    small = []
    start = 0
    for array in vectors:
        mats, cols = array.shape[0] // sizes["rep"], array.shape[1] // sizes["dp"]
        small.append(arrived[start : start + mats * cols].reshape(mats, cols))
        start += mats * cols
    return (
        layer_out,
        row_loss,
        input_grad.reshape(hidden_states.shape),
        attn_grad,
        cross_grad[None],
        ffn_in_grad[None],
        ffn_out_grad[None],
        proj_grad[None],
        small[0],
        small[1],
        small[2],
        small[3],
    )


def solution(mesh):
    placed = (
        P(("dp", "rep"), None, None),
        P(("dp", "rep"), None, None),
        P(("dp", "rep"), None),
        P(),
        P(),
        P(),
        P(),
        P(),
        P(),
        P(),
        P(),
        P(),
        P(("dp", "rep"), None, None),
    )
    sizes = dict(mesh.shape)
    return jax.shard_map(
        functools.partial(shards, sizes=sizes),
        mesh=mesh,
        in_specs=placed,
        out_specs=(
            P(("dp", "rep"), None, None),
            P(("dp", "rep")),
            P(("dp", "rep"), None, None),
            P("rep", "dp", None),
            P("rep", "dp", None),
            P("rep", "dp", None),
            P("rep", "dp", None),
            P("rep", "dp", None),
            P("rep", "dp"),
            P("rep", "dp"),
            P("rep", "dp"),
            P("rep", "dp"),
        ),
        check_vma=False,
    )
```

```python
import functools

import jax
import jax.numpy as jnp
from jax import lax
from jax.experimental import pallas as pl
from jax.experimental.pallas import tpu as pltpu
from jax.sharding import PartitionSpec as P

HEADS = 12
QUERIES = 32
TEXT = 32
SLOTS = QUERIES + TEXT


blocked = -1000000000.0
epsilon = 1e-06
sharpness = 14.0
loss_weight = 16.0


def unit_rows(values):
    return values * lax.rsqrt(jnp.sum(values * values, -1, keepdims=True) + epsilon)


def unit_back(values, grad_rows):
    unused, pullback = jax.vjp(unit_rows, values)
    return pullback(grad_rows)[0]


def caption_layout(length_rows):
    row_count = length_rows.shape[0]
    first_len = length_rows[:, 0:1]
    second_end = first_len + length_rows[:, 1:2]
    slot_index = lax.broadcasted_iota(jnp.int32, (row_count, TEXT), 1)
    text_group = (slot_index >= first_len).astype(jnp.int32) + (slot_index >= second_end).astype(
        jnp.int32
    )
    group_ids = jnp.concatenate([jnp.full((row_count, QUERIES), -1, jnp.int32), text_group], 1)
    allowed = group_ids[:, :, None] == group_ids[:, None, :]
    head_starts = jnp.concatenate([jnp.zeros_like(first_len), first_len], 1)
    pick_mask = slot_index[:, None, :] == head_starts[:, :, None]
    return (allowed, pick_mask)


f32 = jnp.float32
bf16 = jnp.bfloat16
ROOT_HALF = 0.7071067811865476
ROOT_TAU = 0.3989422804014327
MIB = 1024 * 1024


def dot_nn(a, b):
    return lax.dot_general(a, b, (((1,), (0,)), ((), ())), preferred_element_type=f32)


def dot_nt(a, b):
    return lax.dot_general(a, b, (((1,), (1,)), ((), ())), preferred_element_type=f32)


def dot_tn(a, b):
    return lax.dot_general(a, b, (((0,), (0,)), ((), ())), preferred_element_type=f32)


def whole(shape):
    return pl.BlockSpec(shape, lambda *_: (0,) * len(shape))


def held(shape, index):
    return pl.BlockSpec(shape, index, pipeline_mode=pl.Buffered(1))


def cost(micros):
    return pl.CostEstimate(flops=int(micros * 1.1e9), bytes_accessed=0, transcendentals=0)


def store_units(ref, values):
    for place in range(values.shape[1] // 128):
        ref[place] = values[:, place * 128 : (place + 1) * 128].astype(ref.dtype)


def params(mib):
    return pltpu.CompilerParams(vmem_limit_bytes=mib * MIB, dimension_semantics=("arbitrary",))


def norm_parts(values):
    center = values - jnp.mean(values, -1, keepdims=True)
    scale = lax.rsqrt(jnp.mean(center * center, -1, keepdims=True) + epsilon)
    return center * scale, scale


def norm_grads(values, gain_row, grad):
    unit, scale = norm_parts(values)
    inner = grad * gain_row
    first = jnp.mean(inner, -1, keepdims=True)
    second = jnp.mean(inner * unit, -1, keepdims=True)
    return (
        scale * (inner - first - unit * second),
        jnp.sum(grad * unit, 0, keepdims=True),
        jnp.sum(grad, 0, keepdims=True),
    )


def gate_parts(u):
    size = jnp.abs(u) * ROOT_HALF
    t = 1.0 / (1.0 + 0.3275911 * size)
    bell = jnp.exp(-size * size)
    poly = t * (
        0.127414796
        + t * (-0.142248368 + t * (0.7107068705 + t * (-0.7265760135 + t * 0.5307027145)))
    )
    tail = poly * bell
    cdf = jnp.where(u > 0, 1.0 - tail, tail)
    return u * cdf, cdf + (ROOT_TAU * u) * bell


def half_lanes(rows):
    low = (lax.broadcasted_iota(jnp.int32, (rows, 128), 1) < 64).astype(f32)
    return low.astype(bf16), (1.0 - low).astype(bf16)


def spread_heads(x, low, high):
    left, right = x[:, :128], x[:, 128:]
    none = jnp.zeros_like(left)
    return jnp.concatenate(
        [
            jnp.concatenate([left * low, none], 1),
            jnp.concatenate([left * high, none], 1),
            jnp.concatenate([none, right * low], 1),
            jnp.concatenate([none, right * high], 1),
        ],
        0,
    )


def collect_heads(o, n):
    low = lax.broadcasted_iota(jnp.int32, (n, 128), 1) < 64
    left = jnp.where(low, o[:n, :128], o[n : 2 * n, :128])
    right = jnp.where(low, o[2 * n : 3 * n, 128:], o[3 * n :, 128:])
    return jnp.concatenate([left, right], 1)


def columns_softmax(scores):
    raised = jnp.exp(scores - jnp.max(scores, 0, keepdims=True))
    return raised * (1.0 / jnp.sum(raised, 0, keepdims=True))


GROUPS = HEADS // 4


def self_forward_kernel(
    x_ref, w_ref, bias_ref, gain_ref, mask_ref, q_ref, k_ref, v_ref, mix_ref, sum_ref, norm_ref
):
    x = x_ref[...]
    q_ref[...] = (dot_nn(x, w_ref[0]) + bias_ref[0:1]).astype(bf16)
    k_ref[...] = dot_nn(x, w_ref[1]).astype(bf16)
    v_ref[...] = (dot_nn(x, w_ref[2]) + bias_ref[1:2]).astype(bf16)
    low, high = half_lanes(SLOTS)

    def one_row(r, carry):
        rows = pl.ds(pl.multiple_of(r * SLOTS, SLOTS), SLOTS)
        allowed = mask_ref[r] > 0.0
        for g in range(GROUPS):
            cols = slice(g * 256, (g + 1) * 256)
            queries = spread_heads(q_ref[rows, cols] * bf16(0.125), low, high)
            scores = jnp.where(allowed, dot_nt(k_ref[rows, cols], queries), blocked)
            prob = columns_softmax(scores).astype(bf16)
            mixed = dot_tn(prob, v_ref[rows, cols])
            mix_ref[rows, cols] = collect_heads(mixed, SLOTS).astype(bf16)
        return carry

    lax.fori_loop(0, x_ref.shape[0] // SLOTS, one_row, 0)
    total = x.astype(f32) + dot_nn(mix_ref[...], w_ref[3]) + bias_ref[2:3]
    sum_ref[...] = total
    unit, _ = norm_parts(total)
    norm_ref[...] = unit * gain_ref[0:1] + bias_ref[8:9]


def self_forward(x, weights, biases, gains, mask):
    tokens, width = x.shape
    step = 4 * SLOTS
    tile = pl.BlockSpec((step, width), lambda i: (i, 0))
    low, full = jax.ShapeDtypeStruct(x.shape, bf16), jax.ShapeDtypeStruct(x.shape, f32)
    return pl.pallas_call(
        self_forward_kernel,
        grid=(tokens // step,),
        in_specs=[
            tile,
            held((4, width, width), lambda i: (0, 0, 0)),
            whole(biases.shape),
            whole(gains.shape),
            pl.BlockSpec((4,) + mask.shape[1:], lambda i: (i, 0, 0)),
        ],
        out_specs=[tile] * 6,
        out_shape=[low, low, low, low, full, full],
        compiler_params=params(40),
        name="self_forward",
        cost_estimate=cost(27),
    )(x, weights, biases, gains, mask)


def self_backward_kernel(
    x_ref,
    w_ref,
    gain_ref,
    mask_ref,
    q_ref,
    k_ref,
    v_ref,
    mix_ref,
    sum_ref,
    top_ref,
    low_ref,
    dx_ref,
    dw_ref,
    side_ref,
    dq_all,
    dk_all,
    dv_all,
    branch_all,
    dmix_all,
):
    step = pl.program_id(0)
    count = sum_ref.shape[0]
    steps = x_ref.shape[0] // count
    low, high = half_lanes(SLOTS)

    @pl.when(step == 0)
    def _():
        side_ref[...] = jnp.zeros_like(side_ref)

    @pl.when(step < steps)
    def _():
        base = pl.multiple_of(step * count, count)
        here = pl.ds(base, count)
        grad = jnp.concatenate([top_ref[...], low_ref[...]], 1).reshape(count, -1)
        down, dgain, dshift = norm_grads(sum_ref[...], gain_ref[0:1], grad)
        branch = down.astype(bf16)
        branch_all[here] = branch
        dmix_all[...] = dot_nt(branch, w_ref[3]).astype(bf16)

        def one_row(r, carry):
            local = pl.ds(pl.multiple_of(r * SLOTS, SLOTS), SLOTS)
            rows = pl.ds(pl.multiple_of(base + r * SLOTS, SLOTS), SLOTS)
            allowed = mask_ref[r] > 0.0
            for g in range(GROUPS):
                cols = slice(g * 256, (g + 1) * 256)
                keys = k_ref[local, cols]
                queries = spread_heads(q_ref[local, cols] * bf16(0.125), low, high)
                outs = spread_heads(dmix_all[local, cols], low, high)
                prob = columns_softmax(jnp.where(allowed, dot_nt(keys, queries), blocked))
                dprob = dot_nt(v_ref[local, cols], outs)
                dscore = (prob * (dprob - jnp.sum(dprob * prob, 0, keepdims=True))).astype(bf16)
                dv_all[rows, cols] = dot_nn(prob.astype(bf16), outs).astype(bf16)
                dk_all[rows, cols] = dot_nn(dscore, queries).astype(bf16)
                dq_all[rows, cols] = (collect_heads(dot_tn(dscore, keys), SLOTS) * 0.125).astype(bf16)
            return carry

        lax.fori_loop(0, count // SLOTS, one_row, 0)
        dq, dk, dv = dq_all[here], dk_all[here], dv_all[here]
        dx_ref[...] = down + dot_nt(dq, w_ref[0]) + dot_nt(dk, w_ref[1]) + dot_nt(dv, w_ref[2])
        side_ref[0:1] += dgain
        side_ref[1:2] += dshift
        for place, rows in enumerate((dq, dv, branch)):
            side_ref[2 + place : 3 + place] += jnp.sum(rows.astype(f32), 0, keepdims=True)

    for place, right in enumerate((dq_all, dk_all, dv_all, branch_all)):

        @pl.when(step == steps + place)
        def _():
            left = mix_ref if place == 3 else x_ref
            store_units(dw_ref.at[0], dot_tn(left[...], right[...]))


def self_backward(x, weights, gains, mask, q, k, v, mix, total, top, text):
    tokens, width = x.shape
    count = 4 * SLOTS
    steps = tokens // count

    def near(i):
        return jnp.minimum(i, steps - 1)

    tile = pl.BlockSpec((count, width), lambda i: (near(i), 0))
    part = pl.BlockSpec((4, QUERIES, width), lambda i: (near(i), 0, 0))
    scratch = pltpu.VMEM((tokens, width), bf16)
    return pl.pallas_call(
        self_backward_kernel,
        grid=(steps + 4,),
        in_specs=[
            held(x.shape, lambda i: (0, 0)),
            held((4, width, width), lambda i: (0, 0, 0)),
            whole(gains.shape),
            pl.BlockSpec((4,) + mask.shape[1:], lambda i: (near(i), 0, 0)),
            tile,
            tile,
            tile,
            held(x.shape, lambda i: (0, 0)),
            tile,
            part,
            part,
        ],
        out_specs=[
            tile,
            pl.BlockSpec((1, width // 128, width, 128), lambda i: (jnp.maximum(i - steps, 0), 0, 0, 0)),
            whole((8, width)),
        ],
        out_shape=[
            jax.ShapeDtypeStruct(x.shape, f32),
            jax.ShapeDtypeStruct((4, width // 128, width, 128), bf16),
            jax.ShapeDtypeStruct((8, width), f32),
        ],
        scratch_shapes=[scratch] * 4 + [pltpu.VMEM((count, width), bf16)],
        compiler_params=params(48),
        name="self_backward",
        cost_estimate=cost(37),
    )(x, weights, gains, mask, q, k, v, mix, total, top, text)


TAIL = 16


def cross_forward_kernel(
    image_ref,
    end_ref,
    kv_ref,
    w_ref,
    bias_ref,
    gain_ref,
    norm_ref,
    key_ref,
    value_ref,
    key_end_ref,
    value_end_ref,
    q_ref,
    mix_ref,
    sum_ref,
    out_ref,
):
    rows_here = image_ref.shape[0]
    main = image_ref.shape[1] - 1
    width = norm_ref.shape[-1]
    end = end_ref[...].reshape(rows_here * TAIL, -1)
    key_end_ref[...] = dot_nt(end, kv_ref[0]).astype(bf16)
    value_end_ref[...] = (dot_nt(end, kv_ref[1]) + bias_ref[4:5]).astype(bf16)
    residual = norm_ref[...].reshape(rows_here * QUERIES, width)
    q_ref[...] = (dot_nn(residual.astype(bf16), w_ref[0]) + bias_ref[3:4]).astype(bf16)
    low, high = half_lanes(QUERIES)
    shown = lax.broadcasted_iota(jnp.int32, (main + TAIL, 128), 0) <= main

    def one_row(r, carry):
        span = pl.ds(pl.multiple_of(r * main, main), main)
        last = pl.ds(pl.multiple_of(r * TAIL, TAIL), TAIL)
        mine = pl.ds(pl.multiple_of(r * QUERIES, QUERIES), QUERIES)
        tokens = image_ref[r, :main]
        key_ref[span] = dot_nt(tokens, kv_ref[0]).astype(bf16)
        value_ref[span] = (dot_nt(tokens, kv_ref[1]) + bias_ref[4:5]).astype(bf16)
        for g in range(GROUPS):
            cols = slice(g * 256, (g + 1) * 256)
            keys = jnp.concatenate([key_ref[span, cols], key_end_ref[last, cols]], 0)
            values = jnp.concatenate([value_ref[span, cols], value_end_ref[last, cols]], 0)
            queries = spread_heads(q_ref[mine, cols] * bf16(0.125), low, high)
            prob = columns_softmax(jnp.where(shown, dot_nt(keys, queries), blocked)).astype(bf16)
            mix_ref[mine, cols] = collect_heads(dot_tn(prob, values), QUERIES).astype(bf16)
        return carry

    lax.fori_loop(0, rows_here, one_row, 0)
    total = residual + dot_nn(mix_ref[...], w_ref[1]) + bias_ref[5:6]
    sum_ref[...] = total
    unit, _ = norm_parts(total)
    out_ref[...] = unit * gain_ref[1:2] + bias_ref[9:10]


def cross_forward(images, ends, kv, weights, biases, gains, norm):
    rows, patches, vis = images.shape
    main = patches - 1
    width = norm.shape[-1]
    take = 4
    keys = pl.BlockSpec((take * main, width), lambda i: (i, 0))
    tails = pl.BlockSpec((take * TAIL, width), lambda i: (i, 0))
    tile = pl.BlockSpec((take * QUERIES, width), lambda i: (i, 0))

    def shape(count, dtype):
        return jax.ShapeDtypeStruct((rows * count, width), dtype)

    return pl.pallas_call(
        cross_forward_kernel,
        grid=(rows // take,),
        in_specs=[
            pl.BlockSpec((take, patches, vis), lambda i: (i, 0, 0)),
            pl.BlockSpec((take, TAIL, vis), lambda i: (i, 0, 0)),
            held(kv.shape, lambda i: (0, 0, 0)),
            held((2, width, width), lambda i: (2, 0, 0)),
            whole(biases.shape),
            whole(gains.shape),
            pl.BlockSpec((take, QUERIES, width), lambda i: (i, 0, 0)),
        ],
        out_specs=[keys, keys, tails, tails, tile, tile, tile, tile],
        out_shape=[
            shape(main, bf16),
            shape(main, bf16),
            shape(TAIL, bf16),
            shape(TAIL, bf16),
            shape(QUERIES, bf16),
            shape(QUERIES, bf16),
            shape(QUERIES, f32),
            shape(QUERIES, f32),
        ],
        compiler_params=params(48),
        name="cross_forward",
        cost_estimate=cost(55),
    )(images, ends, kv, weights, biases, gains, norm)


def cross_backward_kernel(
    image_ref,
    end_ref,
    w_ref,
    norm_ref,
    key_ref,
    value_ref,
    key_end_ref,
    value_end_ref,
    q_ref,
    mix_ref,
    down_ref,
    order_ref,
    dnorm_ref,
    dkey_w_ref,
    dvalue_w_ref,
    dw_ref,
    side_ref,
    key_sum,
    value_sum,
    w_sum,
    dkey,
    dvalue,
    dkey_end,
    dvalue_end,
    dq_all,
    dmix_all,
):
    del order_ref
    step = pl.program_id(0)
    rows_here = image_ref.shape[0]
    main = image_ref.shape[1] - 1
    width = norm_ref.shape[-1]
    low, high = half_lanes(QUERIES)
    shown = lax.broadcasted_iota(jnp.int32, (main + TAIL, 128), 0) <= main

    @pl.when(step == 0)
    def _():
        side_ref[...] = jnp.zeros_like(side_ref)
        key_sum[...] = jnp.zeros_like(key_sum)
        value_sum[...] = jnp.zeros_like(value_sum)
        w_sum[...] = jnp.zeros_like(w_sum)

    down = down_ref[...]
    branch = down.astype(bf16)
    dmix_all[...] = dot_nt(branch, w_ref[1]).astype(bf16)

    def one_row(r, carry):
        span = pl.ds(pl.multiple_of(r * main, main), main)
        last = pl.ds(pl.multiple_of(r * TAIL, TAIL), TAIL)
        mine = pl.ds(pl.multiple_of(r * QUERIES, QUERIES), QUERIES)
        for g in range(GROUPS):
            cols = slice(g * 256, (g + 1) * 256)
            keys = jnp.concatenate([key_ref[span, cols], key_end_ref[last, cols]], 0)
            values = jnp.concatenate([value_ref[span, cols], value_end_ref[last, cols]], 0)
            queries = spread_heads(q_ref[mine, cols] * bf16(0.125), low, high)
            outs = spread_heads(dmix_all[mine, cols], low, high)
            prob = columns_softmax(jnp.where(shown, dot_nt(keys, queries), blocked))
            dprob = dot_nt(values, outs)
            dscore = (prob * (dprob - jnp.sum(dprob * prob, 0, keepdims=True))).astype(bf16)
            dv = dot_nn(prob.astype(bf16), outs).astype(bf16)
            dk = dot_nn(dscore, queries).astype(bf16)
            dvalue[span, cols] = dv[:main]
            dvalue_end[last, cols] = dv[main:]
            dkey[span, cols] = dk[:main]
            dkey_end[last, cols] = dk[main:]
            dq_all[mine, cols] = (collect_heads(dot_tn(dscore, keys), QUERIES) * 0.125).astype(bf16)
        return carry

    lax.fori_loop(0, rows_here, one_row, 0)
    end = end_ref[...].reshape(rows_here * TAIL, -1)
    for grads, grads_end, gathered in ((dkey, dkey_end, key_sum), (dvalue, dvalue_end, value_sum)):
        gathered[...] += dot_tn(grads_end[...], end)

        def add_row(r, carry):
            span = pl.ds(pl.multiple_of(r * main, main), main)
            gathered[...] += dot_tn(grads[span], image_ref[r, :main])
            return carry

        lax.fori_loop(0, rows_here, add_row, 0)
    dq = dq_all[...]
    dnorm_ref[...] = (down + dot_nt(dq, w_ref[0])).reshape(rows_here, QUERIES, width)
    low_norm = norm_ref[...].reshape(rows_here * QUERIES, width).astype(bf16)
    w_sum[0] += dot_tn(low_norm, dq)
    w_sum[1] += dot_tn(mix_ref[...], branch)
    side_ref[0:1] += jnp.sum(dq.astype(f32), 0, keepdims=True)
    side_ref[1:2] += jnp.sum(dvalue[...].astype(f32), 0, keepdims=True) + jnp.sum(
        dvalue_end[...].astype(f32), 0, keepdims=True
    )
    side_ref[2:3] += jnp.sum(branch.astype(f32), 0, keepdims=True)

    @pl.when(step == pl.num_programs(0) - 1)
    def _():
        store_units(dkey_w_ref, key_sum[...])
        store_units(dvalue_w_ref, value_sum[...])
        store_units(dw_ref.at[0], w_sum[0])
        store_units(dw_ref.at[1], w_sum[1])


def cross_backward(images, ends, weights, norm, keys, values, key_ends, value_ends, q, mix, down, order):
    rows, patches, vis = images.shape
    main = patches - 1
    width = norm.shape[-1]
    take = 2
    span = pl.BlockSpec((take * main, width), lambda i: (i, 0))
    tails = pl.BlockSpec((take * TAIL, width), lambda i: (i, 0))
    tile = pl.BlockSpec((take * QUERIES, width), lambda i: (i, 0))
    part = pl.BlockSpec((take, QUERIES, width), lambda i: (i, 0, 0))
    return pl.pallas_call(
        cross_backward_kernel,
        grid=(rows // take,),
        in_specs=[
            pl.BlockSpec((take, patches, vis), lambda i: (i, 0, 0)),
            pl.BlockSpec((take, TAIL, vis), lambda i: (i, 0, 0)),
            held((2, width, width), lambda i: (2, 0, 0)),
            part,
            span,
            span,
            tails,
            tails,
            tile,
            tile,
            tile,
            pl.BlockSpec(memory_space=pl.ANY),
        ],
        out_specs=[
            part,
            held((vis // 128, width, 128), lambda i: (0, 0, 0)),
            held((vis // 128, width, 128), lambda i: (0, 0, 0)),
            held((2, width // 128, width, 128), lambda i: (0, 0, 0, 0)),
            whole((8, width)),
        ],
        out_shape=[
            jax.ShapeDtypeStruct((rows, QUERIES, width), f32),
            jax.ShapeDtypeStruct((vis // 128, width, 128), bf16),
            jax.ShapeDtypeStruct((vis // 128, width, 128), bf16),
            jax.ShapeDtypeStruct((2, width // 128, width, 128), bf16),
            jax.ShapeDtypeStruct((8, width), f32),
        ],
        scratch_shapes=[
            pltpu.VMEM((width, vis), f32),
            pltpu.VMEM((width, vis), f32),
            pltpu.VMEM((2, width, width), f32),
            pltpu.VMEM((take * main, width), bf16),
            pltpu.VMEM((take * main, width), bf16),
            pltpu.VMEM((take * TAIL, width), bf16),
            pltpu.VMEM((take * TAIL, width), bf16),
            pltpu.VMEM((take * QUERIES, width), bf16),
            pltpu.VMEM((take * QUERIES, width), bf16),
        ],
        compiler_params=params(52),
        name="cross_backward",
        cost_estimate=cost(79),
    )(images, ends, weights, norm, keys, values, key_ends, value_ends, q, mix, down, order)


def ffn_forward_kernel(
    which,
    norm_ref,
    in_ref,
    in_bias_ref,
    out_ref,
    proj_ref,
    proj_bias_ref,
    bias_ref,
    gain_ref,
    *rest,
):
    act_ref, slope_ref, sum_ref, low_ref, raw_ref, embed_ref, rows_low = rest[-7:]
    step = pl.program_id(0)
    tokens, width = sum_ref.shape

    @pl.when(step == 0)
    def _():
        full = norm_ref[...].reshape(tokens, width)
        rows_low[...] = full.astype(bf16)
        sum_ref[...] = full + bias_ref[6 + which : 7 + which]

    u = dot_nn(rows_low[...], in_ref[0]) + in_bias_ref[which : which + 1]
    act, slope = gate_parts(u)
    act = act.astype(bf16)
    act_ref[...] = act
    slope_ref[...] = slope.astype(bf16)
    sum_ref[...] += dot_nn(act, out_ref[0])

    @pl.when(step == pl.num_programs(0) - 1)
    def _():
        unit, _ = norm_parts(sum_ref[...])
        low = (unit * gain_ref[2 + which : 3 + which] + bias_ref[10 + which : 11 + which]).astype(bf16)
        low_ref[...] = low.reshape(low_ref.shape)
        raw = dot_nn(low, proj_ref[0]) + proj_bias_ref[which : which + 1]
        raw_ref[...] = raw
        size = lax.rsqrt(jnp.sum(raw * raw, -1, keepdims=True) + epsilon)
        embed_ref[...] = (raw * size).astype(bf16)


def ffn_forward(which, part, norm, ffn_in, ffn_bias, ffn_out, projections, proj_bias, biases, gains, layer):
    rows, width = norm.shape[0], norm.shape[-1]
    tokens = rows * QUERIES
    hidden = ffn_in.shape[2]
    embed = projections.shape[2]
    chunk = 512
    cols = pl.BlockSpec((tokens, chunk), lambda j: (0, j))
    halves = [] if layer is None else [layer]
    return pl.pallas_call(
        functools.partial(ffn_forward_kernel, which),
        grid=(hidden // chunk,),
        in_specs=[
            held((rows, QUERIES, width), lambda j: (0, part, 0)),
            pl.BlockSpec((1, width, chunk), lambda j: (which, 0, j)),
            pl.BlockSpec((2, chunk), lambda j: (0, j)),
            pl.BlockSpec((1, chunk, width), lambda j: (which, j, 0)),
            held((1, width, embed), lambda j: (which, 0, 0)),
            whole(proj_bias.shape),
            whole(biases.shape),
            whole(gains.shape),
        ]
        + [pl.BlockSpec(memory_space=pl.ANY)] * len(halves),
        out_specs=[
            cols,
            cols,
            whole((tokens, width)),
            pl.BlockSpec((rows, QUERIES, width), lambda j: (0, which, 0)),
            whole((tokens, embed)),
            whole((tokens, embed)),
        ],
        out_shape=[
            jax.ShapeDtypeStruct((tokens, hidden), bf16),
            jax.ShapeDtypeStruct((tokens, hidden), bf16),
            jax.ShapeDtypeStruct((tokens, width), f32),
            jax.ShapeDtypeStruct((rows, SLOTS, width), bf16),
            jax.ShapeDtypeStruct((tokens, embed), f32),
            jax.ShapeDtypeStruct((tokens, embed), bf16),
        ],
        scratch_shapes=[pltpu.VMEM((tokens, width), bf16)],
        input_output_aliases={8: 3} if halves else {},
        compiler_params=params(48),
        name="ffn_forward",
        cost_estimate=cost(15),
    )(norm, ffn_in, ffn_bias, ffn_out, projections, proj_bias, biases, gains, *halves)


def ffn_backward_kernel(
    which,
    norm_ref,
    sum_ref,
    before_ref,
    layer_ref,
    grad_ref,
    raw_ref,
    proj_ref,
    gain_ref,
    in_ref,
    out_ref,
    act_ref,
    slope_ref,
    down_ref,
    din_ref,
    dout_ref,
    dproj_ref,
    side_ref,
    dbias_ref,
    dproj_bias_ref,
    branch_all,
    low_turned,
    rest,
):
    step = pl.program_id(0)
    tokens, width = sum_ref.shape

    @pl.when(step == 0)
    def _():
        raw = raw_ref[...]
        grad = grad_ref[...].reshape(tokens, width).astype(f32) + dot_nt(raw, proj_ref[0])
        down, dgain, dshift = norm_grads(sum_ref[...], gain_ref[2 + which : 3 + which], grad)
        branch = down.astype(bf16)
        branch_all[...] = branch
        rest[...] = down
        side_ref[...] = jnp.zeros_like(side_ref)
        side_ref[0:1] = dgain
        side_ref[1:2] = dshift
        side_ref[2:3] = jnp.sum(branch.astype(f32), 0, keepdims=True)
        store_units(dproj_ref, dot_tn(layer_ref[...].reshape(tokens, width), raw))
        dproj_bias_ref[...] = jnp.broadcast_to(
            jnp.sum(raw.astype(f32), 0, keepdims=True), dproj_bias_ref.shape
        )
        low_turned[...] = norm_ref[...].reshape(tokens, width).astype(bf16).T

    branch = branch_all[...]
    du = (dot_nt(branch, out_ref[0]) * slope_ref[...].astype(f32)).astype(bf16)
    rest[...] += dot_nt(du, in_ref[0])
    store_units(dout_ref, dot_tn(act_ref[...], branch))
    store_units(din_ref, dot_nn(low_turned[...], du))
    dbias_ref[...] = jnp.broadcast_to(jnp.sum(du.astype(f32), 0, keepdims=True), dbias_ref.shape)

    @pl.when(step == pl.num_programs(0) - 1)
    def _():
        if which == 0:
            down, dgain, dshift = norm_grads(before_ref[...], gain_ref[1:2], rest[...])
            side_ref[3:4] = dgain
            side_ref[4:5] = dshift
            down_ref[...] = down.reshape(down_ref.shape)
        else:
            down_ref[...] = rest[...].reshape(down_ref.shape)


def ffn_backward(
    which, part, norm, total, before, layer, grad, raw, projections, gains, ffn_in, ffn_out, act, slope
):
    rows = layer.shape[0]
    tokens, width = total.shape
    hidden = ffn_in.shape[2]
    embed = projections.shape[2]
    chunk = 512
    cols = pl.BlockSpec((tokens, chunk), lambda j: (0, j))
    before_spec = held(before.shape, lambda j: (0, 0))
    return pl.pallas_call(
        functools.partial(ffn_backward_kernel, which),
        grid=(hidden // chunk,),
        in_specs=[
            held((rows, QUERIES, width), lambda j: (0, part, 0)),
            held((tokens, width), lambda j: (0, 0)),
            before_spec,
            held((rows, QUERIES, width), lambda j: (0, which, 0)),
            held((rows, QUERIES, width), lambda j: (0, which, 0)),
            held((tokens, embed), lambda j: (0, 0)),
            held((1, width, embed), lambda j: (which, 0, 0)),
            whole(gains.shape),
            pl.BlockSpec((1, width, chunk), lambda j: (which, 0, j)),
            pl.BlockSpec((1, chunk, width), lambda j: (which, j, 0)),
            cols,
            cols,
        ],
        out_specs=[
            whole((rows, QUERIES, width)),
            pl.BlockSpec((chunk // 128, width, 128), lambda j: (j, 0, 0)),
            pl.BlockSpec((width // 128, chunk, 128), lambda j: (0, j, 0)),
            whole((embed // 128, width, 128)),
            whole((8, width)),
            pl.BlockSpec((8, chunk), lambda j: (0, j)),
            whole((8, embed)),
        ],
        out_shape=[
            jax.ShapeDtypeStruct((rows, QUERIES, width), f32),
            jax.ShapeDtypeStruct((hidden // 128, width, 128), bf16),
            jax.ShapeDtypeStruct((width // 128, hidden, 128), bf16),
            jax.ShapeDtypeStruct((embed // 128, width, 128), bf16),
            jax.ShapeDtypeStruct((8, width), f32),
            jax.ShapeDtypeStruct((8, hidden), f32),
            jax.ShapeDtypeStruct((8, embed), f32),
        ],
        scratch_shapes=[
            pltpu.VMEM((tokens, width), bf16),
            pltpu.VMEM((width, tokens), bf16),
            pltpu.VMEM((tokens, width), f32),
        ],
        compiler_params=params(52),
        name="ffn_backward",
        cost_estimate=cost(20),
    )(norm, total, before, layer, grad, raw, projections, gains, ffn_in, ffn_out, act, slope)


def own_bit(stage):
    axis, bit = stage
    return (lax.axis_index(axis) >> bit) & 1


def swap(values, stage, sizes):
    axis, bit = stage
    return lax.ppermute(values, axis, [(i, i ^ (1 << bit)) for i in range(sizes[axis])])


def pick(term, places):
    array, fixed = term
    starts = [0] * array.ndim
    extent = list(array.shape)
    for dim, place in (fixed | places).items():
        starts[dim] = place
        extent[dim] = 1
    return lax.dynamic_slice(array, starts, extent)


def total(terms, places):
    return sum(pick(term, places).astype(f32) for term in terms)


def swap_all(pieces, stage, sizes):
    flat = [piece.reshape(-1, 128) for piece in pieces]
    sent = flat[0] if len(flat) == 1 else jnp.concatenate(flat, 0)
    arrived = swap(sent, stage, sizes)
    start, got = 0, []
    for piece, rows in zip(pieces, flat):
        got.append(arrived[start : start + rows.shape[0]].reshape(piece.shape))
        start += rows.shape[0]
    return got


def scatter_pairs(pairs, order, sizes):
    depth = sizes["dp"].bit_length() - 1

    def spread(array):
        units, rows, lanes = array.shape
        return array.reshape((units,) + (2,) * depth + (rows // sizes["dp"], lanes))

    streams = [[[(spread(array), {})] for array in pair] for pair in pairs]
    for stage in order:
        mine = own_bit(stage)
        if stage[0] == "rep":
            sums = [[total(terms, {}) for terms in pair] for pair in streams]
            sent = [jnp.where(mine == 0, two, one).astype(bf16) for one, two in sums]
            kept = [jnp.where(mine == 0, one, two).astype(bf16) for one, two in sums]
            got = swap_all(sent, stage, sizes)
            streams = [[[(keep, {}), (piece, {})]] for keep, piece in zip(kept, got)]
        else:
            dim = depth - stage[1]
            sent = [total(terms, {dim: 1 - mine}).astype(bf16) for pair in streams for terms in pair]
            got = iter(swap_all(sent, stage, sizes))
            streams = [
                [
                    [(array, fixed | {dim: mine}) for array, fixed in terms] + [(next(got), {})]
                    for terms in pair
                ]
                for pair in streams
            ]
    results = []
    for (terms,) in streams:
        result = total(terms, {})
        results.append(result.reshape(result.shape[0], result.shape[-2], 128))
    return results


def orders(sizes):
    stages = [("dp", bit) for bit in range(sizes["dp"].bit_length() - 1)]
    head, mid, tail = stages[:1], stages[1:3], stages[3:]
    ring = mid + [("rep", 0)]
    return [head + ring[k:] + ring[:k] + tail for k in range(3)]


def cut_units(array, part):
    units = array.shape[0]
    edges = [(units * k + 1) // 3 for k in range(4)]
    return array[edges[part] : edges[part + 1]]


def scatter_group(pairs, sizes):
    parts = [
        scatter_pairs([tuple(cut_units(array, part) for array in pair) for pair in pairs], order, sizes)
        for part, order in enumerate(orders(sizes))
    ]
    joined = [jnp.concatenate(pieces, 0) for pieces in zip(*parts)]
    return [array.transpose(1, 0, 2).reshape(array.shape[1], -1) for array in joined]


def exchange(values, sizes):
    return lax.all_to_all(values, ("dp", "rep"), 0, 0, tiled=True)


def gather_rows(values, sizes):
    world = sizes["dp"] * sizes["rep"]
    return exchange(jnp.tile(values, (world, 1)), sizes)


def scatter_rows(values, sizes):
    world = sizes["dp"] * sizes["rep"]
    arrived = exchange(values, sizes)
    return jnp.sum(arrived.reshape(world, -1, values.shape[1]).astype(f32), 0)


def shards(
    hidden_states,
    image_features,
    caption_lengths,
    attn_weights,
    cross_kv,
    ffn_in,
    ffn_out,
    projections,
    norm_gains,
    biases,
    ffn_bias,
    proj_bias,
    out_grad,
    sizes,
):
    row_count, slots, width = hidden_states.shape
    captions_here = 2 * row_count
    world = sizes["dp"] * sizes["rep"]
    allowed, pick_mask = caption_layout(caption_lengths)
    pick_low = pick_mask.astype(bf16)
    pick_full = pick_mask.astype(f32)
    mask = jnp.tile(allowed.astype(f32), (1, 1, 4))
    inputs = hidden_states.reshape(row_count * slots, width)
    self_q, self_k, self_v, self_mix, first_sum, first_norm = self_forward(
        inputs, attn_weights, biases, norm_gains, mask
    )
    first_norm = first_norm.reshape(row_count, slots, width)
    text_act, text_slope, fourth_sum, layer_half, caption_raw, caption_all = ffn_forward(
        1, 1, first_norm, ffn_in, ffn_bias, ffn_out, projections, proj_bias, biases, norm_gains, None
    )
    caption_embed = (
        jnp.einsum(
            "rkt,rtd->rkd",
            pick_low,
            caption_all.reshape(row_count, TEXT, -1),
            preferred_element_type=f32,
        )
        .astype(bf16)
        .reshape(captions_here, -1)
    )
    every_caption = gather_rows(caption_embed, sizes)
    image_ends = jnp.pad(image_features[:, -1:], ((0, 0), (0, TAIL - 1), (0, 0)))
    keys, values, key_ends, value_ends, cross_q, cross_mix, second_sum, second_norm = cross_forward(
        image_features, image_ends, cross_kv, attn_weights, biases, norm_gains, first_norm
    )
    second_norm = second_norm.reshape(row_count, QUERIES, width)
    query_act, query_slope, third_sum, layer_out, query_raw, query_embed = ffn_forward(
        0,
        0,
        second_norm,
        ffn_in,
        ffn_bias,
        ffn_out,
        projections,
        proj_bias,
        biases,
        norm_gains,
        layer_half,
    )
    query_raw = query_raw.reshape(row_count, QUERIES, -1)
    query_embed = query_embed.reshape(row_count, QUERIES, -1)
    sims = jnp.einsum("rqp,cp->rqc", query_embed, every_caption, preferred_element_type=f32)
    expo = jnp.exp(sharpness * (sims - 1.0))
    affinity = jnp.mean(expo, 1)
    offset = lax.axis_index(("dp", "rep")) * captions_here
    own_block = lax.dynamic_slice_in_dim(affinity, offset, captions_here, 1).reshape(
        row_count, row_count, 2
    )
    diagonal = (
        lax.broadcasted_iota(jnp.int32, (row_count, row_count), 0)
        == lax.broadcasted_iota(jnp.int32, (row_count, row_count), 1)
    ).astype(f32)
    positive = jnp.sum(own_block * diagonal[:, :, None], 1)
    row_total = jnp.sum(affinity, 1)
    partial_cols = jnp.sum(affinity, 0)
    all_cols = jnp.sum(
        exchange(jnp.broadcast_to(partial_cols[None], (world,) + partial_cols.shape), sizes), 0
    )
    own_cols = lax.dynamic_slice_in_dim(all_cols, offset, captions_here, 0).reshape(row_count, 2)
    inverse_all = 1.0 / all_cols
    row_loss = (
        jnp.log(row_total)
        - jnp.log(positive[:, 0])
        + jnp.sum(jnp.log(own_cols) - jnp.log(positive), 1)
    )
    grad_affinity = loss_weight * (1.0 / row_total[:, None] + inverse_all[None, :])
    pair_weight = jnp.array([2.0, 1.0], f32)
    correction = (loss_weight * diagonal[:, :, None] * pair_weight / own_block).reshape(
        row_count, captions_here
    )
    own_grad = lax.dynamic_slice_in_dim(grad_affinity, offset, captions_here, 1) - correction
    grad_affinity = lax.dynamic_update_slice_in_dim(grad_affinity, own_grad, offset, 1)
    grad_sims = (grad_affinity[:, None, :] * expo * (sharpness / QUERIES)).astype(bf16)
    grad_query_embed = jnp.einsum(
        "rqc,cp->rqp", grad_sims, every_caption, preferred_element_type=f32
    )
    grad_caption_embed = scatter_rows(
        jnp.einsum("rqc,rqp->cp", grad_sims, query_embed, preferred_element_type=f32).astype(bf16),
        sizes,
    )
    query_raw_grad = unit_back(query_raw, grad_query_embed).astype(bf16)
    head_raw = jnp.sum(
        pick_full[:, :, :, None] * caption_raw.reshape(row_count, 1, TEXT, -1), 2
    )
    head_raw_grad = unit_back(head_raw, grad_caption_embed.reshape(row_count, 2, -1)).astype(bf16)
    caption_raw_grad = jnp.einsum(
        "rkt,rkd->rtd", pick_low, head_raw_grad, preferred_element_type=f32
    ).astype(bf16)
    grad_second, query_din, query_dout, query_dproj, query_side, query_dbias, query_dproj_bias = (
        ffn_backward(
            0,
            0,
            second_norm,
            third_sum,
            second_sum,
            layer_out,
            out_grad,
            query_raw_grad.reshape(row_count * QUERIES, -1),
            projections,
            norm_gains,
            ffn_in,
            ffn_out,
            query_act,
            query_slope,
        )
    )
    text_first, text_din, text_dout, text_dproj, text_side, text_dbias, text_dproj_bias = (
        ffn_backward(
            1,
            1,
            first_norm,
            fourth_sum,
            fourth_sum,
            layer_out,
            out_grad,
            caption_raw_grad.reshape(row_count * TEXT, -1),
            projections,
            norm_gains,
            ffn_in,
            ffn_out,
            text_act,
            text_slope,
        )
    )
    ffn_in_grad, ffn_out_grad, proj_grad = scatter_group(
        [(query_din, text_din), (query_dout, text_dout), (query_dproj, text_dproj)], sizes
    )
    query_first, key_grad, value_grad, cross_dw, cross_side = cross_backward(
        image_features,
        image_ends,
        attn_weights,
        first_norm,
        keys,
        values,
        key_ends,
        value_ends,
        cross_q,
        cross_mix,
        grad_second.reshape(row_count * QUERIES, width),
        text_first,
    )
    (cross_grad,) = scatter_group([(key_grad, value_grad)], sizes)
    input_grad, self_dw, self_side = self_backward(
        inputs,
        attn_weights,
        norm_gains,
        mask,
        self_q,
        self_k,
        self_v,
        self_mix,
        first_sum,
        query_first,
        text_first,
    )
    attn_pairs = ((self_dw[0], self_dw[3]), (self_dw[1], cross_dw[0]), (self_dw[2], cross_dw[1]))
    attn_grad = jnp.stack(scatter_group(attn_pairs, sizes))
    gain_grad = jnp.stack([self_side[0], query_side[3], query_side[0], text_side[0]])
    bias_grad = jnp.stack(
        [
            self_side[2],
            self_side[3],
            self_side[4],
            cross_side[0],
            cross_side[1],
            cross_side[2],
            query_side[2],
            text_side[2],
            self_side[1],
            query_side[4],
            query_side[1],
            text_side[1],
        ]
    )
    vectors = (
        gain_grad,
        bias_grad,
        jnp.stack([query_dbias[0], text_dbias[0]]),
        jnp.stack([query_dproj_bias[0], text_dproj_bias[0]]),
    )

    def deal(array):
        mats, cols = array.shape
        cut = array.reshape(sizes["rep"], mats // sizes["rep"], sizes["dp"], cols // sizes["dp"])
        return cut.transpose(2, 0, 1, 3).reshape(world, -1)

    dealt = jnp.concatenate([deal(array) for array in vectors], 1)
    arrived = jnp.sum(exchange(dealt, sizes), 0)
    small = []
    start = 0
    for array in vectors:
        mats, cols = array.shape[0] // sizes["rep"], array.shape[1] // sizes["dp"]
        small.append(arrived[start : start + mats * cols].reshape(mats, cols))
        start += mats * cols
    return (
        layer_out,
        row_loss,
        input_grad.reshape(hidden_states.shape),
        attn_grad,
        cross_grad[None],
        ffn_in_grad[None],
        ffn_out_grad[None],
        proj_grad[None],
        small[0],
        small[1],
        small[2],
        small[3],
    )


def solution(mesh):
    placed = (
        P(("dp", "rep"), None, None),
        P(("dp", "rep"), None, None),
        P(("dp", "rep"), None),
        P(),
        P(),
        P(),
        P(),
        P(),
        P(),
        P(),
        P(),
        P(),
        P(("dp", "rep"), None, None),
    )
    sizes = dict(mesh.shape)
    return jax.shard_map(
        functools.partial(shards, sizes=sizes),
        mesh=mesh,
        in_specs=placed,
        out_specs=(
            P(("dp", "rep"), None, None),
            P(("dp", "rep")),
            P(("dp", "rep"), None, None),
            P("rep", "dp", None),
            P("rep", "dp", None),
            P("rep", "dp", None),
            P("rep", "dp", None),
            P("rep", "dp", None),
            P("rep", "dp"),
            P("rep", "dp"),
            P("rep", "dp"),
            P("rep", "dp"),
        ),
        check_vma=False,
    )
```

```python
import functools

import jax
import jax.numpy as jnp
from jax import lax
from jax.experimental import pallas as pl
from jax.experimental.pallas import tpu as pltpu
from jax.sharding import PartitionSpec as P

HEADS = 12
QUERIES = 32
TEXT = 32
SLOTS = QUERIES + TEXT


blocked = -1000000000.0
epsilon = 1e-06
sharpness = 14.0
loss_weight = 16.0


def unit_rows(values):
    return values * lax.rsqrt(jnp.sum(values * values, -1, keepdims=True) + epsilon)


def unit_back(values, grad_rows):
    unused, pullback = jax.vjp(unit_rows, values)
    return pullback(grad_rows)[0]


def caption_layout(length_rows):
    row_count = length_rows.shape[0]
    first_len = length_rows[:, 0:1]
    second_end = first_len + length_rows[:, 1:2]
    slot_index = lax.broadcasted_iota(jnp.int32, (row_count, TEXT), 1)
    text_group = (slot_index >= first_len).astype(jnp.int32) + (slot_index >= second_end).astype(
        jnp.int32
    )
    group_ids = jnp.concatenate([jnp.full((row_count, QUERIES), -1, jnp.int32), text_group], 1)
    allowed = group_ids[:, :, None] == group_ids[:, None, :]
    head_starts = jnp.concatenate([jnp.zeros_like(first_len), first_len], 1)
    pick_mask = slot_index[:, None, :] == head_starts[:, :, None]
    return (allowed, pick_mask)


f32 = jnp.float32
bf16 = jnp.bfloat16
ROOT_HALF = 0.7071067811865476
ROOT_TAU = 0.3989422804014327
MIB = 1024 * 1024


def dot_nn(a, b):
    return lax.dot_general(a, b, (((1,), (0,)), ((), ())), preferred_element_type=f32)


def dot_nt(a, b):
    return lax.dot_general(a, b, (((1,), (1,)), ((), ())), preferred_element_type=f32)


def dot_tn(a, b):
    return lax.dot_general(a, b, (((0,), (0,)), ((), ())), preferred_element_type=f32)


def whole(shape):
    return pl.BlockSpec(shape, lambda *_: (0,) * len(shape))


def held(shape, index):
    return pl.BlockSpec(shape, index, pipeline_mode=pl.Buffered(1))


def cost(micros):
    return pl.CostEstimate(flops=int(micros * 1.1e9), bytes_accessed=0, transcendentals=0)


def store_units(ref, values):
    for place in range(values.shape[1] // 128):
        ref[place] = values[:, place * 128 : (place + 1) * 128].astype(ref.dtype)


def ordered(kernel, inputs, count):
    def run(*refs):
        kernel(*refs[:inputs], *refs[inputs + count :])

    return run


def unread(count):
    return [pl.BlockSpec(memory_space=pl.ANY)] * count


def params(mib):
    return pltpu.CompilerParams(vmem_limit_bytes=mib * MIB, dimension_semantics=("arbitrary",))


def norm_parts(values):
    center = values - jnp.mean(values, -1, keepdims=True)
    scale = lax.rsqrt(jnp.mean(center * center, -1, keepdims=True) + epsilon)
    return center * scale, scale


def norm_grads(values, gain_row, grad):
    unit, scale = norm_parts(values)
    inner = grad * gain_row
    first = jnp.mean(inner, -1, keepdims=True)
    second = jnp.mean(inner * unit, -1, keepdims=True)
    return (
        scale * (inner - first - unit * second),
        jnp.sum(grad * unit, 0, keepdims=True),
        jnp.sum(grad, 0, keepdims=True),
    )


def gate_parts(u):
    size = jnp.abs(u) * ROOT_HALF
    t = 1.0 / (1.0 + 0.3275911 * size)
    bell = jnp.exp(-size * size)
    poly = t * (
        0.127414796
        + t * (-0.142248368 + t * (0.7107068705 + t * (-0.7265760135 + t * 0.5307027145)))
    )
    tail = poly * bell
    cdf = jnp.where(u > 0, 1.0 - tail, tail)
    return u * cdf, cdf + (ROOT_TAU * u) * bell


def half_lanes(rows):
    low = (lax.broadcasted_iota(jnp.int32, (rows, 128), 1) < 64).astype(f32)
    return low.astype(bf16), (1.0 - low).astype(bf16)


def spread_heads(x, low, high):
    left, right = x[:, :128], x[:, 128:]
    none = jnp.zeros_like(left)
    return jnp.concatenate(
        [
            jnp.concatenate([left * low, none], 1),
            jnp.concatenate([left * high, none], 1),
            jnp.concatenate([none, right * low], 1),
            jnp.concatenate([none, right * high], 1),
        ],
        0,
    )


def collect_heads(o, n):
    low = lax.broadcasted_iota(jnp.int32, (n, 128), 1) < 64
    left = jnp.where(low, o[:n, :128], o[n : 2 * n, :128])
    right = jnp.where(low, o[2 * n : 3 * n, 128:], o[3 * n :, 128:])
    return jnp.concatenate([left, right], 1)


def columns_softmax(scores):
    raised = jnp.exp(scores - jnp.max(scores, 0, keepdims=True))
    return raised * (1.0 / jnp.sum(raised, 0, keepdims=True))


GROUPS = HEADS // 4


def self_forward_kernel(
    x_ref, w_ref, bias_ref, gain_ref, mask_ref, q_ref, k_ref, v_ref, mix_ref, sum_ref, norm_ref
):
    x = x_ref[...]
    q_ref[...] = (dot_nn(x, w_ref[0]) + bias_ref[0:1]).astype(bf16)
    k_ref[...] = dot_nn(x, w_ref[1]).astype(bf16)
    v_ref[...] = (dot_nn(x, w_ref[2]) + bias_ref[1:2]).astype(bf16)
    low, high = half_lanes(SLOTS)

    def one_row(r, carry):
        rows = pl.ds(pl.multiple_of(r * SLOTS, SLOTS), SLOTS)
        allowed = mask_ref[r] > 0.0
        for g in range(GROUPS):
            cols = slice(g * 256, (g + 1) * 256)
            queries = spread_heads(q_ref[rows, cols] * bf16(0.125), low, high)
            scores = jnp.where(allowed, dot_nt(k_ref[rows, cols], queries), blocked)
            prob = columns_softmax(scores).astype(bf16)
            mixed = dot_tn(prob, v_ref[rows, cols])
            mix_ref[rows, cols] = collect_heads(mixed, SLOTS).astype(bf16)
        return carry

    lax.fori_loop(0, x_ref.shape[0] // SLOTS, one_row, 0)
    total = x.astype(f32) + dot_nn(mix_ref[...], w_ref[3]) + bias_ref[2:3]
    sum_ref[...] = total
    unit, _ = norm_parts(total)
    norm_ref[...] = unit * gain_ref[0:1] + bias_ref[8:9]


def self_forward(x, weights, biases, gains, mask):
    tokens, width = x.shape
    step = 4 * SLOTS
    tile = pl.BlockSpec((step, width), lambda i: (i, 0))
    low, full = jax.ShapeDtypeStruct(x.shape, bf16), jax.ShapeDtypeStruct(x.shape, f32)
    return pl.pallas_call(
        self_forward_kernel,
        grid=(tokens // step,),
        in_specs=[
            tile,
            held((4, width, width), lambda i: (0, 0, 0)),
            whole(biases.shape),
            whole(gains.shape),
            pl.BlockSpec((4,) + mask.shape[1:], lambda i: (i, 0, 0)),
        ],
        out_specs=[tile] * 6,
        out_shape=[low, low, low, low, full, full],
        compiler_params=params(58),
        name="self_forward",
        cost_estimate=cost(27),
    )(x, weights, biases, gains, mask)


def self_backward_kernel(
    w_ref,
    gain_ref,
    mask_ref,
    q_ref,
    k_ref,
    v_ref,
    sum_ref,
    top_ref,
    low_ref,
    grad_ref,
    branch_ref,
    down_ref,
    side_ref,
    dmix_all,
):
    step = pl.program_id(0)
    count = sum_ref.shape[0]
    low, high = half_lanes(SLOTS)

    @pl.when(step == 0)
    def _():
        side_ref[...] = jnp.zeros_like(side_ref)

    grad = jnp.concatenate([top_ref[...], low_ref[...]], 1).reshape(count, -1)
    down, dgain, dshift = norm_grads(sum_ref[...], gain_ref[0:1], grad)
    branch = down.astype(bf16)
    down_ref[...] = down
    branch_ref[...] = branch
    dmix_all[...] = dot_nt(branch, w_ref[0]).astype(bf16)

    def one_row(r, carry):
        rows = pl.ds(pl.multiple_of(r * SLOTS, SLOTS), SLOTS)
        allowed = mask_ref[r] > 0.0
        for g in range(GROUPS):
            cols = slice(g * 256, (g + 1) * 256)
            keys = k_ref[rows, cols]
            queries = spread_heads(q_ref[rows, cols] * bf16(0.125), low, high)
            outs = spread_heads(dmix_all[rows, cols], low, high)
            prob = columns_softmax(jnp.where(allowed, dot_nt(keys, queries), blocked))
            dprob = dot_nt(v_ref[rows, cols], outs)
            dscore = (prob * (dprob - jnp.sum(dprob * prob, 0, keepdims=True))).astype(bf16)
            grad_ref[2, rows, cols] = dot_nn(prob.astype(bf16), outs).astype(bf16)
            grad_ref[1, rows, cols] = dot_nn(dscore, queries).astype(bf16)
            turned = collect_heads(dot_tn(dscore, keys), SLOTS) * 0.125
            grad_ref[0, rows, cols] = turned.astype(bf16)
        return carry

    lax.fori_loop(0, count // SLOTS, one_row, 0)
    side_ref[0:1] += dgain
    side_ref[1:2] += dshift
    for place, rows in enumerate((grad_ref[0], grad_ref[2], branch)):
        side_ref[2 + place : 3 + place] += jnp.sum(rows.astype(f32), 0, keepdims=True)


def self_backward(weights, gains, mask, q, k, v, total, top, text, order):
    tokens, width = q.shape
    count = 4 * SLOTS
    tile = pl.BlockSpec((count, width), lambda i: (i, 0))
    part = pl.BlockSpec((4, QUERIES, width), lambda i: (i, 0, 0))
    return pl.pallas_call(
        ordered(self_backward_kernel, 9, len(order)),
        grid=(tokens // count,),
        in_specs=[
            held((1, width, width), lambda i: (3, 0, 0)),
            whole(gains.shape),
            pl.BlockSpec((4,) + mask.shape[1:], lambda i: (i, 0, 0)),
            tile,
            tile,
            tile,
            tile,
            part,
            part,
        ]
        + unread(len(order)),
        out_specs=[
            pl.BlockSpec((3, count, width), lambda i: (0, i, 0)),
            tile,
            tile,
            whole((8, width)),
        ],
        out_shape=[
            jax.ShapeDtypeStruct((3, tokens, width), bf16),
            jax.ShapeDtypeStruct((tokens, width), bf16),
            jax.ShapeDtypeStruct((tokens, width), f32),
            jax.ShapeDtypeStruct((8, width), f32),
        ],
        scratch_shapes=[pltpu.VMEM((count, width), bf16)],
        compiler_params=params(58),
        name="self_backward",
        cost_estimate=cost(25),
    )(weights, gains, mask, q, k, v, total, top, text, *order)


def input_grad_kernel(w_ref, grad_ref, down_ref, dx_ref):
    dx_ref[...] = (
        down_ref[...]
        + dot_nt(grad_ref[0], w_ref[0])
        + dot_nt(grad_ref[1], w_ref[1])
        + dot_nt(grad_ref[2], w_ref[2])
    )


def input_gradient(weights, grads, down, order):
    tokens, width = down.shape
    count = 4 * SLOTS
    tile = pl.BlockSpec((count, width), lambda i: (i, 0))

    return pl.pallas_call(
        ordered(input_grad_kernel, 3, len(order)),
        grid=(tokens // count,),
        in_specs=[
            held((3, width, width), lambda i: (0, 0, 0)),
            pl.BlockSpec((3, count, width), lambda i: (0, i, 0)),
            tile,
        ]
        + unread(len(order)),
        out_specs=tile,
        out_shape=jax.ShapeDtypeStruct((tokens, width), f32),
        compiler_params=params(58),
        name="input_gradient",
        cost_estimate=cost(7),
    )(weights, grads, down, *order)


def place_of(order, row_block, rep):
    return tuple(rep if axis == "rep" else (row_block >> bit) & 1 for axis, bit in order)


def slab_shape(order, units, rows):
    return (2,) * (len(order) - 1) + (units, rows, 128)


def store_halves(core_ref, keep_ref, send_ref, pieces):
    for core in range(2):

        @pl.when(core_ref[0] == core)
        def _():
            for places, block in pieces:
                ref = keep_ref if places[0] == core else send_ref
                ref[places[1:]] = block


core_spec = pl.BlockSpec(memory_space=pltpu.SMEM)


def attn_weight_kernel(fold, core_ref, left_ref, right_ref, left_two_ref, right_two_ref, *outs):
    out_ref = outs[0]
    pieces = []
    for rep, (left, right) in enumerate(((left_ref, right_ref), (left_two_ref, right_two_ref))):
        width = right.shape[-1]
        lhs = left[...].reshape(-1, width).astype(bf16)
        rhs = right[...].reshape(-1, width).astype(bf16)
        grad = dot_tn(lhs, rhs).astype(bf16)
        if fold is None:
            store_units(out_ref.at[rep], grad)
            continue
        rows = out_ref.shape[-2]
        for block in range(width // rows):
            spot = place_of(fold, block, rep)
            for unit in range(width // 128):
                piece = grad[block * rows : (block + 1) * rows, unit * 128 : (unit + 1) * 128]
                pieces.append((spot + (unit,), piece))
    if fold is not None:
        store_halves(core_ref, *outs, pieces)


def attn_weight_grad(part, core, left, grads, left_two, left_two_spec, right_two, fold, rows, order):
    tokens, width = left.shape
    if fold is None:
        shape = (2, width // 128, width, 128)
    else:
        shape = slab_shape(fold, width // 128, rows)
    return pl.pallas_call(
        ordered(functools.partial(attn_weight_kernel, fold), 5, len(order)),
        grid=(1,),
        in_specs=[
            core_spec,
            whole(left.shape),
            pl.BlockSpec((1, tokens, width), lambda i: (part, 0, 0)),
            left_two_spec,
            whole(right_two.shape),
        ]
        + unread(len(order)),
        out_specs=[whole(shape)] * (1 if fold is None else 2),
        out_shape=[jax.ShapeDtypeStruct(shape, bf16)] * (1 if fold is None else 2),
        compiler_params=params(58),
        name="attn_weight_grad",
        cost_estimate=cost(6),
    )(core, left, grads, left_two, right_two, *order)


TAIL = 16


def cross_forward_kernel(
    image_ref,
    end_ref,
    kv_ref,
    w_ref,
    bias_ref,
    gain_ref,
    norm_ref,
    key_ref,
    value_ref,
    key_end_ref,
    value_end_ref,
    q_ref,
    mix_ref,
    sum_ref,
    out_ref,
):
    rows_here = image_ref.shape[0]
    main = image_ref.shape[1] - 1
    width = norm_ref.shape[-1]
    end = end_ref[...].reshape(rows_here * TAIL, -1)
    key_end_ref[...] = dot_nt(end, kv_ref[0]).astype(bf16)
    value_end_ref[...] = (dot_nt(end, kv_ref[1]) + bias_ref[4:5]).astype(bf16)
    residual = norm_ref[...].reshape(rows_here * QUERIES, width)
    q_ref[...] = (dot_nn(residual.astype(bf16), w_ref[0]) + bias_ref[3:4]).astype(bf16)
    low, high = half_lanes(QUERIES)
    shown = lax.broadcasted_iota(jnp.int32, (main + TAIL, 128), 0) <= main
    tokens = image_ref[:, :main].reshape(rows_here * main, -1)
    key_ref[...] = dot_nt(tokens, kv_ref[0]).astype(bf16)
    value_ref[...] = (dot_nt(tokens, kv_ref[1]) + bias_ref[4:5]).astype(bf16)

    def one_row(r, carry):
        span = pl.ds(pl.multiple_of(r * main, main), main)
        last = pl.ds(pl.multiple_of(r * TAIL, TAIL), TAIL)
        mine = pl.ds(pl.multiple_of(r * QUERIES, QUERIES), QUERIES)
        for g in range(GROUPS):
            cols = slice(g * 256, (g + 1) * 256)
            keys = jnp.concatenate([key_ref[span, cols], key_end_ref[last, cols]], 0)
            values = jnp.concatenate([value_ref[span, cols], value_end_ref[last, cols]], 0)
            queries = spread_heads(q_ref[mine, cols] * bf16(0.125), low, high)
            prob = columns_softmax(jnp.where(shown, dot_nt(keys, queries), blocked)).astype(bf16)
            mix_ref[mine, cols] = collect_heads(dot_tn(prob, values), QUERIES).astype(bf16)
        return carry

    lax.fori_loop(0, rows_here, one_row, 0)
    total = residual + dot_nn(mix_ref[...], w_ref[1]) + bias_ref[5:6]
    sum_ref[...] = total
    unit, _ = norm_parts(total)
    out_ref[...] = unit * gain_ref[1:2] + bias_ref[9:10]


def cross_forward(images, ends, kv, weights, biases, gains, norm):
    rows, patches, vis = images.shape
    main = patches - 1
    width = norm.shape[-1]
    take = 4
    keys = pl.BlockSpec((take * main, width), lambda i: (i, 0))
    tails = pl.BlockSpec((take * TAIL, width), lambda i: (i, 0))
    tile = pl.BlockSpec((take * QUERIES, width), lambda i: (i, 0))

    def shape(count, dtype):
        return jax.ShapeDtypeStruct((rows * count, width), dtype)

    return pl.pallas_call(
        cross_forward_kernel,
        grid=(rows // take,),
        in_specs=[
            pl.BlockSpec((take, patches, vis), lambda i: (i, 0, 0)),
            pl.BlockSpec((take, TAIL, vis), lambda i: (i, 0, 0)),
            held(kv.shape, lambda i: (0, 0, 0)),
            held((2, width, width), lambda i: (2, 0, 0)),
            whole(biases.shape),
            whole(gains.shape),
            pl.BlockSpec((take, QUERIES, width), lambda i: (i, 0, 0)),
        ],
        out_specs=[keys, keys, tails, tails, tile, tile, tile, tile],
        out_shape=[
            shape(main, bf16),
            shape(main, bf16),
            shape(TAIL, bf16),
            shape(TAIL, bf16),
            shape(QUERIES, bf16),
            shape(QUERIES, bf16),
            shape(QUERIES, f32),
            shape(QUERIES, f32),
        ],
        compiler_params=params(58),
        name="cross_forward",
        cost_estimate=cost(55),
    )(images, ends, kv, weights, biases, gains, norm)


def cross_backward_kernel(
    w_ref,
    key_ref,
    value_ref,
    key_end_ref,
    value_end_ref,
    q_ref,
    down_ref,
    dnorm_ref,
    dkv_ref,
    dkv_end_ref,
    dq_ref,
    side_ref,
    dmix_all,
):
    step = pl.program_id(0)
    rows_here, _, width = dnorm_ref.shape
    main = key_ref.shape[0] // rows_here
    low, high = half_lanes(QUERIES)
    shown = lax.broadcasted_iota(jnp.int32, (main + TAIL, 128), 0) <= main

    @pl.when(step == 0)
    def _():
        side_ref[...] = jnp.zeros_like(side_ref)

    down = down_ref[...]
    branch = down.astype(bf16)
    dmix_all[...] = dot_nt(branch, w_ref[1]).astype(bf16)

    def one_row(r, carry):
        span = pl.ds(pl.multiple_of(r * main, main), main)
        last = pl.ds(pl.multiple_of(r * TAIL, TAIL), TAIL)
        mine = pl.ds(pl.multiple_of(r * QUERIES, QUERIES), QUERIES)
        for g in range(GROUPS):
            cols = slice(g * 256, (g + 1) * 256)
            keys = jnp.concatenate([key_ref[span, cols], key_end_ref[last, cols]], 0)
            values = jnp.concatenate([value_ref[span, cols], value_end_ref[last, cols]], 0)
            queries = spread_heads(q_ref[mine, cols] * bf16(0.125), low, high)
            outs = spread_heads(dmix_all[mine, cols], low, high)
            prob = columns_softmax(jnp.where(shown, dot_nt(keys, queries), blocked))
            dprob = dot_nt(values, outs)
            dscore = (prob * (dprob - jnp.sum(dprob * prob, 0, keepdims=True))).astype(bf16)
            dv = dot_nn(prob.astype(bf16), outs).astype(bf16)
            dk = dot_nn(dscore, queries).astype(bf16)
            dkv_ref[0, span, cols] = dk[:main]
            dkv_end_ref[0, last, cols] = dk[main:]
            dkv_ref[1, span, cols] = dv[:main]
            dkv_end_ref[1, last, cols] = dv[main:]
            dq_ref[mine, cols] = (collect_heads(dot_tn(dscore, keys), QUERIES) * 0.125).astype(bf16)
        return carry

    lax.fori_loop(0, rows_here, one_row, 0)
    dq = dq_ref[...]
    dnorm_ref[...] = (down + dot_nt(dq, w_ref[0])).reshape(rows_here, QUERIES, width)
    side_ref[0:1] += jnp.sum(dq.astype(f32), 0, keepdims=True)
    side_ref[1:2] += jnp.sum(dkv_ref[1].astype(f32), 0, keepdims=True) + jnp.sum(
        dkv_end_ref[1].astype(f32), 0, keepdims=True
    )
    side_ref[2:3] += jnp.sum(branch.astype(f32), 0, keepdims=True)


def cross_backward(rows, weights, keys, values, key_ends, value_ends, q, down, order):
    width = q.shape[1]
    main = keys.shape[0] // rows
    take = 4
    span = pl.BlockSpec((take * main, width), lambda i: (i, 0))
    tails = pl.BlockSpec((take * TAIL, width), lambda i: (i, 0))
    tile = pl.BlockSpec((take * QUERIES, width), lambda i: (i, 0))
    return pl.pallas_call(
        ordered(cross_backward_kernel, 7, len(order)),
        grid=(rows // take,),
        in_specs=[
            held((2, width, width), lambda i: (2, 0, 0)),
            span,
            span,
            tails,
            tails,
            tile,
            tile,
        ]
        + unread(len(order)),
        out_specs=[
            pl.BlockSpec((take, QUERIES, width), lambda i: (i, 0, 0)),
            pl.BlockSpec((2, take * main, width), lambda i: (0, i, 0)),
            pl.BlockSpec((2, take * TAIL, width), lambda i: (0, i, 0)),
            tile,
            whole((8, width)),
        ],
        out_shape=[
            jax.ShapeDtypeStruct((rows, QUERIES, width), f32),
            jax.ShapeDtypeStruct((2, rows * main, width), bf16),
            jax.ShapeDtypeStruct((2, rows * TAIL, width), bf16),
            jax.ShapeDtypeStruct((rows * QUERIES, width), bf16),
            jax.ShapeDtypeStruct((8, width), f32),
        ],
        scratch_shapes=[pltpu.VMEM((take * QUERIES, width), bf16)],
        compiler_params=params(58),
        name="cross_backward",
        cost_estimate=cost(40),
    )(weights, keys, values, key_ends, value_ends, q, down, *order)


def cross_weight_kernel(fold, core_ref, image_ref, end_ref, grad_ref, grad_end_ref, *rest):
    outs, gathered = rest[:-1], rest[-1]
    rows, patches, vis = image_ref.shape
    main = patches - 1
    take = 4
    gathered[...] = dot_tn(grad_end_ref[0], end_ref[...].reshape(rows * TAIL, vis))

    def add_rows(i, carry):
        span = pl.ds(pl.multiple_of(i * take * main, take * main), take * main)
        tokens = image_ref[pl.ds(i * take, take), :main].reshape(take * main, vis)
        gathered[...] += dot_tn(grad_ref[0, span], tokens)
        return carry

    lax.fori_loop(0, rows // take, add_rows, 0)
    if fold is None:
        store_units(outs[0].at[0], gathered[...])
        return
    units, size = outs[0].shape[-3:-1]
    pieces = []
    for block in range(gathered.shape[0] // size):
        spot = tuple(0 if axis == "rep" or bit == 3 else (block >> bit) & 1 for axis, bit in fold)
        piece = gathered[block * size : (block + 1) * size].astype(bf16)
        for unit in range(units):
            pieces.append((spot + (unit,), piece[:, unit * 128 : (unit + 1) * 128]))
    store_halves(core_ref, *outs, pieces)


def cross_weight_grad(core, images, ends, grads, grads_end, fold, size, order):
    rows, patches, vis = images.shape
    width = grads.shape[2]
    half = width // 2
    units = vis // 128
    if fold is None:
        specs = [pl.BlockSpec((1, units, half, 128), lambda m, h: (m, 0, h, 0))]
        shapes = [(2, units, width, 128)]
    else:
        shapes = [slab_shape(fold, units, size)] * 2
        block = tuple(1 if axis == "rep" or bit == 3 else 2 for axis, bit in fold[1:])

        def index(m, h):
            spot = tuple(m if axis == "rep" else h if bit == 3 else 0 for axis, bit in fold[1:])
            return spot + (0, 0, 0)

        specs = [pl.BlockSpec(block + (units, size, 128), index)] * 2
    return pl.pallas_call(
        ordered(functools.partial(cross_weight_kernel, fold), 5, len(order)),
        grid=(2, 2),
        in_specs=[
            core_spec,
            held(images.shape, lambda m, h: (0, 0, 0)),
            held(ends.shape, lambda m, h: (0, 0, 0)),
            pl.BlockSpec((1, grads.shape[1], half), lambda m, h: (m, 0, h)),
            pl.BlockSpec((1, grads_end.shape[1], half), lambda m, h: (m, 0, h)),
        ]
        + unread(len(order)),
        out_specs=specs,
        out_shape=[jax.ShapeDtypeStruct(shape, bf16) for shape in shapes],
        scratch_shapes=[pltpu.VMEM((half, vis), f32)],
        compiler_params=pltpu.CompilerParams(
            vmem_limit_bytes=58 * MIB, dimension_semantics=("arbitrary", "arbitrary")
        ),
        name="cross_weight_grad",
        cost_estimate=cost(30),
    )(core, images, ends, grads, grads_end, *order)


def ffn_forward_kernel(
    which,
    norm_ref,
    in_ref,
    in_bias_ref,
    out_ref,
    proj_ref,
    proj_bias_ref,
    bias_ref,
    gain_ref,
    *rest,
):
    act_ref, slope_ref, sum_ref, low_ref, raw_ref, embed_ref, rows_low = rest[-7:]
    step = pl.program_id(0)
    tokens, width = sum_ref.shape

    @pl.when(step == 0)
    def _():
        full = norm_ref[...].reshape(tokens, width)
        rows_low[...] = full.astype(bf16)
        sum_ref[...] = full + bias_ref[6 + which : 7 + which]

    u = dot_nn(rows_low[...], in_ref[0]) + in_bias_ref[which : which + 1]
    act, slope = gate_parts(u)
    act = act.astype(bf16)
    act_ref[...] = act
    slope_ref[...] = slope.astype(bf16)
    sum_ref[...] += dot_nn(act, out_ref[0])

    @pl.when(step == pl.num_programs(0) - 1)
    def _():
        unit, _ = norm_parts(sum_ref[...])
        low = (unit * gain_ref[2 + which : 3 + which] + bias_ref[10 + which : 11 + which]).astype(bf16)
        low_ref[...] = low.reshape(low_ref.shape)
        raw = dot_nn(low, proj_ref[0]) + proj_bias_ref[which : which + 1]
        raw_ref[...] = raw
        size = lax.rsqrt(jnp.sum(raw * raw, -1, keepdims=True) + epsilon)
        embed_ref[...] = (raw * size).astype(bf16)


def ffn_forward(which, part, norm, ffn_in, ffn_bias, ffn_out, projections, proj_bias, biases, gains, layer, order=()):
    rows, width = norm.shape[0], norm.shape[-1]
    tokens = rows * QUERIES
    hidden = ffn_in.shape[2]
    embed = projections.shape[2]
    chunk = 512
    cols = pl.BlockSpec((tokens, chunk), lambda j: (0, j))
    halves = [] if layer is None else [layer]
    return pl.pallas_call(
        functools.partial(ffn_forward_kernel, which),
        grid=(hidden // chunk,),
        in_specs=[
            held((rows, QUERIES, width), lambda j: (0, part, 0)),
            pl.BlockSpec((1, width, chunk), lambda j: (which, 0, j)),
            pl.BlockSpec((2, chunk), lambda j: (0, j)),
            pl.BlockSpec((1, chunk, width), lambda j: (which, j, 0)),
            held((1, width, embed), lambda j: (which, 0, 0)),
            whole(proj_bias.shape),
            whole(biases.shape),
            whole(gains.shape),
        ]
        + unread(len(halves) + len(order)),
        out_specs=[
            cols,
            cols,
            whole((tokens, width)),
            pl.BlockSpec((rows, QUERIES, width), lambda j: (0, which, 0)),
            whole((tokens, embed)),
            whole((tokens, embed)),
        ],
        out_shape=[
            jax.ShapeDtypeStruct((tokens, hidden), bf16),
            jax.ShapeDtypeStruct((tokens, hidden), bf16),
            jax.ShapeDtypeStruct((tokens, width), f32),
            jax.ShapeDtypeStruct((rows, SLOTS, width), bf16),
            jax.ShapeDtypeStruct((tokens, embed), f32),
            jax.ShapeDtypeStruct((tokens, embed), bf16),
        ],
        scratch_shapes=[pltpu.VMEM((tokens, width), bf16)],
        input_output_aliases={8: 3} if halves else {},
        compiler_params=params(58),
        name="ffn_forward",
        cost_estimate=cost(15),
    )(norm, ffn_in, ffn_bias, ffn_out, projections, proj_bias, biases, gains, *halves, *order)


def ffn_backward_kernel(
    which,
    folds,
    core_ref,
    norm_ref,
    sum_ref,
    before_ref,
    layer_ref,
    grad_ref,
    raw_ref,
    proj_ref,
    gain_ref,
    in_ref,
    out_ref,
    act_ref,
    slope_ref,
    *rest,
):
    count = 3 if folds is None else 6
    down_ref, side_ref, dbias_ref, dproj_bias_ref = rest[-8 - count : -4 - count]
    weight_refs = rest[-4 - count : -4]
    branch_all, low_turned, left, dproj = rest[-4:]
    step = pl.program_id(0)
    tokens, width = sum_ref.shape

    @pl.when(step == 0)
    def _():
        raw = raw_ref[...]
        grad = grad_ref[...].reshape(tokens, width).astype(f32) + dot_nt(raw, proj_ref[0])
        down, dgain, dshift = norm_grads(sum_ref[...], gain_ref[2 + which : 3 + which], grad)
        branch = down.astype(bf16)
        branch_all[...] = branch
        left[...] = down
        side_ref[...] = jnp.zeros_like(side_ref)
        side_ref[0:1] = dgain
        side_ref[1:2] = dshift
        side_ref[2:3] = jnp.sum(branch.astype(f32), 0, keepdims=True)
        dproj[...] = dot_tn(layer_ref[...].reshape(tokens, width), raw).astype(bf16)
        dproj_bias_ref[...] = jnp.broadcast_to(
            jnp.sum(raw.astype(f32), 0, keepdims=True), dproj_bias_ref.shape
        )
        low_turned[...] = norm_ref[...].reshape(tokens, width).astype(bf16).T

    branch = branch_all[...]
    du = (dot_nt(branch, out_ref[0]) * slope_ref[...].astype(f32)).astype(bf16)
    left[...] += dot_nt(du, in_ref[0])
    dbias_ref[...] = jnp.broadcast_to(jnp.sum(du.astype(f32), 0, keepdims=True), dbias_ref.shape)
    thin = width // 3
    for part in range(3):

        @pl.when(step == part)
        def _():
            din = dot_nn(low_turned[...], du).astype(bf16)
            dout = dot_tn(act_ref[...], branch[:, part * thin : (part + 1) * thin]).astype(bf16)
            if folds is None:
                store_units(weight_refs[0], din)
                store_units(weight_refs[1], dout)
                if part == 0:
                    store_units(weight_refs[2], dproj[...])
                return
            keep, send = weight_refs[2 * part : 2 * part + 2]
            size = keep.shape[-2]
            subs = dout.shape[0] // width
            pieces = []
            for block in range(width // size):
                spot = place_of(folds[part], block, 0)
                at = block * size
                found = [
                    din[at : at + size, unit * 128 : (unit + 1) * 128]
                    for unit in range(din.shape[1] // 128)
                ]
                for sub in range(subs):
                    row = at * subs + sub * size
                    for unit in range(thin // 128):
                        found.append(dout[row : row + size, unit * 128 : (unit + 1) * 128])
                if part == 0:
                    for unit in range(dproj.shape[1] // 128):
                        found.append(dproj[at : at + size, unit * 128 : (unit + 1) * 128])
                pieces += [(spot + (unit,), piece) for unit, piece in enumerate(found)]
            store_halves(core_ref, keep, send, pieces)

    @pl.when(step == pl.num_programs(0) - 1)
    def _():
        if which == 0:
            down, dgain, dshift = norm_grads(before_ref[...], gain_ref[1:2], left[...])
            side_ref[3:4] = dgain
            side_ref[4:5] = dshift
            down_ref[...] = down.reshape(down_ref.shape)
        else:
            down_ref[...] = left[...].reshape(down_ref.shape)


def ffn_backward(
    which,
    part,
    core,
    norm,
    total,
    before,
    layer,
    grad,
    raw,
    projections,
    gains,
    ffn_in,
    ffn_out,
    act,
    slope,
    slabs,
    folds,
    size,
):
    rows = layer.shape[0]
    tokens, width = total.shape
    hidden = ffn_in.shape[2]
    embed = projections.shape[2]
    chunk = hidden // 3
    slabs = list(slabs)
    if folds is None:
        weight_specs = [
            pl.BlockSpec((chunk // 128, width, 128), lambda j: (j, 0, 0)),
            pl.BlockSpec((width // 384, hidden, 128), lambda j: (j, 0, 0)),
            whole((embed // 128, width, 128)),
        ]
        weight_shapes = [
            (hidden // 128, width, 128),
            (width // 128, hidden, 128),
            (embed // 128, width, 128),
        ]
    else:
        units = chunk // 128 + (hidden // width) * (width // 384)
        weight_shapes = [
            slab_shape(fold, units + (embed // 128 if k == 0 else 0), size)
            for k, fold in enumerate(folds)
            for half in range(2)
        ]

        def spec(fold, shape):
            block = tuple(1 if axis == "rep" else 2 for axis, bit in fold[1:])
            spot = tuple(which if axis == "rep" else 0 for axis, bit in fold[1:])
            return held(block + shape[-3:], lambda j: spot + (0, 0, 0))

        weight_specs = [spec(folds[k // 2], shape) for k, shape in enumerate(weight_shapes)]
    return pl.pallas_call(
        functools.partial(ffn_backward_kernel, which, folds),
        grid=(3,),
        in_specs=[
            core_spec,
            held((rows, QUERIES, width), lambda j: (0, part, 0)),
            held((tokens, width), lambda j: (0, 0)),
            held(before.shape, lambda j: (0, 0)),
            held((rows, QUERIES, width), lambda j: (0, which, 0)),
            held((rows, QUERIES, width), lambda j: (0, which, 0)),
            held((tokens, embed), lambda j: (0, 0)),
            held((1, width, embed), lambda j: (which, 0, 0)),
            whole(gains.shape),
            pl.BlockSpec((1, width, chunk), lambda j: (which, 0, j)),
            pl.BlockSpec((1, chunk, width), lambda j: (which, j, 0)),
            held((tokens, hidden), lambda j: (0, 0)),
            pl.BlockSpec((tokens, chunk), lambda j: (0, j)),
        ]
        + [pl.BlockSpec(memory_space=pl.ANY)] * len(slabs),
        out_specs=[
            whole((rows, QUERIES, width)),
            whole((8, width)),
            pl.BlockSpec((8, chunk), lambda j: (0, j)),
            whole((8, embed)),
        ]
        + weight_specs,
        out_shape=[
            jax.ShapeDtypeStruct((rows, QUERIES, width), f32),
            jax.ShapeDtypeStruct((8, width), f32),
            jax.ShapeDtypeStruct((8, hidden), f32),
            jax.ShapeDtypeStruct((8, embed), f32),
        ]
        + [jax.ShapeDtypeStruct(shape, bf16) for shape in weight_shapes],
        scratch_shapes=[
            pltpu.VMEM((tokens, width), bf16),
            pltpu.VMEM((width, tokens), bf16),
            pltpu.VMEM((tokens, width), f32),
            pltpu.VMEM((width, embed), bf16),
        ],
        input_output_aliases={13 + k: 4 + k for k in range(len(slabs))},
        compiler_params=params(60),
        name="ffn_backward",
        cost_estimate=cost(20),
    )(
        core,
        norm,
        total,
        before,
        layer,
        grad,
        raw,
        projections,
        gains,
        ffn_in,
        ffn_out,
        act,
        slope,
        *slabs,
    )


def own_bit(stage):
    axis, bit = stage
    return (lax.axis_index(axis) >> bit) & 1


def swap(values, stage, sizes):
    axis, bit = stage
    return lax.ppermute(values, axis, [(i, i ^ (1 << bit)) for i in range(sizes[axis])])


def total(terms, ahead=()):
    parts = []
    for array, places in terms:
        places = list(places) + list(ahead)
        rest = array.shape[len(places) :]
        if places:
            at = sum(place << shift for shift, place in enumerate(reversed(places)))
            flat = array.reshape((1 << len(places), -1, 128))
            array = lax.dynamic_index_in_dim(flat, at, 0, keepdims=False).reshape(rest)
        parts.append(array.astype(f32))
    return sum(parts)


def stage_order(part, sizes):
    stages = [("dp", bit) for bit in range(sizes["dp"].bit_length() - 1)]
    ring = stages[1:3] + [("rep", 0)]
    return stages[:1] + ring[part:] + ring[:part] + stages[3:]


def fold_pair(part, first, second, sizes):
    depth = sizes["dp"].bit_length() - 1
    both = jnp.stack([first, second])
    units, rows = first.shape[0], first.shape[1] // sizes["dp"]
    both = both.reshape((2, units) + (2,) * depth + (rows, 128))
    front = [0 if axis == "rep" else 1 + depth - bit for axis, bit in stage_order(part, sizes)]
    return both.transpose(front + [1, 2 + depth, 3 + depth])


def begin(part, keep, send, sizes):
    return (1, [(keep, []), (swap(send, stage_order(part, sizes)[0], sizes), [])], send)


def begin_folded(part, slab, sizes):
    mine = own_bit(stage_order(part, sizes)[0])
    halves = [lax.dynamic_index_in_dim(slab, place, 0, keepdims=False) for place in (mine, 1 - mine)]
    return begin(part, *halves, sizes)


def advance(part, state, sizes, after=None):
    stage, terms = state[0], state[1]
    if after is not None:
        array, places = terms[-1]
        terms = terms[:-1] + [(lax.optimization_barrier((array, after))[0], places)]
    axis_bit = stage_order(part, sizes)[stage]
    mine = own_bit(axis_bit)
    sent = total(terms, [1 - mine]).astype(bf16)
    arrived = swap(sent, axis_bit, sizes)
    terms = [(array, places + [mine]) for array, places in terms] + [(arrived, [])]
    return (stage + 1, terms, sent)


def advance_all(states, sizes, after=None):
    return [advance(part, state, sizes, after) for part, state in enumerate(states)]


def finish(part, state, sizes, after=None):
    while state[0] < len(stage_order(part, sizes)):
        state = advance(part, state, sizes, after)
        after = None
    terms = state[1]
    if after is not None:
        array, places = terms[-1]
        terms = terms[:-1] + [(lax.optimization_barrier((array, after))[0], places)]
    return total(terms)


def sends(states):
    return [state[2] for state in states]


def columns_of(units):
    return units.transpose(1, 0, 2).reshape(units.shape[1], -1)


def exchange(values, sizes):
    return lax.all_to_all(values, ("dp", "rep"), 0, 0, tiled=True)


def gather_rows(values, sizes):
    world = sizes["dp"] * sizes["rep"]
    return exchange(jnp.tile(values, (world, 1)), sizes)


def scatter_rows(values, sizes):
    world = sizes["dp"] * sizes["rep"]
    arrived = exchange(values, sizes)
    return jnp.sum(arrived.reshape(world, -1, values.shape[1]).astype(f32), 0)


def shards(
    hidden_states,
    image_features,
    caption_lengths,
    attn_weights,
    cross_kv,
    ffn_in,
    ffn_out,
    projections,
    norm_gains,
    biases,
    ffn_bias,
    proj_bias,
    out_grad,
    sizes,
):
    row_count, slots, width = hidden_states.shape
    captions_here = 2 * row_count
    world = sizes["dp"] * sizes["rep"]
    allowed, pick_mask = caption_layout(caption_lengths)
    pick_low = pick_mask.astype(bf16)
    pick_full = pick_mask.astype(f32)
    mask = jnp.tile(allowed.astype(f32), (1, 1, 4))
    inputs = hidden_states.reshape(row_count * slots, width)
    self_q, self_k, self_v, self_mix, first_sum, first_norm = self_forward(
        inputs, attn_weights, biases, norm_gains, mask
    )
    first_norm = first_norm.reshape(row_count, slots, width)
    image_ends = jnp.pad(image_features[:, -1:], ((0, 0), (0, TAIL - 1), (0, 0)))
    text_act, text_slope, fourth_sum, layer_half, caption_raw, caption_all = ffn_forward(
        1,
        1,
        first_norm,
        ffn_in,
        ffn_bias,
        ffn_out,
        projections,
        proj_bias,
        biases,
        norm_gains,
        None,
        [image_ends],
    )
    caption_embed = (
        jnp.einsum(
            "rkt,rtd->rkd",
            pick_low,
            caption_all.reshape(row_count, TEXT, -1),
            preferred_element_type=f32,
        )
        .astype(bf16)
        .reshape(captions_here, -1)
    )
    every_caption = gather_rows(caption_embed, sizes)
    keys, values, key_ends, value_ends, cross_q, cross_mix, second_sum, second_norm = cross_forward(
        image_features, image_ends, cross_kv, attn_weights, biases, norm_gains, first_norm
    )
    second_norm = second_norm.reshape(row_count, QUERIES, width)
    query_act, query_slope, third_sum, layer_out, query_raw, query_embed = ffn_forward(
        0,
        0,
        second_norm,
        ffn_in,
        ffn_bias,
        ffn_out,
        projections,
        proj_bias,
        biases,
        norm_gains,
        layer_half,
    )
    query_raw = query_raw.reshape(row_count, QUERIES, -1)
    query_embed = query_embed.reshape(row_count, QUERIES, -1)
    sims = jnp.einsum("rqp,cp->rqc", query_embed, every_caption, preferred_element_type=f32)
    expo = jnp.exp(sharpness * (sims - 1.0))
    affinity = jnp.mean(expo, 1)
    offset = lax.axis_index(("dp", "rep")) * captions_here
    own_block = lax.dynamic_slice_in_dim(affinity, offset, captions_here, 1).reshape(
        row_count, row_count, 2
    )
    diagonal = (
        lax.broadcasted_iota(jnp.int32, (row_count, row_count), 0)
        == lax.broadcasted_iota(jnp.int32, (row_count, row_count), 1)
    ).astype(f32)
    positive = jnp.sum(own_block * diagonal[:, :, None], 1)
    row_total = jnp.sum(affinity, 1)
    partial_cols = jnp.sum(affinity, 0)
    all_cols = jnp.sum(
        exchange(jnp.broadcast_to(partial_cols[None], (world,) + partial_cols.shape), sizes), 0
    )
    own_cols = lax.dynamic_slice_in_dim(all_cols, offset, captions_here, 0).reshape(row_count, 2)
    inverse_all = 1.0 / all_cols
    row_loss = (
        jnp.log(row_total)
        - jnp.log(positive[:, 0])
        + jnp.sum(jnp.log(own_cols) - jnp.log(positive), 1)
    )
    grad_affinity = loss_weight * (1.0 / row_total[:, None] + inverse_all[None, :])
    pair_weight = jnp.array([2.0, 1.0], f32)
    correction = (loss_weight * diagonal[:, :, None] * pair_weight / own_block).reshape(
        row_count, captions_here
    )
    own_grad = lax.dynamic_slice_in_dim(grad_affinity, offset, captions_here, 1) - correction
    grad_affinity = lax.dynamic_update_slice_in_dim(grad_affinity, own_grad, offset, 1)
    grad_sims = (grad_affinity[:, None, :] * expo * (sharpness / QUERIES)).astype(bf16)
    grad_query_embed = jnp.einsum(
        "rqc,cp->rqp", grad_sims, every_caption, preferred_element_type=f32
    )
    grad_caption_embed = scatter_rows(
        jnp.einsum("rqc,rqp->cp", grad_sims, query_embed, preferred_element_type=f32).astype(bf16),
        sizes,
    )
    query_raw_grad = unit_back(query_raw, grad_query_embed).astype(bf16)
    head_raw = jnp.sum(
        pick_full[:, :, :, None] * caption_raw.reshape(row_count, 1, TEXT, -1), 2
    )
    head_raw_grad = unit_back(head_raw, grad_caption_embed.reshape(row_count, 2, -1)).astype(bf16)
    caption_raw_grad = jnp.einsum(
        "rkt,rkd->rtd", pick_low, head_raw_grad, preferred_element_type=f32
    ).astype(bf16)
    fold = sizes["dp"] == 16 and sizes["rep"] == 2
    stage_orders = [stage_order(part, sizes) for part in range(3)]
    folds = stage_orders if fold else None
    size = width // sizes["dp"]
    core = (lax.axis_index("dp") & 1).astype(jnp.int32).reshape(1)
    grad_second, query_side, query_dbias, query_dproj_bias, *query_slabs = ffn_backward(
        0,
        0,
        core,
        second_norm,
        third_sum,
        second_sum,
        layer_out,
        out_grad,
        query_raw_grad.reshape(row_count * QUERIES, -1),
        projections,
        norm_gains,
        ffn_in,
        ffn_out,
        query_act,
        query_slope,
        (),
        folds,
        size,
    )
    text_first, text_side, text_dbias, text_dproj_bias, *text_slabs = ffn_backward(
        1,
        1,
        core,
        first_norm,
        fourth_sum,
        fourth_sum,
        layer_out,
        out_grad,
        caption_raw_grad.reshape(row_count * TEXT, -1),
        projections,
        norm_gains,
        ffn_in,
        ffn_out,
        text_act,
        text_slope,
        query_slabs if fold else (),
        folds,
        size,
    )
    tall = ffn_out.shape[1] // width
    if not fold:
        text_slabs = [
            fold_pair(
                part,
                *(
                    jnp.concatenate(
                        [
                            din[part * 8 : part * 8 + 8],
                            dout[2 * part : 2 * part + 2]
                            .reshape(2, sizes["dp"], tall, size, 128)
                            .transpose(2, 0, 1, 3, 4)
                            .reshape(2 * tall, width, 128),
                            dproj[: 2 if part == 0 else 0],
                        ],
                        0,
                    )
                    for din, dout, dproj in (query_slabs, text_slabs)
                ),
                sizes,
            )
            for part in range(3)
        ]
    if fold:
        ffn_states = [
            begin(part, *text_slabs[2 * part : 2 * part + 2], sizes) for part in range(3)
        ]
    else:
        ffn_states = [begin_folded(part, slab, sizes) for part, slab in enumerate(text_slabs)]
    cross_down = grad_second.reshape(row_count * QUERIES, width)
    query_first, dkv, dkv_ends, cross_dq, cross_side = cross_backward(
        row_count,
        attn_weights,
        keys,
        values,
        key_ends,
        value_ends,
        cross_q,
        cross_down,
        [text_first] + sends(ffn_states),
    )
    ffn_states = advance_all(ffn_states, sizes, cross_side)
    cross_slabs = cross_weight_grad(
        core,
        image_features,
        image_ends,
        dkv,
        dkv_ends,
        folds and folds[0],
        size,
        sends(ffn_states),
    )
    ffn_states = advance_all(ffn_states, sizes, cross_slabs[0])
    if fold:
        cross_states = [begin(0, *cross_slabs, sizes)]
    else:
        cross_states = [begin_folded(0, fold_pair(0, *cross_slabs[0], sizes), sizes)]
    self_grads, self_branch, self_down, self_side = self_backward(
        attn_weights,
        norm_gains,
        mask,
        self_q,
        self_k,
        self_v,
        first_sum,
        query_first,
        text_first,
        sends(ffn_states) + sends(cross_states),
    )
    ffn_states = advance_all(ffn_states, sizes, self_side)
    cross_states = advance_all(cross_states, sizes, self_side)
    query_half = pl.BlockSpec((row_count, QUERIES, width), lambda i: (0, 0, 0))
    attn_states = []
    order = sends(ffn_states) + sends(cross_states)
    for part, (left_two, spec, right_two) in enumerate(
        (
            (self_mix, whole(self_mix.shape), self_branch),
            (first_norm, query_half, cross_dq),
            (cross_mix, whole(cross_mix.shape), cross_down),
        )
    ):
        slabs = attn_weight_grad(
            part,
            core,
            inputs,
            self_grads,
            left_two,
            spec,
            right_two,
            folds and folds[part],
            size,
            order,
        )
        made = slabs[0]
        if fold:
            attn_states.append(begin(part, *slabs, sizes))
        else:
            attn_states.append(begin_folded(part, fold_pair(part, *made, sizes), sizes))
        order = sends(attn_states[-1:])
    ffn_states = advance_all(ffn_states, sizes, made)
    cross_states = advance_all(cross_states, sizes, made)
    input_grad = input_gradient(
        attn_weights,
        self_grads,
        self_down,
        order + sends(ffn_states) + sends(cross_states),
    )
    attn_grad = jnp.stack(
        [
            columns_of(finish(part, state, sizes, input_grad))
            for part, state in enumerate(attn_states)
        ]
    )
    ffn_sums = [finish(part, state, sizes, input_grad) for part, state in enumerate(ffn_states)]
    ffn_in_grad = jnp.concatenate([columns_of(each[:8]) for each in ffn_sums], 1)
    ffn_out_grad = jnp.concatenate(
        [
            each[8:16].reshape(tall, 2, size, 128).transpose(0, 2, 1, 3).reshape(tall * size, -1)
            for each in ffn_sums
        ],
        1,
    )
    proj_grad = columns_of(ffn_sums[0][16:])
    cross_grad = columns_of(finish(0, cross_states[0], sizes, input_grad))
    gain_grad = jnp.stack([self_side[0], query_side[3], query_side[0], text_side[0]])
    bias_grad = jnp.stack(
        [
            self_side[2],
            self_side[3],
            self_side[4],
            cross_side[0],
            cross_side[1],
            cross_side[2],
            query_side[2],
            text_side[2],
            self_side[1],
            query_side[4],
            query_side[1],
            text_side[1],
        ]
    )
    vectors = (
        gain_grad,
        bias_grad,
        jnp.stack([query_dbias[0], text_dbias[0]]),
        jnp.stack([query_dproj_bias[0], text_dproj_bias[0]]),
    )

    def deal(array):
        mats, cols = array.shape
        cut = array.reshape(sizes["rep"], mats // sizes["rep"], sizes["dp"], cols // sizes["dp"])
        return cut.transpose(2, 0, 1, 3).reshape(world, -1)

    dealt = jnp.concatenate([deal(array) for array in vectors], 1)
    arrived = jnp.sum(lax.optimization_barrier((exchange(dealt, sizes), input_grad))[0], 0)
    small = []
    start = 0
    for array in vectors:
        mats, cols = array.shape[0] // sizes["rep"], array.shape[1] // sizes["dp"]
        small.append(arrived[start : start + mats * cols].reshape(mats, cols))
        start += mats * cols
    return (
        layer_out,
        row_loss,
        input_grad.reshape(hidden_states.shape),
        attn_grad,
        cross_grad[None],
        ffn_in_grad[None],
        ffn_out_grad[None],
        proj_grad[None],
        small[0],
        small[1],
        small[2],
        small[3],
    )


def solution(mesh):
    placed = (
        P(("dp", "rep"), None, None),
        P(("dp", "rep"), None, None),
        P(("dp", "rep"), None),
        P(),
        P(),
        P(),
        P(),
        P(),
        P(),
        P(),
        P(),
        P(),
        P(("dp", "rep"), None, None),
    )
    sizes = dict(mesh.shape)
    return jax.shard_map(
        functools.partial(shards, sizes=sizes),
        mesh=mesh,
        in_specs=placed,
        out_specs=(
            P(("dp", "rep"), None, None),
            P(("dp", "rep")),
            P(("dp", "rep"), None, None),
            P("rep", "dp", None),
            P("rep", "dp", None),
            P("rep", "dp", None),
            P("rep", "dp", None),
            P("rep", "dp", None),
            P("rep", "dp"),
            P("rep", "dp"),
            P("rep", "dp"),
            P("rep", "dp"),
        ),
        check_vma=False,
    )
```

```python
import functools

import jax
import jax.numpy as jnp
from jax import lax
from jax.experimental import pallas as pl
from jax.experimental.pallas import tpu as pltpu
from jax.sharding import PartitionSpec as P

HEADS = 12
QUERIES = 32
TEXT = 32
SLOTS = QUERIES + TEXT


blocked = -1000000000.0
epsilon = 1e-06
sharpness = 14.0
loss_weight = 16.0


def unit_rows(values):
    return values * lax.rsqrt(jnp.sum(values * values, -1, keepdims=True) + epsilon)


def unit_back(values, grad_rows):
    unused, pullback = jax.vjp(unit_rows, values)
    return pullback(grad_rows)[0]


def caption_layout(length_rows):
    row_count = length_rows.shape[0]
    first_len = length_rows[:, 0:1]
    second_end = first_len + length_rows[:, 1:2]
    slot_index = lax.broadcasted_iota(jnp.int32, (row_count, TEXT), 1)
    text_group = (slot_index >= first_len).astype(jnp.int32) + (slot_index >= second_end).astype(
        jnp.int32
    )
    group_ids = jnp.concatenate([jnp.full((row_count, QUERIES), -1, jnp.int32), text_group], 1)
    allowed = group_ids[:, :, None] == group_ids[:, None, :]
    head_starts = jnp.concatenate([jnp.zeros_like(first_len), first_len], 1)
    pick_mask = slot_index[:, None, :] == head_starts[:, :, None]
    return (allowed, pick_mask)


f32 = jnp.float32
bf16 = jnp.bfloat16
ROOT_HALF = 0.7071067811865476
ROOT_TAU = 0.3989422804014327
MIB = 1024 * 1024


def dot_nn(a, b):
    return lax.dot_general(a, b, (((1,), (0,)), ((), ())), preferred_element_type=f32)


def dot_nt(a, b):
    return lax.dot_general(a, b, (((1,), (1,)), ((), ())), preferred_element_type=f32)


def dot_tn(a, b):
    return lax.dot_general(a, b, (((0,), (0,)), ((), ())), preferred_element_type=f32)


def whole(shape):
    return pl.BlockSpec(shape, lambda *_: (0,) * len(shape))


def held(shape, index):
    return pl.BlockSpec(shape, index, pipeline_mode=pl.Buffered(1))


def cost(micros):
    return pl.CostEstimate(flops=int(micros * 1.1e9), bytes_accessed=0, transcendentals=0)


def store_units(ref, values):
    for place in range(values.shape[1] // 128):
        ref[place] = values[:, place * 128 : (place + 1) * 128].astype(ref.dtype)


def ordered(kernel, inputs, count):
    def run(*refs):
        kernel(*refs[:inputs], *refs[inputs + count :])

    return run


def unread(count):
    return [pl.BlockSpec(memory_space=pl.ANY)] * count


def params(mib):
    return pltpu.CompilerParams(vmem_limit_bytes=mib * MIB, dimension_semantics=("arbitrary",))


def norm_parts(values):
    center = values - jnp.mean(values, -1, keepdims=True)
    scale = lax.rsqrt(jnp.mean(center * center, -1, keepdims=True) + epsilon)
    return center * scale, scale


def norm_grads(values, gain_row, grad):
    unit, scale = norm_parts(values)
    inner = grad * gain_row
    first = jnp.mean(inner, -1, keepdims=True)
    second = jnp.mean(inner * unit, -1, keepdims=True)
    return (
        scale * (inner - first - unit * second),
        jnp.sum(grad * unit, 0, keepdims=True),
        jnp.sum(grad, 0, keepdims=True),
    )


def gate_parts(u):
    size = jnp.abs(u) * ROOT_HALF
    t = 1.0 / (1.0 + 0.3275911 * size)
    bell = jnp.exp(-size * size)
    poly = t * (
        0.127414796
        + t * (-0.142248368 + t * (0.7107068705 + t * (-0.7265760135 + t * 0.5307027145)))
    )
    tail = poly * bell
    cdf = jnp.where(u > 0, 1.0 - tail, tail)
    return u * cdf, cdf + (ROOT_TAU * u) * bell


def half_lanes(rows):
    low = (lax.broadcasted_iota(jnp.int32, (rows, 128), 1) < 64).astype(f32)
    return low.astype(bf16), (1.0 - low).astype(bf16)


def spread_heads(x, low, high):
    left, right = x[:, :128], x[:, 128:]
    none = jnp.zeros_like(left)
    return jnp.concatenate(
        [
            jnp.concatenate([left * low, none], 1),
            jnp.concatenate([left * high, none], 1),
            jnp.concatenate([none, right * low], 1),
            jnp.concatenate([none, right * high], 1),
        ],
        0,
    )


def collect_heads(o, n):
    low = lax.broadcasted_iota(jnp.int32, (n, 128), 1) < 64
    left = jnp.where(low, o[:n, :128], o[n : 2 * n, :128])
    right = jnp.where(low, o[2 * n : 3 * n, 128:], o[3 * n :, 128:])
    return jnp.concatenate([left, right], 1)


def columns_softmax(scores):
    raised = jnp.exp(scores - jnp.max(scores, 0, keepdims=True))
    return raised * (1.0 / jnp.sum(raised, 0, keepdims=True))


GROUPS = HEADS // 4
SELF_ROWS = 4
CROSS_ROWS = 4
SELF_BACK_ROWS = 4
CROSS_BACK_ROWS = 4


def self_forward_kernel(
    x_ref, w_ref, bias_ref, gain_ref, mask_ref, q_ref, k_ref, v_ref, mix_ref, sum_ref, norm_ref
):
    x = x_ref[...]
    q_ref[...] = (dot_nn(x, w_ref[0]) + bias_ref[0:1]).astype(bf16)
    k_ref[...] = dot_nn(x, w_ref[1]).astype(bf16)
    v_ref[...] = (dot_nn(x, w_ref[2]) + bias_ref[1:2]).astype(bf16)
    low, high = half_lanes(SLOTS)

    def some_rows(step, carry):
        spots = []
        for near in range(SELF_ROWS):
            r = step * SELF_ROWS + near
            rows = pl.ds(pl.multiple_of(r * SLOTS, SLOTS), SLOTS)
            spots += [(r, rows, slice(g * 256, (g + 1) * 256)) for g in range(GROUPS)]
        scores = [
            dot_nt(
                k_ref[rows, cols], spread_heads(q_ref[rows, cols] * bf16(0.125), low, high)
            )
            for r, rows, cols in spots
        ]
        probs = [
            columns_softmax(jnp.where(mask_ref[r] > 0.0, score, blocked)).astype(bf16)
            for (r, rows, cols), score in zip(spots, scores)
        ]
        mixed = [dot_tn(prob, v_ref[rows, cols]) for (r, rows, cols), prob in zip(spots, probs)]
        for (r, rows, cols), mix in zip(spots, mixed):
            mix_ref[rows, cols] = collect_heads(mix, SLOTS).astype(bf16)
        return carry

    lax.fori_loop(0, x_ref.shape[0] // (SELF_ROWS * SLOTS), some_rows, 0)
    total = x.astype(f32) + dot_nn(mix_ref[...], w_ref[3]) + bias_ref[2:3]
    sum_ref[...] = total
    unit, _ = norm_parts(total)
    norm_ref[...] = unit * gain_ref[0:1] + bias_ref[8:9]


def self_forward(x, weights, biases, gains, mask):
    tokens, width = x.shape
    step = 4 * SLOTS
    tile = pl.BlockSpec((step, width), lambda i: (i, 0))
    low, full = jax.ShapeDtypeStruct(x.shape, bf16), jax.ShapeDtypeStruct(x.shape, f32)
    return pl.pallas_call(
        self_forward_kernel,
        grid=(tokens // step,),
        in_specs=[
            tile,
            held((4, width, width), lambda i: (0, 0, 0)),
            whole(biases.shape),
            whole(gains.shape),
            pl.BlockSpec((4,) + mask.shape[1:], lambda i: (i, 0, 0)),
        ],
        out_specs=[tile] * 6,
        out_shape=[low, low, low, low, full, full],
        compiler_params=params(58),
        name="self_forward",
        cost_estimate=cost(15),
    )(x, weights, biases, gains, mask)


def self_backward_kernel(
    w_ref,
    gain_ref,
    mask_ref,
    q_ref,
    k_ref,
    v_ref,
    sum_ref,
    top_ref,
    low_ref,
    grad_ref,
    branch_ref,
    down_ref,
    side_ref,
    dmix_all,
):
    step = pl.program_id(0)
    count = sum_ref.shape[0]
    low, high = half_lanes(SLOTS)

    @pl.when(step == 0)
    def _():
        side_ref[...] = jnp.zeros_like(side_ref)

    grad = jnp.concatenate([top_ref[...], low_ref[...]], 1).reshape(count, -1)
    down, dgain, dshift = norm_grads(sum_ref[...], gain_ref[0:1], grad)
    branch = down.astype(bf16)
    down_ref[...] = down
    branch_ref[...] = branch
    dmix_all[...] = dot_nt(branch, w_ref[0]).astype(bf16)

    def some_rows(step, carry):
        spots = []
        for near in range(SELF_BACK_ROWS):
            r = step * SELF_BACK_ROWS + near
            rows = pl.ds(pl.multiple_of(r * SLOTS, SLOTS), SLOTS)
            spots += [(r, rows, slice(g * 256, (g + 1) * 256)) for g in range(GROUPS)]
        queries = [
            spread_heads(q_ref[rows, cols] * bf16(0.125), low, high) for r, rows, cols in spots
        ]
        outs = [spread_heads(dmix_all[rows, cols], low, high) for r, rows, cols in spots]
        scores = [dot_nt(k_ref[spot[1:]], turned) for spot, turned in zip(spots, queries)]
        dprobs = [dot_nt(v_ref[spot[1:]], turned) for spot, turned in zip(spots, outs)]
        probs = [
            columns_softmax(jnp.where(mask_ref[spot[0]] > 0.0, score, blocked))
            for spot, score in zip(spots, scores)
        ]
        for spot, prob, turned in zip(spots, probs, outs):
            grad_ref[(2,) + spot[1:]] = dot_nn(prob.astype(bf16), turned).astype(bf16)
        dscores = [
            (prob * (dprob - jnp.sum(dprob * prob, 0, keepdims=True))).astype(bf16)
            for prob, dprob in zip(probs, dprobs)
        ]
        for spot, dscore, turned in zip(spots, dscores, queries):
            grad_ref[(1,) + spot[1:]] = dot_nn(dscore, turned).astype(bf16)
        dqs = [dot_tn(dscore, k_ref[spot[1:]]) for spot, dscore in zip(spots, dscores)]
        for spot, dq in zip(spots, dqs):
            grad_ref[(0,) + spot[1:]] = (collect_heads(dq, SLOTS) * 0.125).astype(bf16)
        return carry

    lax.fori_loop(0, count // (SELF_BACK_ROWS * SLOTS), some_rows, 0)
    side_ref[0:1] += dgain
    side_ref[1:2] += dshift
    for place, rows in enumerate((grad_ref[0], grad_ref[2], branch)):
        side_ref[2 + place : 3 + place] += jnp.sum(rows.astype(f32), 0, keepdims=True)


def self_backward(weights, gains, mask, q, k, v, total, top, text, order):
    tokens, width = q.shape
    count = 4 * SLOTS
    tile = pl.BlockSpec((count, width), lambda i: (i, 0))
    part = pl.BlockSpec((4, QUERIES, width), lambda i: (i, 0, 0))
    return pl.pallas_call(
        ordered(self_backward_kernel, 9, len(order)),
        grid=(tokens // count,),
        in_specs=[
            held((1, width, width), lambda i: (3, 0, 0)),
            whole(gains.shape),
            pl.BlockSpec((4,) + mask.shape[1:], lambda i: (i, 0, 0)),
            tile,
            tile,
            tile,
            tile,
            part,
            part,
        ]
        + unread(len(order)),
        out_specs=[
            pl.BlockSpec((3, count, width), lambda i: (0, i, 0)),
            tile,
            tile,
            whole((8, width)),
        ],
        out_shape=[
            jax.ShapeDtypeStruct((3, tokens, width), bf16),
            jax.ShapeDtypeStruct((tokens, width), bf16),
            jax.ShapeDtypeStruct((tokens, width), f32),
            jax.ShapeDtypeStruct((8, width), f32),
        ],
        scratch_shapes=[pltpu.VMEM((count, width), bf16)],
        compiler_params=params(58),
        name="self_backward",
        cost_estimate=cost(16),
    )(weights, gains, mask, q, k, v, total, top, text, *order)


def input_grad_kernel(w_ref, grad_ref, down_ref, dx_ref):
    dx_ref[...] = (
        down_ref[...]
        + dot_nt(grad_ref[0], w_ref[0])
        + dot_nt(grad_ref[1], w_ref[1])
        + dot_nt(grad_ref[2], w_ref[2])
    )


def input_gradient(weights, grads, down, order):
    tokens, width = down.shape
    count = 4 * SLOTS
    tile = pl.BlockSpec((count, width), lambda i: (i, 0))

    return pl.pallas_call(
        ordered(input_grad_kernel, 3, len(order)),
        grid=(tokens // count,),
        in_specs=[
            held((3, width, width), lambda i: (0, 0, 0)),
            pl.BlockSpec((3, count, width), lambda i: (0, i, 0)),
            tile,
        ]
        + unread(len(order)),
        out_specs=tile,
        out_shape=jax.ShapeDtypeStruct((tokens, width), f32),
        compiler_params=params(58),
        name="input_gradient",
        cost_estimate=cost(9),
    )(weights, grads, down, *order)


def place_of(order, row_block, rep):
    return tuple(rep if axis == "rep" else (row_block >> bit) & 1 for axis, bit in order)


def slab_shape(order, units, rows):
    return (2,) * (len(order) - 1) + (units, rows, 128)


def store_halves(core_ref, keep_ref, send_ref, pieces):
    for core in range(2):

        @pl.when(core_ref[0] == core)
        def _():
            for places, block in pieces:
                ref = keep_ref if places[0] == core else send_ref
                ref[places[1:]] = block


core_spec = pl.BlockSpec(memory_space=pltpu.SMEM)


def attn_weight_kernel(fold, core_ref, left_ref, right_ref, left_two_ref, right_two_ref, *outs):
    out_ref = outs[0]
    pieces = []
    for rep, (left, right) in enumerate(((left_ref, right_ref), (left_two_ref, right_two_ref))):
        width = right.shape[-1]
        lhs = left[...].reshape(-1, width).astype(bf16)
        rhs = right[...].reshape(-1, width).astype(bf16)
        grad = dot_tn(lhs, rhs).astype(bf16)
        if fold is None:
            store_units(out_ref.at[rep], grad)
            continue
        rows = out_ref.shape[-2]
        for block in range(width // rows):
            spot = place_of(fold, block, rep)
            for unit in range(width // 128):
                piece = grad[block * rows : (block + 1) * rows, unit * 128 : (unit + 1) * 128]
                pieces.append((spot + (unit,), piece))
    if fold is not None:
        store_halves(core_ref, *outs, pieces)


def attn_weight_grad(part, core, left, grads, left_two, left_two_spec, right_two, fold, rows, order):
    tokens, width = left.shape
    if fold is None:
        shape = (2, width // 128, width, 128)
    else:
        shape = slab_shape(fold, width // 128, rows)
    return pl.pallas_call(
        ordered(functools.partial(attn_weight_kernel, fold), 5, len(order)),
        grid=(1,),
        in_specs=[
            core_spec,
            whole(left.shape),
            pl.BlockSpec((1, tokens, width), lambda i: (part, 0, 0)),
            left_two_spec,
            whole(right_two.shape),
        ]
        + unread(len(order)),
        out_specs=[whole(shape)] * (1 if fold is None else 2),
        out_shape=[jax.ShapeDtypeStruct(shape, bf16)] * (1 if fold is None else 2),
        compiler_params=params(58),
        name="attn_weight_grad",
        cost_estimate=cost(7),
    )(core, left, grads, left_two, right_two, *order)


TAIL = 16


def hide_ends(scores, main):
    end = scores[main:]
    shown = lax.broadcasted_iota(jnp.int32, end.shape, 0) < 1
    return jnp.concatenate([scores[:main], jnp.where(shown, end, blocked)], 0)


def cross_forward_kernel(
    image_ref,
    end_ref,
    kv_ref,
    w_ref,
    bias_ref,
    gain_ref,
    norm_ref,
    key_ref,
    value_ref,
    key_end_ref,
    value_end_ref,
    q_ref,
    mix_ref,
    sum_ref,
    out_ref,
):
    rows_here = image_ref.shape[0]
    main = image_ref.shape[1] - 1
    width = norm_ref.shape[-1]
    end = end_ref[...].reshape(rows_here * TAIL, -1)
    key_end_ref[...] = dot_nt(end, kv_ref[0]).astype(bf16)
    value_end_ref[...] = (dot_nt(end, kv_ref[1]) + bias_ref[4:5]).astype(bf16)
    residual = norm_ref[...].reshape(rows_here * QUERIES, width)
    q_ref[...] = (dot_nn(residual.astype(bf16), w_ref[0]) + bias_ref[3:4]).astype(bf16)
    low, high = half_lanes(QUERIES)
    tokens = image_ref[:, :main].reshape(rows_here * main, -1)
    key_ref[...] = dot_nt(tokens, kv_ref[0]).astype(bf16)
    value_ref[...] = (dot_nt(tokens, kv_ref[1]) + bias_ref[4:5]).astype(bf16)

    def some_rows(step, carry):
        spots = []
        for near in range(CROSS_ROWS):
            r = step * CROSS_ROWS + near
            span = pl.ds(pl.multiple_of(r * main, main), main)
            last = pl.ds(pl.multiple_of(r * TAIL, TAIL), TAIL)
            mine = pl.ds(pl.multiple_of(r * QUERIES, QUERIES), QUERIES)
            spots += [(span, last, mine, slice(g * 256, (g + 1) * 256)) for g in range(GROUPS)]
        scores = [
            dot_nt(
                jnp.concatenate([key_ref[span, cols], key_end_ref[last, cols]], 0),
                spread_heads(q_ref[mine, cols] * bf16(0.125), low, high),
            )
            for span, last, mine, cols in spots
        ]
        probs = [columns_softmax(hide_ends(score, main)).astype(bf16) for score in scores]
        mixed = [
            dot_tn(
                prob, jnp.concatenate([value_ref[span, cols], value_end_ref[last, cols]], 0)
            )
            for (span, last, mine, cols), prob in zip(spots, probs)
        ]
        for (span, last, mine, cols), mix in zip(spots, mixed):
            mix_ref[mine, cols] = collect_heads(mix, QUERIES).astype(bf16)
        return carry

    lax.fori_loop(0, rows_here // CROSS_ROWS, some_rows, 0)
    total = residual + dot_nn(mix_ref[...], w_ref[1]) + bias_ref[5:6]
    sum_ref[...] = total
    unit, _ = norm_parts(total)
    out_ref[...] = unit * gain_ref[1:2] + bias_ref[9:10]


def cross_forward(images, ends, kv, weights, biases, gains, norm):
    rows, patches, vis = images.shape
    main = patches - 1
    width = norm.shape[-1]
    take = 4
    keys = pl.BlockSpec((take * main, width), lambda i: (i, 0))
    tails = pl.BlockSpec((take * TAIL, width), lambda i: (i, 0))
    tile = pl.BlockSpec((take * QUERIES, width), lambda i: (i, 0))

    def shape(count, dtype):
        return jax.ShapeDtypeStruct((rows * count, width), dtype)

    return pl.pallas_call(
        cross_forward_kernel,
        grid=(rows // take,),
        in_specs=[
            pl.BlockSpec((take, patches, vis), lambda i: (i, 0, 0)),
            pl.BlockSpec((take, TAIL, vis), lambda i: (i, 0, 0)),
            held(kv.shape, lambda i: (0, 0, 0)),
            held((2, width, width), lambda i: (2, 0, 0)),
            whole(biases.shape),
            whole(gains.shape),
            pl.BlockSpec((take, QUERIES, width), lambda i: (i, 0, 0)),
        ],
        out_specs=[keys, keys, tails, tails, tile, tile, tile, tile],
        out_shape=[
            shape(main, bf16),
            shape(main, bf16),
            shape(TAIL, bf16),
            shape(TAIL, bf16),
            shape(QUERIES, bf16),
            shape(QUERIES, bf16),
            shape(QUERIES, f32),
            shape(QUERIES, f32),
        ],
        compiler_params=params(58),
        name="cross_forward",
        cost_estimate=cost(38),
    )(images, ends, kv, weights, biases, gains, norm)


def cross_backward_kernel(
    w_ref,
    key_ref,
    value_ref,
    key_end_ref,
    value_end_ref,
    q_ref,
    down_ref,
    dnorm_ref,
    dkv_ref,
    dkv_end_ref,
    dq_ref,
    side_ref,
    dmix_all,
):
    step = pl.program_id(0)
    rows_here, _, width = dnorm_ref.shape
    main = key_ref.shape[0] // rows_here
    low, high = half_lanes(QUERIES)

    @pl.when(step == 0)
    def _():
        side_ref[...] = jnp.zeros_like(side_ref)

    down = down_ref[...]
    branch = down.astype(bf16)
    dmix_all[...] = dot_nt(branch, w_ref[1]).astype(bf16)

    def some_rows(step, carry):
        spots = []
        for near in range(CROSS_BACK_ROWS):
            r = step * CROSS_BACK_ROWS + near
            span = pl.ds(pl.multiple_of(r * main, main), main)
            last = pl.ds(pl.multiple_of(r * TAIL, TAIL), TAIL)
            mine = pl.ds(pl.multiple_of(r * QUERIES, QUERIES), QUERIES)
            spots += [(span, last, mine, slice(g * 256, (g + 1) * 256)) for g in range(GROUPS)]
        keys = [
            jnp.concatenate([key_ref[span, cols], key_end_ref[last, cols]], 0)
            for span, last, mine, cols in spots
        ]
        queries = [
            spread_heads(q_ref[mine, cols] * bf16(0.125), low, high)
            for span, last, mine, cols in spots
        ]
        outs = [spread_heads(dmix_all[mine, cols], low, high) for span, last, mine, cols in spots]
        scores = [dot_nt(rows, turned) for rows, turned in zip(keys, queries)]
        dprobs = [
            dot_nt(jnp.concatenate([value_ref[span, cols], value_end_ref[last, cols]], 0), turned)
            for (span, last, mine, cols), turned in zip(spots, outs)
        ]
        probs = [columns_softmax(hide_ends(score, main)) for score in scores]
        for (span, last, mine, cols), prob, turned in zip(spots, probs, outs):
            dv = dot_nn(prob.astype(bf16), turned).astype(bf16)
            dkv_ref[1, span, cols] = dv[:main]
            dkv_end_ref[1, last, cols] = dv[main:]
        dscores = [
            (prob * (dprob - jnp.sum(dprob * prob, 0, keepdims=True))).astype(bf16)
            for prob, dprob in zip(probs, dprobs)
        ]
        for (span, last, mine, cols), dscore, turned in zip(spots, dscores, queries):
            dk = dot_nn(dscore, turned).astype(bf16)
            dkv_ref[0, span, cols] = dk[:main]
            dkv_end_ref[0, last, cols] = dk[main:]
        dqs = [dot_tn(dscore, rows) for dscore, rows in zip(dscores, keys)]
        for (span, last, mine, cols), dq in zip(spots, dqs):
            dq_ref[mine, cols] = (collect_heads(dq, QUERIES) * 0.125).astype(bf16)
        return carry

    lax.fori_loop(0, rows_here // CROSS_BACK_ROWS, some_rows, 0)
    dq = dq_ref[...]
    dnorm_ref[...] = (down + dot_nt(dq, w_ref[0])).reshape(rows_here, QUERIES, width)
    side_ref[0:1] += jnp.sum(dq.astype(f32), 0, keepdims=True)
    side_ref[1:2] += jnp.sum(dkv_ref[1].astype(f32), 0, keepdims=True) + jnp.sum(
        dkv_end_ref[1].astype(f32), 0, keepdims=True
    )
    side_ref[2:3] += jnp.sum(branch.astype(f32), 0, keepdims=True)


def cross_backward(rows, weights, keys, values, key_ends, value_ends, q, down, order):
    width = q.shape[1]
    main = keys.shape[0] // rows
    take = 4
    span = pl.BlockSpec((take * main, width), lambda i: (i, 0))
    tails = pl.BlockSpec((take * TAIL, width), lambda i: (i, 0))
    tile = pl.BlockSpec((take * QUERIES, width), lambda i: (i, 0))
    return pl.pallas_call(
        ordered(cross_backward_kernel, 7, len(order)),
        grid=(rows // take,),
        in_specs=[
            held((2, width, width), lambda i: (2, 0, 0)),
            span,
            span,
            tails,
            tails,
            tile,
            tile,
        ]
        + unread(len(order)),
        out_specs=[
            pl.BlockSpec((take, QUERIES, width), lambda i: (i, 0, 0)),
            pl.BlockSpec((2, take * main, width), lambda i: (0, i, 0)),
            pl.BlockSpec((2, take * TAIL, width), lambda i: (0, i, 0)),
            tile,
            whole((8, width)),
        ],
        out_shape=[
            jax.ShapeDtypeStruct((rows, QUERIES, width), f32),
            jax.ShapeDtypeStruct((2, rows * main, width), bf16),
            jax.ShapeDtypeStruct((2, rows * TAIL, width), bf16),
            jax.ShapeDtypeStruct((rows * QUERIES, width), bf16),
            jax.ShapeDtypeStruct((8, width), f32),
        ],
        scratch_shapes=[pltpu.VMEM((take * QUERIES, width), bf16)],
        compiler_params=params(58),
        name="cross_backward",
        cost_estimate=cost(19),
    )(weights, keys, values, key_ends, value_ends, q, down, *order)


def cross_weight_kernel(fold, core_ref, image_ref, end_ref, grad_ref, grad_end_ref, *rest):
    outs, gathered = rest[:-1], rest[-1]
    rows, patches, vis = image_ref.shape
    main = patches - 1
    take = 4
    gathered[...] = dot_tn(grad_end_ref[0], end_ref[...].reshape(rows * TAIL, vis))

    def add_rows(i, carry):
        span = pl.ds(pl.multiple_of(i * take * main, take * main), take * main)
        tokens = image_ref[pl.ds(i * take, take), :main].reshape(take * main, vis)
        gathered[...] += dot_tn(grad_ref[0, span], tokens)
        return carry

    lax.fori_loop(0, rows // take, add_rows, 0)
    if fold is None:
        store_units(outs[0].at[0], gathered[...])
        return
    units, size = outs[0].shape[-3:-1]
    pieces = []
    for block in range(gathered.shape[0] // size):
        spot = tuple(0 if axis == "rep" or bit == 3 else (block >> bit) & 1 for axis, bit in fold)
        piece = gathered[block * size : (block + 1) * size].astype(bf16)
        for unit in range(units):
            pieces.append((spot + (unit,), piece[:, unit * 128 : (unit + 1) * 128]))
    store_halves(core_ref, *outs, pieces)


def cross_weight_grad(core, images, ends, grads, grads_end, fold, size, order):
    rows, patches, vis = images.shape
    width = grads.shape[2]
    half = width // 2
    units = vis // 128
    if fold is None:
        specs = [pl.BlockSpec((1, units, half, 128), lambda m, h: (m, 0, h, 0))]
        shapes = [(2, units, width, 128)]
    else:
        shapes = [slab_shape(fold, units, size)] * 2
        block = tuple(1 if axis == "rep" or bit == 3 else 2 for axis, bit in fold[1:])

        def index(m, h):
            spot = tuple(m if axis == "rep" else h if bit == 3 else 0 for axis, bit in fold[1:])
            return spot + (0, 0, 0)

        specs = [pl.BlockSpec(block + (units, size, 128), index)] * 2
    return pl.pallas_call(
        ordered(functools.partial(cross_weight_kernel, fold), 5, len(order)),
        grid=(2, 2),
        in_specs=[
            core_spec,
            held(images.shape, lambda m, h: (0, 0, 0)),
            held(ends.shape, lambda m, h: (0, 0, 0)),
            pl.BlockSpec((1, grads.shape[1], half), lambda m, h: (m, 0, h)),
            pl.BlockSpec((1, grads_end.shape[1], half), lambda m, h: (m, 0, h)),
        ]
        + unread(len(order)),
        out_specs=specs,
        out_shape=[jax.ShapeDtypeStruct(shape, bf16) for shape in shapes],
        scratch_shapes=[pltpu.VMEM((half, vis), f32)],
        compiler_params=pltpu.CompilerParams(
            vmem_limit_bytes=58 * MIB, dimension_semantics=("arbitrary", "arbitrary")
        ),
        name="cross_weight_grad",
        cost_estimate=cost(32),
    )(core, images, ends, grads, grads_end, *order)


def ffn_forward_kernel(
    which,
    norm_ref,
    in_ref,
    in_bias_ref,
    out_ref,
    proj_ref,
    proj_bias_ref,
    bias_ref,
    gain_ref,
    *rest,
):
    act_ref, slope_ref, sum_ref, low_ref, raw_ref, embed_ref, rows_low = rest[-7:]
    step = pl.program_id(0)
    tokens, width = sum_ref.shape

    @pl.when(step == 0)
    def _():
        full = norm_ref[...].reshape(tokens, width)
        rows_low[...] = full.astype(bf16)
        sum_ref[...] = full + bias_ref[6 + which : 7 + which]

    low = rows_low[...]
    wide = 256
    pieces = act_ref.shape[1] // wide

    def before_gate(k):
        cols = slice(k * wide, (k + 1) * wide)
        return dot_nn(low, in_ref[0, :, cols]) + in_bias_ref[which : which + 1, cols]

    ahead = [before_gate(k) for k in range(2)]
    gathered = 0.0
    for k in range(pieces):
        if k + 2 < pieces:
            ahead.append(before_gate(k + 2))
        cols = slice(k * wide, (k + 1) * wide)
        act, slope = gate_parts(ahead[k])
        act = act.astype(bf16)
        act_ref[:, cols] = act
        slope_ref[:, cols] = slope.astype(bf16)
        gathered += dot_nn(act, out_ref[0, cols])
    sum_ref[...] += gathered

    @pl.when(step == pl.num_programs(0) - 1)
    def _():
        unit, _ = norm_parts(sum_ref[...])
        low = (unit * gain_ref[2 + which : 3 + which] + bias_ref[10 + which : 11 + which]).astype(bf16)
        low_ref[...] = low.reshape(low_ref.shape)
        raw = dot_nn(low, proj_ref[0]) + proj_bias_ref[which : which + 1]
        raw_ref[...] = raw
        size = lax.rsqrt(jnp.sum(raw * raw, -1, keepdims=True) + epsilon)
        embed_ref[...] = (raw * size).astype(bf16)


def ffn_forward(which, part, norm, ffn_in, ffn_bias, ffn_out, projections, proj_bias, biases, gains, layer, order=()):
    rows, width = norm.shape[0], norm.shape[-1]
    tokens = rows * QUERIES
    hidden = ffn_in.shape[2]
    embed = projections.shape[2]
    chunk = 1024
    cols = pl.BlockSpec((tokens, chunk), lambda j: (0, j))
    halves = [] if layer is None else [layer]
    return pl.pallas_call(
        functools.partial(ffn_forward_kernel, which),
        grid=(hidden // chunk,),
        in_specs=[
            held((rows, QUERIES, width), lambda j: (0, part, 0)),
            pl.BlockSpec((1, width, chunk), lambda j: (which, 0, j)),
            pl.BlockSpec((2, chunk), lambda j: (0, j)),
            pl.BlockSpec((1, chunk, width), lambda j: (which, j, 0)),
            held((1, width, embed), lambda j: (which, 0, 0)),
            whole(proj_bias.shape),
            whole(biases.shape),
            whole(gains.shape),
        ]
        + unread(len(halves) + len(order)),
        out_specs=[
            cols,
            cols,
            whole((tokens, width)),
            pl.BlockSpec((rows, QUERIES, width), lambda j: (0, which, 0)),
            whole((tokens, embed)),
            whole((tokens, embed)),
        ],
        out_shape=[
            jax.ShapeDtypeStruct((tokens, hidden), bf16),
            jax.ShapeDtypeStruct((tokens, hidden), bf16),
            jax.ShapeDtypeStruct((tokens, width), f32),
            jax.ShapeDtypeStruct((rows, SLOTS, width), bf16),
            jax.ShapeDtypeStruct((tokens, embed), f32),
            jax.ShapeDtypeStruct((tokens, embed), bf16),
        ],
        scratch_shapes=[pltpu.VMEM((tokens, width), bf16)],
        input_output_aliases={8: 3} if halves else {},
        compiler_params=params(58),
        name="ffn_forward",
        cost_estimate=cost(15),
    )(norm, ffn_in, ffn_bias, ffn_out, projections, proj_bias, biases, gains, *halves, *order)


def ffn_backward_kernel(
    which,
    folds,
    core_ref,
    norm_ref,
    sum_ref,
    before_ref,
    layer_ref,
    grad_ref,
    raw_ref,
    proj_ref,
    gain_ref,
    in_ref,
    out_ref,
    act_ref,
    slope_ref,
    *rest,
):
    count = 3 if folds is None else 6
    down_ref, side_ref, dbias_ref, dproj_bias_ref = rest[-8 - count : -4 - count]
    weight_refs = rest[-4 - count : -4]
    branch_all, low_turned, left, dproj = rest[-4:]
    step = pl.program_id(0)
    tokens, width = sum_ref.shape

    @pl.when(step == 0)
    def _():
        raw = raw_ref[...]
        grad = grad_ref[...].reshape(tokens, width).astype(f32) + dot_nt(raw, proj_ref[0])
        down, dgain, dshift = norm_grads(sum_ref[...], gain_ref[2 + which : 3 + which], grad)
        branch = down.astype(bf16)
        branch_all[...] = branch
        left[...] = down
        side_ref[...] = jnp.zeros_like(side_ref)
        side_ref[0:1] = dgain
        side_ref[1:2] = dshift
        side_ref[2:3] = jnp.sum(branch.astype(f32), 0, keepdims=True)
        dproj[...] = dot_tn(layer_ref[...].reshape(tokens, width), raw).astype(bf16)
        dproj_bias_ref[...] = jnp.broadcast_to(
            jnp.sum(raw.astype(f32), 0, keepdims=True), dproj_bias_ref.shape
        )
        low_turned[...] = norm_ref[...].reshape(tokens, width).astype(bf16).T

    branch = branch_all[...]
    du = (dot_nt(branch, out_ref[0]) * slope_ref[...].astype(f32)).astype(bf16)
    left[...] += dot_nt(du, in_ref[0])
    dbias_ref[...] = jnp.broadcast_to(jnp.sum(du.astype(f32), 0, keepdims=True), dbias_ref.shape)
    thin = width // 3
    for part in range(3):

        @pl.when(step == part)
        def _():
            din = dot_nn(low_turned[...], du).astype(bf16)
            dout = dot_tn(act_ref[...], branch[:, part * thin : (part + 1) * thin]).astype(bf16)
            if folds is None:
                store_units(weight_refs[0], din)
                store_units(weight_refs[1], dout)
                if part == 0:
                    store_units(weight_refs[2], dproj[...])
                return
            keep, send = weight_refs[2 * part : 2 * part + 2]
            size = keep.shape[-2]
            subs = dout.shape[0] // width
            pieces = []
            for block in range(width // size):
                spot = place_of(folds[part], block, 0)
                at = block * size
                found = [
                    din[at : at + size, unit * 128 : (unit + 1) * 128]
                    for unit in range(din.shape[1] // 128)
                ]
                for sub in range(subs):
                    row = at * subs + sub * size
                    for unit in range(thin // 128):
                        found.append(dout[row : row + size, unit * 128 : (unit + 1) * 128])
                if part == 0:
                    for unit in range(dproj.shape[1] // 128):
                        found.append(dproj[at : at + size, unit * 128 : (unit + 1) * 128])
                pieces += [(spot + (unit,), piece) for unit, piece in enumerate(found)]
            store_halves(core_ref, keep, send, pieces)

    @pl.when(step == pl.num_programs(0) - 1)
    def _():
        if which == 0:
            down, dgain, dshift = norm_grads(before_ref[...], gain_ref[1:2], left[...])
            side_ref[3:4] = dgain
            side_ref[4:5] = dshift
            down_ref[...] = down.reshape(down_ref.shape)
        else:
            down_ref[...] = left[...].reshape(down_ref.shape)


def ffn_backward(
    which,
    part,
    core,
    norm,
    total,
    before,
    layer,
    grad,
    raw,
    projections,
    gains,
    ffn_in,
    ffn_out,
    act,
    slope,
    slabs,
    folds,
    size,
):
    rows = layer.shape[0]
    tokens, width = total.shape
    hidden = ffn_in.shape[2]
    embed = projections.shape[2]
    chunk = hidden // 3
    slabs = list(slabs)
    if folds is None:
        weight_specs = [
            pl.BlockSpec((chunk // 128, width, 128), lambda j: (j, 0, 0)),
            pl.BlockSpec((width // 384, hidden, 128), lambda j: (j, 0, 0)),
            whole((embed // 128, width, 128)),
        ]
        weight_shapes = [
            (hidden // 128, width, 128),
            (width // 128, hidden, 128),
            (embed // 128, width, 128),
        ]
    else:
        units = chunk // 128 + (hidden // width) * (width // 384)
        weight_shapes = [
            slab_shape(fold, units + (embed // 128 if k == 0 else 0), size)
            for k, fold in enumerate(folds)
            for half in range(2)
        ]

        def spec(fold, shape):
            block = tuple(1 if axis == "rep" else 2 for axis, bit in fold[1:])
            spot = tuple(which if axis == "rep" else 0 for axis, bit in fold[1:])
            return held(block + shape[-3:], lambda j: spot + (0, 0, 0))

        weight_specs = [spec(folds[k // 2], shape) for k, shape in enumerate(weight_shapes)]
    return pl.pallas_call(
        functools.partial(ffn_backward_kernel, which, folds),
        grid=(3,),
        in_specs=[
            core_spec,
            held((rows, QUERIES, width), lambda j: (0, part, 0)),
            held((tokens, width), lambda j: (0, 0)),
            held(before.shape, lambda j: (0, 0)),
            held((rows, QUERIES, width), lambda j: (0, which, 0)),
            held((rows, QUERIES, width), lambda j: (0, which, 0)),
            held((tokens, embed), lambda j: (0, 0)),
            held((1, width, embed), lambda j: (which, 0, 0)),
            whole(gains.shape),
            pl.BlockSpec((1, width, chunk), lambda j: (which, 0, j)),
            pl.BlockSpec((1, chunk, width), lambda j: (which, j, 0)),
            held((tokens, hidden), lambda j: (0, 0)),
            pl.BlockSpec((tokens, chunk), lambda j: (0, j)),
        ]
        + [pl.BlockSpec(memory_space=pl.ANY)] * len(slabs),
        out_specs=[
            whole((rows, QUERIES, width)),
            whole((8, width)),
            pl.BlockSpec((8, chunk), lambda j: (0, j)),
            whole((8, embed)),
        ]
        + weight_specs,
        out_shape=[
            jax.ShapeDtypeStruct((rows, QUERIES, width), f32),
            jax.ShapeDtypeStruct((8, width), f32),
            jax.ShapeDtypeStruct((8, hidden), f32),
            jax.ShapeDtypeStruct((8, embed), f32),
        ]
        + [jax.ShapeDtypeStruct(shape, bf16) for shape in weight_shapes],
        scratch_shapes=[
            pltpu.VMEM((tokens, width), bf16),
            pltpu.VMEM((width, tokens), bf16),
            pltpu.VMEM((tokens, width), f32),
            pltpu.VMEM((width, embed), bf16),
        ],
        input_output_aliases={13 + k: 4 + k for k in range(len(slabs))},
        compiler_params=params(60),
        name="ffn_backward",
        cost_estimate=cost(25),
    )(
        core,
        norm,
        total,
        before,
        layer,
        grad,
        raw,
        projections,
        gains,
        ffn_in,
        ffn_out,
        act,
        slope,
        *slabs,
    )


def own_bit(stage):
    axis, bit = stage
    return (lax.axis_index(axis) >> bit) & 1


def swap(values, stage, sizes):
    axis, bit = stage
    return lax.ppermute(values, axis, [(i, i ^ (1 << bit)) for i in range(sizes[axis])])


def total(terms, ahead=()):
    parts = []
    for array, places in terms:
        places = list(places) + list(ahead)
        rest = array.shape[len(places) :]
        if places:
            at = sum(place << shift for shift, place in enumerate(reversed(places)))
            flat = array.reshape((1 << len(places), -1, 128))
            array = lax.dynamic_index_in_dim(flat, at, 0, keepdims=False).reshape(rest)
        parts.append(array.astype(f32))
    return sum(parts)


def stage_order(part, sizes):
    stages = [("dp", bit) for bit in range(sizes["dp"].bit_length() - 1)]
    ring = stages[1:3] + [("rep", 0)]
    return stages[:1] + ring[part:] + ring[:part] + stages[3:]


def fold_pair(part, first, second, sizes):
    depth = sizes["dp"].bit_length() - 1
    both = jnp.stack([first, second])
    units, rows = first.shape[0], first.shape[1] // sizes["dp"]
    both = both.reshape((2, units) + (2,) * depth + (rows, 128))
    front = [0 if axis == "rep" else 1 + depth - bit for axis, bit in stage_order(part, sizes)]
    return both.transpose(front + [1, 2 + depth, 3 + depth])


def begin(part, keep, send, sizes):
    return (1, [(keep, []), (swap(send, stage_order(part, sizes)[0], sizes), [])], send)


def begin_folded(part, slab, sizes):
    mine = own_bit(stage_order(part, sizes)[0])
    halves = [lax.dynamic_index_in_dim(slab, place, 0, keepdims=False) for place in (mine, 1 - mine)]
    return begin(part, *halves, sizes)


def advance(part, state, sizes, after=None):
    stage, terms = state[0], state[1]
    if after is not None:
        array, places = terms[-1]
        terms = terms[:-1] + [(lax.optimization_barrier((array, after))[0], places)]
    axis_bit = stage_order(part, sizes)[stage]
    mine = own_bit(axis_bit)
    sent = total(terms, [1 - mine]).astype(bf16)
    arrived = swap(sent, axis_bit, sizes)
    terms = [(array, places + [mine]) for array, places in terms] + [(arrived, [])]
    return (stage + 1, terms, sent)


def advance_all(states, sizes, after=None):
    return [advance(part, state, sizes, after) for part, state in enumerate(states)]


def finish(part, state, sizes, after=None):
    while state[0] < len(stage_order(part, sizes)):
        state = advance(part, state, sizes, after)
        after = None
    terms = state[1]
    if after is not None:
        array, places = terms[-1]
        terms = terms[:-1] + [(lax.optimization_barrier((array, after))[0], places)]
    return total(terms)


def sends(states):
    return [state[2] for state in states]


def columns_of(units):
    return units.transpose(1, 0, 2).reshape(units.shape[1], -1)


def exchange(values, sizes):
    return lax.all_to_all(values, ("dp", "rep"), 0, 0, tiled=True)


def gather_rows(values, sizes):
    world = sizes["dp"] * sizes["rep"]
    return exchange(jnp.tile(values, (world, 1)), sizes)


def scatter_rows(values, sizes):
    world = sizes["dp"] * sizes["rep"]
    arrived = exchange(values, sizes)
    return jnp.sum(arrived.reshape(world, -1, values.shape[1]).astype(f32), 0)


def shards(
    hidden_states,
    image_features,
    caption_lengths,
    attn_weights,
    cross_kv,
    ffn_in,
    ffn_out,
    projections,
    norm_gains,
    biases,
    ffn_bias,
    proj_bias,
    out_grad,
    sizes,
):
    row_count, slots, width = hidden_states.shape
    captions_here = 2 * row_count
    world = sizes["dp"] * sizes["rep"]
    allowed, pick_mask = caption_layout(caption_lengths)
    pick_low = pick_mask.astype(bf16)
    pick_full = pick_mask.astype(f32)
    mask = jnp.tile(allowed.astype(f32), (1, 1, 4))
    inputs = hidden_states.reshape(row_count * slots, width)
    self_q, self_k, self_v, self_mix, first_sum, first_norm = self_forward(
        inputs, attn_weights, biases, norm_gains, mask
    )
    first_norm = first_norm.reshape(row_count, slots, width)
    image_ends = jnp.pad(image_features[:, -1:], ((0, 0), (0, TAIL - 1), (0, 0)))
    text_act, text_slope, fourth_sum, layer_half, caption_raw, caption_all = ffn_forward(
        1,
        1,
        first_norm,
        ffn_in,
        ffn_bias,
        ffn_out,
        projections,
        proj_bias,
        biases,
        norm_gains,
        None,
        [image_ends],
    )
    caption_embed = (
        jnp.einsum(
            "rkt,rtd->rkd",
            pick_low,
            caption_all.reshape(row_count, TEXT, -1),
            preferred_element_type=f32,
        )
        .astype(bf16)
        .reshape(captions_here, -1)
    )
    every_caption = gather_rows(caption_embed, sizes)
    keys, values, key_ends, value_ends, cross_q, cross_mix, second_sum, second_norm = cross_forward(
        image_features, image_ends, cross_kv, attn_weights, biases, norm_gains, first_norm
    )
    second_norm = second_norm.reshape(row_count, QUERIES, width)
    query_act, query_slope, third_sum, layer_out, query_raw, query_embed = ffn_forward(
        0,
        0,
        second_norm,
        ffn_in,
        ffn_bias,
        ffn_out,
        projections,
        proj_bias,
        biases,
        norm_gains,
        layer_half,
    )
    query_raw = query_raw.reshape(row_count, QUERIES, -1)
    query_embed = query_embed.reshape(row_count, QUERIES, -1)
    sims = jnp.einsum("rqp,cp->rqc", query_embed, every_caption, preferred_element_type=f32)
    expo = jnp.exp(sharpness * (sims - 1.0))
    affinity = jnp.mean(expo, 1)
    offset = lax.axis_index(("dp", "rep")) * captions_here
    own_block = lax.dynamic_slice_in_dim(affinity, offset, captions_here, 1).reshape(
        row_count, row_count, 2
    )
    diagonal = (
        lax.broadcasted_iota(jnp.int32, (row_count, row_count), 0)
        == lax.broadcasted_iota(jnp.int32, (row_count, row_count), 1)
    ).astype(f32)
    positive = jnp.sum(own_block * diagonal[:, :, None], 1)
    row_total = jnp.sum(affinity, 1)
    partial_cols = jnp.sum(affinity, 0)
    all_cols = jnp.sum(
        exchange(jnp.broadcast_to(partial_cols[None], (world,) + partial_cols.shape), sizes), 0
    )
    own_cols = lax.dynamic_slice_in_dim(all_cols, offset, captions_here, 0).reshape(row_count, 2)
    inverse_all = 1.0 / all_cols
    row_loss = (
        jnp.log(row_total)
        - jnp.log(positive[:, 0])
        + jnp.sum(jnp.log(own_cols) - jnp.log(positive), 1)
    )
    grad_affinity = loss_weight * (1.0 / row_total[:, None] + inverse_all[None, :])
    pair_weight = jnp.array([2.0, 1.0], f32)
    correction = (loss_weight * diagonal[:, :, None] * pair_weight / own_block).reshape(
        row_count, captions_here
    )
    own_grad = lax.dynamic_slice_in_dim(grad_affinity, offset, captions_here, 1) - correction
    grad_affinity = lax.dynamic_update_slice_in_dim(grad_affinity, own_grad, offset, 1)
    grad_sims = (grad_affinity[:, None, :] * expo * (sharpness / QUERIES)).astype(bf16)
    grad_query_embed = jnp.einsum(
        "rqc,cp->rqp", grad_sims, every_caption, preferred_element_type=f32
    )
    grad_caption_embed = scatter_rows(
        jnp.einsum("rqc,rqp->cp", grad_sims, query_embed, preferred_element_type=f32).astype(bf16),
        sizes,
    )
    query_raw_grad = unit_back(query_raw, grad_query_embed).astype(bf16)
    head_raw = jnp.sum(
        pick_full[:, :, :, None] * caption_raw.reshape(row_count, 1, TEXT, -1), 2
    )
    head_raw_grad = unit_back(head_raw, grad_caption_embed.reshape(row_count, 2, -1)).astype(bf16)
    caption_raw_grad = jnp.einsum(
        "rkt,rkd->rtd", pick_low, head_raw_grad, preferred_element_type=f32
    ).astype(bf16)
    fold = sizes["dp"] == 16 and sizes["rep"] == 2
    stage_orders = [stage_order(part, sizes) for part in range(3)]
    folds = stage_orders if fold else None
    size = width // sizes["dp"]
    core = (lax.axis_index("dp") & 1).astype(jnp.int32).reshape(1)
    grad_second, query_side, query_dbias, query_dproj_bias, *query_slabs = ffn_backward(
        0,
        0,
        core,
        second_norm,
        third_sum,
        second_sum,
        layer_out,
        out_grad,
        query_raw_grad.reshape(row_count * QUERIES, -1),
        projections,
        norm_gains,
        ffn_in,
        ffn_out,
        query_act,
        query_slope,
        (),
        folds,
        size,
    )
    text_first, text_side, text_dbias, text_dproj_bias, *text_slabs = ffn_backward(
        1,
        1,
        core,
        first_norm,
        fourth_sum,
        fourth_sum,
        layer_out,
        out_grad,
        caption_raw_grad.reshape(row_count * TEXT, -1),
        projections,
        norm_gains,
        ffn_in,
        ffn_out,
        text_act,
        text_slope,
        query_slabs if fold else (),
        folds,
        size,
    )
    tall = ffn_out.shape[1] // width
    if not fold:
        text_slabs = [
            fold_pair(
                part,
                *(
                    jnp.concatenate(
                        [
                            din[part * 8 : part * 8 + 8],
                            dout[2 * part : 2 * part + 2]
                            .reshape(2, sizes["dp"], tall, size, 128)
                            .transpose(2, 0, 1, 3, 4)
                            .reshape(2 * tall, width, 128),
                            dproj[: 2 if part == 0 else 0],
                        ],
                        0,
                    )
                    for din, dout, dproj in (query_slabs, text_slabs)
                ),
                sizes,
            )
            for part in range(3)
        ]
    if fold:
        ffn_states = [
            begin(part, *text_slabs[2 * part : 2 * part + 2], sizes) for part in range(3)
        ]
    else:
        ffn_states = [begin_folded(part, slab, sizes) for part, slab in enumerate(text_slabs)]
    cross_down = grad_second.reshape(row_count * QUERIES, width)
    query_first, dkv, dkv_ends, cross_dq, cross_side = cross_backward(
        row_count,
        attn_weights,
        keys,
        values,
        key_ends,
        value_ends,
        cross_q,
        cross_down,
        [text_first] + sends(ffn_states),
    )
    ffn_states = advance_all(ffn_states, sizes, cross_side)
    cross_slabs = cross_weight_grad(
        core,
        image_features,
        image_ends,
        dkv,
        dkv_ends,
        folds and folds[0],
        size,
        sends(ffn_states),
    )
    ffn_states = advance_all(ffn_states, sizes, cross_slabs[0])
    if fold:
        cross_states = [begin(0, *cross_slabs, sizes)]
    else:
        cross_states = [begin_folded(0, fold_pair(0, *cross_slabs[0], sizes), sizes)]
    self_grads, self_branch, self_down, self_side = self_backward(
        attn_weights,
        norm_gains,
        mask,
        self_q,
        self_k,
        self_v,
        first_sum,
        query_first,
        text_first,
        sends(ffn_states) + sends(cross_states),
    )
    ffn_states = advance_all(ffn_states, sizes, self_side)
    cross_states = advance_all(cross_states, sizes, self_side)
    query_half = pl.BlockSpec((row_count, QUERIES, width), lambda i: (0, 0, 0))
    attn_states = []
    order = sends(ffn_states) + sends(cross_states)
    for part, (left_two, spec, right_two) in enumerate(
        (
            (self_mix, whole(self_mix.shape), self_branch),
            (first_norm, query_half, cross_dq),
            (cross_mix, whole(cross_mix.shape), cross_down),
        )
    ):
        slabs = attn_weight_grad(
            part,
            core,
            inputs,
            self_grads,
            left_two,
            spec,
            right_two,
            folds and folds[part],
            size,
            order,
        )
        made = slabs[0]
        if fold:
            attn_states.append(begin(part, *slabs, sizes))
        else:
            attn_states.append(begin_folded(part, fold_pair(part, *made, sizes), sizes))
        order = sends(attn_states[-1:])
    ffn_states = advance_all(ffn_states, sizes, made)
    cross_states = advance_all(cross_states, sizes, made)
    input_grad = input_gradient(
        attn_weights,
        self_grads,
        self_down,
        order + sends(ffn_states) + sends(cross_states),
    )
    attn_grad = jnp.stack(
        [
            columns_of(finish(part, state, sizes, input_grad))
            for part, state in enumerate(attn_states)
        ]
    )
    ffn_sums = [finish(part, state, sizes, input_grad) for part, state in enumerate(ffn_states)]
    ffn_in_grad = jnp.concatenate([columns_of(each[:8]) for each in ffn_sums], 1)
    ffn_out_grad = jnp.concatenate(
        [
            each[8:16].reshape(tall, 2, size, 128).transpose(0, 2, 1, 3).reshape(tall * size, -1)
            for each in ffn_sums
        ],
        1,
    )
    proj_grad = columns_of(ffn_sums[0][16:])
    cross_grad = columns_of(finish(0, cross_states[0], sizes, input_grad))
    gain_grad = jnp.stack([self_side[0], query_side[3], query_side[0], text_side[0]])
    bias_grad = jnp.stack(
        [
            self_side[2],
            self_side[3],
            self_side[4],
            cross_side[0],
            cross_side[1],
            cross_side[2],
            query_side[2],
            text_side[2],
            self_side[1],
            query_side[4],
            query_side[1],
            text_side[1],
        ]
    )
    vectors = (
        gain_grad,
        bias_grad,
        jnp.stack([query_dbias[0], text_dbias[0]]),
        jnp.stack([query_dproj_bias[0], text_dproj_bias[0]]),
    )

    def deal(array):
        mats, cols = array.shape
        cut = array.reshape(sizes["rep"], mats // sizes["rep"], sizes["dp"], cols // sizes["dp"])
        return cut.transpose(2, 0, 1, 3).reshape(world, -1)

    dealt = jnp.concatenate([deal(array) for array in vectors], 1)
    arrived = jnp.sum(lax.optimization_barrier((exchange(dealt, sizes), input_grad))[0], 0)
    small = []
    start = 0
    for array in vectors:
        mats, cols = array.shape[0] // sizes["rep"], array.shape[1] // sizes["dp"]
        small.append(arrived[start : start + mats * cols].reshape(mats, cols))
        start += mats * cols
    return (
        layer_out,
        row_loss,
        input_grad.reshape(hidden_states.shape),
        attn_grad,
        cross_grad[None],
        ffn_in_grad[None],
        ffn_out_grad[None],
        proj_grad[None],
        small[0],
        small[1],
        small[2],
        small[3],
    )


def solution(mesh):
    placed = (
        P(("dp", "rep"), None, None),
        P(("dp", "rep"), None, None),
        P(("dp", "rep"), None),
        P(),
        P(),
        P(),
        P(),
        P(),
        P(),
        P(),
        P(),
        P(),
        P(("dp", "rep"), None, None),
    )
    sizes = dict(mesh.shape)
    return jax.shard_map(
        functools.partial(shards, sizes=sizes),
        mesh=mesh,
        in_specs=placed,
        out_specs=(
            P(("dp", "rep"), None, None),
            P(("dp", "rep")),
            P(("dp", "rep"), None, None),
            P("rep", "dp", None),
            P("rep", "dp", None),
            P("rep", "dp", None),
            P("rep", "dp", None),
            P("rep", "dp", None),
            P("rep", "dp"),
            P("rep", "dp"),
            P("rep", "dp"),
            P("rep", "dp"),
        ),
        check_vma=False,
    )
```

```python
import functools

import jax
import jax.numpy as jnp
from jax import lax
from jax.experimental import pallas as pl
from jax.experimental.pallas import tpu as pltpu
from jax.sharding import PartitionSpec as P

HEADS = 12
QUERIES = 32
TEXT = 32
SLOTS = QUERIES + TEXT


blocked = -1000000000.0
epsilon = 1e-06
sharpness = 14.0
loss_weight = 16.0


def unit_rows(values):
    return values * lax.rsqrt(jnp.sum(values * values, -1, keepdims=True) + epsilon)


def unit_back(values, grad_rows):
    unused, pullback = jax.vjp(unit_rows, values)
    return pullback(grad_rows)[0]


def caption_layout(length_rows):
    row_count = length_rows.shape[0]
    first_len = length_rows[:, 0:1]
    second_end = first_len + length_rows[:, 1:2]
    slot_index = lax.broadcasted_iota(jnp.int32, (row_count, TEXT), 1)
    text_group = (slot_index >= first_len).astype(jnp.int32) + (slot_index >= second_end).astype(
        jnp.int32
    )
    group_ids = jnp.concatenate([jnp.full((row_count, QUERIES), -1, jnp.int32), text_group], 1)
    allowed = group_ids[:, :, None] == group_ids[:, None, :]
    head_starts = jnp.concatenate([jnp.zeros_like(first_len), first_len], 1)
    pick_mask = slot_index[:, None, :] == head_starts[:, :, None]
    return (allowed, pick_mask)


f32 = jnp.float32
bf16 = jnp.bfloat16
ROOT_HALF = 0.7071067811865476
ROOT_TAU = 0.3989422804014327
MIB = 1024 * 1024


def dot_nn(a, b):
    return lax.dot_general(a, b, (((1,), (0,)), ((), ())), preferred_element_type=f32)


def dot_nt(a, b):
    return lax.dot_general(a, b, (((1,), (1,)), ((), ())), preferred_element_type=f32)


def dot_tn(a, b):
    return lax.dot_general(a, b, (((0,), (0,)), ((), ())), preferred_element_type=f32)


def whole(shape):
    return pl.BlockSpec(shape, lambda *_: (0,) * len(shape))


def held(shape, index):
    return pl.BlockSpec(shape, index, pipeline_mode=pl.Buffered(1))


def cost(micros):
    return pl.CostEstimate(flops=int(micros * 1.1e9), bytes_accessed=0, transcendentals=0)


def put_row(ref, place, row, add=False):
    units = row.shape[1] // 128
    for unit in range(units):
        at = slice(place * units + unit, place * units + unit + 1)
        piece = row[:, unit * 128 : (unit + 1) * 128]
        ref[at] = ref[at] + piece if add else piece


def store_units(ref, values):
    for place in range(values.shape[1] // 128):
        ref[place] = values[:, place * 128 : (place + 1) * 128].astype(ref.dtype)


def ordered(kernel, inputs, count):
    def run(*refs):
        kernel(*refs[:inputs], *refs[inputs + count :])

    return run


def unread(count):
    return [pl.BlockSpec(memory_space=pl.ANY)] * count


def params(mib):
    return pltpu.CompilerParams(vmem_limit_bytes=mib * MIB, dimension_semantics=("arbitrary",))


def norm_parts(values):
    center = values - jnp.mean(values, -1, keepdims=True)
    scale = lax.rsqrt(jnp.mean(center * center, -1, keepdims=True) + epsilon)
    return center * scale, scale


def norm_grads(values, gain_row, grad):
    unit, scale = norm_parts(values)
    inner = grad * gain_row
    first = jnp.mean(inner, -1, keepdims=True)
    second = jnp.mean(inner * unit, -1, keepdims=True)
    return (
        scale * (inner - first - unit * second),
        jnp.sum(grad * unit, 0, keepdims=True),
        jnp.sum(grad, 0, keepdims=True),
    )


def gate_parts(u):
    size = jnp.abs(u) * ROOT_HALF
    t = 1.0 / (1.0 + 0.3275911 * size)
    bell = jnp.exp(-size * size)
    poly = t * (
        0.127414796
        + t * (-0.142248368 + t * (0.7107068705 + t * (-0.7265760135 + t * 0.5307027145)))
    )
    tail = poly * bell
    cdf = jnp.where(u > 0, 1.0 - tail, tail)
    return u * cdf, cdf + (ROOT_TAU * u) * bell


def half_lanes(rows):
    low = (lax.broadcasted_iota(jnp.int32, (rows, 128), 1) < 64).astype(f32)
    return low.astype(bf16), (1.0 - low).astype(bf16)


def spread_heads(x, low, high):
    left, right = x[:, :128], x[:, 128:]
    none = jnp.zeros_like(left)
    return jnp.concatenate(
        [
            jnp.concatenate([left * low, none], 1),
            jnp.concatenate([left * high, none], 1),
            jnp.concatenate([none, right * low], 1),
            jnp.concatenate([none, right * high], 1),
        ],
        0,
    )


def collect_heads(o, n):
    low = lax.broadcasted_iota(jnp.int32, (n, 128), 1) < 64
    left = jnp.where(low, o[:n, :128], o[n : 2 * n, :128])
    right = jnp.where(low, o[2 * n : 3 * n, 128:], o[3 * n :, 128:])
    return jnp.concatenate([left, right], 1)


def columns_softmax(scores):
    raised = jnp.exp(scores - jnp.max(scores, 0, keepdims=True))
    return raised * (1.0 / jnp.sum(raised, 0, keepdims=True))


GROUPS = HEADS // 4
SELF_ROWS = 4
CROSS_ROWS = 4
SELF_BACK_ROWS = 4
CROSS_BACK_ROWS = 4


def self_forward_kernel(
    x_ref, w_ref, bias_ref, gain_ref, mask_ref, q_ref, k_ref, v_ref, mix_ref, sum_ref, norm_ref
):
    x = x_ref[...]
    q_ref[...] = (dot_nn(x, w_ref[0]) + bias_ref[0:1]).astype(bf16)
    k_ref[...] = dot_nn(x, w_ref[1]).astype(bf16)
    v_ref[...] = (dot_nn(x, w_ref[2]) + bias_ref[1:2]).astype(bf16)
    low, high = half_lanes(SLOTS)

    def some_rows(step, carry):
        spots = []
        for near in range(SELF_ROWS):
            r = step * SELF_ROWS + near
            rows = pl.ds(pl.multiple_of(r * SLOTS, SLOTS), SLOTS)
            spots += [(r, rows, slice(g * 256, (g + 1) * 256)) for g in range(GROUPS)]
        scores = [
            dot_nt(
                k_ref[rows, cols], spread_heads(q_ref[rows, cols] * bf16(0.125), low, high)
            )
            for r, rows, cols in spots
        ]
        probs = [
            columns_softmax(jnp.where(mask_ref[r] > 0.0, score, blocked)).astype(bf16)
            for (r, rows, cols), score in zip(spots, scores)
        ]
        mixed = [dot_tn(prob, v_ref[rows, cols]) for (r, rows, cols), prob in zip(spots, probs)]
        for (r, rows, cols), mix in zip(spots, mixed):
            mix_ref[rows, cols] = collect_heads(mix, SLOTS).astype(bf16)
        return carry

    lax.fori_loop(0, x_ref.shape[0] // (SELF_ROWS * SLOTS), some_rows, 0)
    total = x.astype(f32) + dot_nn(mix_ref[...], w_ref[3]) + bias_ref[2:3]
    sum_ref[...] = total
    unit, _ = norm_parts(total)
    norm_ref[...] = unit * gain_ref[0:1] + bias_ref[8:9]


def self_forward(x, weights, biases, gains, mask):
    tokens, width = x.shape
    step = 4 * SLOTS
    tile = pl.BlockSpec((step, width), lambda i: (i, 0))
    low, full = jax.ShapeDtypeStruct(x.shape, bf16), jax.ShapeDtypeStruct(x.shape, f32)
    return pl.pallas_call(
        self_forward_kernel,
        grid=(tokens // step,),
        in_specs=[
            tile,
            held((4, width, width), lambda i: (0, 0, 0)),
            whole(biases.shape),
            whole(gains.shape),
            pl.BlockSpec((4,) + mask.shape[1:], lambda i: (i, 0, 0)),
        ],
        out_specs=[tile] * 6,
        out_shape=[low, low, low, low, full, full],
        compiler_params=params(58),
        name="self_forward",
        cost_estimate=cost(15),
    )(x, weights, biases, gains, mask)


def self_backward_kernel(
    w_ref,
    gain_ref,
    mask_ref,
    q_ref,
    k_ref,
    v_ref,
    sum_ref,
    top_ref,
    low_ref,
    grad_ref,
    branch_ref,
    down_ref,
    side_ref,
    dmix_all,
):
    step = pl.program_id(0)
    count = sum_ref.shape[0]
    low, high = half_lanes(SLOTS)

    @pl.when(step == 0)
    def _():
        side_ref[...] = jnp.zeros_like(side_ref)

    grad = jnp.concatenate([top_ref[...], low_ref[...]], 1).reshape(count, -1)
    down, dgain, dshift = norm_grads(sum_ref[...], gain_ref[0:1], grad)
    branch = down.astype(bf16)
    down_ref[...] = down
    branch_ref[...] = branch
    dmix_all[...] = dot_nt(branch, w_ref[0]).astype(bf16)

    def some_rows(step, carry):
        spots = []
        for near in range(SELF_BACK_ROWS):
            r = step * SELF_BACK_ROWS + near
            rows = pl.ds(pl.multiple_of(r * SLOTS, SLOTS), SLOTS)
            spots += [(r, rows, slice(g * 256, (g + 1) * 256)) for g in range(GROUPS)]
        queries = [
            spread_heads(q_ref[rows, cols] * bf16(0.125), low, high) for r, rows, cols in spots
        ]
        outs = [spread_heads(dmix_all[rows, cols], low, high) for r, rows, cols in spots]
        scores = [dot_nt(k_ref[spot[1:]], turned) for spot, turned in zip(spots, queries)]
        dprobs = [dot_nt(v_ref[spot[1:]], turned) for spot, turned in zip(spots, outs)]
        probs = [
            columns_softmax(jnp.where(mask_ref[spot[0]] > 0.0, score, blocked))
            for spot, score in zip(spots, scores)
        ]
        for spot, prob, turned in zip(spots, probs, outs):
            grad_ref[(2,) + spot[1:]] = dot_nn(prob.astype(bf16), turned).astype(bf16)
        dscores = [
            (prob * (dprob - jnp.sum(dprob * prob, 0, keepdims=True))).astype(bf16)
            for prob, dprob in zip(probs, dprobs)
        ]
        for spot, dscore, turned in zip(spots, dscores, queries):
            grad_ref[(1,) + spot[1:]] = dot_nn(dscore, turned).astype(bf16)
        dqs = [dot_tn(dscore, k_ref[spot[1:]]) for spot, dscore in zip(spots, dscores)]
        for spot, dq in zip(spots, dqs):
            grad_ref[(0,) + spot[1:]] = (collect_heads(dq, SLOTS) * 0.125).astype(bf16)
        return carry

    lax.fori_loop(0, count // (SELF_BACK_ROWS * SLOTS), some_rows, 0)
    put_row(side_ref, 0, dgain, True)
    put_row(side_ref, 1, dshift, True)
    for place, rows in enumerate((grad_ref[0], grad_ref[2], branch)):
        put_row(side_ref, 2 + place, jnp.sum(rows.astype(f32), 0, keepdims=True), True)


def self_backward(weights, gains, mask, q, k, v, total, top, text, order):
    tokens, width = q.shape
    count = 4 * SLOTS
    tile = pl.BlockSpec((count, width), lambda i: (i, 0))
    part = pl.BlockSpec((4, QUERIES, width), lambda i: (i, 0, 0))
    return pl.pallas_call(
        ordered(self_backward_kernel, 9, len(order)),
        grid=(tokens // count,),
        in_specs=[
            held((1, width, width), lambda i: (3, 0, 0)),
            whole(gains.shape),
            pl.BlockSpec((4,) + mask.shape[1:], lambda i: (i, 0, 0)),
            tile,
            tile,
            tile,
            tile,
            part,
            part,
        ]
        + unread(len(order)),
        out_specs=[
            pl.BlockSpec((3, count, width), lambda i: (0, i, 0)),
            tile,
            tile,
            whole((width // 16, 128)),
        ],
        out_shape=[
            jax.ShapeDtypeStruct((3, tokens, width), bf16),
            jax.ShapeDtypeStruct((tokens, width), bf16),
            jax.ShapeDtypeStruct((tokens, width), f32),
            jax.ShapeDtypeStruct((width // 16, 128), f32),
        ],
        scratch_shapes=[pltpu.VMEM((count, width), bf16)],
        compiler_params=params(58),
        name="self_backward",
        cost_estimate=cost(16),
    )(weights, gains, mask, q, k, v, total, top, text, *order)


def input_grad_kernel(w_ref, grad_ref, down_ref, dx_ref):
    dx_ref[...] = (
        down_ref[...]
        + dot_nt(grad_ref[0], w_ref[0])
        + dot_nt(grad_ref[1], w_ref[1])
        + dot_nt(grad_ref[2], w_ref[2])
    )


def input_gradient(weights, grads, down, order):
    tokens, width = down.shape
    count = 4 * SLOTS
    tile = pl.BlockSpec((count, width), lambda i: (i, 0))

    return pl.pallas_call(
        ordered(input_grad_kernel, 3, len(order)),
        grid=(tokens // count,),
        in_specs=[
            held((3, width, width), lambda i: (0, 0, 0)),
            pl.BlockSpec((3, count, width), lambda i: (0, i, 0)),
            tile,
        ]
        + unread(len(order)),
        out_specs=tile,
        out_shape=jax.ShapeDtypeStruct((tokens, width), f32),
        compiler_params=params(58),
        name="input_gradient",
        cost_estimate=cost(9),
    )(weights, grads, down, *order)


def place_of(order, row_block, rep):
    return tuple(rep if axis == "rep" else (row_block >> bit) & 1 for axis, bit in order)


def slab_shape(order, units, rows):
    return (2,) * (len(order) - 1) + (units, rows, 128)


def store_halves(core_ref, keep_ref, send_ref, pieces):
    for core in range(2):

        @pl.when(core_ref[0] == core)
        def _():
            for places, block in pieces:
                ref = keep_ref if places[0] == core else send_ref
                ref[places[1:]] = block


core_spec = pl.BlockSpec(memory_space=pltpu.SMEM)


def attn_weight_kernel(folds, core_ref, left_ref, right_ref, *rest):
    step = pl.program_id(0)
    outs = rest[6:]
    width = right_ref.shape[-1]
    for part in range(3):

        @pl.when(step == part)
        def _():
            pieces = []
            pairs = ((left_ref, right_ref), rest[2 * part : 2 * part + 2])
            for rep, (left, right) in enumerate(pairs):
                lhs = left[...].reshape(-1, width).astype(bf16)
                rhs = right[...].reshape(-1, width).astype(bf16)
                grad = dot_tn(lhs, rhs).astype(bf16)
                if folds is None:
                    store_units(outs[part].at[rep], grad)
                    continue
                rows = outs[0].shape[-2]
                for block in range(width // rows):
                    spot = place_of(folds[part], block, rep)
                    for unit in range(width // 128):
                        piece = grad[
                            block * rows : (block + 1) * rows, unit * 128 : (unit + 1) * 128
                        ]
                        pieces.append((spot + (unit,), piece))
            if folds is not None:
                store_halves(core_ref, *outs[2 * part : 2 * part + 2], pieces)


def attn_weight_grad(core, left, grads, others, folds, rows, order):
    tokens, width = left.shape
    if folds is None:
        shapes = [(2, width // 128, width, 128)] * 3
    else:
        shapes = [slab_shape(fold, width // 128, rows) for fold in folds for half in range(2)]
    return pl.pallas_call(
        ordered(functools.partial(attn_weight_kernel, folds), 9, len(order)),
        grid=(3,),
        in_specs=[
            core_spec,
            held(left.shape, lambda i: (0, 0)),
            pl.BlockSpec((1, tokens, width), lambda i: (i, 0, 0)),
        ]
        + [held(block, lambda i, zeros=(0,) * len(block): zeros) for _, block in others]
        + unread(len(order)),
        out_specs=[held(shape, lambda i, zeros=(0,) * len(shape): zeros) for shape in shapes],
        out_shape=[jax.ShapeDtypeStruct(shape, bf16) for shape in shapes],
        compiler_params=params(58),
        name="attn_weight_grad",
        cost_estimate=cost(20),
    )(core, left, grads, *(array for array, _ in others), *order)


TAIL = 16


def hide_ends(scores, main):
    end = scores[main:]
    shown = lax.broadcasted_iota(jnp.int32, end.shape, 0) < 1
    return jnp.concatenate([scores[:main], jnp.where(shown, end, blocked)], 0)


def cross_forward_kernel(
    image_ref,
    end_ref,
    kv_ref,
    w_ref,
    bias_ref,
    gain_ref,
    norm_ref,
    key_ref,
    value_ref,
    key_end_ref,
    value_end_ref,
    q_ref,
    mix_ref,
    sum_ref,
    out_ref,
):
    rows_here = image_ref.shape[0]
    main = image_ref.shape[1] - 1
    width = norm_ref.shape[-1]
    end = end_ref[...].reshape(rows_here * TAIL, -1)
    key_end_ref[...] = dot_nt(end, kv_ref[0]).astype(bf16)
    value_end_ref[...] = (dot_nt(end, kv_ref[1]) + bias_ref[4:5]).astype(bf16)
    residual = norm_ref[...].reshape(rows_here * QUERIES, width)
    q_ref[...] = (dot_nn(residual.astype(bf16), w_ref[0]) + bias_ref[3:4]).astype(bf16)
    low, high = half_lanes(QUERIES)
    tokens = image_ref[:, :main].reshape(rows_here * main, -1)
    key_ref[...] = dot_nt(tokens, kv_ref[0]).astype(bf16)
    value_ref[...] = (dot_nt(tokens, kv_ref[1]) + bias_ref[4:5]).astype(bf16)

    def some_rows(step, carry):
        spots = []
        for near in range(CROSS_ROWS):
            r = step * CROSS_ROWS + near
            span = pl.ds(pl.multiple_of(r * main, main), main)
            last = pl.ds(pl.multiple_of(r * TAIL, TAIL), TAIL)
            mine = pl.ds(pl.multiple_of(r * QUERIES, QUERIES), QUERIES)
            spots += [(span, last, mine, slice(g * 256, (g + 1) * 256)) for g in range(GROUPS)]
        scores = [
            dot_nt(
                jnp.concatenate([key_ref[span, cols], key_end_ref[last, cols]], 0),
                spread_heads(q_ref[mine, cols] * bf16(0.125), low, high),
            )
            for span, last, mine, cols in spots
        ]
        probs = [columns_softmax(hide_ends(score, main)).astype(bf16) for score in scores]
        mixed = [
            dot_tn(
                prob, jnp.concatenate([value_ref[span, cols], value_end_ref[last, cols]], 0)
            )
            for (span, last, mine, cols), prob in zip(spots, probs)
        ]
        for (span, last, mine, cols), mix in zip(spots, mixed):
            mix_ref[mine, cols] = collect_heads(mix, QUERIES).astype(bf16)
        return carry

    lax.fori_loop(0, rows_here // CROSS_ROWS, some_rows, 0)
    total = residual + dot_nn(mix_ref[...], w_ref[1]) + bias_ref[5:6]
    sum_ref[...] = total
    unit, _ = norm_parts(total)
    out_ref[...] = unit * gain_ref[1:2] + bias_ref[9:10]


def cross_forward(images, ends, kv, weights, biases, gains, norm):
    rows, patches, vis = images.shape
    main = patches - 1
    width = norm.shape[-1]
    take = 4
    keys = pl.BlockSpec((take * main, width), lambda i: (i, 0))
    tails = pl.BlockSpec((take * TAIL, width), lambda i: (i, 0))
    tile = pl.BlockSpec((take * QUERIES, width), lambda i: (i, 0))

    def shape(count, dtype):
        return jax.ShapeDtypeStruct((rows * count, width), dtype)

    return pl.pallas_call(
        cross_forward_kernel,
        grid=(rows // take,),
        in_specs=[
            pl.BlockSpec((take, patches, vis), lambda i: (i, 0, 0)),
            pl.BlockSpec((take, TAIL, vis), lambda i: (i, 0, 0)),
            held(kv.shape, lambda i: (0, 0, 0)),
            held((2, width, width), lambda i: (2, 0, 0)),
            whole(biases.shape),
            whole(gains.shape),
            pl.BlockSpec((take, QUERIES, width), lambda i: (i, 0, 0)),
        ],
        out_specs=[keys, keys, tails, tails, tile, tile, tile, tile],
        out_shape=[
            shape(main, bf16),
            shape(main, bf16),
            shape(TAIL, bf16),
            shape(TAIL, bf16),
            shape(QUERIES, bf16),
            shape(QUERIES, bf16),
            shape(QUERIES, f32),
            shape(QUERIES, f32),
        ],
        compiler_params=params(58),
        name="cross_forward",
        cost_estimate=cost(38),
    )(images, ends, kv, weights, biases, gains, norm)


def cross_backward_kernel(
    w_ref,
    key_ref,
    value_ref,
    key_end_ref,
    value_end_ref,
    q_ref,
    down_ref,
    dnorm_ref,
    dkv_ref,
    dkv_end_ref,
    dq_ref,
    side_ref,
    dmix_all,
):
    step = pl.program_id(0)
    rows_here, _, width = dnorm_ref.shape
    main = key_ref.shape[0] // rows_here
    low, high = half_lanes(QUERIES)

    @pl.when(step == 0)
    def _():
        side_ref[...] = jnp.zeros_like(side_ref)

    down = down_ref[...]
    branch = down.astype(bf16)
    dmix_all[...] = dot_nt(branch, w_ref[1]).astype(bf16)

    def some_rows(step, carry):
        spots = []
        for near in range(CROSS_BACK_ROWS):
            r = step * CROSS_BACK_ROWS + near
            span = pl.ds(pl.multiple_of(r * main, main), main)
            last = pl.ds(pl.multiple_of(r * TAIL, TAIL), TAIL)
            mine = pl.ds(pl.multiple_of(r * QUERIES, QUERIES), QUERIES)
            spots += [(span, last, mine, slice(g * 256, (g + 1) * 256)) for g in range(GROUPS)]
        keys = [
            jnp.concatenate([key_ref[span, cols], key_end_ref[last, cols]], 0)
            for span, last, mine, cols in spots
        ]
        queries = [
            spread_heads(q_ref[mine, cols] * bf16(0.125), low, high)
            for span, last, mine, cols in spots
        ]
        outs = [spread_heads(dmix_all[mine, cols], low, high) for span, last, mine, cols in spots]
        scores = [dot_nt(rows, turned) for rows, turned in zip(keys, queries)]
        dprobs = [
            dot_nt(jnp.concatenate([value_ref[span, cols], value_end_ref[last, cols]], 0), turned)
            for (span, last, mine, cols), turned in zip(spots, outs)
        ]
        probs = [columns_softmax(hide_ends(score, main)) for score in scores]
        for (span, last, mine, cols), prob, turned in zip(spots, probs, outs):
            dv = dot_nn(prob.astype(bf16), turned).astype(bf16)
            dkv_ref[1, span, cols] = dv[:main]
            dkv_end_ref[1, last, cols] = dv[main:]
        dscores = [
            (prob * (dprob - jnp.sum(dprob * prob, 0, keepdims=True))).astype(bf16)
            for prob, dprob in zip(probs, dprobs)
        ]
        for (span, last, mine, cols), dscore, turned in zip(spots, dscores, queries):
            dk = dot_nn(dscore, turned).astype(bf16)
            dkv_ref[0, span, cols] = dk[:main]
            dkv_end_ref[0, last, cols] = dk[main:]
        dqs = [dot_tn(dscore, rows) for dscore, rows in zip(dscores, keys)]
        for (span, last, mine, cols), dq in zip(spots, dqs):
            dq_ref[mine, cols] = (collect_heads(dq, QUERIES) * 0.125).astype(bf16)
        return carry

    lax.fori_loop(0, rows_here // CROSS_BACK_ROWS, some_rows, 0)
    dq = dq_ref[...]
    dnorm_ref[...] = (down + dot_nt(dq, w_ref[0])).reshape(rows_here, QUERIES, width)
    put_row(side_ref, 0, jnp.sum(dq.astype(f32), 0, keepdims=True), True)
    dvalue = jnp.sum(dkv_ref[1].astype(f32), 0, keepdims=True)
    dvalue += jnp.sum(dkv_end_ref[1].astype(f32), 0, keepdims=True)
    put_row(side_ref, 1, dvalue, True)
    put_row(side_ref, 2, jnp.sum(branch.astype(f32), 0, keepdims=True), True)


def cross_backward(rows, weights, keys, values, key_ends, value_ends, q, down, order):
    width = q.shape[1]
    main = keys.shape[0] // rows
    take = 4
    span = pl.BlockSpec((take * main, width), lambda i: (i, 0))
    tails = pl.BlockSpec((take * TAIL, width), lambda i: (i, 0))
    tile = pl.BlockSpec((take * QUERIES, width), lambda i: (i, 0))
    return pl.pallas_call(
        ordered(cross_backward_kernel, 7, len(order)),
        grid=(rows // take,),
        in_specs=[
            held((2, width, width), lambda i: (2, 0, 0)),
            span,
            span,
            tails,
            tails,
            tile,
            tile,
        ]
        + unread(len(order)),
        out_specs=[
            pl.BlockSpec((take, QUERIES, width), lambda i: (i, 0, 0)),
            pl.BlockSpec((2, take * main, width), lambda i: (0, i, 0)),
            pl.BlockSpec((2, take * TAIL, width), lambda i: (0, i, 0)),
            tile,
            whole((width // 16, 128)),
        ],
        out_shape=[
            jax.ShapeDtypeStruct((rows, QUERIES, width), f32),
            jax.ShapeDtypeStruct((2, rows * main, width), bf16),
            jax.ShapeDtypeStruct((2, rows * TAIL, width), bf16),
            jax.ShapeDtypeStruct((rows * QUERIES, width), bf16),
            jax.ShapeDtypeStruct((width // 16, 128), f32),
        ],
        scratch_shapes=[pltpu.VMEM((take * QUERIES, width), bf16)],
        compiler_params=params(58),
        name="cross_backward",
        cost_estimate=cost(19),
    )(weights, keys, values, key_ends, value_ends, q, down, *order)


def third_units(units):
    edges = [(units * k + 2) // 3 for k in range(4)]
    return [edges[k + 1] - edges[k] for k in range(3)]


def cross_weight_kernel(folds, core_ref, image_ref, end_ref, grad_ref, grad_end_ref, *rest):
    outs, gathered = rest[:-1], rest[-1]
    rows, patches, vis = image_ref.shape
    main = patches - 1
    take = 4
    gathered[...] = dot_tn(grad_end_ref[0], end_ref[...].reshape(rows * TAIL, vis))

    def add_rows(i, carry):
        span = pl.ds(pl.multiple_of(i * take * main, take * main), take * main)
        tokens = image_ref[pl.ds(i * take, take), :main].reshape(take * main, vis)
        gathered[...] += dot_tn(grad_ref[0, span], tokens)
        return carry

    lax.fori_loop(0, rows // take, add_rows, 0)
    if folds is None:
        store_units(outs[0].at[0], gathered[...])
        return
    first = 0
    for part, fold in enumerate(folds):
        keep, send = outs[2 * part : 2 * part + 2]
        units, size = keep.shape[-3:-1]
        pieces = []
        for block in range(gathered.shape[0] // size):
            spot = tuple(
                0 if axis == "rep" or bit == 3 else (block >> bit) & 1 for axis, bit in fold
            )
            piece = gathered[block * size : (block + 1) * size].astype(bf16)
            for unit in range(units):
                at = (first + unit) * 128
                pieces.append((spot + (unit,), piece[:, at : at + 128]))
        store_halves(core_ref, keep, send, pieces)
        first += units


def cross_weight_grad(core, images, ends, grads, grads_end, folds, size, order):
    rows, patches, vis = images.shape
    width = grads.shape[2]
    half = width // 2
    units = vis // 128
    if folds is None:
        specs = [pl.BlockSpec((1, units, half, 128), lambda m, h: (m, 0, h, 0))]
        shapes = [(2, units, width, 128)]
    else:
        specs, shapes = [], []
        for fold, count in zip(folds, third_units(units) if len(folds) == 3 else [units]):
            block = tuple(1 if axis == "rep" or bit == 3 else 2 for axis, bit in fold[1:])

            def index(m, h, fold=fold):
                spot = tuple(
                    m if axis == "rep" else h if bit == 3 else 0 for axis, bit in fold[1:]
                )
                return spot + (0, 0, 0)

            specs += [pl.BlockSpec(block + (count, size, 128), index)] * 2
            shapes += [slab_shape(fold, count, size)] * 2
    return pl.pallas_call(
        ordered(functools.partial(cross_weight_kernel, folds), 5, len(order)),
        grid=(2, 2),
        in_specs=[
            core_spec,
            held(images.shape, lambda m, h: (0, 0, 0)),
            held(ends.shape, lambda m, h: (0, 0, 0)),
            pl.BlockSpec((1, grads.shape[1], half), lambda m, h: (m, 0, h)),
            pl.BlockSpec((1, grads_end.shape[1], half), lambda m, h: (m, 0, h)),
        ]
        + unread(len(order)),
        out_specs=specs,
        out_shape=[jax.ShapeDtypeStruct(shape, bf16) for shape in shapes],
        scratch_shapes=[pltpu.VMEM((half, vis), f32)],
        compiler_params=pltpu.CompilerParams(
            vmem_limit_bytes=58 * MIB, dimension_semantics=("arbitrary", "arbitrary")
        ),
        name="cross_weight_grad",
        cost_estimate=cost(32),
    )(core, images, ends, grads, grads_end, *order)


def ffn_forward_kernel(
    which,
    norm_ref,
    in_ref,
    in_bias_ref,
    out_ref,
    proj_ref,
    proj_bias_ref,
    bias_ref,
    gain_ref,
    *rest,
):
    act_ref, slope_ref, sum_ref, low_ref, raw_ref, embed_ref, rows_low = rest[-7:]
    step = pl.program_id(0)
    tokens, width = sum_ref.shape

    @pl.when(step == 0)
    def _():
        full = norm_ref[...].reshape(tokens, width)
        rows_low[...] = full.astype(bf16)
        sum_ref[...] = full + bias_ref[6 + which : 7 + which]

    low = rows_low[...]
    wide = 256
    pieces = act_ref.shape[1] // wide

    def before_gate(k):
        cols = slice(k * wide, (k + 1) * wide)
        return dot_nn(low, in_ref[0, :, cols]) + in_bias_ref[which : which + 1, cols]

    ahead = [before_gate(k) for k in range(2)]
    gathered = 0.0
    for k in range(pieces):
        if k + 2 < pieces:
            ahead.append(before_gate(k + 2))
        cols = slice(k * wide, (k + 1) * wide)
        act, slope = gate_parts(ahead[k])
        act = act.astype(bf16)
        act_ref[:, cols] = act
        slope_ref[:, cols] = slope.astype(bf16)
        gathered += dot_nn(act, out_ref[0, cols])
    sum_ref[...] += gathered

    @pl.when(step == pl.num_programs(0) - 1)
    def _():
        unit, _ = norm_parts(sum_ref[...])
        low = (unit * gain_ref[2 + which : 3 + which] + bias_ref[10 + which : 11 + which]).astype(bf16)
        low_ref[...] = low.reshape(low_ref.shape)
        raw = dot_nn(low, proj_ref[0]) + proj_bias_ref[which : which + 1]
        raw_ref[...] = raw
        size = lax.rsqrt(jnp.sum(raw * raw, -1, keepdims=True) + epsilon)
        embed_ref[...] = (raw * size).astype(bf16)


def ffn_forward(which, part, norm, ffn_in, ffn_bias, ffn_out, projections, proj_bias, biases, gains, layer, order=()):
    rows, width = norm.shape[0], norm.shape[-1]
    tokens = rows * QUERIES
    hidden = ffn_in.shape[2]
    embed = projections.shape[2]
    chunk = 1024
    cols = pl.BlockSpec((tokens, chunk), lambda j: (0, j))
    halves = [] if layer is None else [layer]
    return pl.pallas_call(
        functools.partial(ffn_forward_kernel, which),
        grid=(hidden // chunk,),
        in_specs=[
            held((rows, QUERIES, width), lambda j: (0, part, 0)),
            pl.BlockSpec((1, width, chunk), lambda j: (which, 0, j)),
            pl.BlockSpec((2, chunk), lambda j: (0, j)),
            pl.BlockSpec((1, chunk, width), lambda j: (which, j, 0)),
            held((1, width, embed), lambda j: (which, 0, 0)),
            whole(proj_bias.shape),
            whole(biases.shape),
            whole(gains.shape),
        ]
        + unread(len(halves) + len(order)),
        out_specs=[
            cols,
            cols,
            whole((tokens, width)),
            pl.BlockSpec((rows, QUERIES, width), lambda j: (0, which, 0)),
            whole((tokens, embed)),
            whole((tokens, embed)),
        ],
        out_shape=[
            jax.ShapeDtypeStruct((tokens, hidden), bf16),
            jax.ShapeDtypeStruct((tokens, hidden), bf16),
            jax.ShapeDtypeStruct((tokens, width), f32),
            jax.ShapeDtypeStruct((rows, SLOTS, width), bf16),
            jax.ShapeDtypeStruct((tokens, embed), f32),
            jax.ShapeDtypeStruct((tokens, embed), bf16),
        ],
        scratch_shapes=[pltpu.VMEM((tokens, width), bf16)],
        input_output_aliases={8: 3} if halves else {},
        compiler_params=params(58),
        name="ffn_forward",
        cost_estimate=cost(15),
    )(norm, ffn_in, ffn_bias, ffn_out, projections, proj_bias, biases, gains, *halves, *order)


def ffn_backward_kernel(
    which,
    folds,
    core_ref,
    norm_ref,
    sum_ref,
    before_ref,
    layer_ref,
    grad_ref,
    raw_ref,
    proj_ref,
    gain_ref,
    in_ref,
    out_ref,
    act_ref,
    slope_ref,
    *rest,
):
    count = 3 if folds is None else 6
    down_ref, side_ref, dbias_ref, dproj_bias_ref = rest[-8 - count : -4 - count]
    weight_refs = rest[-4 - count : -4]
    branch_all, low_turned, left, dproj = rest[-4:]
    step = pl.program_id(0)
    tokens, width = sum_ref.shape

    @pl.when(step == 0)
    def _():
        raw = raw_ref[...]
        grad = grad_ref[...].reshape(tokens, width).astype(f32) + dot_nt(raw, proj_ref[0])
        down, dgain, dshift = norm_grads(sum_ref[...], gain_ref[2 + which : 3 + which], grad)
        branch = down.astype(bf16)
        branch_all[...] = branch
        left[...] = down
        side_ref[...] = jnp.zeros_like(side_ref)
        put_row(side_ref, 0, dgain)
        put_row(side_ref, 1, dshift)
        put_row(side_ref, 2, jnp.sum(branch.astype(f32), 0, keepdims=True))
        dproj[...] = dot_tn(layer_ref[...].reshape(tokens, width), raw).astype(bf16)
        put_row(dproj_bias_ref, 0, jnp.sum(raw.astype(f32), 0, keepdims=True))
        low_turned[...] = norm_ref[...].reshape(tokens, width).astype(bf16).T

    branch = branch_all[...]
    du = (dot_nt(branch, out_ref[0]) * slope_ref[...].astype(f32)).astype(bf16)
    left[...] += dot_nt(du, in_ref[0])
    put_row(dbias_ref, 0, jnp.sum(du.astype(f32), 0, keepdims=True))
    thin = width // 3
    for part in range(3):

        @pl.when(step == part)
        def _():
            din = dot_nn(low_turned[...], du).astype(bf16)
            dout = dot_tn(act_ref[...], branch[:, part * thin : (part + 1) * thin]).astype(bf16)
            if folds is None:
                store_units(weight_refs[0], din)
                store_units(weight_refs[1], dout)
                if part == 0:
                    store_units(weight_refs[2], dproj[...])
                return
            keep, send = weight_refs[2 * part : 2 * part + 2]
            size = keep.shape[-2]
            subs = dout.shape[0] // width
            pieces = []
            for block in range(width // size):
                spot = place_of(folds[part], block, 0)
                at = block * size
                found = [
                    din[at : at + size, unit * 128 : (unit + 1) * 128]
                    for unit in range(din.shape[1] // 128)
                ]
                for sub in range(subs):
                    row = at * subs + sub * size
                    for unit in range(thin // 128):
                        found.append(dout[row : row + size, unit * 128 : (unit + 1) * 128])
                if part == 0:
                    for unit in range(dproj.shape[1] // 128):
                        found.append(dproj[at : at + size, unit * 128 : (unit + 1) * 128])
                pieces += [(spot + (unit,), piece) for unit, piece in enumerate(found)]
            store_halves(core_ref, keep, send, pieces)

    @pl.when(step == pl.num_programs(0) - 1)
    def _():
        if which == 0:
            down, dgain, dshift = norm_grads(before_ref[...], gain_ref[1:2], left[...])
            put_row(side_ref, 3, dgain)
            put_row(side_ref, 4, dshift)
            down_ref[...] = down.reshape(down_ref.shape)
        else:
            down_ref[...] = left[...].reshape(down_ref.shape)


def ffn_backward(
    which,
    part,
    core,
    norm,
    total,
    before,
    layer,
    grad,
    raw,
    projections,
    gains,
    ffn_in,
    ffn_out,
    act,
    slope,
    slabs,
    folds,
    size,
):
    rows = layer.shape[0]
    tokens, width = total.shape
    hidden = ffn_in.shape[2]
    embed = projections.shape[2]
    chunk = hidden // 3
    slabs = list(slabs)
    if folds is None:
        weight_specs = [
            pl.BlockSpec((chunk // 128, width, 128), lambda j: (j, 0, 0)),
            pl.BlockSpec((width // 384, hidden, 128), lambda j: (j, 0, 0)),
            whole((embed // 128, width, 128)),
        ]
        weight_shapes = [
            (hidden // 128, width, 128),
            (width // 128, hidden, 128),
            (embed // 128, width, 128),
        ]
    else:
        units = chunk // 128 + (hidden // width) * (width // 384)
        weight_shapes = [
            slab_shape(fold, units + (embed // 128 if k == 0 else 0), size)
            for k, fold in enumerate(folds)
            for half in range(2)
        ]

        def spec(fold, shape):
            block = tuple(1 if axis == "rep" else 2 for axis, bit in fold[1:])
            spot = tuple(which if axis == "rep" else 0 for axis, bit in fold[1:])
            return held(block + shape[-3:], lambda j: spot + (0, 0, 0))

        weight_specs = [spec(folds[k // 2], shape) for k, shape in enumerate(weight_shapes)]
    return pl.pallas_call(
        functools.partial(ffn_backward_kernel, which, folds),
        grid=(3,),
        in_specs=[
            core_spec,
            held((rows, QUERIES, width), lambda j: (0, part, 0)),
            held((tokens, width), lambda j: (0, 0)),
            held(before.shape, lambda j: (0, 0)),
            held((rows, QUERIES, width), lambda j: (0, which, 0)),
            held((rows, QUERIES, width), lambda j: (0, which, 0)),
            held((tokens, embed), lambda j: (0, 0)),
            held((1, width, embed), lambda j: (which, 0, 0)),
            whole(gains.shape),
            pl.BlockSpec((1, width, chunk), lambda j: (which, 0, j)),
            pl.BlockSpec((1, chunk, width), lambda j: (which, j, 0)),
            held((tokens, hidden), lambda j: (0, 0)),
            pl.BlockSpec((tokens, chunk), lambda j: (0, j)),
        ]
        + [pl.BlockSpec(memory_space=pl.ANY)] * len(slabs),
        out_specs=[
            whole((rows, QUERIES, width)),
            whole((width // 16, 128)),
            pl.BlockSpec((chunk // 128, 128), lambda j: (j, 0)),
            whole((embed // 128, 128)),
        ]
        + weight_specs,
        out_shape=[
            jax.ShapeDtypeStruct((rows, QUERIES, width), f32),
            jax.ShapeDtypeStruct((width // 16, 128), f32),
            jax.ShapeDtypeStruct((hidden // 128, 128), f32),
            jax.ShapeDtypeStruct((embed // 128, 128), f32),
        ]
        + [jax.ShapeDtypeStruct(shape, bf16) for shape in weight_shapes],
        scratch_shapes=[
            pltpu.VMEM((tokens, width), bf16),
            pltpu.VMEM((width, tokens), bf16),
            pltpu.VMEM((tokens, width), f32),
            pltpu.VMEM((width, embed), bf16),
        ],
        input_output_aliases={13 + k: 4 + k for k in range(len(slabs))},
        compiler_params=params(60),
        name="ffn_backward",
        cost_estimate=cost(25),
    )(
        core,
        norm,
        total,
        before,
        layer,
        grad,
        raw,
        projections,
        gains,
        ffn_in,
        ffn_out,
        act,
        slope,
        *slabs,
    )


def swap(values, stage, sizes):
    axis, bit = stage
    return lax.ppermute(values, axis, [(i, i ^ (1 << bit)) for i in range(sizes[axis])])


def stage_order(part, sizes):
    stages = [("dp", bit) for bit in range(sizes["dp"].bit_length() - 1)]
    ring = stages[1:3] + [("rep", 0)]
    if part == 3:
        return stages[:1] + ring[:2] + stages[3:] + ring[2:]
    return stages[:1] + ring[part:] + ring[:part] + stages[3:]


def fold_pair(part, first, second, sizes):
    depth = sizes["dp"].bit_length() - 1
    both = jnp.stack([first, second])
    units, rows = first.shape[0], first.shape[1] // sizes["dp"]
    both = both.reshape((2, units) + (2,) * depth + (rows, 128))
    front = [0 if axis == "rep" else 1 + depth - bit for axis, bit in stage_order(part, sizes)]
    return both.transpose(front + [1, 2 + depth, 3 + depth])


def own_bits(sizes):
    depth = sizes["dp"].bit_length() - 1
    shifts = jnp.arange(depth + 1, dtype=jnp.int32)
    both = lax.axis_index("dp") + (lax.axis_index("rep") << depth)
    return ((both >> shifts) & 1).astype(jnp.int32)


def bit_place(stage, sizes):
    return sizes["dp"].bit_length() - 1 if stage[0] == "rep" else stage[1]


def picked(place_bits, bits_ref):
    at = 0
    for bit, other in place_bits:
        own = bits_ref[bit]
        at = 2 * at + (1 - own if other else own)
    return at


def sum_kernel(plan, arrays, bits_ref, *refs):
    sources, refs = refs[:arrays], refs[arrays:]
    outs, refs = refs[: len(plan)], refs[len(plan) :]
    count = sum(len(terms) for jobs in plan for _, terms in jobs)
    held_terms, held_outs = refs[:count], refs[count : count + len(plan)]
    in_sems, out_sems = refs[-2:]
    fetches = []
    for jobs in plan:
        for rows, terms in jobs:
            for source, start, place_bits in terms:
                first = start + picked(place_bits, bits_ref) * rows
                here = len(fetches)
                fetches.append(
                    pltpu.make_async_copy(
                        sources[source].at[pl.ds(pl.multiple_of(first, 16), rows)],
                        held_terms[here],
                        in_sems.at[here],
                    )
                )
    for fetch in fetches:
        fetch.start()
    here = 0
    stores = []
    for place, jobs in enumerate(plan):
        at = 0
        for rows, terms in jobs:
            found = None
            for _ in terms:
                fetches[here].wait()
                part = held_terms[here][...].astype(f32)
                found = part if found is None else found + part
                here += 1
            held_outs[place][at : at + rows] = found.astype(held_outs[place].dtype)
            at += rows
        store = pltpu.make_async_copy(held_outs[place], outs[place], out_sems.at[place])
        store.start()
        stores.append(store)
    for store in stores:
        store.wait()


def sum_jobs(outputs, bits):
    arrays, plan, buffers = [], [], []

    def number_of(array):
        for number, known in enumerate(arrays):
            if known is array:
                return number
        arrays.append(array)
        return len(arrays) - 1

    shapes, moved = [], 0
    for dtype, jobs in outputs:
        planned = []
        for rows, terms in jobs:
            planned.append((rows, [(number_of(array), start, bit) for array, start, bit in terms]))
            buffers += [pltpu.VMEM((rows, 128), array.dtype) for array, _, _ in terms]
            moved += rows * (1 + len(terms))
        plan.append(planned)
        shapes.append(jax.ShapeDtypeStruct((sum(rows for rows, _ in jobs), 128), dtype))
    return pl.pallas_call(
        functools.partial(sum_kernel, plan, len(arrays)),
        in_specs=[core_spec] + unread(len(arrays)),
        out_specs=unread(len(plan)),
        out_shape=shapes,
        scratch_shapes=buffers
        + [pltpu.VMEM(shape.shape, shape.dtype) for shape in shapes]
        + [pltpu.SemaphoreType.DMA((len(buffers),)), pltpu.SemaphoreType.DMA((len(plan),))],
        compiler_params=pltpu.CompilerParams(vmem_limit_bytes=60 * MIB),
        name="sum_terms",
        cost_estimate=cost(3),
    )(bits, *arrays)


def sum_jobs_plain(outputs, bits):
    results = []
    for dtype, jobs in outputs:
        pieces = []
        for rows, terms in jobs:
            found = [
                lax.dynamic_slice_in_dim(array, start + picked(bit, bits) * rows, rows, 0)
                for array, start, bit in terms
            ]
            pieces.append(sum(part.astype(f32) for part in found).astype(dtype))
        results.append(pieces[0] if len(pieces) == 1 else jnp.concatenate(pieces, 0))
    return results


def begin(part, keep, send, sizes):
    keep, send = keep.reshape(-1, 128), send.reshape(-1, 128)
    arrived = swap(send, stage_order(part, sizes)[0], sizes)
    return (part, 1, [(keep, 0, keep.shape[0], []), (arrived, 0, send.shape[0], [])], send)


def begin_folded(part, slab, sizes):
    own = lax.axis_index("dp") & 1
    halves = [lax.dynamic_index_in_dim(slab, place, 0, keepdims=False) for place in (own, 1 - own)]
    return begin(part, *halves, sizes)


def begin_whole(values, sizes):
    send = values.astype(bf16)
    arrived = swap(send, stage_order(0, sizes)[0], sizes)
    return (None, 1, [(values, 0, len(values), []), (arrived, 0, len(values), [])], send)


def advance(states, bits, sizes, plain, after=None):
    last = len(stage_order(0, sizes))
    changed = {}
    fresh = []
    for part, at, terms, sent in states:
        array = terms[-1][0]
        if after is not None:
            if id(array) not in changed:
                changed[id(array)] = (array, lax.optimization_barrier((array, after))[0])
            array = changed[id(array)][1]
        fresh.append((part, at, terms[:-1] + [(array,) + terms[-1][1:]], sent))
    groups, finals = {}, []
    for number, (part, at, terms, _) in enumerate(fresh):
        if at == last:
            finals.append(number)
        else:
            groups.setdefault(stage_order(part or 0, sizes)[at], []).append(number)

    def job(number, ahead):
        rows = fresh[number][2][0][2] >> (len(fresh[number][2][0][3]) + len(ahead))
        return (
            rows,
            [(array, start, places + ahead) for array, start, _, places in fresh[number][2]],
        )

    outputs = []
    for stage, members in groups.items():
        jobs = []
        for number in members:
            ahead = [] if fresh[number][0] is None else [(bit_place(stage, sizes), True)]
            jobs.append(job(number, ahead))
        outputs.append((bf16, jobs))
    outputs += [(f32, [job(number, [])]) for number in finals]
    made = (sum_jobs_plain if plain else sum_jobs)(outputs, bits)
    results = [None] * len(fresh)
    for (stage, members), (_, jobs), sent in zip(groups.items(), outputs, made):
        arrived = swap(sent, stage, sizes)
        start = 0
        for number, (rows, _) in zip(members, jobs):
            part, at, terms, _ = fresh[number]
            kept = [] if part is None else [(bit_place(stage, sizes), False)]
            terms = [(array, first, size, places + kept) for array, first, size, places in terms]
            results[number] = (part, at + 1, terms + [(arrived, start, rows, [])], sent)
            start += rows
    for number, found in zip(finals, made[len(groups) :]):
        results[number] = found
    return results


def sends(states):
    found = []
    for state in states:
        if not any(state[3] is known for known in found):
            found.append(state[3])
    return found


def columns_of(units):
    return units.transpose(1, 0, 2).reshape(units.shape[1], -1)


def exchange(values, sizes):
    return lax.all_to_all(values, ("dp", "rep"), 0, 0, tiled=True)


def gather_rows(values, sizes):
    world = sizes["dp"] * sizes["rep"]
    return exchange(jnp.tile(values, (world, 1)), sizes)


def scatter_rows(values, sizes):
    world = sizes["dp"] * sizes["rep"]
    arrived = exchange(values, sizes)
    return jnp.sum(arrived.reshape(world, -1, values.shape[1]).astype(f32), 0)


def shards(
    hidden_states,
    image_features,
    caption_lengths,
    attn_weights,
    cross_kv,
    ffn_in,
    ffn_out,
    projections,
    norm_gains,
    biases,
    ffn_bias,
    proj_bias,
    out_grad,
    sizes,
):
    row_count, slots, width = hidden_states.shape
    captions_here = 2 * row_count
    world = sizes["dp"] * sizes["rep"]
    allowed, pick_mask = caption_layout(caption_lengths)
    pick_low = pick_mask.astype(bf16)
    pick_full = pick_mask.astype(f32)
    mask = jnp.tile(allowed.astype(f32), (1, 1, 4))
    inputs = hidden_states.reshape(row_count * slots, width)
    self_q, self_k, self_v, self_mix, first_sum, first_norm = self_forward(
        inputs, attn_weights, biases, norm_gains, mask
    )
    first_norm = first_norm.reshape(row_count, slots, width)
    image_ends = jnp.pad(image_features[:, -1:], ((0, 0), (0, TAIL - 1), (0, 0)))
    text_act, text_slope, fourth_sum, layer_half, caption_raw, caption_all = ffn_forward(
        1,
        1,
        first_norm,
        ffn_in,
        ffn_bias,
        ffn_out,
        projections,
        proj_bias,
        biases,
        norm_gains,
        None,
        [image_ends],
    )
    caption_embed = (
        jnp.einsum(
            "rkt,rtd->rkd",
            pick_low,
            caption_all.reshape(row_count, TEXT, -1),
            preferred_element_type=f32,
        )
        .astype(bf16)
        .reshape(captions_here, -1)
    )
    every_caption = gather_rows(caption_embed, sizes)
    keys, values, key_ends, value_ends, cross_q, cross_mix, second_sum, second_norm = cross_forward(
        image_features, image_ends, cross_kv, attn_weights, biases, norm_gains, first_norm
    )
    second_norm = second_norm.reshape(row_count, QUERIES, width)
    query_act, query_slope, third_sum, layer_out, query_raw, query_embed = ffn_forward(
        0,
        0,
        second_norm,
        ffn_in,
        ffn_bias,
        ffn_out,
        projections,
        proj_bias,
        biases,
        norm_gains,
        layer_half,
    )
    query_raw = query_raw.reshape(row_count, QUERIES, -1)
    query_embed = query_embed.reshape(row_count, QUERIES, -1)
    sims = jnp.einsum("rqp,cp->rqc", query_embed, every_caption, preferred_element_type=f32)
    expo = jnp.exp(sharpness * (sims - 1.0))
    affinity = jnp.mean(expo, 1)
    offset = lax.axis_index(("dp", "rep")) * captions_here
    own_block = lax.dynamic_slice_in_dim(affinity, offset, captions_here, 1).reshape(
        row_count, row_count, 2
    )
    diagonal = (
        lax.broadcasted_iota(jnp.int32, (row_count, row_count), 0)
        == lax.broadcasted_iota(jnp.int32, (row_count, row_count), 1)
    ).astype(f32)
    positive = jnp.sum(own_block * diagonal[:, :, None], 1)
    row_total = jnp.sum(affinity, 1)
    partial_cols = jnp.sum(affinity, 0)
    all_cols = jnp.sum(
        exchange(jnp.broadcast_to(partial_cols[None], (world,) + partial_cols.shape), sizes), 0
    )
    own_cols = lax.dynamic_slice_in_dim(all_cols, offset, captions_here, 0).reshape(row_count, 2)
    inverse_all = 1.0 / all_cols
    row_loss = (
        jnp.log(row_total)
        - jnp.log(positive[:, 0])
        + jnp.sum(jnp.log(own_cols) - jnp.log(positive), 1)
    )
    grad_affinity = loss_weight * (1.0 / row_total[:, None] + inverse_all[None, :])
    pair_weight = jnp.array([2.0, 1.0], f32)
    correction = (loss_weight * diagonal[:, :, None] * pair_weight / own_block).reshape(
        row_count, captions_here
    )
    own_grad = lax.dynamic_slice_in_dim(grad_affinity, offset, captions_here, 1) - correction
    grad_affinity = lax.dynamic_update_slice_in_dim(grad_affinity, own_grad, offset, 1)
    grad_sims = (grad_affinity[:, None, :] * expo * (sharpness / QUERIES)).astype(bf16)
    grad_query_embed = jnp.einsum(
        "rqc,cp->rqp", grad_sims, every_caption, preferred_element_type=f32
    )
    grad_caption_embed = scatter_rows(
        jnp.einsum("rqc,rqp->cp", grad_sims, query_embed, preferred_element_type=f32).astype(bf16),
        sizes,
    )
    query_raw_grad = unit_back(query_raw, grad_query_embed).astype(bf16)
    head_raw = jnp.sum(
        pick_full[:, :, :, None] * caption_raw.reshape(row_count, 1, TEXT, -1), 2
    )
    head_raw_grad = unit_back(head_raw, grad_caption_embed.reshape(row_count, 2, -1)).astype(bf16)
    caption_raw_grad = jnp.einsum(
        "rkt,rkd->rtd", pick_low, head_raw_grad, preferred_element_type=f32
    ).astype(bf16)
    fold = sizes["dp"] == 16 and sizes["rep"] == 2
    stage_orders = [stage_order(part, sizes) for part in range(3)]
    folds = stage_orders if fold else None
    ffn_parts = (3, 1, 2)
    ffn_folds = [stage_order(part, sizes) for part in ffn_parts] if fold else None
    size = width // sizes["dp"]
    bits = own_bits(sizes)
    core = bits[:1]
    grad_second, query_side, query_dbias, query_dproj_bias, *query_slabs = ffn_backward(
        0,
        0,
        core,
        second_norm,
        third_sum,
        second_sum,
        layer_out,
        out_grad,
        query_raw_grad.reshape(row_count * QUERIES, -1),
        projections,
        norm_gains,
        ffn_in,
        ffn_out,
        query_act,
        query_slope,
        (),
        ffn_folds,
        size,
    )
    text_first, text_side, text_dbias, text_dproj_bias, *text_slabs = ffn_backward(
        1,
        1,
        core,
        first_norm,
        fourth_sum,
        fourth_sum,
        layer_out,
        out_grad,
        caption_raw_grad.reshape(row_count * TEXT, -1),
        projections,
        norm_gains,
        ffn_in,
        ffn_out,
        text_act,
        text_slope,
        query_slabs if fold else (),
        ffn_folds,
        size,
    )
    tall = ffn_out.shape[1] // width
    if not fold:
        text_slabs = [
            fold_pair(
                ffn_parts[part],
                *(
                    jnp.concatenate(
                        [
                            din[part * 8 : part * 8 + 8],
                            dout[2 * part : 2 * part + 2]
                            .reshape(2, sizes["dp"], tall, size, 128)
                            .transpose(2, 0, 1, 3, 4)
                            .reshape(2 * tall, width, 128),
                            dproj[: 2 if part == 0 else 0],
                        ],
                        0,
                    )
                    for din, dout, dproj in (query_slabs, text_slabs)
                ),
                sizes,
            )
            for part in range(3)
        ]
    if fold:
        ffn = [
            begin(ffn_parts[part], *text_slabs[2 * part : 2 * part + 2], sizes) for part in range(3)
        ]
    else:
        ffn = [begin_folded(part, slab, sizes) for part, slab in zip(ffn_parts, text_slabs)]
    cross_down = grad_second.reshape(row_count * QUERIES, width)
    query_first, dkv, dkv_ends, cross_dq, cross_side = cross_backward(
        row_count,
        attn_weights,
        keys,
        values,
        key_ends,
        value_ends,
        cross_q,
        cross_down,
        [text_first] + sends(ffn),
    )
    plain = not fold
    ffn = advance(ffn, bits, sizes, plain, cross_side)
    cross_slabs = cross_weight_grad(
        core, image_features, image_ends, dkv, dkv_ends, folds, size, sends(ffn)
    )
    if fold:
        cross = [begin(part, *cross_slabs[2 * part : 2 * part + 2], sizes) for part in range(3)]
    else:
        edges = [0, 4, 8, cross_slabs[0].shape[1]]
        cross = [
            begin_folded(
                part,
                fold_pair(part, *cross_slabs[0][:, edges[part] : edges[part + 1]], sizes),
                sizes,
            )
            for part in range(3)
        ]
    ffn = advance(ffn, bits, sizes, plain, cross_slabs[0])
    self_grads, self_branch, self_down, self_side = self_backward(
        attn_weights,
        norm_gains,
        mask,
        self_q,
        self_k,
        self_v,
        first_sum,
        query_first,
        text_first,
        sends(ffn + cross),
    )
    rows = [
        self_side,
        cross_side,
        query_side,
        text_side,
        query_dbias,
        text_dbias,
        query_dproj_bias,
        text_dproj_bias,
    ]
    used = sum(array.shape[0] for array in rows)
    packed = jnp.concatenate(rows + [jnp.zeros((-used % 64, 128), f32)], 0)
    states = advance(ffn + cross, bits, sizes, plain, self_side)
    vector = begin_whole(packed, sizes)
    half = (row_count, QUERIES, width)
    attn_slabs = attn_weight_grad(
        core,
        inputs,
        self_grads,
        [
            (self_mix, self_mix.shape),
            (self_branch, self_branch.shape),
            (first_norm, half),
            (cross_dq, cross_dq.shape),
            (cross_mix, cross_mix.shape),
            (cross_down, cross_down.shape),
        ],
        folds,
        size,
        sends(states + [vector]),
    )
    if fold:
        attn = [begin(part, *attn_slabs[2 * part : 2 * part + 2], sizes) for part in range(3)]
    else:
        attn = [
            begin_folded(part, fold_pair(part, *slab, sizes), sizes)
            for part, slab in enumerate(attn_slabs)
        ]
    states = advance(states + [vector], bits, sizes, plain, attn_slabs[0])
    input_grad = input_gradient(attn_weights, self_grads, self_down, sends(states + attn))
    ffn, cross, vector = states[:3], states[3:6], states[6]
    last = len(stage_orders[0])
    states = ffn + attn + cross + [vector]
    done = [None] * len(states)
    places = list(range(len(states)))
    after = input_grad
    while states:
        ready = [state[1] == last for state in states]
        states = advance(states, bits, sizes, plain, after)
        after = None
        for place, state, end in zip(places, states, ready):
            if end:
                done[place] = state
        places = [place for place, end in zip(places, ready) if not end]
        states = [state for state, end in zip(states, ready) if not end]
    vector = done.pop()
    shaped = [each.reshape(-1, size, 128) for each in done]
    ffn_sums, attn_sums, cross_sums = shaped[:3], shaped[3:6], shaped[6:]
    attn_grad = jnp.stack([columns_of(each) for each in attn_sums])
    cross_grad = jnp.concatenate([columns_of(each) for each in cross_sums], 1)
    ffn_in_grad = jnp.concatenate([columns_of(each[:8]) for each in ffn_sums], 1)
    ffn_out_grad = jnp.concatenate(
        [
            each[8:16].reshape(tall, 2, size, 128).transpose(0, 2, 1, 3).reshape(tall * size, -1)
            for each in ffn_sums
        ],
        1,
    )
    proj_grad = columns_of(ffn_sums[0][16:])
    vectors = []
    start = 0
    for array, cols in zip(rows, (width,) * 4 + (ffn_in.shape[2],) * 2 + (projections.shape[2],) * 2):
        piece = vector[start : start + array.shape[0]]
        vectors.append(piece.reshape(-1, cols))
        start += array.shape[0]
    selfs, crosses, queries, texts = vectors[:4]
    gain_grad = jnp.stack([selfs[0], queries[3], queries[0], texts[0]])
    bias_grad = jnp.concatenate(
        [
            selfs[2:5],
            crosses[0:3],
            queries[2:3],
            texts[2:3],
            selfs[1:2],
            queries[4:5],
            queries[1:2],
            texts[1:2],
        ],
        0,
    )

    def mine(array):
        mats, cols = array.shape[0] // sizes["rep"], array.shape[1] // sizes["dp"]
        starts = (lax.axis_index("rep") * mats, lax.axis_index("dp") * cols)
        return lax.dynamic_slice(array, starts, (mats, cols))

    small = [
        mine(gain_grad),
        mine(bias_grad),
        mine(jnp.concatenate(vectors[4:6], 0)),
        mine(jnp.concatenate(vectors[6:8], 0)),
    ]
    return (
        layer_out,
        row_loss,
        input_grad.reshape(hidden_states.shape),
        attn_grad,
        cross_grad[None],
        ffn_in_grad[None],
        ffn_out_grad[None],
        proj_grad[None],
        small[0],
        small[1],
        small[2],
        small[3],
    )


def solution(mesh):
    placed = (
        P(("dp", "rep"), None, None),
        P(("dp", "rep"), None, None),
        P(("dp", "rep"), None),
        P(),
        P(),
        P(),
        P(),
        P(),
        P(),
        P(),
        P(),
        P(),
        P(("dp", "rep"), None, None),
    )
    sizes = dict(mesh.shape)
    return jax.shard_map(
        functools.partial(shards, sizes=sizes),
        mesh=mesh,
        in_specs=placed,
        out_specs=(
            P(("dp", "rep"), None, None),
            P(("dp", "rep")),
            P(("dp", "rep"), None, None),
            P("rep", "dp", None),
            P("rep", "dp", None),
            P("rep", "dp", None),
            P("rep", "dp", None),
            P("rep", "dp", None),
            P("rep", "dp"),
            P("rep", "dp"),
            P("rep", "dp"),
            P("rep", "dp"),
        ),
        check_vma=False,
    )
```

```python
import functools

import jax
import jax.numpy as jnp
from jax import lax
from jax.experimental import pallas as pl
from jax.experimental.pallas import tpu as pltpu
from jax.sharding import PartitionSpec as P

HEADS = 12
QUERIES = 32
TEXT = 32
SLOTS = QUERIES + TEXT


blocked = -1000000000.0
epsilon = 1e-06
sharpness = 14.0
loss_weight = 16.0


def unit_rows(values):
    return values * lax.rsqrt(jnp.sum(values * values, -1, keepdims=True) + epsilon)


def unit_back(values, grad_rows):
    unused, pullback = jax.vjp(unit_rows, values)
    return pullback(grad_rows)[0]


def caption_layout(length_rows):
    row_count = length_rows.shape[0]
    first_len = length_rows[:, 0:1]
    second_end = first_len + length_rows[:, 1:2]
    slot_index = lax.broadcasted_iota(jnp.int32, (row_count, TEXT), 1)
    text_group = (slot_index >= first_len).astype(jnp.int32) + (slot_index >= second_end).astype(
        jnp.int32
    )
    group_ids = jnp.concatenate([jnp.full((row_count, QUERIES), -1, jnp.int32), text_group], 1)
    allowed = group_ids[:, :, None] == group_ids[:, None, :]
    head_starts = jnp.concatenate([jnp.zeros_like(first_len), first_len], 1)
    pick_mask = slot_index[:, None, :] == head_starts[:, :, None]
    return (allowed, pick_mask)


f32 = jnp.float32
bf16 = jnp.bfloat16
ROOT_HALF = 0.7071067811865476
ROOT_TAU = 0.3989422804014327
MIB = 1024 * 1024


def dot_nn(a, b):
    return lax.dot_general(a, b, (((1,), (0,)), ((), ())), preferred_element_type=f32)


def dot_nt(a, b):
    return lax.dot_general(a, b, (((1,), (1,)), ((), ())), preferred_element_type=f32)


def dot_tn(a, b):
    return lax.dot_general(a, b, (((0,), (0,)), ((), ())), preferred_element_type=f32)


def whole(shape):
    return pl.BlockSpec(shape, lambda *_: (0,) * len(shape))


def held(shape, index):
    return pl.BlockSpec(shape, index, pipeline_mode=pl.Buffered(1))


def cost(micros):
    return pl.CostEstimate(flops=int(micros * 1.1e9), bytes_accessed=0, transcendentals=0)


def put_row(ref, place, row, add=False):
    units = row.shape[1] // 128
    for unit in range(units):
        at = slice(place * units + unit, place * units + unit + 1)
        piece = row[:, unit * 128 : (unit + 1) * 128]
        ref[at] = ref[at] + piece if add else piece


def store_units(ref, values):
    for place in range(values.shape[1] // 128):
        ref[place] = values[:, place * 128 : (place + 1) * 128].astype(ref.dtype)


def ordered(kernel, inputs, count):
    def run(*refs):
        kernel(*refs[:inputs], *refs[inputs + count :])

    return run


def unread(count):
    return [pl.BlockSpec(memory_space=pltpu.HBM)] * count


def params(mib):
    return pltpu.CompilerParams(vmem_limit_bytes=mib * MIB, dimension_semantics=("arbitrary",))


def norm_parts(values):
    center = values - jnp.mean(values, -1, keepdims=True)
    scale = lax.rsqrt(jnp.mean(center * center, -1, keepdims=True) + epsilon)
    return center * scale, scale


def norm_grads(values, gain_row, grad):
    unit, scale = norm_parts(values)
    inner = grad * gain_row
    first = jnp.mean(inner, -1, keepdims=True)
    second = jnp.mean(inner * unit, -1, keepdims=True)
    return (
        scale * (inner - first - unit * second),
        jnp.sum(grad * unit, 0, keepdims=True),
        jnp.sum(grad, 0, keepdims=True),
    )


def gate_parts(u):
    size = jnp.abs(u) * ROOT_HALF
    t = 1.0 / (1.0 + 0.3275911 * size)
    bell = jnp.exp(-size * size)
    poly = t * (
        0.127414796
        + t * (-0.142248368 + t * (0.7107068705 + t * (-0.7265760135 + t * 0.5307027145)))
    )
    tail = poly * bell
    cdf = jnp.where(u > 0, 1.0 - tail, tail)
    return u * cdf, cdf + (ROOT_TAU * u) * bell


def half_lanes(rows):
    low = (lax.broadcasted_iota(jnp.int32, (rows, 128), 1) < 64).astype(f32)
    return low.astype(bf16), (1.0 - low).astype(bf16)


def spread_heads(x, low, high):
    left, right = x[:, :128], x[:, 128:]
    none = jnp.zeros_like(left)
    return jnp.concatenate(
        [
            jnp.concatenate([left * low, none], 1),
            jnp.concatenate([left * high, none], 1),
            jnp.concatenate([none, right * low], 1),
            jnp.concatenate([none, right * high], 1),
        ],
        0,
    )


def collect_heads(o, n):
    low = lax.broadcasted_iota(jnp.int32, (n, 128), 1) < 64
    left = jnp.where(low, o[:n, :128], o[n : 2 * n, :128])
    right = jnp.where(low, o[2 * n : 3 * n, 128:], o[3 * n :, 128:])
    return jnp.concatenate([left, right], 1)


def columns_softmax(scores):
    raised = jnp.exp(scores - jnp.max(scores, 0, keepdims=True))
    return raised * (1.0 / jnp.sum(raised, 0, keepdims=True))


GROUPS = HEADS // 4
SELF_ROWS = 4
CROSS_ROWS = 4
SELF_BACK_ROWS = 4
CROSS_BACK_ROWS = 4


def self_forward_kernel(
    x_ref, w_ref, bias_ref, gain_ref, mask_ref, q_ref, k_ref, v_ref, mix_ref, sum_ref, norm_ref
):
    x = x_ref[...]
    q_ref[...] = (dot_nn(x, w_ref[0]) + bias_ref[0:1]).astype(bf16)
    k_ref[...] = dot_nn(x, w_ref[1]).astype(bf16)
    v_ref[...] = (dot_nn(x, w_ref[2]) + bias_ref[1:2]).astype(bf16)
    low, high = half_lanes(SLOTS)

    def some_rows(step, carry):
        spots = []
        for near in range(SELF_ROWS):
            r = step * SELF_ROWS + near
            rows = pl.ds(pl.multiple_of(r * SLOTS, SLOTS), SLOTS)
            spots += [(r, rows, slice(g * 256, (g + 1) * 256)) for g in range(GROUPS)]
        scores = [
            dot_nt(
                k_ref[rows, cols], spread_heads(q_ref[rows, cols] * bf16(0.125), low, high)
            )
            for r, rows, cols in spots
        ]
        probs = [
            columns_softmax(jnp.where(mask_ref[r] > 0.0, score, blocked)).astype(bf16)
            for (r, rows, cols), score in zip(spots, scores)
        ]
        mixed = [dot_tn(prob, v_ref[rows, cols]) for (r, rows, cols), prob in zip(spots, probs)]
        for (r, rows, cols), mix in zip(spots, mixed):
            mix_ref[rows, cols] = collect_heads(mix, SLOTS).astype(bf16)
        return carry

    lax.fori_loop(0, x_ref.shape[0] // (SELF_ROWS * SLOTS), some_rows, 0)
    total = x.astype(f32) + dot_nn(mix_ref[...], w_ref[3]) + bias_ref[2:3]
    sum_ref[...] = total
    unit, _ = norm_parts(total)
    norm_ref[...] = unit * gain_ref[0:1] + bias_ref[8:9]


def self_forward(x, weights, biases, gains, mask):
    tokens, width = x.shape
    step = 4 * SLOTS
    tile = pl.BlockSpec((step, width), lambda i: (i, 0))
    low, full = jax.ShapeDtypeStruct(x.shape, bf16), jax.ShapeDtypeStruct(x.shape, f32)
    return pl.pallas_call(
        self_forward_kernel,
        grid=(tokens // step,),
        in_specs=[
            tile,
            held((4, width, width), lambda i: (0, 0, 0)),
            whole(biases.shape),
            whole(gains.shape),
            pl.BlockSpec((4,) + mask.shape[1:], lambda i: (i, 0, 0)),
        ],
        out_specs=[tile] * 6,
        out_shape=[low, low, low, low, full, full],
        compiler_params=params(58),
        name="self_forward",
        cost_estimate=cost(15),
    )(x, weights, biases, gains, mask)


def self_backward_kernel(
    w_ref,
    gain_ref,
    mask_ref,
    q_ref,
    k_ref,
    v_ref,
    sum_ref,
    top_ref,
    low_ref,
    grad_ref,
    branch_ref,
    down_ref,
    side_ref,
    dmix_all,
):
    step = pl.program_id(0)
    count = sum_ref.shape[0]
    low, high = half_lanes(SLOTS)

    @pl.when(step == 0)
    def _():
        side_ref[...] = jnp.zeros_like(side_ref)

    grad = jnp.concatenate([top_ref[...], low_ref[...]], 1).reshape(count, -1)
    down, dgain, dshift = norm_grads(sum_ref[...], gain_ref[0:1], grad)
    branch = down.astype(bf16)
    down_ref[...] = down
    branch_ref[...] = branch
    dmix_all[...] = dot_nt(branch, w_ref[0]).astype(bf16)

    def some_rows(step, carry):
        spots = []
        for near in range(SELF_BACK_ROWS):
            r = step * SELF_BACK_ROWS + near
            rows = pl.ds(pl.multiple_of(r * SLOTS, SLOTS), SLOTS)
            spots += [(r, rows, slice(g * 256, (g + 1) * 256)) for g in range(GROUPS)]
        queries = [
            spread_heads(q_ref[rows, cols] * bf16(0.125), low, high) for r, rows, cols in spots
        ]
        outs = [spread_heads(dmix_all[rows, cols], low, high) for r, rows, cols in spots]
        scores = [dot_nt(k_ref[spot[1:]], turned) for spot, turned in zip(spots, queries)]
        dprobs = [dot_nt(v_ref[spot[1:]], turned) for spot, turned in zip(spots, outs)]
        probs = [
            columns_softmax(jnp.where(mask_ref[spot[0]] > 0.0, score, blocked))
            for spot, score in zip(spots, scores)
        ]
        for spot, prob, turned in zip(spots, probs, outs):
            grad_ref[(2,) + spot[1:]] = dot_nn(prob.astype(bf16), turned).astype(bf16)
        dscores = [
            (prob * (dprob - jnp.sum(dprob * prob, 0, keepdims=True))).astype(bf16)
            for prob, dprob in zip(probs, dprobs)
        ]
        for spot, dscore, turned in zip(spots, dscores, queries):
            grad_ref[(1,) + spot[1:]] = dot_nn(dscore, turned).astype(bf16)
        dqs = [dot_tn(dscore, k_ref[spot[1:]]) for spot, dscore in zip(spots, dscores)]
        for spot, dq in zip(spots, dqs):
            grad_ref[(0,) + spot[1:]] = (collect_heads(dq, SLOTS) * 0.125).astype(bf16)
        return carry

    lax.fori_loop(0, count // (SELF_BACK_ROWS * SLOTS), some_rows, 0)
    put_row(side_ref, 0, dgain, True)
    put_row(side_ref, 1, dshift, True)
    for place, rows in enumerate((grad_ref[0], grad_ref[2], branch)):
        put_row(side_ref, 2 + place, jnp.sum(rows.astype(f32), 0, keepdims=True), True)


def self_backward(weights, gains, mask, q, k, v, total, top, text, order):
    tokens, width = q.shape
    count = 4 * SLOTS
    tile = pl.BlockSpec((count, width), lambda i: (i, 0))
    part = pl.BlockSpec((4, QUERIES, width), lambda i: (i, 0, 0))
    return pl.pallas_call(
        ordered(self_backward_kernel, 9, len(order)),
        grid=(tokens // count,),
        in_specs=[
            held((1, width, width), lambda i: (3, 0, 0)),
            whole(gains.shape),
            pl.BlockSpec((4,) + mask.shape[1:], lambda i: (i, 0, 0)),
            tile,
            tile,
            tile,
            tile,
            part,
            part,
        ]
        + unread(len(order)),
        out_specs=[
            pl.BlockSpec((3, count, width), lambda i: (0, i, 0)),
            tile,
            tile,
            whole((width // 16, 128)),
        ],
        out_shape=[
            jax.ShapeDtypeStruct((3, tokens, width), bf16),
            jax.ShapeDtypeStruct((tokens, width), bf16),
            jax.ShapeDtypeStruct((tokens, width), f32),
            jax.ShapeDtypeStruct((width // 16, 128), f32),
        ],
        scratch_shapes=[pltpu.VMEM((count, width), bf16)],
        compiler_params=params(58),
        name="self_backward",
        cost_estimate=cost(16),
    )(weights, gains, mask, q, k, v, total, top, text, *order)


def input_grad_kernel(w_ref, grad_ref, down_ref, dx_ref):
    dx_ref[...] = (
        down_ref[...]
        + dot_nt(grad_ref[0], w_ref[0])
        + dot_nt(grad_ref[1], w_ref[1])
        + dot_nt(grad_ref[2], w_ref[2])
    )


def input_gradient(weights, grads, down, order, first, last, prior=()):
    tokens, width = down.shape
    count = 4 * SLOTS
    tile = pl.BlockSpec((count, width), lambda i: (first + i, 0))
    order = list(prior) + list(order)
    return pl.pallas_call(
        ordered(input_grad_kernel, 3, len(order)),
        grid=(last - first,),
        in_specs=[
            held((3, width, width), lambda i: (0, 0, 0)),
            pl.BlockSpec((3, count, width), lambda i: (0, first + i, 0)),
            tile,
        ]
        + unread(len(order)),
        out_specs=tile,
        out_shape=jax.ShapeDtypeStruct((tokens, width), f32),
        input_output_aliases={3: 0} if prior else {},
        compiler_params=params(58),
        name="input_gradient",
        cost_estimate=cost(5),
    )(weights, grads, down, *order)


def place_of(order, row_block, rep):
    return tuple(rep if axis == "rep" else (row_block >> bit) & 1 for axis, bit in order)


def slab_shape(order, units, rows):
    return (2,) * (len(order) - 1) + (units, rows, 128)


def store_halves(core_ref, keep_ref, send_ref, pieces):
    for core in range(2):

        @pl.when(core_ref[0] == core)
        def _():
            for places, block in pieces:
                ref = keep_ref if places[0] == core else send_ref
                ref[places[1:]] = block


core_spec = pl.BlockSpec(memory_space=pltpu.SMEM)


def attn_weight_kernel(folds, core_ref, left_ref, right_ref, *rest):
    step = pl.program_id(0)
    outs = rest[6:]
    width = right_ref.shape[-1]
    for part in range(3):

        @pl.when(step == part)
        def _():
            pieces = []
            pairs = ((left_ref, right_ref), rest[2 * part : 2 * part + 2])
            for rep, (left, right) in enumerate(pairs):
                lhs = left[...].reshape(-1, width).astype(bf16)
                rhs = right[...].reshape(-1, width).astype(bf16)
                grad = dot_tn(lhs, rhs).astype(bf16)
                if folds is None:
                    store_units(outs[part].at[rep], grad)
                    continue
                rows = outs[0].shape[-2]
                for block in range(width // rows):
                    spot = place_of(folds[part], block, rep)
                    for unit in range(width // 128):
                        piece = grad[
                            block * rows : (block + 1) * rows, unit * 128 : (unit + 1) * 128
                        ]
                        pieces.append((spot + (unit,), piece))
            if folds is not None:
                store_halves(core_ref, *outs[2 * part : 2 * part + 2], pieces)


def attn_weight_grad(core, left, grads, others, folds, rows, order):
    tokens, width = left.shape
    if folds is None:
        shapes = [(2, width // 128, width, 128)] * 3
    else:
        shapes = [slab_shape(fold, width // 128, rows) for fold in folds for half in range(2)]
    return pl.pallas_call(
        ordered(functools.partial(attn_weight_kernel, folds), 9, len(order)),
        grid=(3,),
        in_specs=[
            core_spec,
            held(left.shape, lambda i: (0, 0)),
            pl.BlockSpec((1, tokens, width), lambda i: (i, 0, 0)),
        ]
        + [held(block, lambda i, zeros=(0,) * len(block): zeros) for _, block in others]
        + unread(len(order)),
        out_specs=[held(shape, lambda i, zeros=(0,) * len(shape): zeros) for shape in shapes],
        out_shape=[jax.ShapeDtypeStruct(shape, bf16) for shape in shapes],
        compiler_params=params(58),
        name="attn_weight_grad",
        cost_estimate=cost(20),
    )(core, left, grads, *(array for array, _ in others), *order)


TAIL = 16


def hide_ends(scores, main):
    end = scores[main:]
    shown = lax.broadcasted_iota(jnp.int32, end.shape, 0) < 1
    return jnp.concatenate([scores[:main], jnp.where(shown, end, blocked)], 0)


def cross_forward_kernel(
    image_ref,
    end_ref,
    kv_ref,
    w_ref,
    bias_ref,
    gain_ref,
    norm_ref,
    key_ref,
    value_ref,
    key_end_ref,
    value_end_ref,
    q_ref,
    mix_ref,
    sum_ref,
    out_ref,
):
    rows_here = image_ref.shape[0]
    main = image_ref.shape[1] - 1
    width = norm_ref.shape[-1]
    end = end_ref[...].reshape(rows_here * TAIL, -1)
    key_end_ref[...] = dot_nt(end, kv_ref[0]).astype(bf16)
    value_end_ref[...] = (dot_nt(end, kv_ref[1]) + bias_ref[4:5]).astype(bf16)
    residual = norm_ref[...].reshape(rows_here * QUERIES, width)
    q_ref[...] = (dot_nn(residual.astype(bf16), w_ref[0]) + bias_ref[3:4]).astype(bf16)
    low, high = half_lanes(QUERIES)
    tokens = image_ref[:, :main].reshape(rows_here * main, -1)
    key_ref[...] = dot_nt(tokens, kv_ref[0]).astype(bf16)
    value_ref[...] = (dot_nt(tokens, kv_ref[1]) + bias_ref[4:5]).astype(bf16)

    def some_rows(step, carry):
        spots = []
        for near in range(CROSS_ROWS):
            r = step * CROSS_ROWS + near
            span = pl.ds(pl.multiple_of(r * main, main), main)
            last = pl.ds(pl.multiple_of(r * TAIL, TAIL), TAIL)
            mine = pl.ds(pl.multiple_of(r * QUERIES, QUERIES), QUERIES)
            spots += [(span, last, mine, slice(g * 256, (g + 1) * 256)) for g in range(GROUPS)]
        scores = [
            dot_nt(
                jnp.concatenate([key_ref[span, cols], key_end_ref[last, cols]], 0),
                spread_heads(q_ref[mine, cols] * bf16(0.125), low, high),
            )
            for span, last, mine, cols in spots
        ]
        probs = [columns_softmax(hide_ends(score, main)).astype(bf16) for score in scores]
        mixed = [
            dot_tn(
                prob, jnp.concatenate([value_ref[span, cols], value_end_ref[last, cols]], 0)
            )
            for (span, last, mine, cols), prob in zip(spots, probs)
        ]
        for (span, last, mine, cols), mix in zip(spots, mixed):
            mix_ref[mine, cols] = collect_heads(mix, QUERIES).astype(bf16)
        return carry

    lax.fori_loop(0, rows_here // CROSS_ROWS, some_rows, 0)
    total = residual + dot_nn(mix_ref[...], w_ref[1]) + bias_ref[5:6]
    sum_ref[...] = total
    unit, _ = norm_parts(total)
    out_ref[...] = unit * gain_ref[1:2] + bias_ref[9:10]


def cross_forward(images, ends, kv, weights, biases, gains, norm):
    rows, patches, vis = images.shape
    main = patches - 1
    width = norm.shape[-1]
    take = 4
    keys = pl.BlockSpec((take * main, width), lambda i: (i, 0))
    tails = pl.BlockSpec((take * TAIL, width), lambda i: (i, 0))
    tile = pl.BlockSpec((take * QUERIES, width), lambda i: (i, 0))

    def shape(count, dtype):
        return jax.ShapeDtypeStruct((rows * count, width), dtype)

    return pl.pallas_call(
        cross_forward_kernel,
        grid=(rows // take,),
        in_specs=[
            pl.BlockSpec((take, patches, vis), lambda i: (i, 0, 0)),
            pl.BlockSpec((take, TAIL, vis), lambda i: (i, 0, 0)),
            held(kv.shape, lambda i: (0, 0, 0)),
            held((2, width, width), lambda i: (2, 0, 0)),
            whole(biases.shape),
            whole(gains.shape),
            pl.BlockSpec((take, QUERIES, width), lambda i: (i, 0, 0)),
        ],
        out_specs=[keys, keys, tails, tails, tile, tile, tile, tile],
        out_shape=[
            shape(main, bf16),
            shape(main, bf16),
            shape(TAIL, bf16),
            shape(TAIL, bf16),
            shape(QUERIES, bf16),
            shape(QUERIES, bf16),
            shape(QUERIES, f32),
            shape(QUERIES, f32),
        ],
        compiler_params=params(58),
        name="cross_forward",
        cost_estimate=cost(38),
    )(images, ends, kv, weights, biases, gains, norm)


def cross_backward_kernel(
    w_ref,
    key_ref,
    value_ref,
    key_end_ref,
    value_end_ref,
    q_ref,
    down_ref,
    dnorm_ref,
    dkv_ref,
    dkv_end_ref,
    dq_ref,
    side_ref,
    dmix_all,
):
    step = pl.program_id(0)
    rows_here, _, width = dnorm_ref.shape
    main = key_ref.shape[0] // rows_here
    low, high = half_lanes(QUERIES)

    @pl.when(step == 0)
    def _():
        side_ref[...] = jnp.zeros_like(side_ref)

    down = down_ref[...]
    branch = down.astype(bf16)
    dmix_all[...] = dot_nt(branch, w_ref[1]).astype(bf16)

    def some_rows(step, carry):
        spots = []
        for near in range(CROSS_BACK_ROWS):
            r = step * CROSS_BACK_ROWS + near
            span = pl.ds(pl.multiple_of(r * main, main), main)
            last = pl.ds(pl.multiple_of(r * TAIL, TAIL), TAIL)
            mine = pl.ds(pl.multiple_of(r * QUERIES, QUERIES), QUERIES)
            spots += [(span, last, mine, slice(g * 256, (g + 1) * 256)) for g in range(GROUPS)]
        keys = [
            jnp.concatenate([key_ref[span, cols], key_end_ref[last, cols]], 0)
            for span, last, mine, cols in spots
        ]
        queries = [
            spread_heads(q_ref[mine, cols] * bf16(0.125), low, high)
            for span, last, mine, cols in spots
        ]
        outs = [spread_heads(dmix_all[mine, cols], low, high) for span, last, mine, cols in spots]
        scores = [dot_nt(rows, turned) for rows, turned in zip(keys, queries)]
        dprobs = [
            dot_nt(jnp.concatenate([value_ref[span, cols], value_end_ref[last, cols]], 0), turned)
            for (span, last, mine, cols), turned in zip(spots, outs)
        ]
        probs = [columns_softmax(hide_ends(score, main)) for score in scores]
        for (span, last, mine, cols), prob, turned in zip(spots, probs, outs):
            dv = dot_nn(prob.astype(bf16), turned).astype(bf16)
            dkv_ref[1, span, cols] = dv[:main]
            dkv_end_ref[1, last, cols] = dv[main:]
        dscores = [
            (prob * (dprob - jnp.sum(dprob * prob, 0, keepdims=True))).astype(bf16)
            for prob, dprob in zip(probs, dprobs)
        ]
        for (span, last, mine, cols), dscore, turned in zip(spots, dscores, queries):
            dk = dot_nn(dscore, turned).astype(bf16)
            dkv_ref[0, span, cols] = dk[:main]
            dkv_end_ref[0, last, cols] = dk[main:]
        dqs = [dot_tn(dscore, rows) for dscore, rows in zip(dscores, keys)]
        for (span, last, mine, cols), dq in zip(spots, dqs):
            dq_ref[mine, cols] = (collect_heads(dq, QUERIES) * 0.125).astype(bf16)
        return carry

    lax.fori_loop(0, rows_here // CROSS_BACK_ROWS, some_rows, 0)
    dq = dq_ref[...]
    dnorm_ref[...] = (down + dot_nt(dq, w_ref[0])).reshape(rows_here, QUERIES, width)
    put_row(side_ref, 0, jnp.sum(dq.astype(f32), 0, keepdims=True), True)
    dvalue = jnp.sum(dkv_ref[1].astype(f32), 0, keepdims=True)
    dvalue += jnp.sum(dkv_end_ref[1].astype(f32), 0, keepdims=True)
    put_row(side_ref, 1, dvalue, True)
    put_row(side_ref, 2, jnp.sum(branch.astype(f32), 0, keepdims=True), True)


def cross_backward(rows, weights, keys, values, key_ends, value_ends, q, down, order):
    width = q.shape[1]
    main = keys.shape[0] // rows
    take = 4
    span = pl.BlockSpec((take * main, width), lambda i: (i, 0))
    tails = pl.BlockSpec((take * TAIL, width), lambda i: (i, 0))
    tile = pl.BlockSpec((take * QUERIES, width), lambda i: (i, 0))
    return pl.pallas_call(
        ordered(cross_backward_kernel, 7, len(order)),
        grid=(rows // take,),
        in_specs=[
            held((2, width, width), lambda i: (2, 0, 0)),
            span,
            span,
            tails,
            tails,
            tile,
            tile,
        ]
        + unread(len(order)),
        out_specs=[
            pl.BlockSpec((take, QUERIES, width), lambda i: (i, 0, 0)),
            pl.BlockSpec((2, take * main, width), lambda i: (0, i, 0)),
            pl.BlockSpec((2, take * TAIL, width), lambda i: (0, i, 0)),
            tile,
            whole((width // 16, 128)),
        ],
        out_shape=[
            jax.ShapeDtypeStruct((rows, QUERIES, width), f32),
            jax.ShapeDtypeStruct((2, rows * main, width), bf16),
            jax.ShapeDtypeStruct((2, rows * TAIL, width), bf16),
            jax.ShapeDtypeStruct((rows * QUERIES, width), bf16),
            jax.ShapeDtypeStruct((width // 16, 128), f32),
        ],
        scratch_shapes=[pltpu.VMEM((take * QUERIES, width), bf16)],
        compiler_params=params(58),
        name="cross_backward",
        cost_estimate=cost(19),
    )(weights, keys, values, key_ends, value_ends, q, down, *order)


def third_units(units):
    edges = [(units * k + 2) // 3 for k in range(4)]
    return [edges[k + 1] - edges[k] for k in range(3)]


def cross_weight_kernel(folds, core_ref, image_ref, end_ref, grad_ref, grad_end_ref, *rest):
    outs, gathered = rest[:-1], rest[-1]
    rows, patches, vis = image_ref.shape
    main = patches - 1
    take = 4
    gathered[...] = dot_tn(grad_end_ref[0], end_ref[...].reshape(rows * TAIL, vis))

    def add_rows(i, carry):
        span = pl.ds(pl.multiple_of(i * take * main, take * main), take * main)
        tokens = image_ref[pl.ds(i * take, take), :main].reshape(take * main, vis)
        gathered[...] += dot_tn(grad_ref[0, span], tokens)
        return carry

    lax.fori_loop(0, rows // take, add_rows, 0)
    if folds is None:
        store_units(outs[0].at[0], gathered[...])
        return
    first = 0
    for part, fold in enumerate(folds):
        keep, send = outs[2 * part : 2 * part + 2]
        units, size = keep.shape[-3:-1]
        pieces = []
        for block in range(gathered.shape[0] // size):
            spot = tuple(
                0 if axis == "rep" or bit == 3 else (block >> bit) & 1 for axis, bit in fold
            )
            piece = gathered[block * size : (block + 1) * size].astype(bf16)
            for unit in range(units):
                at = (first + unit) * 128
                pieces.append((spot + (unit,), piece[:, at : at + 128]))
        store_halves(core_ref, keep, send, pieces)
        first += units


def cross_weight_grad(core, images, ends, grads, grads_end, folds, size, order):
    rows, patches, vis = images.shape
    width = grads.shape[2]
    half = width // 2
    units = vis // 128
    if folds is None:
        specs = [pl.BlockSpec((1, units, half, 128), lambda m, h: (m, 0, h, 0))]
        shapes = [(2, units, width, 128)]
    else:
        specs, shapes = [], []
        for fold, count in zip(folds, third_units(units) if len(folds) == 3 else [units]):
            block = tuple(1 if axis == "rep" or bit == 3 else 2 for axis, bit in fold[1:])

            def index(m, h, fold=fold):
                spot = tuple(
                    m if axis == "rep" else h if bit == 3 else 0 for axis, bit in fold[1:]
                )
                return spot + (0, 0, 0)

            specs += [pl.BlockSpec(block + (count, size, 128), index)] * 2
            shapes += [slab_shape(fold, count, size)] * 2
    return pl.pallas_call(
        ordered(functools.partial(cross_weight_kernel, folds), 5, len(order)),
        grid=(2, 2),
        in_specs=[
            core_spec,
            held(images.shape, lambda m, h: (0, 0, 0)),
            held(ends.shape, lambda m, h: (0, 0, 0)),
            pl.BlockSpec((1, grads.shape[1], half), lambda m, h: (m, 0, h)),
            pl.BlockSpec((1, grads_end.shape[1], half), lambda m, h: (m, 0, h)),
        ]
        + unread(len(order)),
        out_specs=specs,
        out_shape=[jax.ShapeDtypeStruct(shape, bf16) for shape in shapes],
        scratch_shapes=[pltpu.VMEM((half, vis), f32)],
        compiler_params=pltpu.CompilerParams(
            vmem_limit_bytes=58 * MIB, dimension_semantics=("arbitrary", "arbitrary")
        ),
        name="cross_weight_grad",
        cost_estimate=cost(32),
    )(core, images, ends, grads, grads_end, *order)


def ffn_forward_kernel(
    which,
    norm_ref,
    in_ref,
    in_bias_ref,
    out_ref,
    proj_ref,
    proj_bias_ref,
    bias_ref,
    gain_ref,
    *rest,
):
    act_ref, slope_ref, sum_ref, low_ref, raw_ref, embed_ref, rows_low = rest[-7:]
    step = pl.program_id(0)
    tokens, width = sum_ref.shape

    @pl.when(step == 0)
    def _():
        full = norm_ref[...].reshape(tokens, width)
        rows_low[...] = full.astype(bf16)
        sum_ref[...] = full + bias_ref[6 + which : 7 + which]

    low = rows_low[...]
    wide = 256
    pieces = act_ref.shape[1] // wide

    def before_gate(k):
        cols = slice(k * wide, (k + 1) * wide)
        return dot_nn(low, in_ref[0, :, cols]) + in_bias_ref[which : which + 1, cols]

    ahead = [before_gate(k) for k in range(2)]
    gathered = 0.0
    for k in range(pieces):
        if k + 2 < pieces:
            ahead.append(before_gate(k + 2))
        cols = slice(k * wide, (k + 1) * wide)
        act, slope = gate_parts(ahead[k])
        act = act.astype(bf16)
        act_ref[:, cols] = act
        slope_ref[:, cols] = slope.astype(bf16)
        gathered += dot_nn(act, out_ref[0, cols])
    sum_ref[...] += gathered

    @pl.when(step == pl.num_programs(0) - 1)
    def _():
        unit, _ = norm_parts(sum_ref[...])
        low = (unit * gain_ref[2 + which : 3 + which] + bias_ref[10 + which : 11 + which]).astype(bf16)
        low_ref[...] = low.reshape(low_ref.shape)
        raw = dot_nn(low, proj_ref[0]) + proj_bias_ref[which : which + 1]
        raw_ref[...] = raw
        size = lax.rsqrt(jnp.sum(raw * raw, -1, keepdims=True) + epsilon)
        embed_ref[...] = (raw * size).astype(bf16)


def ffn_forward(which, part, norm, ffn_in, ffn_bias, ffn_out, projections, proj_bias, biases, gains, layer, order=()):
    rows, width = norm.shape[0], norm.shape[-1]
    tokens = rows * QUERIES
    hidden = ffn_in.shape[2]
    embed = projections.shape[2]
    chunk = 1024
    cols = pl.BlockSpec((tokens, chunk), lambda j: (0, j))
    halves = [] if layer is None else [layer]
    return pl.pallas_call(
        functools.partial(ffn_forward_kernel, which),
        grid=(hidden // chunk,),
        in_specs=[
            held((rows, QUERIES, width), lambda j: (0, part, 0)),
            pl.BlockSpec((1, width, chunk), lambda j: (which, 0, j)),
            pl.BlockSpec((2, chunk), lambda j: (0, j)),
            pl.BlockSpec((1, chunk, width), lambda j: (which, j, 0)),
            held((1, width, embed), lambda j: (which, 0, 0)),
            whole(proj_bias.shape),
            whole(biases.shape),
            whole(gains.shape),
        ]
        + unread(len(halves) + len(order)),
        out_specs=[
            cols,
            cols,
            whole((tokens, width)),
            pl.BlockSpec((rows, QUERIES, width), lambda j: (0, which, 0)),
            whole((tokens, embed)),
            whole((tokens, embed)),
        ],
        out_shape=[
            jax.ShapeDtypeStruct((tokens, hidden), bf16),
            jax.ShapeDtypeStruct((tokens, hidden), bf16),
            jax.ShapeDtypeStruct((tokens, width), f32),
            jax.ShapeDtypeStruct((rows, SLOTS, width), bf16),
            jax.ShapeDtypeStruct((tokens, embed), f32),
            jax.ShapeDtypeStruct((tokens, embed), bf16),
        ],
        scratch_shapes=[pltpu.VMEM((tokens, width), bf16)],
        input_output_aliases={8: 3} if halves else {},
        compiler_params=params(58),
        name="ffn_forward",
        cost_estimate=cost(15),
    )(norm, ffn_in, ffn_bias, ffn_out, projections, proj_bias, biases, gains, *halves, *order)


def ffn_backward_kernel(
    which,
    folds,
    core_ref,
    norm_ref,
    sum_ref,
    before_ref,
    layer_ref,
    grad_ref,
    raw_ref,
    proj_ref,
    gain_ref,
    in_ref,
    out_ref,
    act_ref,
    slope_ref,
    *rest,
):
    count = 3 if folds is None else 6
    down_ref, side_ref, dbias_ref, dproj_bias_ref = rest[-8 - count : -4 - count]
    weight_refs = rest[-4 - count : -4]
    branch_all, low_turned, left, dproj = rest[-4:]
    step = pl.program_id(0)
    tokens, width = sum_ref.shape

    @pl.when(step == 0)
    def _():
        raw = raw_ref[...]
        grad = grad_ref[...].reshape(tokens, width).astype(f32) + dot_nt(raw, proj_ref[0])
        down, dgain, dshift = norm_grads(sum_ref[...], gain_ref[2 + which : 3 + which], grad)
        branch = down.astype(bf16)
        branch_all[...] = branch
        left[...] = down
        side_ref[...] = jnp.zeros_like(side_ref)
        put_row(side_ref, 0, dgain)
        put_row(side_ref, 1, dshift)
        put_row(side_ref, 2, jnp.sum(branch.astype(f32), 0, keepdims=True))
        dproj[...] = dot_tn(layer_ref[...].reshape(tokens, width), raw).astype(bf16)
        put_row(dproj_bias_ref, 0, jnp.sum(raw.astype(f32), 0, keepdims=True))
        low_turned[...] = norm_ref[...].reshape(tokens, width).astype(bf16).T

    branch = branch_all[...]
    du = (dot_nt(branch, out_ref[0]) * slope_ref[...].astype(f32)).astype(bf16)
    left[...] += dot_nt(du, in_ref[0])
    put_row(dbias_ref, 0, jnp.sum(du.astype(f32), 0, keepdims=True))
    thin = width // 3
    for part in range(3):

        @pl.when(step == part)
        def _():
            din = dot_nn(low_turned[...], du).astype(bf16)
            dout = dot_tn(act_ref[...], branch[:, part * thin : (part + 1) * thin]).astype(bf16)
            if folds is None:
                store_units(weight_refs[0], din)
                store_units(weight_refs[1], dout)
                if part == 0:
                    store_units(weight_refs[2], dproj[...])
                return
            keep, send = weight_refs[2 * part : 2 * part + 2]
            size = keep.shape[-2]
            subs = dout.shape[0] // width
            pieces = []
            for block in range(width // size):
                spot = place_of(folds[part], block, 0)
                at = block * size
                found = [
                    din[at : at + size, unit * 128 : (unit + 1) * 128]
                    for unit in range(din.shape[1] // 128)
                ]
                for sub in range(subs):
                    row = at * subs + sub * size
                    for unit in range(thin // 128):
                        found.append(dout[row : row + size, unit * 128 : (unit + 1) * 128])
                if part == 0:
                    for unit in range(dproj.shape[1] // 128):
                        found.append(dproj[at : at + size, unit * 128 : (unit + 1) * 128])
                pieces += [(spot + (unit,), piece) for unit, piece in enumerate(found)]
            store_halves(core_ref, keep, send, pieces)

    @pl.when(step == pl.num_programs(0) - 1)
    def _():
        if which == 0:
            down, dgain, dshift = norm_grads(before_ref[...], gain_ref[1:2], left[...])
            put_row(side_ref, 3, dgain)
            put_row(side_ref, 4, dshift)
            down_ref[...] = down.reshape(down_ref.shape)
        else:
            down_ref[...] = left[...].reshape(down_ref.shape)


def ffn_backward(
    which,
    part,
    core,
    norm,
    total,
    before,
    layer,
    grad,
    raw,
    projections,
    gains,
    ffn_in,
    ffn_out,
    act,
    slope,
    slabs,
    folds,
    size,
):
    rows = layer.shape[0]
    tokens, width = total.shape
    hidden = ffn_in.shape[2]
    embed = projections.shape[2]
    chunk = hidden // 3
    slabs = list(slabs)
    if folds is None:
        weight_specs = [
            pl.BlockSpec((chunk // 128, width, 128), lambda j: (j, 0, 0)),
            pl.BlockSpec((width // 384, hidden, 128), lambda j: (j, 0, 0)),
            whole((embed // 128, width, 128)),
        ]
        weight_shapes = [
            (hidden // 128, width, 128),
            (width // 128, hidden, 128),
            (embed // 128, width, 128),
        ]
    else:
        units = chunk // 128 + (hidden // width) * (width // 384)
        weight_shapes = [
            slab_shape(fold, units + (embed // 128 if k == 0 else 0), size)
            for k, fold in enumerate(folds)
            for half in range(2)
        ]

        def spec(fold, shape):
            block = tuple(1 if axis == "rep" else 2 for axis, bit in fold[1:])
            spot = tuple(which if axis == "rep" else 0 for axis, bit in fold[1:])
            return held(block + shape[-3:], lambda j: spot + (0, 0, 0))

        weight_specs = [spec(folds[k // 2], shape) for k, shape in enumerate(weight_shapes)]
    return pl.pallas_call(
        functools.partial(ffn_backward_kernel, which, folds),
        grid=(3,),
        in_specs=[
            core_spec,
            held((rows, QUERIES, width), lambda j: (0, part, 0)),
            held((tokens, width), lambda j: (0, 0)),
            held(before.shape, lambda j: (0, 0)),
            held((rows, QUERIES, width), lambda j: (0, which, 0)),
            held((rows, QUERIES, width), lambda j: (0, which, 0)),
            held((tokens, embed), lambda j: (0, 0)),
            held((1, width, embed), lambda j: (which, 0, 0)),
            whole(gains.shape),
            pl.BlockSpec((1, width, chunk), lambda j: (which, 0, j)),
            pl.BlockSpec((1, chunk, width), lambda j: (which, j, 0)),
            held((tokens, hidden), lambda j: (0, 0)),
            pl.BlockSpec((tokens, chunk), lambda j: (0, j)),
        ]
        + unread(len(slabs)),
        out_specs=[
            whole((rows, QUERIES, width)),
            whole((width // 16, 128)),
            pl.BlockSpec((chunk // 128, 128), lambda j: (j, 0)),
            whole((embed // 128, 128)),
        ]
        + weight_specs,
        out_shape=[
            jax.ShapeDtypeStruct((rows, QUERIES, width), f32),
            jax.ShapeDtypeStruct((width // 16, 128), f32),
            jax.ShapeDtypeStruct((hidden // 128, 128), f32),
            jax.ShapeDtypeStruct((embed // 128, 128), f32),
        ]
        + [jax.ShapeDtypeStruct(shape, bf16) for shape in weight_shapes],
        scratch_shapes=[
            pltpu.VMEM((tokens, width), bf16),
            pltpu.VMEM((width, tokens), bf16),
            pltpu.VMEM((tokens, width), f32),
            pltpu.VMEM((width, embed), bf16),
        ],
        input_output_aliases={13 + k: 4 + k for k in range(len(slabs))},
        compiler_params=params(60),
        name="ffn_backward",
        cost_estimate=cost(25),
    )(
        core,
        norm,
        total,
        before,
        layer,
        grad,
        raw,
        projections,
        gains,
        ffn_in,
        ffn_out,
        act,
        slope,
        *slabs,
    )


def swap(values, stage, sizes):
    axis, bit = stage
    return lax.ppermute(values, axis, [(i, i ^ (1 << bit)) for i in range(sizes[axis])])


def stage_order(part, sizes):
    stages = [("dp", bit) for bit in range(sizes["dp"].bit_length() - 1)]
    ring = stages[1:3] + [("rep", 0)]
    if part == 3:
        return stages[:1] + ring[:2] + stages[3:] + ring[2:]
    return stages[:1] + ring[part:] + ring[:part] + stages[3:]


def fold_pair(part, first, second, sizes):
    depth = sizes["dp"].bit_length() - 1
    both = jnp.stack([first, second])
    units, rows = first.shape[0], first.shape[1] // sizes["dp"]
    both = both.reshape((2, units) + (2,) * depth + (rows, 128))
    front = [0 if axis == "rep" else 1 + depth - bit for axis, bit in stage_order(part, sizes)]
    return both.transpose(front + [1, 2 + depth, 3 + depth])


def own_bits(sizes):
    depth = sizes["dp"].bit_length() - 1
    shifts = jnp.arange(depth + 1, dtype=jnp.int32)
    both = lax.axis_index("dp") + (lax.axis_index("rep") << depth)
    return ((both >> shifts) & 1).astype(jnp.int32)


def bit_place(stage, sizes):
    return sizes["dp"].bit_length() - 1 if stage[0] == "rep" else stage[1]


def picked(place_bits, bits_ref):
    at = 0
    for bit, other in place_bits:
        own = bits_ref[bit]
        at = 2 * at + (1 - own if other else own)
    return at


def sum_kernel(plan, arrays, bits_ref, *refs):
    sources, refs = refs[:arrays], refs[arrays:]
    outs, refs = refs[: len(plan)], refs[len(plan) :]
    count = sum(len(terms) for jobs in plan for _, terms in jobs)
    held_terms, held_outs = refs[:count], refs[count : count + len(plan)]
    in_sems, out_sems = refs[-2:]
    fetches = []
    for jobs in plan:
        for rows, terms in jobs:
            for source, start, place_bits in terms:
                first = start + picked(place_bits, bits_ref) * rows
                here = len(fetches)
                fetches.append(
                    pltpu.make_async_copy(
                        sources[source].at[pl.ds(pl.multiple_of(first, 16), rows)],
                        held_terms[here],
                        in_sems.at[here],
                    )
                )
    for fetch in fetches:
        fetch.start()
    here = 0
    stores = []
    for place, jobs in enumerate(plan):
        at = 0
        for rows, terms in jobs:
            found = None
            for _ in terms:
                fetches[here].wait()
                part = held_terms[here][...].astype(f32)
                found = part if found is None else found + part
                here += 1
            size, cols = held_outs[place].shape
            for unit in range(cols // 128 if cols > 128 else 0):
                lanes = slice(unit * 128, (unit + 1) * 128)
                held_outs[place][:, lanes] = found[unit * size : (unit + 1) * size]
            if cols == 128:
                held_outs[place][at : at + rows] = found.astype(held_outs[place].dtype)
            at += rows
        store = pltpu.make_async_copy(held_outs[place], outs[place], out_sems.at[place])
        store.start()
        stores.append(store)
    for store in stores:
        store.wait()


def sum_jobs(outputs, bits):
    arrays, plan, buffers = [], [], []

    def number_of(array):
        for number, known in enumerate(arrays):
            if known is array:
                return number
        arrays.append(array)
        return len(arrays) - 1

    shapes, moved = [], 0
    for dtype, jobs, tall in outputs:
        planned = []
        for rows, terms in jobs:
            planned.append((rows, [(number_of(array), start, bit) for array, start, bit in terms]))
            buffers += [pltpu.VMEM((rows, 128), array.dtype) for array, _, _ in terms]
            moved += rows * (1 + len(terms))
        plan.append(planned)
        total = sum(rows for rows, _ in jobs)
        shape = (tall, total // tall * 128) if tall else (total, 128)
        shapes.append(jax.ShapeDtypeStruct(shape, dtype))
    return pl.pallas_call(
        functools.partial(sum_kernel, plan, len(arrays)),
        in_specs=[core_spec] + unread(len(arrays)),
        out_specs=unread(len(plan)),
        out_shape=shapes,
        scratch_shapes=buffers
        + [pltpu.VMEM(shape.shape, shape.dtype) for shape in shapes]
        + [pltpu.SemaphoreType.DMA((len(buffers),)), pltpu.SemaphoreType.DMA((len(plan),))],
        compiler_params=pltpu.CompilerParams(vmem_limit_bytes=121 * MIB // 2),
        name="sum_terms",
        cost_estimate=cost(3),
    )(bits, *arrays)


def sum_jobs_plain(outputs, bits):
    results = []
    for dtype, jobs, tall in outputs:
        pieces = []
        for rows, terms in jobs:
            found = [
                lax.dynamic_slice_in_dim(array, start + picked(bit, bits) * rows, rows, 0)
                for array, start, bit in terms
            ]
            pieces.append(sum(part.astype(f32) for part in found).astype(dtype))
        made = pieces[0] if len(pieces) == 1 else jnp.concatenate(pieces, 0)
        results.append(columns_of(made.reshape(-1, tall, 128)) if tall else made)
    return results


def begin(part, keep, send, sizes):
    keep, send = keep.reshape(-1, 128), send.reshape(-1, 128)
    arrived = swap(send, stage_order(part, sizes)[0], sizes)
    return (part, 1, [(keep, 0, keep.shape[0], []), (arrived, 0, send.shape[0], [])], send)


def begin_together(parts, keep, send, sizes):
    count = len(parts)
    keep, send = keep.reshape(-1, 128), send.reshape(-1, 128)
    rows = keep.shape[0] // count
    arrived = swap(send, stage_order(0, sizes)[0], sizes)
    return [
        (part, 1, [(keep, at * rows, rows, []), (arrived, at * rows, rows, [])], send)
        for at, part in enumerate(parts)
    ]


def begin_folded(part, slab, sizes):
    own = lax.axis_index("dp") & 1
    halves = [lax.dynamic_index_in_dim(slab, place, 0, keepdims=False) for place in (own, 1 - own)]
    return begin(part, *halves, sizes)


def begin_whole(values, sizes):
    send = values.astype(bf16)
    arrived = swap(send, stage_order(0, sizes)[0], sizes)
    return (None, 1, [(values, 0, len(values), []), (arrived, 0, len(values), [])], send)


def advance(states, bits, sizes, plain, tall, after=None):
    last = len(stage_order(0, sizes))
    changed = {}
    fresh = []
    for part, at, terms, sent in states:
        array = terms[-1][0]
        if after is not None:
            if id(array) not in changed:
                changed[id(array)] = (array, lax.optimization_barrier((array, after))[0])
            array = changed[id(array)][1]
        fresh.append((part, at, terms[:-1] + [(array,) + terms[-1][1:]], sent))
    groups, finals = {}, []
    for number, (part, at, terms, _) in enumerate(fresh):
        if at == last:
            finals.append(number)
        else:
            groups.setdefault(stage_order(part or 0, sizes)[at], []).append(number)

    def job(number, ahead):
        rows = fresh[number][2][0][2] >> (len(fresh[number][2][0][3]) + len(ahead))
        return (
            rows,
            [(array, start, places + ahead) for array, start, _, places in fresh[number][2]],
        )

    outputs = []
    for stage, members in groups.items():
        jobs = []
        for number in members:
            ahead = [] if fresh[number][0] is None else [(bit_place(stage, sizes), True)]
            jobs.append(job(number, ahead))
        outputs.append((bf16, jobs, 0))
    outputs += [
        (f32, [job(number, [])], 0 if fresh[number][0] is None else tall) for number in finals
    ]
    made = (sum_jobs_plain if plain else sum_jobs)(outputs, bits)
    results = [None] * len(fresh)
    for (stage, members), (_, jobs, _), sent in zip(groups.items(), outputs, made):
        arrived = swap(sent, stage, sizes)
        start = 0
        for number, (rows, _) in zip(members, jobs):
            part, at, terms, _ = fresh[number]
            kept = [] if part is None else [(bit_place(stage, sizes), False)]
            terms = [(array, first, size, places + kept) for array, first, size, places in terms]
            results[number] = (part, at + 1, terms + [(arrived, start, rows, [])], sent)
            start += rows
    for number, found in zip(finals, made[len(groups) :]):
        results[number] = found
    return results


def sends(states):
    found = []
    for state in states:
        if not any(state[3] is known for known in found):
            found.append(state[3])
    return found


def columns_of(units):
    return units.transpose(1, 0, 2).reshape(units.shape[1], -1)


def exchange(values, sizes):
    return lax.all_to_all(values, ("dp", "rep"), 0, 0, tiled=True)


def gather_rows(values, sizes):
    world = sizes["dp"] * sizes["rep"]
    return exchange(jnp.tile(values, (world, 1)), sizes)


def scatter_rows(values, sizes):
    world = sizes["dp"] * sizes["rep"]
    arrived = exchange(values, sizes)
    return jnp.sum(arrived.reshape(world, -1, values.shape[1]).astype(f32), 0)


def shards(
    hidden_states,
    image_features,
    caption_lengths,
    attn_weights,
    cross_kv,
    ffn_in,
    ffn_out,
    projections,
    norm_gains,
    biases,
    ffn_bias,
    proj_bias,
    out_grad,
    sizes,
):
    row_count, slots, width = hidden_states.shape
    captions_here = 2 * row_count
    world = sizes["dp"] * sizes["rep"]
    allowed, pick_mask = caption_layout(caption_lengths)
    pick_low = pick_mask.astype(bf16)
    pick_full = pick_mask.astype(f32)
    mask = jnp.tile(allowed, (1, 1, 4)).astype(f32)
    inputs = hidden_states.reshape(row_count * slots, width)
    self_q, self_k, self_v, self_mix, first_sum, first_norm = self_forward(
        inputs, attn_weights, biases, norm_gains, mask
    )
    first_norm = first_norm.reshape(row_count, slots, width)
    image_ends = jnp.pad(image_features[:, -1:], ((0, 0), (0, TAIL - 1), (0, 0)))
    text_act, text_slope, fourth_sum, layer_half, caption_raw, caption_all = ffn_forward(
        1,
        1,
        first_norm,
        ffn_in,
        ffn_bias,
        ffn_out,
        projections,
        proj_bias,
        biases,
        norm_gains,
        None,
        [image_ends],
    )
    caption_embed = (
        jnp.einsum(
            "rkt,rtd->rkd",
            pick_low,
            caption_all.reshape(row_count, TEXT, -1),
            preferred_element_type=f32,
        )
        .astype(bf16)
        .reshape(captions_here, -1)
    )
    every_caption = gather_rows(caption_embed, sizes)
    keys, values, key_ends, value_ends, cross_q, cross_mix, second_sum, second_norm = cross_forward(
        image_features, image_ends, cross_kv, attn_weights, biases, norm_gains, first_norm
    )
    second_norm = second_norm.reshape(row_count, QUERIES, width)
    query_act, query_slope, third_sum, layer_out, query_raw, query_embed = ffn_forward(
        0,
        0,
        second_norm,
        ffn_in,
        ffn_bias,
        ffn_out,
        projections,
        proj_bias,
        biases,
        norm_gains,
        layer_half,
    )
    query_raw = query_raw.reshape(row_count, QUERIES, -1)
    query_embed = query_embed.reshape(row_count, QUERIES, -1)
    sims = jnp.einsum("rqp,cp->rqc", query_embed, every_caption, preferred_element_type=f32)
    expo = jnp.exp(sharpness * (sims - 1.0))
    affinity = jnp.mean(expo, 1)
    offset = lax.axis_index(("dp", "rep")) * captions_here
    own_block = lax.dynamic_slice_in_dim(affinity, offset, captions_here, 1).reshape(
        row_count, row_count, 2
    )
    diagonal = (
        lax.broadcasted_iota(jnp.int32, (row_count, row_count), 0)
        == lax.broadcasted_iota(jnp.int32, (row_count, row_count), 1)
    ).astype(f32)
    positive = jnp.sum(own_block * diagonal[:, :, None], 1)
    row_total = jnp.sum(affinity, 1)
    partial_cols = jnp.sum(affinity, 0)
    all_cols = jnp.sum(
        exchange(jnp.broadcast_to(partial_cols[None], (world,) + partial_cols.shape), sizes), 0
    )
    own_cols = lax.dynamic_slice_in_dim(all_cols, offset, captions_here, 0).reshape(row_count, 2)
    inverse_all = 1.0 / all_cols
    row_loss = (
        jnp.log(row_total)
        - jnp.log(positive[:, 0])
        + jnp.sum(jnp.log(own_cols) - jnp.log(positive), 1)
    )
    grad_affinity = loss_weight * (1.0 / row_total[:, None] + inverse_all[None, :])
    pair_weight = jnp.array([2.0, 1.0], f32)
    correction = (loss_weight * diagonal[:, :, None] * pair_weight / own_block).reshape(
        row_count, captions_here
    )
    own_grad = lax.dynamic_slice_in_dim(grad_affinity, offset, captions_here, 1) - correction
    grad_affinity = lax.dynamic_update_slice_in_dim(grad_affinity, own_grad, offset, 1)
    grad_sims = (grad_affinity[:, None, :] * expo * (sharpness / QUERIES)).astype(bf16)
    grad_query_embed = jnp.einsum(
        "rqc,cp->rqp", grad_sims, every_caption, preferred_element_type=f32
    )
    grad_caption_embed = scatter_rows(
        jnp.einsum("rqc,rqp->cp", grad_sims, query_embed, preferred_element_type=f32).astype(bf16),
        sizes,
    )
    query_raw_grad = unit_back(query_raw, grad_query_embed).astype(bf16)
    head_raw = jnp.sum(
        pick_full[:, :, :, None] * caption_raw.reshape(row_count, 1, TEXT, -1), 2
    )
    head_raw_grad = unit_back(head_raw, grad_caption_embed.reshape(row_count, 2, -1)).astype(bf16)
    caption_raw_grad = jnp.einsum(
        "rkt,rkd->rtd", pick_low, head_raw_grad, preferred_element_type=f32
    ).astype(bf16)
    fold = sizes["dp"] == 16 and sizes["rep"] == 2
    stage_orders = [stage_order(part, sizes) for part in range(3)]
    folds = stage_orders if fold else None
    ffn_parts = (3, 1, 2)
    ffn_folds = [stage_order(part, sizes) for part in ffn_parts] if fold else None
    size = width // sizes["dp"]
    bits = own_bits(sizes)
    core = bits[:1]
    grad_second, query_side, query_dbias, query_dproj_bias, *query_slabs = ffn_backward(
        0,
        0,
        core,
        second_norm,
        third_sum,
        second_sum,
        layer_out,
        out_grad,
        query_raw_grad.reshape(row_count * QUERIES, -1),
        projections,
        norm_gains,
        ffn_in,
        ffn_out,
        query_act,
        query_slope,
        (),
        ffn_folds,
        size,
    )
    text_first, text_side, text_dbias, text_dproj_bias, *text_slabs = ffn_backward(
        1,
        1,
        core,
        first_norm,
        fourth_sum,
        fourth_sum,
        layer_out,
        out_grad,
        caption_raw_grad.reshape(row_count * TEXT, -1),
        projections,
        norm_gains,
        ffn_in,
        ffn_out,
        text_act,
        text_slope,
        query_slabs if fold else (),
        ffn_folds,
        size,
    )
    tall = ffn_out.shape[1] // width
    if not fold:
        text_slabs = [
            fold_pair(
                ffn_parts[part],
                *(
                    jnp.concatenate(
                        [
                            din[part * 8 : part * 8 + 8],
                            dout[2 * part : 2 * part + 2]
                            .reshape(2, sizes["dp"], tall, size, 128)
                            .transpose(2, 0, 1, 3, 4)
                            .reshape(2 * tall, width, 128),
                            dproj[: 2 if part == 0 else 0],
                        ],
                        0,
                    )
                    for din, dout, dproj in (query_slabs, text_slabs)
                ),
                sizes,
            )
            for part in range(3)
        ]
    if fold:
        ffn = [
            begin(ffn_parts[part], *text_slabs[2 * part : 2 * part + 2], sizes) for part in range(3)
        ]
    else:
        ffn = [begin_folded(part, slab, sizes) for part, slab in zip(ffn_parts, text_slabs)]
    cross_down = grad_second.reshape(row_count * QUERIES, width)
    query_first, dkv, dkv_ends, cross_dq, cross_side = cross_backward(
        row_count,
        attn_weights,
        keys,
        values,
        key_ends,
        value_ends,
        cross_q,
        cross_down,
        [text_first] + sends(ffn),
    )
    plain = not fold
    ffn = advance(ffn, bits, sizes, plain, size, cross_side)
    cross_slabs = cross_weight_grad(
        core, image_features, image_ends, dkv, dkv_ends, folds, size, sends(ffn)
    )
    if fold:
        cross = [begin(part, *cross_slabs[2 * part : 2 * part + 2], sizes) for part in range(3)]
    else:
        edges = [0, 4, 8, cross_slabs[0].shape[1]]
        cross = [
            begin_folded(
                part,
                fold_pair(part, *cross_slabs[0][:, edges[part] : edges[part + 1]], sizes),
                sizes,
            )
            for part in range(3)
        ]
    ffn = advance(ffn, bits, sizes, plain, size, cross_slabs[0])
    self_grads, self_branch, self_down, self_side = self_backward(
        attn_weights,
        norm_gains,
        mask,
        self_q,
        self_k,
        self_v,
        first_sum,
        query_first,
        text_first,
        sends(ffn + cross),
    )
    rows = [
        self_side,
        cross_side,
        query_side,
        text_side,
        query_dbias,
        text_dbias,
        query_dproj_bias,
        text_dproj_bias,
    ]
    used = sum(array.shape[0] for array in rows)
    packed = jnp.concatenate(rows + [jnp.zeros((-used % 64, 128), f32)], 0)
    states = advance(ffn + cross, bits, sizes, plain, size, self_side)
    vector = begin_whole(packed, sizes)
    half = (row_count, QUERIES, width)
    attn_slabs = attn_weight_grad(
        core,
        inputs,
        self_grads,
        [
            (self_mix, self_mix.shape),
            (self_branch, self_branch.shape),
            (first_norm, half),
            (cross_dq, cross_dq.shape),
            (cross_mix, cross_mix.shape),
            (cross_down, cross_down.shape),
        ],
        folds,
        size,
        sends(states + [vector]),
    )
    if fold:
        attn = [begin(part, *attn_slabs[2 * part : 2 * part + 2], sizes) for part in range(3)]
    else:
        attn = [
            begin_folded(part, fold_pair(part, *slab, sizes), sizes)
            for part, slab in enumerate(attn_slabs)
        ]
    ffn, cross = states[:3], states[3:6]
    states = advance(ffn + cross + [vector], bits, sizes, plain, size, attn_slabs[0])
    blocks = row_count // 4
    begun = input_gradient(attn_weights, self_grads, self_down, sends(states), 0, 1)
    *attn, vector = advance(attn + states[6:], bits, sizes, plain, size, begun)
    input_grad = input_gradient(
        attn_weights, self_grads, self_down, sends(attn), 1, blocks, [begun]
    )
    states = states[:3] + attn + states[3:6] + [vector]
    last = len(stage_orders[0])
    done = [None] * len(states)
    places = list(range(len(states)))
    after = input_grad
    while len(states) > 3:
        ready = [state[1] == last for state in states]
        states = advance(states, bits, sizes, plain, size, after)
        after = None
        for place, state, end in zip(places, states, ready):
            if end:
                done[place] = state
        places = [place for place, end in zip(places, ready) if not end]
        states = [state for state, end in zip(states, ready) if not end]
    vector = done.pop()
    ffn_sums, cross_sums = done[:3], done[6:]
    cross_grad = jnp.concatenate(cross_sums, 1)
    chunk = ffn_in.shape[2] // 3
    ffn_in_grad = jnp.concatenate([each[:, :chunk] for each in ffn_sums], 1)
    ffn_out_grad = jnp.concatenate(
        [
            each[:, chunk : 2 * chunk]
            .reshape(size, tall, -1)
            .transpose(1, 0, 2)
            .reshape(tall * size, -1)
            for each in ffn_sums
        ],
        1,
    )
    proj_grad = ffn_sums[0][:, 2 * chunk :]
    vectors = []
    start = 0
    for array, cols in zip(rows, (width,) * 4 + (ffn_in.shape[2],) * 2 + (projections.shape[2],) * 2):
        piece = vector[start : start + array.shape[0]]
        vectors.append(piece.reshape(-1, cols))
        start += array.shape[0]
    selfs, crosses, queries, texts = vectors[:4]
    gain_grad = jnp.stack([selfs[0], queries[3], queries[0], texts[0]])
    bias_grad = jnp.concatenate(
        [
            selfs[2:5],
            crosses[0:3],
            queries[2:3],
            texts[2:3],
            selfs[1:2],
            queries[4:5],
            queries[1:2],
            texts[1:2],
        ],
        0,
    )

    def mine(array):
        mats, cols = array.shape[0] // sizes["rep"], array.shape[1] // sizes["dp"]
        starts = (lax.axis_index("rep") * mats, lax.axis_index("dp") * cols)
        return lax.dynamic_slice(array, starts, (mats, cols))

    small = [
        mine(gain_grad),
        mine(bias_grad),
        mine(jnp.concatenate(vectors[4:6], 0)),
        mine(jnp.concatenate(vectors[6:8], 0)),
    ]
    attn_sums = advance(
        states, bits, sizes, plain, size, (small, cross_grad, ffn_in_grad, ffn_out_grad, proj_grad)
    )
    attn_grad = jnp.stack(attn_sums)
    return (
        layer_out,
        row_loss,
        input_grad.reshape(hidden_states.shape),
        attn_grad,
        cross_grad[None],
        ffn_in_grad[None],
        ffn_out_grad[None],
        proj_grad[None],
        small[0],
        small[1],
        small[2],
        small[3],
    )


def solution(mesh):
    placed = (
        P(("dp", "rep"), None, None),
        P(("dp", "rep"), None, None),
        P(("dp", "rep"), None),
        P(),
        P(),
        P(),
        P(),
        P(),
        P(),
        P(),
        P(),
        P(),
        P(("dp", "rep"), None, None),
    )
    sizes = dict(mesh.shape)
    return jax.shard_map(
        functools.partial(shards, sizes=sizes),
        mesh=mesh,
        in_specs=placed,
        out_specs=(
            P(("dp", "rep"), None, None),
            P(("dp", "rep")),
            P(("dp", "rep"), None, None),
            P("rep", "dp", None),
            P("rep", "dp", None),
            P("rep", "dp", None),
            P("rep", "dp", None),
            P("rep", "dp", None),
            P("rep", "dp"),
            P("rep", "dp"),
            P("rep", "dp"),
            P("rep", "dp"),
        ),
        check_vma=False,
    )
```

```python
import functools

import jax
import jax.numpy as jnp
from jax import lax
from jax.experimental import pallas as pl
from jax.experimental.pallas import tpu as pltpu
from jax.sharding import PartitionSpec as P

HEADS = 12
QUERIES = 32
TEXT = 32
SLOTS = QUERIES + TEXT


blocked = -1000000000.0
epsilon = 1e-06
sharpness = 14.0
loss_weight = 16.0


def unit_rows(values):
    return values * lax.rsqrt(jnp.sum(values * values, -1, keepdims=True) + epsilon)


def unit_back(values, grad_rows):
    unused, pullback = jax.vjp(unit_rows, values)
    return pullback(grad_rows)[0]


def caption_layout(length_rows):
    row_count = length_rows.shape[0]
    first_len = length_rows[:, 0:1]
    second_end = first_len + length_rows[:, 1:2]
    slot_index = lax.broadcasted_iota(jnp.int32, (row_count, TEXT), 1)
    text_group = (slot_index >= first_len).astype(jnp.int32) + (slot_index >= second_end).astype(
        jnp.int32
    )
    group_ids = jnp.concatenate([jnp.full((row_count, QUERIES), -1, jnp.int32), text_group], 1)
    allowed = group_ids[:, :, None] == group_ids[:, None, :]
    head_starts = jnp.concatenate([jnp.zeros_like(first_len), first_len], 1)
    pick_mask = slot_index[:, None, :] == head_starts[:, :, None]
    return (allowed, pick_mask)


f32 = jnp.float32
bf16 = jnp.bfloat16
ROOT_HALF = 0.7071067811865476
ROOT_TAU = 0.3989422804014327
MIB = 1024 * 1024


def dot_nn(a, b):
    return lax.dot_general(a, b, (((1,), (0,)), ((), ())), preferred_element_type=f32)


def dot_nt(a, b):
    return lax.dot_general(a, b, (((1,), (1,)), ((), ())), preferred_element_type=f32)


def dot_tn(a, b):
    return lax.dot_general(a, b, (((0,), (0,)), ((), ())), preferred_element_type=f32)


def whole(shape):
    return pl.BlockSpec(shape, lambda *_: (0,) * len(shape))


def held(shape, index):
    return pl.BlockSpec(shape, index, pipeline_mode=pl.Buffered(1))


def cost(micros):
    return pl.CostEstimate(flops=int(micros * 1.1e9), bytes_accessed=0, transcendentals=0)


def put_row(ref, place, row, add=False):
    units = row.shape[1] // 128
    for unit in range(units):
        at = slice(place * units + unit, place * units + unit + 1)
        piece = row[:, unit * 128 : (unit + 1) * 128]
        ref[at] = ref[at] + piece if add else piece


def store_units(ref, values):
    for place in range(values.shape[1] // 128):
        ref[place] = values[:, place * 128 : (place + 1) * 128].astype(ref.dtype)


def ordered(kernel, inputs, count):
    def run(*refs):
        kernel(*refs[:inputs], *refs[inputs + count :])

    return run


def unread(count):
    return [pl.BlockSpec(memory_space=pltpu.HBM)] * count


def params(mib):
    return pltpu.CompilerParams(vmem_limit_bytes=mib * MIB, dimension_semantics=("arbitrary",))


def norm_parts(values):
    center = values - jnp.mean(values, -1, keepdims=True)
    scale = lax.rsqrt(jnp.mean(center * center, -1, keepdims=True) + epsilon)
    return center * scale, scale


def norm_grads(values, gain_row, grad):
    unit, scale = norm_parts(values)
    inner = grad * gain_row
    first = jnp.mean(inner, -1, keepdims=True)
    second = jnp.mean(inner * unit, -1, keepdims=True)
    return (
        scale * (inner - first - unit * second),
        jnp.sum(grad * unit, 0, keepdims=True),
        jnp.sum(grad, 0, keepdims=True),
    )


def gate_parts(u):
    size = jnp.abs(u) * ROOT_HALF
    t = 1.0 / (1.0 + 0.3275911 * size)
    bell = jnp.exp(-size * size)
    poly = t * (
        0.127414796
        + t * (-0.142248368 + t * (0.7107068705 + t * (-0.7265760135 + t * 0.5307027145)))
    )
    tail = poly * bell
    cdf = jnp.where(u > 0, 1.0 - tail, tail)
    return u * cdf, cdf + (ROOT_TAU * u) * bell


def half_lanes(rows):
    low = (lax.broadcasted_iota(jnp.int32, (rows, 128), 1) < 64).astype(f32)
    return low.astype(bf16), (1.0 - low).astype(bf16)


def spread_heads(x, low, high):
    left, right = x[:, :128], x[:, 128:]
    none = jnp.zeros_like(left)
    return jnp.concatenate(
        [
            jnp.concatenate([left * low, none], 1),
            jnp.concatenate([left * high, none], 1),
            jnp.concatenate([none, right * low], 1),
            jnp.concatenate([none, right * high], 1),
        ],
        0,
    )


def collect_heads(o, n):
    low = lax.broadcasted_iota(jnp.int32, (n, 128), 1) < 64
    left = jnp.where(low, o[:n, :128], o[n : 2 * n, :128])
    right = jnp.where(low, o[2 * n : 3 * n, 128:], o[3 * n :, 128:])
    return jnp.concatenate([left, right], 1)


def columns_softmax(scores):
    raised = jnp.exp(scores - jnp.max(scores, 0, keepdims=True))
    return raised * (1.0 / jnp.sum(raised, 0, keepdims=True))


GROUPS = HEADS // 4
SELF_ROWS = 4
CROSS_ROWS = 8
SELF_BACK_ROWS = 4
CROSS_BACK_ROWS = 4


def self_forward_kernel(
    x_ref, w_ref, bias_ref, gain_ref, mask_ref, q_ref, k_ref, v_ref, mix_ref, sum_ref, norm_ref
):
    x = x_ref[...]
    q_ref[...] = (dot_nn(x, w_ref[0]) + bias_ref[0:1]).astype(bf16)
    k_ref[...] = dot_nn(x, w_ref[1]).astype(bf16)
    v_ref[...] = (dot_nn(x, w_ref[2]) + bias_ref[1:2]).astype(bf16)
    low, high = half_lanes(SLOTS)

    def some_rows(step, carry):
        spots = []
        for near in range(SELF_ROWS):
            r = step * SELF_ROWS + near
            rows = pl.ds(pl.multiple_of(r * SLOTS, SLOTS), SLOTS)
            spots += [(r, rows, slice(g * 256, (g + 1) * 256)) for g in range(GROUPS)]
        scores = [
            dot_nt(
                k_ref[rows, cols], spread_heads(q_ref[rows, cols] * bf16(0.125), low, high)
            )
            for r, rows, cols in spots
        ]
        probs = [
            columns_softmax(jnp.where(mask_ref[r].astype(f32) > 0.0, score, blocked)).astype(bf16)
            for (r, rows, cols), score in zip(spots, scores)
        ]
        mixed = [dot_tn(prob, v_ref[rows, cols]) for (r, rows, cols), prob in zip(spots, probs)]
        for (r, rows, cols), mix in zip(spots, mixed):
            mix_ref[rows, cols] = collect_heads(mix, SLOTS).astype(bf16)
        return carry

    lax.fori_loop(0, x_ref.shape[0] // (SELF_ROWS * SLOTS), some_rows, 0)
    total = x.astype(f32) + dot_nn(mix_ref[...], w_ref[3]) + bias_ref[2:3]
    sum_ref[...] = total
    unit, _ = norm_parts(total)
    norm_ref[...] = unit * gain_ref[0:1] + bias_ref[8:9]


def self_forward(x, weights, biases, gains, mask):
    tokens, width = x.shape
    step = 4 * SLOTS
    tile = pl.BlockSpec((step, width), lambda i: (i, 0))
    low, full = jax.ShapeDtypeStruct(x.shape, bf16), jax.ShapeDtypeStruct(x.shape, f32)
    return pl.pallas_call(
        self_forward_kernel,
        grid=(tokens // step,),
        in_specs=[
            tile,
            held((4, width, width), lambda i: (0, 0, 0)),
            whole(biases.shape),
            whole(gains.shape),
            pl.BlockSpec((4,) + mask.shape[1:], lambda i: (i, 0, 0)),
        ],
        out_specs=[tile] * 6,
        out_shape=[low, low, low, low, full, full],
        compiler_params=params(58),
        name="self_forward",
        cost_estimate=cost(15),
    )(x, weights, biases, gains, mask)


def self_backward_kernel(
    w_ref,
    gain_ref,
    mask_ref,
    q_ref,
    k_ref,
    v_ref,
    sum_ref,
    top_ref,
    low_ref,
    grad_ref,
    branch_ref,
    down_ref,
    side_ref,
    dmix_all,
):
    step = pl.program_id(0)
    count = sum_ref.shape[0]
    low, high = half_lanes(SLOTS)

    @pl.when(step == 0)
    def _():
        side_ref[...] = jnp.zeros_like(side_ref)

    grad = jnp.concatenate([top_ref[...], low_ref[...]], 1).reshape(count, -1)
    down, dgain, dshift = norm_grads(sum_ref[...], gain_ref[0:1], grad)
    branch = down.astype(bf16)
    down_ref[...] = down
    branch_ref[...] = branch
    dmix_all[...] = dot_nt(branch, w_ref[0]).astype(bf16)

    def some_rows(step, carry):
        spots = []
        for near in range(SELF_BACK_ROWS):
            r = step * SELF_BACK_ROWS + near
            rows = pl.ds(pl.multiple_of(r * SLOTS, SLOTS), SLOTS)
            spots += [(r, rows, slice(g * 256, (g + 1) * 256)) for g in range(GROUPS)]
        queries = [
            spread_heads(q_ref[rows, cols] * bf16(0.125), low, high) for r, rows, cols in spots
        ]
        outs = [spread_heads(dmix_all[rows, cols], low, high) for r, rows, cols in spots]
        scores = [dot_nt(k_ref[spot[1:]], turned) for spot, turned in zip(spots, queries)]
        dprobs = [dot_nt(v_ref[spot[1:]], turned) for spot, turned in zip(spots, outs)]
        probs = [
            columns_softmax(jnp.where(mask_ref[spot[0]].astype(f32) > 0.0, score, blocked))
            for spot, score in zip(spots, scores)
        ]
        for spot, prob, turned in zip(spots, probs, outs):
            grad_ref[(2,) + spot[1:]] = dot_nn(prob.astype(bf16), turned).astype(bf16)
        dscores = [
            (prob * (dprob - jnp.sum(dprob * prob, 0, keepdims=True))).astype(bf16)
            for prob, dprob in zip(probs, dprobs)
        ]
        for spot, dscore, turned in zip(spots, dscores, queries):
            grad_ref[(1,) + spot[1:]] = dot_nn(dscore, turned).astype(bf16)
        dqs = [dot_tn(dscore, k_ref[spot[1:]]) for spot, dscore in zip(spots, dscores)]
        for spot, dq in zip(spots, dqs):
            grad_ref[(0,) + spot[1:]] = (collect_heads(dq, SLOTS) * 0.125).astype(bf16)
        return carry

    lax.fori_loop(0, count // (SELF_BACK_ROWS * SLOTS), some_rows, 0)
    put_row(side_ref, 0, dgain, True)
    put_row(side_ref, 1, dshift, True)
    for place, rows in enumerate((grad_ref[0], grad_ref[2], branch)):
        put_row(side_ref, 2 + place, jnp.sum(rows.astype(f32), 0, keepdims=True), True)


def self_backward(weights, gains, mask, q, k, v, total, top, text, order):
    tokens, width = q.shape
    count = 4 * SLOTS
    tile = pl.BlockSpec((count, width), lambda i: (i, 0))
    part = pl.BlockSpec((4, QUERIES, width), lambda i: (i, 0, 0))
    return pl.pallas_call(
        ordered(self_backward_kernel, 9, len(order)),
        grid=(tokens // count,),
        in_specs=[
            held((1, width, width), lambda i: (3, 0, 0)),
            whole(gains.shape),
            pl.BlockSpec((4,) + mask.shape[1:], lambda i: (i, 0, 0)),
            tile,
            tile,
            tile,
            tile,
            part,
            part,
        ]
        + unread(len(order)),
        out_specs=[
            pl.BlockSpec((3, count, width), lambda i: (0, i, 0)),
            tile,
            tile,
            whole((width // 16, 128)),
        ],
        out_shape=[
            jax.ShapeDtypeStruct((3, tokens, width), bf16),
            jax.ShapeDtypeStruct((tokens, width), bf16),
            jax.ShapeDtypeStruct((tokens, width), f32),
            jax.ShapeDtypeStruct((width // 16, 128), f32),
        ],
        scratch_shapes=[pltpu.VMEM((count, width), bf16)],
        compiler_params=params(58),
        name="self_backward",
        cost_estimate=cost(16),
    )(weights, gains, mask, q, k, v, total, top, text, *order)


def input_grad_kernel(w_ref, grad_ref, down_ref, dx_ref):
    dx_ref[...] = (
        down_ref[...]
        + dot_nt(grad_ref[0], w_ref[0])
        + dot_nt(grad_ref[1], w_ref[1])
        + dot_nt(grad_ref[2], w_ref[2])
    )


def input_gradient(weights, grads, down, order, first, last, prior=()):
    tokens, width = down.shape
    count = 4 * SLOTS
    tile = pl.BlockSpec((count, width), lambda i: (first + i, 0))
    order = list(prior) + list(order)
    return pl.pallas_call(
        ordered(input_grad_kernel, 3, len(order)),
        grid=(last - first,),
        in_specs=[
            held((3, width, width), lambda i: (0, 0, 0)),
            pl.BlockSpec((3, count, width), lambda i: (0, first + i, 0)),
            tile,
        ]
        + unread(len(order)),
        out_specs=tile,
        out_shape=jax.ShapeDtypeStruct((tokens, width), f32),
        input_output_aliases={3: 0} if prior else {},
        compiler_params=params(58),
        name="input_gradient",
        cost_estimate=cost(5),
    )(weights, grads, down, *order)


def place_of(order, row_block, rep):
    return tuple(rep if axis == "rep" else (row_block >> bit) & 1 for axis, bit in order)


def slab_shape(order, units, rows):
    return (2,) * (len(order) - 1) + (units, rows, 128)


def store_halves(core_ref, keep_ref, send_ref, pieces):
    for core in range(2):

        @pl.when(core_ref[0] == core)
        def _():
            for places, block in pieces:
                ref = keep_ref if places[0] == core else send_ref
                ref[places[1:]] = block


core_spec = pl.BlockSpec(memory_space=pltpu.SMEM)


def attn_weight_kernel(folds, core_ref, left_ref, right_ref, *rest):
    step = pl.program_id(0)
    outs = rest[6:]
    width = right_ref.shape[-1]
    for part in range(3):

        @pl.when(step == part)
        def _():
            pieces = []
            pairs = ((left_ref, right_ref), rest[2 * part : 2 * part + 2])
            for rep, (left, right) in enumerate(pairs):
                lhs = left[...].reshape(-1, width).astype(bf16)
                rhs = right[...].reshape(-1, width).astype(bf16)
                grad = dot_tn(lhs, rhs).astype(bf16)
                if folds is None:
                    store_units(outs[part].at[rep], grad)
                    continue
                rows = outs[0].shape[-2]
                for block in range(width // rows):
                    spot = place_of(folds[part], block, rep)
                    for unit in range(width // 128):
                        piece = grad[
                            block * rows : (block + 1) * rows, unit * 128 : (unit + 1) * 128
                        ]
                        pieces.append((spot + (unit,), piece))
            if folds is not None:
                store_halves(core_ref, *outs[2 * part : 2 * part + 2], pieces)


def attn_weight_grad(core, left, grads, others, folds, rows, order):
    tokens, width = left.shape
    if folds is None:
        shapes = [(2, width // 128, width, 128)] * 3
    else:
        shapes = [slab_shape(fold, width // 128, rows) for fold in folds for half in range(2)]
    return pl.pallas_call(
        ordered(functools.partial(attn_weight_kernel, folds), 9, len(order)),
        grid=(3,),
        in_specs=[
            core_spec,
            held(left.shape, lambda i: (0, 0)),
            pl.BlockSpec((1, tokens, width), lambda i: (i, 0, 0)),
        ]
        + [held(block, lambda i, zeros=(0,) * len(block): zeros) for _, block in others]
        + unread(len(order)),
        out_specs=[held(shape, lambda i, zeros=(0,) * len(shape): zeros) for shape in shapes],
        out_shape=[jax.ShapeDtypeStruct(shape, bf16) for shape in shapes],
        compiler_params=params(58),
        name="attn_weight_grad",
        cost_estimate=cost(20),
    )(core, left, grads, *(array for array, _ in others), *order)


TAIL = 16


def hide_ends(scores, main):
    end = scores[main:]
    shown = lax.broadcasted_iota(jnp.int32, end.shape, 0) < 1
    return jnp.concatenate([scores[:main], jnp.where(shown, end, blocked)], 0)


def cross_forward_kernel(
    image_ref,
    end_ref,
    kv_ref,
    w_ref,
    bias_ref,
    gain_ref,
    norm_ref,
    key_ref,
    value_ref,
    key_end_ref,
    value_end_ref,
    q_ref,
    mix_ref,
    sum_ref,
    out_ref,
):
    rows_here = image_ref.shape[0]
    main = image_ref.shape[1] - 1
    width = norm_ref.shape[-1]
    end = end_ref[...].reshape(rows_here * TAIL, -1)
    key_end_ref[...] = dot_nt(end, kv_ref[0]).astype(bf16)
    value_end_ref[...] = (dot_nt(end, kv_ref[1]) + bias_ref[4:5]).astype(bf16)
    residual = norm_ref[...].reshape(rows_here * QUERIES, width)
    q_ref[...] = (dot_nn(residual.astype(bf16), w_ref[0]) + bias_ref[3:4]).astype(bf16)
    low, high = half_lanes(QUERIES)
    tokens = image_ref[:, :main].reshape(rows_here * main, -1)
    key_ref[...] = dot_nt(tokens, kv_ref[0]).astype(bf16)
    value_ref[...] = (dot_nt(tokens, kv_ref[1]) + bias_ref[4:5]).astype(bf16)

    def some_rows(step, carry):
        spots = []
        for near in range(CROSS_ROWS):
            r = step * CROSS_ROWS + near
            span = pl.ds(pl.multiple_of(r * main, main), main)
            last = pl.ds(pl.multiple_of(r * TAIL, TAIL), TAIL)
            mine = pl.ds(pl.multiple_of(r * QUERIES, QUERIES), QUERIES)
            spots += [(span, last, mine, slice(g * 256, (g + 1) * 256)) for g in range(GROUPS)]
        scores = [
            dot_nt(
                jnp.concatenate([key_ref[span, cols], key_end_ref[last, cols]], 0),
                spread_heads(q_ref[mine, cols] * bf16(0.125), low, high),
            )
            for span, last, mine, cols in spots
        ]
        probs = [columns_softmax(hide_ends(score, main)).astype(bf16) for score in scores]
        mixed = [
            dot_tn(
                prob, jnp.concatenate([value_ref[span, cols], value_end_ref[last, cols]], 0)
            )
            for (span, last, mine, cols), prob in zip(spots, probs)
        ]
        for (span, last, mine, cols), mix in zip(spots, mixed):
            mix_ref[mine, cols] = collect_heads(mix, QUERIES).astype(bf16)
        return carry

    lax.fori_loop(0, rows_here // CROSS_ROWS, some_rows, 0)
    total = residual + dot_nn(mix_ref[...], w_ref[1]) + bias_ref[5:6]
    sum_ref[...] = total
    unit, _ = norm_parts(total)
    out_ref[...] = unit * gain_ref[1:2] + bias_ref[9:10]


def cross_forward(images, ends, kv, weights, biases, gains, norm):
    rows, patches, vis = images.shape
    main = patches - 1
    width = norm.shape[-1]
    take = 8
    keys = pl.BlockSpec((take * main, width), lambda i: (i, 0))
    tails = pl.BlockSpec((take * TAIL, width), lambda i: (i, 0))
    tile = pl.BlockSpec((take * QUERIES, width), lambda i: (i, 0))

    def shape(count, dtype):
        return jax.ShapeDtypeStruct((rows * count, width), dtype)

    return pl.pallas_call(
        cross_forward_kernel,
        grid=(rows // take,),
        in_specs=[
            pl.BlockSpec((take, patches, vis), lambda i: (i, 0, 0)),
            pl.BlockSpec((take, TAIL, vis), lambda i: (i, 0, 0)),
            held(kv.shape, lambda i: (0, 0, 0)),
            held((2, width, width), lambda i: (2, 0, 0)),
            whole(biases.shape),
            whole(gains.shape),
            pl.BlockSpec((take, QUERIES, width), lambda i: (i, 0, 0)),
        ],
        out_specs=[keys, keys, tails, tails, tile, tile, tile, tile],
        out_shape=[
            shape(main, bf16),
            shape(main, bf16),
            shape(TAIL, bf16),
            shape(TAIL, bf16),
            shape(QUERIES, bf16),
            shape(QUERIES, bf16),
            shape(QUERIES, f32),
            shape(QUERIES, f32),
        ],
        compiler_params=params(58),
        name="cross_forward",
        cost_estimate=cost(38),
    )(images, ends, kv, weights, biases, gains, norm)


def cross_backward_kernel(
    w_ref,
    key_ref,
    value_ref,
    key_end_ref,
    value_end_ref,
    q_ref,
    down_ref,
    dnorm_ref,
    dkv_ref,
    dkv_end_ref,
    dq_ref,
    side_ref,
    dmix_all,
):
    step = pl.program_id(0)
    rows_here, _, width = dnorm_ref.shape
    main = key_ref.shape[0] // rows_here
    low, high = half_lanes(QUERIES)

    @pl.when(step == 0)
    def _():
        side_ref[...] = jnp.zeros_like(side_ref)

    down = down_ref[...]
    branch = down.astype(bf16)
    dmix_all[...] = dot_nt(branch, w_ref[1]).astype(bf16)

    def some_rows(step, carry):
        spots = []
        for near in range(CROSS_BACK_ROWS):
            r = step * CROSS_BACK_ROWS + near
            span = pl.ds(pl.multiple_of(r * main, main), main)
            last = pl.ds(pl.multiple_of(r * TAIL, TAIL), TAIL)
            mine = pl.ds(pl.multiple_of(r * QUERIES, QUERIES), QUERIES)
            spots += [(span, last, mine, slice(g * 256, (g + 1) * 256)) for g in range(GROUPS)]
        keys = [
            jnp.concatenate([key_ref[span, cols], key_end_ref[last, cols]], 0)
            for span, last, mine, cols in spots
        ]
        queries = [
            spread_heads(q_ref[mine, cols] * bf16(0.125), low, high)
            for span, last, mine, cols in spots
        ]
        outs = [spread_heads(dmix_all[mine, cols], low, high) for span, last, mine, cols in spots]
        scores = [dot_nt(rows, turned) for rows, turned in zip(keys, queries)]
        dprobs = [
            dot_nt(jnp.concatenate([value_ref[span, cols], value_end_ref[last, cols]], 0), turned)
            for (span, last, mine, cols), turned in zip(spots, outs)
        ]
        probs = [columns_softmax(hide_ends(score, main)) for score in scores]
        for (span, last, mine, cols), prob, turned in zip(spots, probs, outs):
            dv = dot_nn(prob.astype(bf16), turned).astype(bf16)
            dkv_ref[1, span, cols] = dv[:main]
            dkv_end_ref[1, last, cols] = dv[main:]
        dscores = [
            (prob * (dprob - jnp.sum(dprob * prob, 0, keepdims=True))).astype(bf16)
            for prob, dprob in zip(probs, dprobs)
        ]
        for (span, last, mine, cols), dscore, turned in zip(spots, dscores, queries):
            dk = dot_nn(dscore, turned).astype(bf16)
            dkv_ref[0, span, cols] = dk[:main]
            dkv_end_ref[0, last, cols] = dk[main:]
        dqs = [dot_tn(dscore, rows) for dscore, rows in zip(dscores, keys)]
        for (span, last, mine, cols), dq in zip(spots, dqs):
            dq_ref[mine, cols] = (collect_heads(dq, QUERIES) * 0.125).astype(bf16)
        return carry

    lax.fori_loop(0, rows_here // CROSS_BACK_ROWS, some_rows, 0)
    dq = dq_ref[...]
    dnorm_ref[...] = (down + dot_nt(dq, w_ref[0])).reshape(rows_here, QUERIES, width)
    put_row(side_ref, 0, jnp.sum(dq.astype(f32), 0, keepdims=True), True)
    dvalue = jnp.sum(dkv_ref[1].astype(f32), 0, keepdims=True)
    dvalue += jnp.sum(dkv_end_ref[1].astype(f32), 0, keepdims=True)
    put_row(side_ref, 1, dvalue, True)
    put_row(side_ref, 2, jnp.sum(branch.astype(f32), 0, keepdims=True), True)


def cross_backward(rows, weights, keys, values, key_ends, value_ends, q, down, order):
    width = q.shape[1]
    main = keys.shape[0] // rows
    take = 4
    span = pl.BlockSpec((take * main, width), lambda i: (i, 0))
    tails = pl.BlockSpec((take * TAIL, width), lambda i: (i, 0))
    tile = pl.BlockSpec((take * QUERIES, width), lambda i: (i, 0))
    return pl.pallas_call(
        ordered(cross_backward_kernel, 7, len(order)),
        grid=(rows // take,),
        in_specs=[
            held((2, width, width), lambda i: (2, 0, 0)),
            span,
            span,
            tails,
            tails,
            tile,
            tile,
        ]
        + unread(len(order)),
        out_specs=[
            pl.BlockSpec((take, QUERIES, width), lambda i: (i, 0, 0)),
            pl.BlockSpec((2, take * main, width), lambda i: (0, i, 0)),
            pl.BlockSpec((2, take * TAIL, width), lambda i: (0, i, 0)),
            tile,
            whole((width // 16, 128)),
        ],
        out_shape=[
            jax.ShapeDtypeStruct((rows, QUERIES, width), f32),
            jax.ShapeDtypeStruct((2, rows * main, width), bf16),
            jax.ShapeDtypeStruct((2, rows * TAIL, width), bf16),
            jax.ShapeDtypeStruct((rows * QUERIES, width), bf16),
            jax.ShapeDtypeStruct((width // 16, 128), f32),
        ],
        scratch_shapes=[pltpu.VMEM((take * QUERIES, width), bf16)],
        compiler_params=params(58),
        name="cross_backward",
        cost_estimate=cost(19),
    )(weights, keys, values, key_ends, value_ends, q, down, *order)


def third_units(units):
    edges = [(units * k + 2) // 3 for k in range(4)]
    return [edges[k + 1] - edges[k] for k in range(3)]


def cross_weight_kernel(folds, core_ref, image_ref, end_ref, grad_ref, grad_end_ref, *rest):
    outs, gathered = rest[:-1], rest[-1]
    rows, patches, vis = image_ref.shape
    main = patches - 1
    take = 4
    gathered[...] = dot_tn(grad_end_ref[0], end_ref[...].reshape(rows * TAIL, vis))

    def add_rows(i, carry):
        span = pl.ds(pl.multiple_of(i * take * main, take * main), take * main)
        tokens = image_ref[pl.ds(i * take, take), :main].reshape(take * main, vis)
        gathered[...] += dot_tn(grad_ref[0, span], tokens)
        return carry

    lax.fori_loop(0, rows // take, add_rows, 0)
    if folds is None:
        store_units(outs[0].at[0], gathered[...])
        return
    first = 0
    for part, fold in enumerate(folds):
        keep, send = outs[2 * part : 2 * part + 2]
        units, size = keep.shape[-3:-1]
        pieces = []
        for block in range(gathered.shape[0] // size):
            spot = tuple(
                0 if axis == "rep" or bit == 3 else (block >> bit) & 1 for axis, bit in fold
            )
            piece = gathered[block * size : (block + 1) * size].astype(bf16)
            for unit in range(units):
                at = (first + unit) * 128
                pieces.append((spot + (unit,), piece[:, at : at + 128]))
        store_halves(core_ref, keep, send, pieces)
        first += units


def cross_weight_grad(core, images, ends, grads, grads_end, folds, size, order):
    rows, patches, vis = images.shape
    width = grads.shape[2]
    half = width // 2
    units = vis // 128
    if folds is None:
        specs = [pl.BlockSpec((1, units, half, 128), lambda m, h: (m, 0, h, 0))]
        shapes = [(2, units, width, 128)]
    else:
        specs, shapes = [], []
        for fold, count in zip(folds, third_units(units) if len(folds) == 3 else [units]):
            block = tuple(1 if axis == "rep" or bit == 3 else 2 for axis, bit in fold[1:])

            def index(m, h, fold=fold):
                spot = tuple(
                    m if axis == "rep" else h if bit == 3 else 0 for axis, bit in fold[1:]
                )
                return spot + (0, 0, 0)

            specs += [pl.BlockSpec(block + (count, size, 128), index)] * 2
            shapes += [slab_shape(fold, count, size)] * 2
    return pl.pallas_call(
        ordered(functools.partial(cross_weight_kernel, folds), 5, len(order)),
        grid=(2, 2),
        in_specs=[
            core_spec,
            held(images.shape, lambda m, h: (0, 0, 0)),
            held(ends.shape, lambda m, h: (0, 0, 0)),
            pl.BlockSpec((1, grads.shape[1], half), lambda m, h: (m, 0, h)),
            pl.BlockSpec((1, grads_end.shape[1], half), lambda m, h: (m, 0, h)),
        ]
        + unread(len(order)),
        out_specs=specs,
        out_shape=[jax.ShapeDtypeStruct(shape, bf16) for shape in shapes],
        scratch_shapes=[pltpu.VMEM((half, vis), f32)],
        compiler_params=pltpu.CompilerParams(
            vmem_limit_bytes=58 * MIB, dimension_semantics=("arbitrary", "arbitrary")
        ),
        name="cross_weight_grad",
        cost_estimate=cost(32),
    )(core, images, ends, grads, grads_end, *order)


def ffn_forward_kernel(
    which,
    norm_ref,
    in_ref,
    in_bias_ref,
    out_ref,
    proj_ref,
    proj_bias_ref,
    bias_ref,
    gain_ref,
    *rest,
):
    act_ref, slope_ref, sum_ref, low_ref, raw_ref, embed_ref, rows_low = rest[-7:]
    step = pl.program_id(0)
    tokens, width = sum_ref.shape

    @pl.when(step == 0)
    def _():
        full = norm_ref[...].reshape(tokens, width)
        rows_low[...] = full.astype(bf16)
        sum_ref[...] = full + bias_ref[6 + which : 7 + which]

    low = rows_low[...]
    wide = 256
    pieces = act_ref.shape[1] // wide

    def before_gate(k):
        cols = slice(k * wide, (k + 1) * wide)
        return dot_nn(low, in_ref[0, :, cols]) + in_bias_ref[which : which + 1, cols]

    ahead = [before_gate(k) for k in range(2)]
    gathered = 0.0
    for k in range(pieces):
        if k + 2 < pieces:
            ahead.append(before_gate(k + 2))
        cols = slice(k * wide, (k + 1) * wide)
        act, slope = gate_parts(ahead[k])
        act = act.astype(bf16)
        act_ref[:, cols] = act
        slope_ref[:, cols] = slope.astype(bf16)
        gathered += dot_nn(act, out_ref[0, cols])
    sum_ref[...] += gathered

    @pl.when(step == pl.num_programs(0) - 1)
    def _():
        unit, _ = norm_parts(sum_ref[...])
        low = (unit * gain_ref[2 + which : 3 + which] + bias_ref[10 + which : 11 + which]).astype(bf16)
        low_ref[...] = low.reshape(low_ref.shape)
        raw = dot_nn(low, proj_ref[0]) + proj_bias_ref[which : which + 1]
        raw_ref[...] = raw
        size = lax.rsqrt(jnp.sum(raw * raw, -1, keepdims=True) + epsilon)
        embed_ref[...] = (raw * size).astype(bf16)


def ffn_forward(which, part, norm, ffn_in, ffn_bias, ffn_out, projections, proj_bias, biases, gains, layer, order=()):
    rows, width = norm.shape[0], norm.shape[-1]
    tokens = rows * QUERIES
    hidden = ffn_in.shape[2]
    embed = projections.shape[2]
    chunk = 1024
    cols = pl.BlockSpec((tokens, chunk), lambda j: (0, j))
    halves = [] if layer is None else [layer]
    return pl.pallas_call(
        functools.partial(ffn_forward_kernel, which),
        grid=(hidden // chunk,),
        in_specs=[
            held((rows, QUERIES, width), lambda j: (0, part, 0)),
            pl.BlockSpec((1, width, chunk), lambda j: (which, 0, j)),
            pl.BlockSpec((2, chunk), lambda j: (0, j)),
            pl.BlockSpec((1, chunk, width), lambda j: (which, j, 0)),
            held((1, width, embed), lambda j: (which, 0, 0)),
            whole(proj_bias.shape),
            whole(biases.shape),
            whole(gains.shape),
        ]
        + unread(len(halves) + len(order)),
        out_specs=[
            cols,
            cols,
            whole((tokens, width)),
            pl.BlockSpec((rows, QUERIES, width), lambda j: (0, which, 0)),
            whole((tokens, embed)),
            whole((tokens, embed)),
        ],
        out_shape=[
            jax.ShapeDtypeStruct((tokens, hidden), bf16),
            jax.ShapeDtypeStruct((tokens, hidden), bf16),
            jax.ShapeDtypeStruct((tokens, width), f32),
            jax.ShapeDtypeStruct((rows, SLOTS, width), bf16),
            jax.ShapeDtypeStruct((tokens, embed), f32),
            jax.ShapeDtypeStruct((tokens, embed), bf16),
        ],
        scratch_shapes=[pltpu.VMEM((tokens, width), bf16)],
        input_output_aliases={8: 3} if halves else {},
        compiler_params=params(58),
        name="ffn_forward",
        cost_estimate=cost(15),
    )(norm, ffn_in, ffn_bias, ffn_out, projections, proj_bias, biases, gains, *halves, *order)


def ffn_backward_kernel(
    which,
    folds,
    core_ref,
    norm_ref,
    sum_ref,
    before_ref,
    layer_ref,
    grad_ref,
    raw_ref,
    proj_ref,
    gain_ref,
    in_ref,
    out_ref,
    act_ref,
    slope_ref,
    *rest,
):
    count = 3 if folds is None else 6
    down_ref, side_ref, dbias_ref, dproj_bias_ref = rest[-8 - count : -4 - count]
    weight_refs = rest[-4 - count : -4]
    branch_all, low_turned, left, dproj = rest[-4:]
    step = pl.program_id(0)
    tokens, width = sum_ref.shape

    @pl.when(step == 0)
    def _():
        raw = raw_ref[...]
        grad = grad_ref[...].reshape(tokens, width).astype(f32) + dot_nt(raw, proj_ref[0])
        down, dgain, dshift = norm_grads(sum_ref[...], gain_ref[2 + which : 3 + which], grad)
        branch = down.astype(bf16)
        branch_all[...] = branch
        left[...] = down
        side_ref[...] = jnp.zeros_like(side_ref)
        put_row(side_ref, 0, dgain)
        put_row(side_ref, 1, dshift)
        put_row(side_ref, 2, jnp.sum(branch.astype(f32), 0, keepdims=True))
        dproj[...] = dot_tn(layer_ref[...].reshape(tokens, width), raw).astype(bf16)
        put_row(dproj_bias_ref, 0, jnp.sum(raw.astype(f32), 0, keepdims=True))
        low_turned[...] = norm_ref[...].reshape(tokens, width).astype(bf16).T

    branch = branch_all[...]
    du = (dot_nt(branch, out_ref[0]) * slope_ref[...].astype(f32)).astype(bf16)
    left[...] += dot_nt(du, in_ref[0])
    put_row(dbias_ref, 0, jnp.sum(du.astype(f32), 0, keepdims=True))
    thin = width // 3
    for part in range(3):

        @pl.when(step == part)
        def _():
            din = dot_nn(low_turned[...], du).astype(bf16)
            dout = dot_tn(act_ref[...], branch[:, part * thin : (part + 1) * thin]).astype(bf16)
            if folds is None:
                store_units(weight_refs[0], din)
                store_units(weight_refs[1], dout)
                if part == 0:
                    store_units(weight_refs[2], dproj[...])
                return
            keep, send = weight_refs[2 * part : 2 * part + 2]
            size = keep.shape[-2]
            subs = dout.shape[0] // width
            pieces = []
            for block in range(width // size):
                spot = place_of(folds[part], block, 0)
                at = block * size
                found = [
                    din[at : at + size, unit * 128 : (unit + 1) * 128]
                    for unit in range(din.shape[1] // 128)
                ]
                for sub in range(subs):
                    row = at * subs + sub * size
                    for unit in range(thin // 128):
                        found.append(dout[row : row + size, unit * 128 : (unit + 1) * 128])
                if part == 0:
                    for unit in range(dproj.shape[1] // 128):
                        found.append(dproj[at : at + size, unit * 128 : (unit + 1) * 128])
                pieces += [(spot + (unit,), piece) for unit, piece in enumerate(found)]
            store_halves(core_ref, keep, send, pieces)

    @pl.when(step == pl.num_programs(0) - 1)
    def _():
        if which == 0:
            down, dgain, dshift = norm_grads(before_ref[...], gain_ref[1:2], left[...])
            put_row(side_ref, 3, dgain)
            put_row(side_ref, 4, dshift)
            down_ref[...] = down.reshape(down_ref.shape)
        else:
            down_ref[...] = left[...].reshape(down_ref.shape)


def ffn_backward(
    which,
    part,
    core,
    norm,
    total,
    before,
    layer,
    grad,
    raw,
    projections,
    gains,
    ffn_in,
    ffn_out,
    act,
    slope,
    slabs,
    folds,
    size,
):
    rows = layer.shape[0]
    tokens, width = total.shape
    hidden = ffn_in.shape[2]
    embed = projections.shape[2]
    chunk = hidden // 3
    slabs = list(slabs)
    before_spec = held(before.shape, lambda j: (0, 0))
    if folds is None:
        weight_specs = [
            pl.BlockSpec((chunk // 128, width, 128), lambda j: (j, 0, 0)),
            pl.BlockSpec((width // 384, hidden, 128), lambda j: (j, 0, 0)),
            whole((embed // 128, width, 128)),
        ]
        weight_shapes = [
            (hidden // 128, width, 128),
            (width // 128, hidden, 128),
            (embed // 128, width, 128),
        ]
    else:
        units = chunk // 128 + (hidden // width) * (width // 384)
        weight_shapes = [
            slab_shape(fold, units + (embed // 128 if k == 0 else 0), size)
            for k, fold in enumerate(folds)
            for half in range(2)
        ]

        def spec(fold, shape):
            block = tuple(1 if axis == "rep" else 2 for axis, bit in fold[1:])
            spot = tuple(which if axis == "rep" else 0 for axis, bit in fold[1:])
            return held(block + shape[-3:], lambda j: spot + (0, 0, 0))

        weight_specs = [spec(folds[k // 2], shape) for k, shape in enumerate(weight_shapes)]
    return pl.pallas_call(
        functools.partial(ffn_backward_kernel, which, folds),
        grid=(3,),
        in_specs=[
            core_spec,
            held((rows, QUERIES, width), lambda j: (0, part, 0)),
            held((tokens, width), lambda j: (0, 0)),
            before_spec,
            held((rows, QUERIES, width), lambda j: (0, which, 0)),
            held((rows, QUERIES, width), lambda j: (0, which, 0)),
            held((tokens, embed), lambda j: (0, 0)),
            held((1, width, embed), lambda j: (which, 0, 0)),
            whole(gains.shape),
            pl.BlockSpec((1, width, chunk), lambda j: (which, 0, j)),
            pl.BlockSpec((1, chunk, width), lambda j: (which, j, 0)),
            held((tokens, hidden), lambda j: (0, 0)),
            pl.BlockSpec((tokens, chunk), lambda j: (0, j)),
        ]
        + unread(len(slabs)),
        out_specs=[
            whole((rows, QUERIES, width)),
            whole((width // 16, 128)),
            pl.BlockSpec((chunk // 128, 128), lambda j: (j, 0)),
            whole((embed // 128, 128)),
        ]
        + weight_specs,
        out_shape=[
            jax.ShapeDtypeStruct((rows, QUERIES, width), f32),
            jax.ShapeDtypeStruct((width // 16, 128), f32),
            jax.ShapeDtypeStruct((hidden // 128, 128), f32),
            jax.ShapeDtypeStruct((embed // 128, 128), f32),
        ]
        + [jax.ShapeDtypeStruct(shape, bf16) for shape in weight_shapes],
        scratch_shapes=[
            pltpu.VMEM((tokens, width), bf16),
            pltpu.VMEM((width, tokens), bf16),
            pltpu.VMEM((tokens, width), f32),
            pltpu.VMEM((width, embed), bf16),
        ],
        input_output_aliases={13 + k: 4 + k for k in range(len(slabs))},
        compiler_params=params(60),
        name="ffn_backward",
        cost_estimate=cost(25),
    )(
        core,
        norm,
        total,
        before,
        layer,
        grad,
        raw,
        projections,
        gains,
        ffn_in,
        ffn_out,
        act,
        slope,
        *slabs,
    )


def swap(values, stage, sizes):
    axis, bit = stage
    return lax.ppermute(values, axis, [(i, i ^ (1 << bit)) for i in range(sizes[axis])])


def stage_order(part, sizes):
    stages = [("dp", bit) for bit in range(sizes["dp"].bit_length() - 1)]
    ring = stages[1:3] + [("rep", 0)]
    if part == 3:
        return stages[:1] + ring[:2] + stages[3:] + ring[2:]
    return stages[:1] + ring[part:] + ring[:part] + stages[3:]


def fold_pair(part, first, second, sizes):
    depth = sizes["dp"].bit_length() - 1
    both = jnp.stack([first, second])
    units, rows = first.shape[0], first.shape[1] // sizes["dp"]
    both = both.reshape((2, units) + (2,) * depth + (rows, 128))
    front = [0 if axis == "rep" else 1 + depth - bit for axis, bit in stage_order(part, sizes)]
    return both.transpose(front + [1, 2 + depth, 3 + depth])


def own_bits(sizes):
    depth = sizes["dp"].bit_length() - 1
    shifts = jnp.arange(depth + 1, dtype=jnp.int32)
    both = lax.axis_index("dp") + (lax.axis_index("rep") << depth)
    return ((both >> shifts) & 1).astype(jnp.int32)


def bit_place(stage, sizes):
    return sizes["dp"].bit_length() - 1 if stage[0] == "rep" else stage[1]


def picked(place_bits, bits_ref):
    at = 0
    for bit, other in place_bits:
        own = bits_ref[bit]
        at = 2 * at + (1 - own if other else own)
    return at


def sum_kernel(plan, arrays, bits_ref, *refs):
    sources, refs = refs[:arrays], refs[arrays:]
    outs, refs = refs[: len(plan)], refs[len(plan) :]
    count = sum(len(terms) for jobs in plan for _, terms in jobs)
    held_terms, held_outs = refs[:count], refs[count : count + len(plan)]
    in_sems, out_sems = refs[-2:]
    fetches = []
    for jobs in plan:
        for rows, terms in jobs:
            for source, start, place_bits in terms:
                first = start + picked(place_bits, bits_ref) * rows
                here = len(fetches)
                fetches.append(
                    pltpu.make_async_copy(
                        sources[source].at[pl.ds(pl.multiple_of(first, 16), rows)],
                        held_terms[here],
                        in_sems.at[here],
                    )
                )
    for fetch in fetches:
        fetch.start()
    here = 0
    stores = []
    for place, jobs in enumerate(plan):
        at = 0
        for rows, terms in jobs:
            found = None
            for _ in terms:
                fetches[here].wait()
                part = held_terms[here][...].astype(f32)
                found = part if found is None else found + part
                here += 1
            size, cols = held_outs[place].shape
            for unit in range(cols // 128 if cols > 128 else 0):
                lanes = slice(unit * 128, (unit + 1) * 128)
                held_outs[place][:, lanes] = found[unit * size : (unit + 1) * size]
            if cols == 128:
                held_outs[place][at : at + rows] = found.astype(held_outs[place].dtype)
            at += rows
        store = pltpu.make_async_copy(held_outs[place], outs[place], out_sems.at[place])
        store.start()
        stores.append(store)
    for store in stores:
        store.wait()


def sum_jobs(outputs, bits):
    arrays, plan, buffers = [], [], []

    def number_of(array):
        for number, known in enumerate(arrays):
            if known is array:
                return number
        arrays.append(array)
        return len(arrays) - 1

    shapes, moved = [], 0
    for dtype, jobs, tall in outputs:
        planned = []
        for rows, terms in jobs:
            planned.append((rows, [(number_of(array), start, bit) for array, start, bit in terms]))
            buffers += [pltpu.VMEM((rows, 128), array.dtype) for array, _, _ in terms]
            moved += rows * (1 + len(terms))
        plan.append(planned)
        total = sum(rows for rows, _ in jobs)
        shape = (tall, total // tall * 128) if tall else (total, 128)
        shapes.append(jax.ShapeDtypeStruct(shape, dtype))
    return pl.pallas_call(
        functools.partial(sum_kernel, plan, len(arrays)),
        in_specs=[core_spec] + unread(len(arrays)),
        out_specs=unread(len(plan)),
        out_shape=shapes,
        scratch_shapes=buffers
        + [pltpu.VMEM(shape.shape, shape.dtype) for shape in shapes]
        + [pltpu.SemaphoreType.DMA((len(buffers),)), pltpu.SemaphoreType.DMA((len(plan),))],
        compiler_params=pltpu.CompilerParams(vmem_limit_bytes=121 * MIB // 2),
        name="sum_terms",
        cost_estimate=cost(3),
    )(bits, *arrays)


def sum_jobs_plain(outputs, bits):
    results = []
    for dtype, jobs, tall in outputs:
        pieces = []
        for rows, terms in jobs:
            found = [
                lax.dynamic_slice_in_dim(array, start + picked(bit, bits) * rows, rows, 0)
                for array, start, bit in terms
            ]
            pieces.append(sum(part.astype(f32) for part in found).astype(dtype))
        made = pieces[0] if len(pieces) == 1 else jnp.concatenate(pieces, 0)
        results.append(columns_of(made.reshape(-1, tall, 128)) if tall else made)
    return results


def begin(part, keep, send, sizes):
    keep, send = keep.reshape(-1, 128), send.reshape(-1, 128)
    arrived = swap(send, stage_order(part, sizes)[0], sizes)
    return (part, 1, [(keep, 0, keep.shape[0], []), (arrived, 0, send.shape[0], [])], send)


def begin_together(parts, keep, send, sizes):
    count = len(parts)
    keep, send = keep.reshape(-1, 128), send.reshape(-1, 128)
    rows = keep.shape[0] // count
    arrived = swap(send, stage_order(0, sizes)[0], sizes)
    return [
        (part, 1, [(keep, at * rows, rows, []), (arrived, at * rows, rows, [])], send)
        for at, part in enumerate(parts)
    ]


def begin_folded(part, slab, sizes):
    own = lax.axis_index("dp") & 1
    halves = [lax.dynamic_index_in_dim(slab, place, 0, keepdims=False) for place in (own, 1 - own)]
    return begin(part, *halves, sizes)


def begin_whole(values, sizes):
    send = values.astype(bf16)
    arrived = swap(send, stage_order(0, sizes)[0], sizes)
    return (None, 1, [(values, 0, len(values), []), (arrived, 0, len(values), [])], send)


def advance(states, bits, sizes, plain, tall, after=None):
    last = len(stage_order(0, sizes))
    changed = {}
    fresh = []
    for part, at, terms, sent in states:
        array = terms[-1][0]
        if after is not None:
            if id(array) not in changed:
                changed[id(array)] = (array, lax.optimization_barrier((array, after))[0])
            array = changed[id(array)][1]
        fresh.append((part, at, terms[:-1] + [(array,) + terms[-1][1:]], sent))
    groups, finals = {}, []
    for number, (part, at, terms, _) in enumerate(fresh):
        if at == last:
            finals.append(number)
        else:
            groups.setdefault(stage_order(part or 0, sizes)[at], []).append(number)

    def job(number, ahead):
        rows = fresh[number][2][0][2] >> (len(fresh[number][2][0][3]) + len(ahead))
        return (
            rows,
            [(array, start, places + ahead) for array, start, _, places in fresh[number][2]],
        )

    outputs = []
    for stage, members in groups.items():
        jobs = []
        for number in members:
            ahead = [] if fresh[number][0] is None else [(bit_place(stage, sizes), True)]
            jobs.append(job(number, ahead))
        outputs.append((bf16, jobs, 0))
    outputs += [
        (f32, [job(number, [])], 0 if fresh[number][0] is None else tall) for number in finals
    ]
    made = (sum_jobs_plain if plain else sum_jobs)(outputs, bits)
    results = [None] * len(fresh)
    for (stage, members), (_, jobs, _), sent in zip(groups.items(), outputs, made):
        arrived = swap(sent, stage, sizes)
        start = 0
        for number, (rows, _) in zip(members, jobs):
            part, at, terms, _ = fresh[number]
            kept = [] if part is None else [(bit_place(stage, sizes), False)]
            terms = [(array, first, size, places + kept) for array, first, size, places in terms]
            results[number] = (part, at + 1, terms + [(arrived, start, rows, [])], sent)
            start += rows
    for number, found in zip(finals, made[len(groups) :]):
        results[number] = found
    return results


def sends(states):
    found = []
    for state in states:
        if not any(state[3] is known for known in found):
            found.append(state[3])
    return found


def columns_of(units):
    return units.transpose(1, 0, 2).reshape(units.shape[1], -1)


def exchange(values, sizes):
    return lax.all_to_all(values, ("dp", "rep"), 0, 0, tiled=True)


def gather_rows(values, sizes):
    world = sizes["dp"] * sizes["rep"]
    return exchange(jnp.tile(values, (world, 1)), sizes)


def scatter_rows(values, sizes):
    world = sizes["dp"] * sizes["rep"]
    arrived = exchange(values, sizes)
    return jnp.sum(arrived.reshape(world, -1, values.shape[1]).astype(f32), 0)


def shards(
    hidden_states,
    image_features,
    caption_lengths,
    attn_weights,
    cross_kv,
    ffn_in,
    ffn_out,
    projections,
    norm_gains,
    biases,
    ffn_bias,
    proj_bias,
    out_grad,
    sizes,
):
    row_count, slots, width = hidden_states.shape
    captions_here = 2 * row_count
    world = sizes["dp"] * sizes["rep"]
    allowed, pick_mask = caption_layout(caption_lengths)
    pick_low = pick_mask.astype(bf16)
    pick_full = pick_mask.astype(f32)
    mask = jnp.tile(allowed.astype(bf16), (1, 1, 4))
    inputs = hidden_states.reshape(row_count * slots, width)
    self_q, self_k, self_v, self_mix, first_sum, first_norm = self_forward(
        inputs, attn_weights, biases, norm_gains, mask
    )
    first_norm = first_norm.reshape(row_count, slots, width)
    image_ends = jnp.pad(image_features[:, -1:], ((0, 0), (0, TAIL - 1), (0, 0)))
    text_act, text_slope, fourth_sum, layer_half, caption_raw, caption_all = ffn_forward(
        1,
        1,
        first_norm,
        ffn_in,
        ffn_bias,
        ffn_out,
        projections,
        proj_bias,
        biases,
        norm_gains,
        None,
        [image_ends],
    )
    caption_embed = (
        jnp.einsum(
            "rkt,rtd->rkd",
            pick_low,
            caption_all.reshape(row_count, TEXT, -1),
            preferred_element_type=f32,
        )
        .astype(bf16)
        .reshape(captions_here, -1)
    )
    every_caption = gather_rows(caption_embed, sizes)
    keys, values, key_ends, value_ends, cross_q, cross_mix, second_sum, second_norm = cross_forward(
        image_features, image_ends, cross_kv, attn_weights, biases, norm_gains, first_norm
    )
    second_norm = second_norm.reshape(row_count, QUERIES, width)
    query_act, query_slope, third_sum, layer_out, query_raw, query_embed = ffn_forward(
        0,
        0,
        second_norm,
        ffn_in,
        ffn_bias,
        ffn_out,
        projections,
        proj_bias,
        biases,
        norm_gains,
        layer_half,
    )
    query_raw = query_raw.reshape(row_count, QUERIES, -1)
    query_embed = query_embed.reshape(row_count, QUERIES, -1)
    sims = jnp.einsum("rqp,cp->rqc", query_embed, every_caption, preferred_element_type=f32)
    expo = jnp.exp(sharpness * (sims - 1.0))
    affinity = jnp.mean(expo, 1)
    offset = lax.axis_index(("dp", "rep")) * captions_here
    own_block = lax.dynamic_slice_in_dim(affinity, offset, captions_here, 1).reshape(
        row_count, row_count, 2
    )
    diagonal = (
        lax.broadcasted_iota(jnp.int32, (row_count, row_count), 0)
        == lax.broadcasted_iota(jnp.int32, (row_count, row_count), 1)
    ).astype(f32)
    positive = jnp.sum(own_block * diagonal[:, :, None], 1)
    row_total = jnp.sum(affinity, 1)
    partial_cols = jnp.sum(affinity, 0)
    all_cols = jnp.sum(
        exchange(jnp.broadcast_to(partial_cols[None], (world,) + partial_cols.shape), sizes), 0
    )
    own_cols = lax.dynamic_slice_in_dim(all_cols, offset, captions_here, 0).reshape(row_count, 2)
    inverse_all = 1.0 / all_cols
    row_loss = (
        jnp.log(row_total)
        - jnp.log(positive[:, 0])
        + jnp.sum(jnp.log(own_cols) - jnp.log(positive), 1)
    )
    grad_affinity = loss_weight * (1.0 / row_total[:, None] + inverse_all[None, :])
    pair_weight = jnp.array([2.0, 1.0], f32)
    correction = (loss_weight * diagonal[:, :, None] * pair_weight / own_block).reshape(
        row_count, captions_here
    )
    own_grad = lax.dynamic_slice_in_dim(grad_affinity, offset, captions_here, 1) - correction
    grad_affinity = lax.dynamic_update_slice_in_dim(grad_affinity, own_grad, offset, 1)
    grad_sims = (grad_affinity[:, None, :] * expo * (sharpness / QUERIES)).astype(bf16)
    grad_query_embed = jnp.einsum(
        "rqc,cp->rqp", grad_sims, every_caption, preferred_element_type=f32
    )
    grad_caption_embed = scatter_rows(
        jnp.einsum("rqc,rqp->cp", grad_sims, query_embed, preferred_element_type=f32).astype(bf16),
        sizes,
    )
    query_raw_grad = unit_back(query_raw, grad_query_embed).astype(bf16)
    head_raw = jnp.sum(
        pick_full[:, :, :, None] * caption_raw.reshape(row_count, 1, TEXT, -1), 2
    )
    head_raw_grad = unit_back(head_raw, grad_caption_embed.reshape(row_count, 2, -1)).astype(bf16)
    caption_raw_grad = jnp.einsum(
        "rkt,rkd->rtd", pick_low, head_raw_grad, preferred_element_type=f32
    ).astype(bf16)
    fold = sizes["dp"] == 16 and sizes["rep"] == 2
    stage_orders = [stage_order(part, sizes) for part in range(3)]
    folds = stage_orders if fold else None
    ffn_parts = (3, 1, 2)
    ffn_folds = [stage_order(part, sizes) for part in ffn_parts] if fold else None
    size = width // sizes["dp"]
    bits = own_bits(sizes)
    core = bits[:1]
    grad_second, query_side, query_dbias, query_dproj_bias, *query_slabs = ffn_backward(
        0,
        0,
        core,
        second_norm,
        third_sum,
        second_sum,
        layer_out,
        out_grad,
        query_raw_grad.reshape(row_count * QUERIES, -1),
        projections,
        norm_gains,
        ffn_in,
        ffn_out,
        query_act,
        query_slope,
        (),
        ffn_folds,
        size,
    )
    text_first, text_side, text_dbias, text_dproj_bias, *text_slabs = ffn_backward(
        1,
        1,
        core,
        first_norm,
        fourth_sum,
        norm_gains,
        layer_out,
        out_grad,
        caption_raw_grad.reshape(row_count * TEXT, -1),
        projections,
        norm_gains,
        ffn_in,
        ffn_out,
        text_act,
        text_slope,
        query_slabs if fold else (),
        ffn_folds,
        size,
    )
    tall = ffn_out.shape[1] // width
    if not fold:
        text_slabs = [
            fold_pair(
                ffn_parts[part],
                *(
                    jnp.concatenate(
                        [
                            din[part * 8 : part * 8 + 8],
                            dout[2 * part : 2 * part + 2]
                            .reshape(2, sizes["dp"], tall, size, 128)
                            .transpose(2, 0, 1, 3, 4)
                            .reshape(2 * tall, width, 128),
                            dproj[: 2 if part == 0 else 0],
                        ],
                        0,
                    )
                    for din, dout, dproj in (query_slabs, text_slabs)
                ),
                sizes,
            )
            for part in range(3)
        ]
    if fold:
        ffn = [
            begin(ffn_parts[part], *text_slabs[2 * part : 2 * part + 2], sizes) for part in range(3)
        ]
    else:
        ffn = [begin_folded(part, slab, sizes) for part, slab in zip(ffn_parts, text_slabs)]
    cross_down = grad_second.reshape(row_count * QUERIES, width)
    query_first, dkv, dkv_ends, cross_dq, cross_side = cross_backward(
        row_count,
        attn_weights,
        keys,
        values,
        key_ends,
        value_ends,
        cross_q,
        cross_down,
        [text_first] + sends(ffn),
    )
    plain = not fold
    ffn = advance(ffn, bits, sizes, plain, size, cross_side)
    cross_slabs = cross_weight_grad(
        core, image_features, image_ends, dkv, dkv_ends, folds, size, sends(ffn)
    )
    if fold:
        cross = [begin(part, *cross_slabs[2 * part : 2 * part + 2], sizes) for part in range(3)]
    else:
        edges = [0, 4, 8, cross_slabs[0].shape[1]]
        cross = [
            begin_folded(
                part,
                fold_pair(part, *cross_slabs[0][:, edges[part] : edges[part + 1]], sizes),
                sizes,
            )
            for part in range(3)
        ]
    ffn = advance(ffn, bits, sizes, plain, size, cross_slabs[0])
    self_grads, self_branch, self_down, self_side = self_backward(
        attn_weights,
        norm_gains,
        mask,
        self_q,
        self_k,
        self_v,
        first_sum,
        query_first,
        text_first,
        sends(ffn + cross),
    )
    rows = [
        self_side,
        cross_side,
        query_side,
        text_side,
        query_dbias,
        text_dbias,
        query_dproj_bias,
        text_dproj_bias,
    ]
    used = sum(array.shape[0] for array in rows)
    packed = jnp.concatenate(rows + [jnp.zeros((-used % 64, 128), f32)], 0)
    states = advance(ffn + cross, bits, sizes, plain, size, self_side)
    vector = begin_whole(packed, sizes)
    half = (row_count, QUERIES, width)
    attn_slabs = attn_weight_grad(
        core,
        inputs,
        self_grads,
        [
            (self_mix, self_mix.shape),
            (self_branch, self_branch.shape),
            (first_norm, half),
            (cross_dq, cross_dq.shape),
            (cross_mix, cross_mix.shape),
            (cross_down, cross_down.shape),
        ],
        folds,
        size,
        sends(states + [vector]),
    )
    if fold:
        attn = [begin(part, *attn_slabs[2 * part : 2 * part + 2], sizes) for part in range(3)]
    else:
        attn = [
            begin_folded(part, fold_pair(part, *slab, sizes), sizes)
            for part, slab in enumerate(attn_slabs)
        ]
    ffn, cross = states[:3], states[3:6]
    states = advance(ffn + cross + [vector], bits, sizes, plain, size, attn_slabs[0])
    blocks = row_count // 4
    begun = input_gradient(attn_weights, self_grads, self_down, sends(states), 0, 1)
    *attn, vector = advance(attn + states[6:], bits, sizes, plain, size, begun)
    input_grad = input_gradient(
        attn_weights, self_grads, self_down, sends(attn), 1, blocks, [begun]
    )
    states = states[:3] + attn + states[3:6] + [vector]
    last = len(stage_orders[0])
    done = [None] * len(states)
    places = list(range(len(states)))
    after = input_grad
    while len(states) > 3:
        ready = [state[1] == last for state in states]
        states = advance(states, bits, sizes, plain, size, after)
        after = None
        for place, state, end in zip(places, states, ready):
            if end:
                done[place] = state
        places = [place for place, end in zip(places, ready) if not end]
        states = [state for state, end in zip(states, ready) if not end]
    vector = done.pop()
    ffn_sums, cross_sums = done[:3], done[6:]
    cross_grad = jnp.concatenate(cross_sums, 1)
    chunk = ffn_in.shape[2] // 3
    ffn_in_grad = jnp.concatenate([each[:, :chunk] for each in ffn_sums], 1)
    ffn_out_grad = jnp.concatenate(
        [
            each[:, chunk : 2 * chunk]
            .reshape(size, tall, -1)
            .transpose(1, 0, 2)
            .reshape(tall * size, -1)
            for each in ffn_sums
        ],
        1,
    )
    proj_grad = ffn_sums[0][:, 2 * chunk :]
    vectors = []
    start = 0
    for array, cols in zip(rows, (width,) * 4 + (ffn_in.shape[2],) * 2 + (projections.shape[2],) * 2):
        piece = vector[start : start + array.shape[0]]
        vectors.append(piece.reshape(-1, cols))
        start += array.shape[0]
    selfs, crosses, queries, texts = vectors[:4]
    gain_grad = jnp.stack([selfs[0], queries[3], queries[0], texts[0]])
    bias_grad = jnp.concatenate(
        [
            selfs[2:5],
            crosses[0:3],
            queries[2:3],
            texts[2:3],
            selfs[1:2],
            queries[4:5],
            queries[1:2],
            texts[1:2],
        ],
        0,
    )

    def mine(array):
        mats, cols = array.shape[0] // sizes["rep"], array.shape[1] // sizes["dp"]
        starts = (lax.axis_index("rep") * mats, lax.axis_index("dp") * cols)
        return lax.dynamic_slice(array, starts, (mats, cols))

    small = [
        mine(gain_grad),
        mine(bias_grad),
        mine(jnp.concatenate(vectors[4:6], 0)),
        mine(jnp.concatenate(vectors[6:8], 0)),
    ]
    attn_sums = advance(
        states, bits, sizes, plain, size, (small, cross_grad, ffn_in_grad, ffn_out_grad, proj_grad)
    )
    attn_grad = jnp.stack(attn_sums)
    return (
        layer_out,
        row_loss,
        input_grad.reshape(hidden_states.shape),
        attn_grad,
        cross_grad[None],
        ffn_in_grad[None],
        ffn_out_grad[None],
        proj_grad[None],
        small[0],
        small[1],
        small[2],
        small[3],
    )


def solution(mesh):
    placed = (
        P(("dp", "rep"), None, None),
        P(("dp", "rep"), None, None),
        P(("dp", "rep"), None),
        P(),
        P(),
        P(),
        P(),
        P(),
        P(),
        P(),
        P(),
        P(),
        P(("dp", "rep"), None, None),
    )
    sizes = dict(mesh.shape)
    return jax.shard_map(
        functools.partial(shards, sizes=sizes),
        mesh=mesh,
        in_specs=placed,
        out_specs=(
            P(("dp", "rep"), None, None),
            P(("dp", "rep")),
            P(("dp", "rep"), None, None),
            P("rep", "dp", None),
            P("rep", "dp", None),
            P("rep", "dp", None),
            P("rep", "dp", None),
            P("rep", "dp", None),
            P("rep", "dp"),
            P("rep", "dp"),
            P("rep", "dp"),
            P("rep", "dp"),
        ),
        check_vma=False,
    )
```
